32 devices in a mesh: seq: 8 (over y, x, core), batch: 4 (over z).
Axes of the slice: x: 2, y: 2, z: 4, core: 2. Of those that a mesh axis runs over, the one named last changes fastest.
Arguments:
- tokens: bfloat16 [8, 2048, 1024], P('batch', 'seq'), may hold values from -6 to 6
- cotangent: bfloat16 [8, 2048, 1024], P('batch', 'seq'), may hold values from -6 to 6
- lengths: int32 [8], P('batch'), may hold values from 128 to 2048, as said below
- gate_proj: bfloat16 [1024, 1536], P(('seq', 'batch')), may hold values from -0.1875 to 0.1875
- input_proj: bfloat16 [1024, 1536], P(('seq', 'batch')), may hold values from -0.1875 to 0.1875
- rate_proj: bfloat16 [1536, 1536], P(('seq', 'batch')), may hold values from -0.15625 to 0.15625
- entry_proj: bfloat16 [1536, 1536], P(('seq', 'batch')), may hold values from -0.15625 to 0.15625
- out_proj: bfloat16 [1536, 1024], P(('seq', 'batch')), may hold values from -0.4375 to 0.4375
- ffn_gate: bfloat16 [1024, 3072], P(('seq', 'batch')), may hold values from -0.1875 to 0.1875
- ffn_up: bfloat16 [1024, 3072], P(('seq', 'batch')), may hold values from -0.1875 to 0.1875
- ffn_down: bfloat16 [3072, 1024], P(('seq', 'batch')), may hold values from -0.21875 to 0.21875
- norm_gain: bfloat16 [1024], P(('seq', 'batch')), may hold values from 0.5 to 1.5
- ffn_gain: bfloat16 [1024], P(('seq', 'batch')), may hold values from 0.5 to 1.5
- conv_taps: bfloat16 [4, 1536], P(None, ('seq', 'batch')), may hold values from -3 to 3
- conv_bias: bfloat16 [1536], P(('seq', 'batch')), may hold values from -3 to 3
- rate_bias: bfloat16 [1536], P(('seq', 'batch')), may hold values from -4 to 4
- entry_bias: bfloat16 [1536], P(('seq', 'batch')), may hold values from -4 to 4
- decay_logit: bfloat16 [1536], P(('seq', 'batch')), may hold values from 4 to 13
Outputs:
- block_out: float32 [8, 2048, 1024], P('batch', 'seq')
- token_grad: float32 [8, 2048, 1024], P('batch', 'seq')
- grad_gate_proj: float32 [1024, 1536], P(('seq', 'batch'))
- grad_input_proj: float32 [1024, 1536], P(('seq', 'batch'))
- grad_rate_proj: float32 [1536, 1536], P(('seq', 'batch'))
- grad_entry_proj: float32 [1536, 1536], P(('seq', 'batch'))
- grad_out_proj: float32 [1536, 1024], P(('seq', 'batch'))
- grad_ffn_gate: float32 [1024, 3072], P(('seq', 'batch'))
- grad_ffn_up: float32 [1024, 3072], P(('seq', 'batch'))
- grad_ffn_down: float32 [3072, 1024], P(('seq', 'batch'))
- grad_norm_gain: float32 [1024], P(('seq', 'batch'))
- grad_ffn_gain: float32 [1024], P(('seq', 'batch'))
- grad_conv_taps: float32 [4, 1536], P(None, ('seq', 'batch'))
- grad_conv_bias: float32 [1536], P(('seq', 'batch'))
- grad_rate_bias: float32 [1536], P(('seq', 'batch'))
- grad_entry_bias: float32 [1536], P(('seq', 'batch'))
- grad_decay_logit: float32 [1536], P(('seq', 'batch'))
The draws below stay inside these ranges and needn't reach their ends.
Inputs may be any that keep to these rules, and one draw needn't show every extreme that they name: `lengths`: among the rows of each batch device (2 consecutive rows) one has length 2048.
All inputs are finite; a program needn't handle non-finite values.
Results may differ from the reference program's by a relative error of at most 0.015.
Values may be sent and summed in bfloat16 or wider, within the bound.
A program may use at most 320 MiB of HBM per device.

```python
import math
import jax
import jax.numpy as jnp
from jax import lax

D = 1024
R = 1536
F = 3072
CONV = 4
LENGTH = 2048
ROWS_DEV = 2
ROWS = 8


def draw_lengths(key, part):
    key = jax.random.fold_in(key, 11)
    first_key, second_key = jax.random.split(key)
    drawn = jax.random.randint(first_key, (ROWS,), LENGTH // 16, LENGTH + 1, dtype=jnp.int32)
    chosen = jax.random.randint(second_key, (ROWS // ROWS_DEV,), 0, ROWS_DEV, dtype=jnp.int32)
    place = jnp.arange(ROWS, dtype=jnp.int32)
    picked = jnp.repeat(chosen, ROWS_DEV)
    return jnp.where(place % ROWS_DEV == picked, LENGTH, drawn).astype(jnp.int32)


def draw_decay_logit(key, part):
    key = jax.random.fold_in(key, 23)
    least_rate, most_rate = (0.05 / LENGTH, 0.05)
    unit = jax.random.uniform(key, (R,), jnp.float32)
    rate = jnp.exp(jnp.log(least_rate) + unit * (jnp.log(most_rate) - jnp.log(least_rate)))
    return (-jnp.log(jnp.expm1(0.25 * rate))).astype(jnp.bfloat16)


def block_scale(own_key, shape, cuts, least, top_value):
    level = 1.0
    for dim, shards_of in cuts:
        heights = jax.random.uniform(jax.random.fold_in(jax.random.fold_in(own_key, 6), dim), (shards_of,), jnp.float32, least / len(cuts), top_value / len(cuts))
        level = level * jnp.repeat(jnp.exp(heights), shape[dim] // shards_of).reshape((-1,) + (1,) * (len(shape) - 1 - dim))
    return level


def scatter_about(own_key, shape, scale, most, cuts=(), kind=jnp.bfloat16):
    factor_of = block_scale(own_key, shape, cuts, -0.22, 0.18) if cuts else 1.0
    values = jax.random.normal(own_key, shape, jnp.float32) * scale * factor_of
    return jnp.minimum(jnp.maximum(values, -most), most).astype(kind)


def setup_inputs(seed: int = 0) -> dict:
    key_list = jax.random.split(jax.random.key(seed), 19)
    tokens = scatter_about(key_list[0], (ROWS, LENGTH, D), 1.0, 6.0, ((0, 4), (1, 8)))
    cotangent = scatter_about(key_list[1], (ROWS, LENGTH, D), 1.0, 6.0, ((0, 4), (1, 8)))
    lengths = draw_lengths(jax.random.fold_in(key_list[18], 71), 0)
    gate_proj = scatter_about(key_list[3], (D, R), D ** -0.5, 0.1875, ((0, 32),))
    input_proj = scatter_about(key_list[4], (D, R), D ** -0.5, 0.1875, ((0, 32),))
    rate_proj = scatter_about(key_list[5], (R, R), R ** -0.5, 0.15625, ((0, 32),))
    entry_proj = scatter_about(key_list[6], (R, R), R ** -0.5, 0.15625, ((0, 32),))
    out_proj = scatter_about(key_list[7], (R, D), (R // 8) ** -0.5, 0.4375, ((0, 32),))
    ffn_gate = scatter_about(key_list[8], (D, F), D ** -0.5, 0.1875, ((0, 32),))
    ffn_up = scatter_about(key_list[9], (D, F), D ** -0.5, 0.1875, ((0, 32),))
    ffn_down = scatter_about(key_list[10], (F, D), (F // 4) ** -0.5, 0.21875, ((0, 32),))
    norm_gain = jnp.clip(1.0 + 0.1 * jax.random.normal(key_list[11], (D,), jnp.float32), 0.5, 1.5).astype(jnp.bfloat16)
    ffn_gain = jnp.clip(1.0 + 0.1 * jax.random.normal(key_list[12], (D,), jnp.float32), 0.5, 1.5).astype(jnp.bfloat16)
    conv_taps = scatter_about(key_list[13], (CONV, R), 0.5, 3.0, ((1, 32),))
    conv_bias = scatter_about(key_list[14], (R,), 0.5, 3.0, ((0, 32),))
    rate_bias = scatter_about(key_list[15], (R,), 1.0, 4.0, ((0, 32),))
    entry_bias = scatter_about(key_list[16], (R,), 1.0, 4.0, ((0, 32),))
    decay_logit = draw_decay_logit(jax.random.fold_in(key_list[18], 71), 0)
    return {"tokens": tokens, "cotangent": cotangent, "lengths": lengths, "gate_proj": gate_proj, "input_proj": input_proj, "rate_proj": rate_proj, "entry_proj": entry_proj, "out_proj": out_proj, "ffn_gate": ffn_gate, "ffn_up": ffn_up, "ffn_down": ffn_down, "norm_gain": norm_gain, "ffn_gain": ffn_gain, "conv_taps": conv_taps, "conv_bias": conv_bias, "rate_bias": rate_bias, "entry_bias": entry_bias, "decay_logit": decay_logit}


@jax.custom_vjp
def low(v):
    return lax.optimization_barrier(v.astype(jnp.bfloat16)).astype(jnp.float32)

@jax.custom_vjp
def low_back(v):
    return v

def low_keep(v):
    return (low(v), None)

def low_pass(kept, grad):
    return (grad,)

def back_keep(v):
    return (v, None)

def back_low(kept, grad):
    return (low(grad),)
low.defvjp(low_keep, low_pass)
low_back.defvjp(back_keep, back_low)
eps = 1e-06
lru_scale = 8.0

def norm_rows(value, gain):
    return value * lax.rsqrt(lax.optimization_barrier(jnp.mean(value * value, axis=-1, keepdims=True)) + eps) * gain

def matmul(left, right):
    return jnp.einsum('btd,de->bte', left, right, precision=lax.Precision.HIGHEST)

def recur_step(state, pair):
    decay, drive = pair
    state = decay * state + drive
    return (state, state)

def forward(values, mask, params):
    gate_proj, input_proj, rate_proj, entry_proj, out_proj, ffn_gate, ffn_up, ffn_down, norm_gain, ffn_gain, conv_taps, conv_bias, rate_bias, entry_bias, decay_logit = params
    normed = low(norm_rows(values, norm_gain))
    gate_pre = low_back(matmul(normed, gate_proj))
    inner = low_back(matmul(normed, input_proj))
    padded = jnp.pad(inner, ((0, 0), (CONV - 1, 0), (0, 0)))
    conv = conv_bias + jnp.zeros_like(inner)
    for lag in range(CONV):
        start = CONV - 1 - lag
        conv = conv + conv_taps[lag] * padded[:, start:start + LENGTH]
    mixed = low(conv)
    rate = jax.nn.sigmoid(low_back(matmul(mixed, rate_proj)) + rate_bias)
    entry = jax.nn.sigmoid(low_back(matmul(mixed, entry_proj)) + entry_bias)
    log_decay = -lru_scale * jax.nn.softplus(-decay_logit) * rate
    decay = jnp.exp(mask * log_decay)
    drive = mask * jnp.sqrt(-jnp.expm1(2.0 * log_decay)) * entry * mixed
    init = jnp.zeros((values.shape[0], R), values.dtype)
    _, states = lax.scan(jax.checkpoint(recur_step), init, (jnp.swapaxes(decay, 0, 1), jnp.swapaxes(drive, 0, 1)))
    states = jnp.swapaxes(states, 0, 1)
    gated = low(states * jax.nn.gelu(gate_pre))
    first = values + low_back(matmul(gated, out_proj))
    normed_two = low(norm_rows(first, ffn_gain))
    up_pre = low_back(matmul(normed_two, ffn_gate))
    mix_pre = low_back(matmul(normed_two, ffn_up))
    hidden = low(jax.nn.gelu(up_pre) * mix_pre)
    return mask * (first + low_back(matmul(hidden, ffn_down)))

def reference(tokens, cotangent, lengths, gate_proj, input_proj, rate_proj, entry_proj, out_proj, ffn_gate, ffn_up, ffn_down, norm_gain, ffn_gain, conv_taps, conv_bias, rate_bias, entry_bias, decay_logit):
    params = tuple((item.astype(jnp.float32) for item in (gate_proj, input_proj, rate_proj, entry_proj, out_proj, ffn_gate, ffn_up, ffn_down, norm_gain, ffn_gain, conv_taps, conv_bias, rate_bias, entry_bias, decay_logit)))
    place = jnp.arange(LENGTH, dtype=jnp.int32)
    masks = (place[None, :] < lengths[:, None].astype(jnp.int32)).astype(jnp.float32)[:, :, None]
    group = math.gcd(ROWS, max(1, 4096 // LENGTH))
    count = ROWS // group
    values = tokens.astype(jnp.float32).reshape(count, group, LENGTH, D)
    cots = cotangent.astype(jnp.float32).reshape(count, group, LENGTH, D)
    masks = masks.reshape(count, group, LENGTH, 1)

    def one_group(totals, pieces):
        value, cot, mask = pieces
        result, pull = jax.vjp(lambda xv, pv: forward(xv, mask, pv), value, params)
        token_grad, grads = pull(cot)
        return (jax.tree.map(jnp.add, totals, grads), (result, token_grad))
    zeros = jax.tree.map(jnp.zeros_like, params)
    grads, (results, token_grads) = lax.scan(one_group, zeros, (values, cots, masks))
    return (results.reshape(ROWS, LENGTH, D), token_grads.reshape(ROWS, LENGTH, D), grads[0], grads[1], grads[2], grads[3], grads[4], grads[5], grads[6], grads[7], grads[8], grads[9], grads[10], grads[11], grads[12], grads[13], grads[14])
```

```python
import functools

import jax
import jax.numpy as jnp
from jax import lax
from jax.experimental import pallas as pl
from jax.experimental.pallas import tpu as pltpu
from jax.sharding import PartitionSpec as P

MICRO = 2


eps = 1e-06
lru_scale = 8.0


def from_behind(value, axis, steps):
    count = lax.axis_size(axis)
    initial, last = (max(0, -steps), min(count, count - steps))
    return lax.ppermute(value, axis, [(source, source + steps) for source in range(initial, last)])


def entering(array, axis, combine, identity):
    size, place = (lax.axis_size(axis), lax.axis_index(axis))
    everything = jax.tree.map(lambda part: lax.all_gather(part, axis), array)
    start = jax.tree.map(
        lambda part, zero: jnp.broadcast_to(jnp.asarray(zero, part.dtype), part.shape),
        array,
        identity,
    )

    def entering_turn(k, before):
        reached = k < place
        new = combine(before, jax.tree.map(lambda part: part[k], everything))
        return jax.tree.map(lambda a, b: jnp.where(reached, a, b), new, before)

    return lax.fori_loop(0, size, entering_turn, start)


def carried_in(array, axis, combine, identity):
    size, place = (lax.axis_size(axis), lax.axis_index(axis))
    everything = jax.tree.map(
        lambda part, kind: lax.all_gather(part.astype(kind), axis),
        array,
        (jnp.bfloat16, jnp.bfloat16),
    )
    start = jax.tree.map(
        lambda part, zero: jnp.broadcast_to(jnp.asarray(zero, part.dtype), part.shape),
        array,
        identity,
    )

    def carried_turn(k, before):
        at = size - 1 - k
        reached = at > place
        new = combine(
            before, jax.tree.map(lambda part, own: part[at].astype(own.dtype), everything, array)
        )
        return jax.tree.map(lambda a, b: jnp.where(reached, a, b), new, before)

    return lax.fori_loop(0, size, carried_turn, start)


def for_sending(array):

    def short(part):
        return part.astype(jnp.bfloat16) if part.dtype == jnp.float32 else part

    return jax.tree.map(short, array)


def project(left, right):
    return jnp.einsum("btd,de->bte", left, right, preferred_element_type=jnp.float32)


def project_back(left, right):
    return jnp.einsum("bte,de->btd", left, right, preferred_element_type=jnp.float32)


def outer_sum(left, right):
    return jnp.einsum("btd,bte->de", left, right, preferred_element_type=jnp.float32)


def link(earlier, later):
    return (earlier[0] * later[0], later[0] * earlier[1] + later[1])


def norm_back(value, scale, gain, grad):
    weighted = grad * gain
    gain_grad = jnp.sum(grad * value * scale, axis=(0, 1))
    spread = jnp.mean(weighted * value, axis=-1, keepdims=True)
    return (scale * weighted - value * scale**3 * spread, gain_grad)


def fetch(shards):
    (
        gate_proj,
        input_proj,
        rate_proj,
        entry_proj,
        out_proj,
        ffn_gate,
        ffn_up,
        ffn_down,
        norm_gain,
        ffn_gain,
        conv_taps,
        conv_bias,
        rate_bias,
        entry_bias,
        decay_logit,
    ) = shards
    return (
        lax.all_gather(gate_proj, ("seq", "batch"), axis=0, tiled=True),
        lax.all_gather(input_proj, ("seq", "batch"), axis=0, tiled=True),
        lax.all_gather(rate_proj, ("seq", "batch"), axis=0, tiled=True),
        lax.all_gather(entry_proj, ("seq", "batch"), axis=0, tiled=True),
        lax.all_gather(out_proj, ("seq", "batch"), axis=0, tiled=True),
        lax.all_gather(ffn_gate, ("seq", "batch"), axis=0, tiled=True),
        lax.all_gather(ffn_up, ("seq", "batch"), axis=0, tiled=True),
        lax.all_gather(ffn_down, ("seq", "batch"), axis=0, tiled=True),
        lax.all_gather(norm_gain, ("seq", "batch"), axis=0, tiled=True),
        lax.all_gather(ffn_gain, ("seq", "batch"), axis=0, tiled=True),
        lax.all_gather(conv_taps, ("seq", "batch"), axis=1, tiled=True),
        lax.all_gather(conv_bias, ("seq", "batch"), axis=0, tiled=True),
        lax.all_gather(rate_bias, ("seq", "batch"), axis=0, tiled=True),
        lax.all_gather(entry_bias, ("seq", "batch"), axis=0, tiled=True),
        lax.all_gather(decay_logit, ("seq", "batch"), axis=0, tiled=True),
    )


def forward_part(tokens, mask, weights):
    (
        gate_proj,
        input_proj,
        rate_proj,
        entry_proj,
        out_proj,
        ffn_gate,
        ffn_up,
        ffn_down,
        norm_gain,
        ffn_gain,
        conv_taps,
        conv_bias,
        rate_bias,
        entry_bias,
        decay_logit,
    ) = weights
    width = tokens.shape[1]
    taps_count = conv_taps.shape[0]
    values = tokens.astype(jnp.float32)
    scale_one = lax.rsqrt(jnp.mean(values * values, axis=-1, keepdims=True) + eps)
    normed = (values * scale_one * norm_gain).astype(jnp.bfloat16)
    gate_pre = project(normed, gate_proj)
    inner = project(normed, input_proj)
    rim = from_behind(inner[:, width - (taps_count - 1) :], "seq", 1)
    extended = jnp.concatenate([rim, inner], axis=1)
    conv = jnp.zeros_like(inner) + conv_bias
    for lag in range(taps_count):
        start = taps_count - 1 - lag
        conv = conv + conv_taps[lag] * extended[:, start : start + width]
    mixed = conv.astype(jnp.bfloat16)
    mixed_full = mixed.astype(jnp.float32)
    rate = jax.nn.sigmoid(project(mixed, rate_proj) + rate_bias)
    entry = jax.nn.sigmoid(project(mixed, entry_proj) + entry_bias)
    logit = decay_logit.astype(jnp.float32)
    log_decay = -lru_scale * jax.nn.softplus(-logit) * rate
    decay = jnp.exp(mask * log_decay)
    root = jnp.sqrt(-jnp.expm1(2.0 * log_decay))
    drive = mask * root * entry * mixed_full
    reach, local = lax.associative_scan(link, (decay, drive), axis=1)
    unit_state = (jnp.ones_like(reach[:, -1]), jnp.zeros_like(local[:, -1]))
    start_state = entering((reach[:, -1], local[:, -1]), "seq", link, unit_state)[1]
    states = local + reach * start_state[:, None]
    gated = (states * jax.nn.gelu(gate_pre)).astype(jnp.bfloat16)
    first = values + project(gated, out_proj)
    scale_two = lax.rsqrt(jnp.mean(first * first, axis=-1, keepdims=True) + eps)
    normed_two = (first * scale_two * ffn_gain).astype(jnp.bfloat16)
    up_pre = project(normed_two, ffn_gate)
    mix_pre = project(normed_two, ffn_up)
    hidden = (jax.nn.gelu(up_pre) * mix_pre).astype(jnp.bfloat16)
    block_out = mask * (first + project(hidden, ffn_down))
    saved = (
        values,
        scale_one,
        normed,
        gate_pre,
        extended,
        mixed,
        mixed_full,
        rate,
        entry,
        log_decay,
        decay,
        root,
        start_state,
        states,
        gated,
        first,
        scale_two,
        normed_two,
        up_pre,
        mix_pre,
        hidden,
    )
    return (block_out, saved)


def backward_part(cotangent, mask, weights, saved):
    (
        gate_proj,
        input_proj,
        rate_proj,
        entry_proj,
        out_proj,
        ffn_gate,
        ffn_up,
        ffn_down,
        norm_gain,
        ffn_gain,
        conv_taps,
        conv_bias,
        rate_bias,
        entry_bias,
        decay_logit,
    ) = weights
    (
        values,
        scale_one,
        normed,
        gate_pre,
        extended,
        mixed,
        mixed_full,
        rate,
        entry,
        log_decay,
        decay,
        root,
        start_state,
        states,
        gated,
        first,
        scale_two,
        normed_two,
        up_pre,
        mix_pre,
        hidden,
    ) = saved
    width = values.shape[1]
    taps_count = conv_taps.shape[0]
    cot_full = mask * cotangent.astype(jnp.float32)
    cot_low = cot_full.astype(jnp.bfloat16)
    grad_ffn_down = outer_sum(hidden, cot_low)
    d_hidden = project_back(cot_low, ffn_down)
    gelu_up, gelu_pull = jax.vjp(jax.nn.gelu, up_pre)
    d_up = gelu_pull(d_hidden * mix_pre)[0].astype(jnp.bfloat16)
    d_mix = (d_hidden * gelu_up).astype(jnp.bfloat16)
    grad_ffn_gate = outer_sum(normed_two, d_up)
    grad_ffn_up = outer_sum(normed_two, d_mix)
    d_normed_two = project_back(d_up, ffn_gate) + project_back(d_mix, ffn_up)
    back_two, grad_ffn_gain = norm_back(first, scale_two, ffn_gain, d_normed_two)
    d_first = cot_full + back_two
    d_first_low = d_first.astype(jnp.bfloat16)
    grad_out_proj = outer_sum(gated, d_first_low)
    d_gated = project_back(d_first_low, out_proj)
    gate, gate_pull = jax.vjp(jax.nn.gelu, gate_pre)
    d_states = d_gated * gate
    d_gate_pre = gate_pull(d_gated * states)[0].astype(jnp.bfloat16)
    following = jnp.concatenate([decay[:, 1:], jnp.ones_like(decay[:, :1])], axis=1)
    reach_back, local_back = lax.associative_scan(link, (following, d_states), reverse=True, axis=1)
    unit_grad = (jnp.ones_like(decay[:, 0]), jnp.zeros_like(decay[:, 0]))
    end_grad = carried_in(
        (decay[:, 0] * reach_back[:, 0], decay[:, 0] * local_back[:, 0]), "seq", link, unit_grad
    )[1]
    carried = local_back + reach_back * end_grad[:, None]
    previous = jnp.concatenate([start_state[:, None], states[:, :-1]], axis=1)
    masked_grad = mask * carried
    d_log = (
        masked_grad * previous * decay
        - masked_grad * entry * mixed_full * jnp.exp(2.0 * log_decay) / root
    )
    logit = decay_logit.astype(jnp.float32)
    grad_decay_logit = jnp.sum(lru_scale * d_log * rate * jax.nn.sigmoid(-logit), axis=(0, 1))
    d_rate_pre = -lru_scale * jax.nn.softplus(-logit) * d_log * rate * (1.0 - rate)
    d_entry_pre = masked_grad * root * mixed_full * entry * (1.0 - entry)
    grad_rate_bias = jnp.sum(d_rate_pre, axis=(0, 1))
    grad_entry_bias = jnp.sum(d_entry_pre, axis=(0, 1))
    rate_low = d_rate_pre.astype(jnp.bfloat16)
    entry_low = d_entry_pre.astype(jnp.bfloat16)
    grad_rate_proj = outer_sum(mixed, rate_low)
    grad_entry_proj = outer_sum(mixed, entry_low)
    d_mixed = (
        masked_grad * root * entry
        + project_back(rate_low, rate_proj)
        + project_back(entry_low, entry_proj)
    )
    grad_conv_bias = jnp.sum(d_mixed, axis=(0, 1))
    tap_grads = []
    for lag in range(taps_count):
        start = taps_count - 1 - lag
        tap_grads.append(jnp.sum(d_mixed * extended[:, start : start + width], axis=(0, 1)))
    grad_conv_taps = jnp.stack(tap_grads, axis=0)
    rim_back = from_behind(for_sending(d_mixed[:, : taps_count - 1]), "seq", -1)
    later = jnp.concatenate([d_mixed, rim_back], axis=1)
    d_inner = jnp.zeros_like(d_mixed)
    for lag in range(taps_count):
        d_inner = d_inner + conv_taps[lag] * later[:, lag : lag + width]
    d_inner = d_inner.astype(jnp.bfloat16)
    grad_input_proj = outer_sum(normed, d_inner)
    grad_gate_proj = outer_sum(normed, d_gate_pre)
    d_normed = project_back(d_gate_pre, gate_proj) + project_back(d_inner, input_proj)
    back_one, grad_norm_gain = norm_back(values, scale_one, norm_gain, d_normed)
    token_grad = d_first + back_one
    grads = (
        grad_gate_proj,
        grad_input_proj,
        grad_rate_proj,
        grad_entry_proj,
        grad_out_proj,
        grad_ffn_gate,
        grad_ffn_up,
        grad_ffn_down,
        grad_norm_gain,
        grad_ffn_gain,
        grad_conv_taps,
        grad_conv_bias,
        grad_rate_bias,
        grad_entry_bias,
        grad_decay_logit,
    )
    return (token_grad, grads)


def reduce_grads(totals):
    shaped = []
    for index, item in enumerate(totals):
        if index == 10:
            item = item.T
        if item.ndim == 1:
            item = item[:, None]
        shaped.append(item[None])
    spread = (
        lax.all_to_all(
            shaped[0].astype(jnp.bfloat16), "seq", split_axis=1, concat_axis=0, tiled=True
        ).astype(jnp.float32),
        lax.all_to_all(
            shaped[1].astype(jnp.bfloat16), "seq", split_axis=1, concat_axis=0, tiled=True
        ).astype(jnp.float32),
        lax.all_to_all(
            shaped[2].astype(jnp.bfloat16), "seq", split_axis=1, concat_axis=0, tiled=True
        ).astype(jnp.float32),
        lax.all_to_all(
            shaped[3].astype(jnp.bfloat16), "seq", split_axis=1, concat_axis=0, tiled=True
        ).astype(jnp.float32),
        lax.all_to_all(
            shaped[4].astype(jnp.bfloat16), "seq", split_axis=1, concat_axis=0, tiled=True
        ).astype(jnp.float32),
        lax.all_to_all(
            shaped[5].astype(jnp.bfloat16), "seq", split_axis=1, concat_axis=0, tiled=True
        ).astype(jnp.float32),
        lax.all_to_all(
            shaped[6].astype(jnp.bfloat16), "seq", split_axis=1, concat_axis=0, tiled=True
        ).astype(jnp.float32),
        lax.all_to_all(
            shaped[7].astype(jnp.bfloat16), "seq", split_axis=1, concat_axis=0, tiled=True
        ).astype(jnp.float32),
        lax.all_to_all(
            shaped[8].astype(jnp.bfloat16), "seq", split_axis=1, concat_axis=0, tiled=True
        ).astype(jnp.float32),
        lax.all_to_all(
            shaped[9].astype(jnp.bfloat16), "seq", split_axis=1, concat_axis=0, tiled=True
        ).astype(jnp.float32),
        lax.all_to_all(for_sending(shaped[10]), "seq", split_axis=1, concat_axis=0, tiled=True),
        lax.all_to_all(for_sending(shaped[11]), "seq", split_axis=1, concat_axis=0, tiled=True),
        lax.all_to_all(for_sending(shaped[12]), "seq", split_axis=1, concat_axis=0, tiled=True),
        lax.all_to_all(for_sending(shaped[13]), "seq", split_axis=1, concat_axis=0, tiled=True),
        lax.all_to_all(for_sending(shaped[14]), "seq", split_axis=1, concat_axis=0, tiled=True),
    )
    folded = [jnp.sum(piece, axis=0) for piece in spread]
    summed = (
        lax.psum_scatter(
            folded[0].astype(jnp.bfloat16), "batch", scatter_dimension=0, tiled=True
        ).astype(jnp.float32),
        lax.psum_scatter(
            folded[1].astype(jnp.bfloat16), "batch", scatter_dimension=0, tiled=True
        ).astype(jnp.float32),
        lax.psum_scatter(
            folded[2].astype(jnp.bfloat16), "batch", scatter_dimension=0, tiled=True
        ).astype(jnp.float32),
        lax.psum_scatter(
            folded[3].astype(jnp.bfloat16), "batch", scatter_dimension=0, tiled=True
        ).astype(jnp.float32),
        lax.psum_scatter(
            folded[4].astype(jnp.bfloat16), "batch", scatter_dimension=0, tiled=True
        ).astype(jnp.float32),
        lax.psum_scatter(
            folded[5].astype(jnp.bfloat16), "batch", scatter_dimension=0, tiled=True
        ).astype(jnp.float32),
        lax.psum_scatter(
            folded[6].astype(jnp.bfloat16), "batch", scatter_dimension=0, tiled=True
        ).astype(jnp.float32),
        lax.psum_scatter(
            folded[7].astype(jnp.bfloat16), "batch", scatter_dimension=0, tiled=True
        ).astype(jnp.float32),
        lax.psum_scatter(
            folded[8].astype(jnp.bfloat16), "batch", scatter_dimension=0, tiled=True
        ).astype(jnp.float32),
        lax.psum_scatter(
            folded[9].astype(jnp.bfloat16), "batch", scatter_dimension=0, tiled=True
        ).astype(jnp.float32),
        lax.psum_scatter(
            folded[10].astype(jnp.bfloat16), "batch", scatter_dimension=0, tiled=True
        ).astype(jnp.float32),
        lax.psum_scatter(
            folded[11].astype(jnp.bfloat16), "batch", scatter_dimension=0, tiled=True
        ).astype(jnp.float32),
        lax.psum_scatter(
            folded[12].astype(jnp.bfloat16), "batch", scatter_dimension=0, tiled=True
        ).astype(jnp.float32),
        lax.psum_scatter(
            folded[13].astype(jnp.bfloat16), "batch", scatter_dimension=0, tiled=True
        ).astype(jnp.float32),
        lax.psum_scatter(
            folded[14].astype(jnp.bfloat16), "batch", scatter_dimension=0, tiled=True
        ).astype(jnp.float32),
    )
    result = []
    for index, item in enumerate(summed):
        if index == 10:
            result.append(item.T)
        elif totals[index].ndim == 1:
            result.append(item[:, 0])
        else:
            result.append(item)
    return tuple(result)


def per_device(
    tokens,
    cotangent,
    lengths,
    gate_proj,
    input_proj,
    rate_proj,
    entry_proj,
    out_proj,
    ffn_gate,
    ffn_up,
    ffn_down,
    norm_gain,
    ffn_gain,
    conv_taps,
    conv_bias,
    rate_bias,
    entry_bias,
    decay_logit,
):
    shards = (
        gate_proj,
        input_proj,
        rate_proj,
        entry_proj,
        out_proj,
        ffn_gate,
        ffn_up,
        ffn_down,
        norm_gain,
        ffn_gain,
        conv_taps,
        conv_bias,
        rate_bias,
        entry_bias,
        decay_logit,
    )
    rows, width = (tokens.shape[0], tokens.shape[1])
    place = lax.axis_index("seq") * width + lax.iota(jnp.int32, width)
    mask_all = (place[None, :] < lengths[:, None]).astype(jnp.float32)[:, :, None]
    group = rows // MICRO
    totals = None
    block_parts = []
    grad_parts = []
    for part in range(MICRO):
        lower = part * group
        mask = mask_all[lower : lower + group]
        weights = fetch(shards)
        block_out, saved = forward_part(tokens[lower : lower + group], mask, weights)
        weights = fetch(shards)
        token_grad, grads = backward_part(cotangent[lower : lower + group], mask, weights, saved)
        totals = grads if part == 0 else jax.tree.map(jnp.add, totals, grads)
        block_parts.append(block_out)
        grad_parts.append(token_grad)
    summed = reduce_grads(totals)
    return (jnp.concatenate(block_parts, axis=0), jnp.concatenate(grad_parts, axis=0)) + summed


F32 = jnp.float32
BF16 = jnp.bfloat16
W = 512
SEGS = 8
CHUNK = 16
TALL = 64
LANES = 128
GELU_A = 0.7978845608028654
GELU_B = 0.044715
TAPS, CONV_BIAS, RATE_BIAS, ENTRY_BIAS, COEF, SIG = 0, 4, 5, 6, 7, 8


def dot(left, right):
    return lax.dot_general(left, right, (((1,), (0,)), ((), ())), preferred_element_type=F32)


def dot_back(left, right):
    return lax.dot_general(left, right, (((1,), (1,)), ((), ())), preferred_element_type=F32)


def dot_outer(left, right):
    return lax.dot_general(left, right, (((0,), (0,)), ((), ())), preferred_element_type=F32)


def rows_at(start, count=CHUNK):
    return pl.ds(pl.multiple_of(start, CHUNK), count)


def gelu_both(value):
    square = value * value
    inside = GELU_A * value * (1.0 + GELU_B * square)
    tanh = jnp.tanh(inside)
    half = 0.5 + 0.5 * tanh
    slope = half + 0.5 * value * (1.0 - tanh * tanh) * (GELU_A * (1.0 + 3.0 * GELU_B * square))
    return value * half, slope


def sigmoid(value):
    return 1.0 / (1.0 + jnp.exp(-value))


def one_less_exp(z, exp_z):
    series = 1.0 + z * (1 / 2 + z * (1 / 6 + z * (1 / 24 + z * (1 / 120 + z * (1 / 720)))))
    return jnp.where(z > -0.25, -z * series, 1.0 - exp_z)


def in_row(row, width, shape):
    return row + lax.broadcasted_iota(jnp.int32, shape, 0)


def each_chunk(batch, width, body, carry=0):
    per = width // CHUNK
    for b in range(batch):
        carry = lax.fori_loop(0, per, lambda i, c, b=b: body(b, i * CHUNK, b * width + i * CHUNK, c), carry)
    return carry


def each_tile(batch, width, tiles, body, carry=None):
    carries = []
    for t in range(tiles):
        kept = carry
        for b in range(batch):
            def one(i, c, t=t, b=b):
                return body(t, b, i * TALL, rows_at(b * width + i * TALL, TALL), slice(t * LANES, (t + 1) * LANES), c)
            kept = lax.fori_loop(0, width // TALL, one, 0 if kept is None else kept)
        carries.append(kept)
    return carries


def strided(b, width, step):
    return pl.ds(b * width + step, SEGS, stride=width // SEGS)


def lanes(t):
    return slice(t * LANES, (t + 1) * LANES)


def spread(ref, value):
    for t in range(ref.shape[0]):
        ref[t] = value[:, lanes(t)]


def tiled(tokens, block, index):
    return pl.BlockSpec((block // LANES, tokens, LANES), lambda j: (index(j), 0, 0))


def inverse_norm(value, depth):
    return lax.rsqrt(jnp.sum(value * value, axis=-1, keepdims=True) * (1.0 / depth) + eps)


def fold8(value):
    total = value[:8]
    for i in range(8, value.shape[0], 8):
        total = total + value[i : i + 8]
    return total


def branch_kernel(batch, width, x_ref, rim_ref, gain_ref, wg_ref, wi_ref, vec_ref,
                  gate_ref, inner_ref, mixed_ref, normed_ref, ext):
    step = pl.program_id(0)
    tokens, depth = x_ref.shape
    gain = gain_ref[:1]

    @pl.when(step == 0)
    def _():
        def norm(i, _):
            at = rows_at(i * CHUNK)
            value = x_ref[at].astype(F32)
            normed = (value * inverse_norm(value, depth) * gain).astype(BF16)
            ext[at] = normed
            normed_ref[at] = normed
            return 0
        lax.fori_loop(0, tokens // CHUNK, norm, 0)
        rim = rim_ref[...].astype(F32)
        ext[pl.ds(tokens, rim.shape[0])] = (rim * inverse_norm(rim, depth) * gain).astype(BF16)

    spread(gate_ref, dot(ext[:tokens], wg_ref[...].reshape(depth, W)))
    inner = dot(ext[...], wi_ref[...].reshape(depth, W))
    span = width + 8
    for b in range(batch):
        inner_ref[b * span : b * span + 8] = inner[tokens + 8 * b : tokens + 8 * b + 8]
        inner_ref[b * span + 8 : (b + 1) * span] = inner[b * width : (b + 1) * width]
    for b in range(batch):
        conv = vec_ref[CONV_BIAS : CONV_BIAS + 1]
        for lag in range(4):
            conv = conv + vec_ref[lag : lag + 1] * inner_ref[b * span + 8 - lag : (b + 1) * span - lag]
        mixed_ref[b * width : (b + 1) * width] = conv.astype(BF16)


def branch(tokens2, rim, gain, packed, vec, batch):
    tokens, depth = tokens2.shape
    width = tokens // batch
    full = lambda a: pl.BlockSpec(a.shape, lambda j: (0,) * a.ndim)
    r = vec.shape[1]
    col = lambda rows: pl.BlockSpec((rows, W), lambda j: (0, j))
    n = packed.shape[0]
    rows = depth // n
    return pl.pallas_call(
        functools.partial(branch_kernel, batch, width),
        grid=(r // W,),
        in_specs=[full(tokens2), full(rim), full(gain),
                  pl.BlockSpec((n, rows, W), lambda j: (0, GATE_AT // rows + j, 0)),
                  pl.BlockSpec((n, rows, W), lambda j: (0, INPUT_AT // rows + j, 0)),
                  col(vec.shape[0])],
        out_specs=[tiled(tokens, W, lambda j: j), col(tokens + 8 * batch), col(tokens), pl.BlockSpec((tokens, depth), lambda j: (0, 0))],
        out_shape=[jax.ShapeDtypeStruct((r // LANES, tokens, LANES), F32), jax.ShapeDtypeStruct((tokens + 8 * batch, r), F32),
                   jax.ShapeDtypeStruct((tokens, r), BF16), jax.ShapeDtypeStruct((tokens, depth), BF16)],
        scratch_shapes=[pltpu.VMEM((tokens + 8 * batch, depth), BF16)],
        compiler_params=pltpu.CompilerParams(vmem_limit_bytes=50 << 20),
    )(tokens2, rim, gain, packed, packed, vec)


def gates_kernel(batch, width, info_ref, mixed_ref, wr_ref, we_ref, vec_ref,
                 rate_ref, entry_ref, decay_ref, drive_ref, pseg_ref, hseg_ref, tot_ref):
    step = pl.program_id(0)
    r = mixed_ref.shape[1]
    spread(rate_ref, dot(mixed_ref[...], wr_ref[...].reshape(r, W)))
    spread(entry_ref, dot(mixed_ref[...], we_ref[...].reshape(r, W)))
    tiles = W // LANES

    def gating(t, b, spot, at, cols, _):
        rate = sigmoid(rate_ref[t, at] + vec_ref[RATE_BIAS : RATE_BIAS + 1, cols])
        entry = sigmoid(entry_ref[t, at] + vec_ref[ENTRY_BIAS : ENTRY_BIAS + 1, cols])
        log_decay = vec_ref[COEF : COEF + 1, cols] * rate
        z = 2.0 * log_decay
        root = jnp.sqrt(one_less_exp(z, jnp.exp(z)))
        valid = in_row(spot, width, rate.shape) < info_ref[b]
        rate_ref[t, at] = rate
        entry_ref[t, at] = entry
        decay_ref[t, at] = jnp.where(valid, jnp.exp(log_decay), 1.0)
        mixed = mixed_ref[at, pl.ds(pl.multiple_of(step * W + t * LANES, LANES), LANES)].astype(F32)
        drive_ref[t, at] = jnp.where(valid, root * entry * mixed, 0.0)
        return 0

    each_tile(batch, width, tiles, gating)
    tot_ref[...] = jnp.zeros_like(tot_ref)
    for t in range(tiles):
        cols = lanes(t)
        for b in range(batch):
            prod = jnp.ones((SEGS, LANES), F32)
            state = jnp.zeros((SEGS, LANES), F32)
            for s in range(width // SEGS):
                at = strided(b, width, s)
                a = decay_ref[t, at]
                state = a * state + drive_ref[t, at]
                prod = prod * a
            pseg_ref[b * SEGS : (b + 1) * SEGS, cols] = prod
            hseg_ref[b * SEGS : (b + 1) * SEGS, cols] = state
            whole, end = prod[:1], state[:1]
            for i in range(1, SEGS):
                whole = whole * prod[i : i + 1]
                end = prod[i : i + 1] * end + state[i : i + 1]
            tot_ref[b : b + 1, cols] = whole
            tot_ref[batch + b : batch + b + 1, cols] = end


def gates(info, mixed, packed, vec, batch):
    tokens, r = mixed.shape
    width = tokens // batch
    n = packed.shape[0]
    rows = r // n
    col = lambda count: pl.BlockSpec((count, W), lambda j: (0, j))
    big = jax.ShapeDtypeStruct((r // LANES, tokens, LANES), F32)
    seg = jax.ShapeDtypeStruct((batch * SEGS, r), F32)
    return pl.pallas_call(
        functools.partial(gates_kernel, batch, width),
        grid=(r // W,),
        in_specs=[pl.BlockSpec(memory_space=pltpu.SMEM), pl.BlockSpec((tokens, r), lambda j: (0, 0)),
                  pl.BlockSpec((n, rows, W), lambda j: (0, RATE_AT // rows + j, 0)),
                  pl.BlockSpec((n, rows, W), lambda j: (0, ENTRY_AT // rows + j, 0)),
                  col(vec.shape[0])],
        out_specs=[tiled(tokens, W, lambda j: j)] * 4 + [col(batch * SEGS)] * 2 + [col(8)],
        out_shape=[big] * 4 + [seg] * 2 + [jax.ShapeDtypeStruct((8, r), F32)],
        compiler_params=pltpu.CompilerParams(vmem_limit_bytes=50 << 20),
    )(info, mixed, packed, packed, vec)


def exchange_kernel(n, x_ref, o_ref, send, recv, own):
    me, z = lax.axis_index("seq"), lax.axis_index("batch")
    bar = pltpu.get_barrier_semaphore()
    for k in range(1, n):
        pl.semaphore_signal(bar, inc=1, device_id=(lax.rem(me + k, n), z), device_id_type=MESH)
    pl.semaphore_wait(bar, n - 1)
    mine = pltpu.make_async_copy(x_ref, o_ref.at[me], own)
    mine.start()
    copies = []
    for k in range(1, n):
        copies.append(pltpu.make_async_remote_copy(
            x_ref, o_ref.at[me], send.at[k], recv.at[k],
            device_id=(lax.rem(me + k, n), z), device_id_type=MESH))
    for copy in copies:
        copy.start()
    mine.wait()
    for copy in copies:
        copy.wait()


def exchange(value, n, ident):
    D = pltpu.SemaphoreType.DMA
    return pl.pallas_call(
        functools.partial(exchange_kernel, n),
        out_shape=jax.ShapeDtypeStruct((n,) + value.shape, value.dtype),
        in_specs=[pl.BlockSpec(memory_space=pltpu.VMEM)],
        out_specs=pl.BlockSpec(memory_space=pltpu.VMEM),
        scratch_shapes=[D((n,)), D((n,)), D],
        compiler_params=pltpu.CompilerParams(collective_id=ident, has_side_effects=True),
    )(value)


def states_kernel(batch, width, n_seq, info_ref, decay_ref, drive_ref, gate_ref, pseg_ref, hseg_ref, all_ref,
                  x_ref, wo_ref, gain_ref, states_ref, sstart_ref, gated_ref, first_ref, normed_ref):
    step = pl.program_id(0)
    tokens, depth = x_ref.shape
    r = gated_ref.shape[1]
    parts = r // W

    @pl.when(step < parts)
    def _():
        me = info_ref[batch]
        for b in range(batch):
            start = jnp.zeros((1, W), F32)
            for k in range(n_seq):
                new = all_ref[k, b : b + 1] * start + all_ref[k, batch + b : batch + b + 1]
                start = jnp.where(k < me, new, start)
            for i in range(SEGS):
                at = b * SEGS + i
                sstart_ref[at : at + 1] = start
                start = pseg_ref[at : at + 1] * start + hseg_ref[at : at + 1]
            for t in range(W // LANES):
                state = sstart_ref[b * SEGS : (b + 1) * SEGS, lanes(t)]
                for s in range(width // SEGS):
                    at = strided(b, width, s)
                    state = decay_ref[t, at] * state + drive_ref[t, at]
                    states_ref[t, at] = state
        j = jnp.minimum(step, parts - 1)

        def gating(t, b, spot, at, cols, _):
            gate = gelu_both(gate_ref[t, at])[0]
            gated_ref[at, pl.ds(pl.multiple_of(j * W + t * LANES, LANES), LANES)] = (states_ref[t, at] * gate).astype(BF16)
            return 0
        each_tile(batch, width, W // LANES, gating)

    for half in range(depth // W):
        @pl.when(step == parts + half)
        def _():
            cols = slice(half * W, (half + 1) * W)
            first_ref[:, cols] = x_ref[:, cols].astype(F32) + dot(gated_ref[...], wo_ref[...].reshape(r, W))

    @pl.when(step == pl.num_programs(0) - 1)
    def _():
        def norm(i, _):
            at = rows_at(i * CHUNK)
            value = first_ref[at]
            normed_ref[at] = (value * inverse_norm(value, depth) * gain_ref[:1]).astype(BF16)
            return 0
        lax.fori_loop(0, tokens // CHUNK, norm, 0)


def states_and_first(info, decay, drive, gate_pre, pseg, hseg, everyone, tokens2, packed, gain, batch):
    tokens, depth = tokens2.shape
    r = pseg.shape[1]
    width = tokens // batch
    n = packed.shape[0]
    rows = r // n
    parts = r // W
    col = lambda count: pl.BlockSpec((count, W), lambda j: (0, jnp.minimum(j, parts - 1)))
    full = lambda shape: pl.BlockSpec(shape, lambda j: (0,) * len(shape))
    return pl.pallas_call(
        functools.partial(states_kernel, batch, width, everyone.shape[0]),
        grid=(parts + depth // W,),
        in_specs=[pl.BlockSpec(memory_space=pltpu.SMEM)] + [tiled(tokens, W, lambda j: jnp.minimum(j, parts - 1))] * 3 + [
                  col(batch * SEGS), col(batch * SEGS),
                  pl.BlockSpec((everyone.shape[0], 8, W), lambda j: (0, 0, jnp.minimum(j, parts - 1))),
                  full(tokens2.shape),
                  pl.BlockSpec((n, rows, W), lambda j: (0, OUT_AT // rows + jnp.maximum(j - parts, 0), 0)),
                  full(gain.shape)],
        out_specs=[tiled(tokens, W, lambda j: jnp.minimum(j, parts - 1)), col(batch * SEGS), full((tokens, r)),
                   full((tokens, depth)), full((tokens, depth))],
        out_shape=[jax.ShapeDtypeStruct((r // LANES, tokens, LANES), F32), jax.ShapeDtypeStruct((batch * SEGS, r), F32),
                   jax.ShapeDtypeStruct((tokens, r), BF16), jax.ShapeDtypeStruct((tokens, depth), F32),
                   jax.ShapeDtypeStruct((tokens, depth), BF16)],
        compiler_params=pltpu.CompilerParams(vmem_limit_bytes=50 << 20),
    )(info, decay, drive, gate_pre, pseg, hseg, everyone, tokens2, packed, gain)


def put(stage, sem, slot, dst, value, used):
    copy = pltpu.make_async_copy(stage.at[slot], dst, sem.at[slot])
    if used is True:
        copy.wait()
    elif used is not False:
        pl.when(used)(copy.wait)
    stage[slot] = value
    copy.start()


def ffn_kernel(batch, width, info_ref, first_ref, normed_ref, cot_ref, gain_ref, wg_ref, wu_ref, wd_ref,
               out_ref, dfirst_ref, dlow_ref, ggain_ref, grad_ref,
               low, dh, hid, acc, dn, up_s, mix_s, du, dm, nt, ltr, stage, dstage, sem, dsem):
    step = pl.program_id(0)
    tokens, depth = first_ref.shape
    n = grad_ref.shape[0]
    f = hid.shape[1]
    wide = wd_ref.shape[0] * wd_ref.shape[1] // 2
    nd, nw = f // wide, f // W
    rows = depth // n
    drows = wd_ref.shape[1] // 2

    @pl.when(step == 0)
    def _():
        def masked(b, spot, row, _):
            at = rows_at(row)
            value = cot_ref[at]
            valid = in_row(spot, width, value.shape) < info_ref[b]
            low[at] = jnp.where(valid, value.astype(F32), 0.0).astype(BF16)
            return 0
        each_chunk(batch, width, masked)

    @pl.when(step < nd)
    def _():
        here = pl.ds(pl.multiple_of(jnp.minimum(step, nd - 1) * wide, wide), wide)
        total = dot_back(low[:, :W], wd_ref[:, :drows].reshape(wide, W))
        dh[:, here] = total + dot_back(low[:, W:], wd_ref[:, drows:].reshape(wide, W))

    @pl.when(jnp.logical_and(step >= nd, step < nd + nw))
    def _():
        j = step - nd
        here = pl.ds(pl.multiple_of(j * W, W), W)
        wg = wg_ref[...].reshape(depth, W)
        wu = wu_ref[...].reshape(depth, W)
        up_s[...] = dot(normed_ref[...], wg)
        mix_s[...] = dot(normed_ref[...], wu)

        def gating(i, _):
            at = rows_at(i * CHUNK)
            gate, slope = gelu_both(up_s[at])
            mix, d = mix_s[at], dh[at, here]
            hid[at, here] = (gate * mix).astype(BF16)
            du[at] = (d * mix * slope).astype(BF16)
            dm[at] = (d * gate).astype(BF16)
            return 0
        lax.fori_loop(0, tokens // CHUNK, gating, 0)
        more = dot_back(du[...], wg) + dot_back(dm[...], wu)

        @pl.when(j == 0)
        def _():
            dn[...] = more

        @pl.when(j > 0)
        def _():
            dn[...] += more
        for which, low_grad in ((0, du), (1, dm)):
            value = dot_outer(normed_ref[...], low_grad[...]).astype(BF16).reshape(n, rows, W)
            dst = grad_ref.at[:, pl.ds(pl.multiple_of(which * nw * rows + j * rows, rows), rows)]
            put(stage, sem, which, dst, value, j > 0)

    @pl.when(step >= nd + nw)
    def _():
        k = step - nd - nw
        here = pl.ds(pl.multiple_of(k * wide, wide), wide)
        block = hid[:, here]
        for half in range(2):
            cols = slice(half * W, (half + 1) * W)
            more = dot(block, wd_ref[:, half * drows : (half + 1) * drows].reshape(wide, W))

            @pl.when(k == 0)
            def _():
                acc[:, cols] = more

            @pl.when(k > 0)
            def _():
                acc[:, cols] += more
            value = dot_outer(block, low[:, cols]).astype(BF16).reshape(wide // drows, drows, W)
            dst = grad_ref.at[pl.ds(k * (wide // drows), wide // drows),
                              pl.ds(2 * nw * rows + half * drows, drows)]
            put(dstage, dsem, half, dst, value, k > 0)

    @pl.when(step == pl.num_programs(0) - 1)
    def _():
        def finish(b, spot, row, total):
            at = rows_at(row)
            first, cot = first_ref[at], low[at].astype(F32)
            valid = in_row(spot, width, first.shape) < info_ref[b]
            out_ref[at] = jnp.where(valid, first + acc[at], 0.0)
            grad = dn[at]
            scale = inverse_norm(first, depth)
            weighted = grad * gain_ref[:1]
            spread = jnp.sum(weighted * first, axis=-1, keepdims=True) * (1.0 / depth)
            back = cot + scale * weighted - first * (scale * scale * scale * spread)
            dfirst_ref[at] = back
            dlow_ref[at] = back.astype(BF16)
            return total + fold8(grad * first * scale)
        total = each_chunk(batch, width, finish, jnp.zeros((8, depth), F32))
        ggain_ref[...] = total
        for which in range(2):
            pltpu.make_async_copy(stage.at[which], grad_ref.at[:, pl.ds(0, rows)], sem.at[which]).wait()
            pltpu.make_async_copy(dstage.at[which], grad_ref.at[pl.ds(0, wide // drows), pl.ds(0, drows)], dsem.at[which]).wait()


def feed_forward(info, first, normed_two, cot, gain, packed, f, batch):
    tokens, depth = first.shape
    width = tokens // batch
    n = packed.shape[0]
    rows, drows = depth // n, f // n
    group = 8
    wide = group * drows
    nd, nw = f // wide, f // W
    full = lambda shape: pl.BlockSpec(shape, lambda j: (0,) * len(shape))
    clamp = lambda j, low, count: jnp.clip(j - low, 0, count - 1)
    down = FFN_DOWN_AT // (2 * drows)

    def down_block(j):
        return (jnp.where(j < nd, jnp.minimum(j, nd - 1), clamp(j, nd + nw, nd)), down, 0)
    vm = pltpu.VMEM
    return pl.pallas_call(
        functools.partial(ffn_kernel, batch, width),
        grid=(nd + nw + nd,),
        in_specs=[pl.BlockSpec(memory_space=pltpu.SMEM), full(first.shape), full(normed_two.shape), full(cot.shape),
                  full(gain.shape),
                  pl.BlockSpec((n, rows, W), lambda j: (0, FFN_GATE_AT // rows + clamp(j, nd, nw), 0)),
                  pl.BlockSpec((n, rows, W), lambda j: (0, FFN_UP_AT // rows + clamp(j, nd, nw), 0)),
                  pl.BlockSpec((group, 2 * drows, W), down_block)],
        out_specs=[full((tokens, depth))] * 3 + [full((8, depth)), pl.BlockSpec(memory_space=pl.ANY)],
        out_shape=[jax.ShapeDtypeStruct((tokens, depth), F32), jax.ShapeDtypeStruct((tokens, depth), F32),
                   jax.ShapeDtypeStruct((tokens, depth), BF16), jax.ShapeDtypeStruct((8, depth), F32),
                   jax.ShapeDtypeStruct((n, 2 * nw * rows + 2 * drows, W), BF16)],
        scratch_shapes=[vm((tokens, depth), BF16), vm((tokens, f), F32), vm((tokens, f), BF16), vm((tokens, depth), F32),
                        vm((tokens, depth), F32), vm((tokens, W), F32), vm((tokens, W), F32), vm((tokens, W), BF16),
                        vm((tokens, W), BF16), vm((8, 128), BF16), vm((8, 128), BF16),
                        vm((2, n, rows, W), BF16), vm((2, group, drows, W), BF16),
                        pltpu.SemaphoreType.DMA((2,)), pltpu.SemaphoreType.DMA((2,))],
        compiler_params=pltpu.CompilerParams(vmem_limit_bytes=60 << 20),
    )(info, first, normed_two, cot, gain, packed, packed, packed)


def unproject_kernel(batch, width, dlow_ref, wo_ref, gated_ref, gate_ref, states_ref, decay_ref, pseg_ref,
                     dstates_ref, dgate_ref, gseg_ref, gtot_ref, grad_ref, stage, sem):
    step = pl.program_id(0)
    tokens, depth = dlow_ref.shape
    orows = wo_ref.shape[1] // 2
    group = wo_ref.shape[0]
    wide = group * orows
    dg = dot_back(dlow_ref[:, :W], wo_ref[:, :orows].reshape(wide, W))
    spread(dstates_ref, dg + dot_back(dlow_ref[:, W:], wo_ref[:, orows:].reshape(wide, W)))

    def gating(t, b, spot, at, cols, _):
        gate, slope = gelu_both(gate_ref[t, at])
        d = dstates_ref[t, at]
        dstates_ref[t, at] = d * gate
        dgate_ref[at, cols] = (d * states_ref[t, at] * slope).astype(BF16)
        return 0
    each_tile(batch, width, wide // LANES, gating)
    for half in range(2):
        value = dot_outer(gated_ref[...], dlow_ref[:, half * W : (half + 1) * W]).astype(BF16)
        dst = grad_ref.at[pl.ds(step * group, group), pl.ds(OUT_AT + half * orows, orows)]
        put(stage, sem, half, dst, value.reshape(group, orows, W), step > 0)
    gtot_ref[...] = jnp.zeros_like(gtot_ref)
    for t in range(wide // LANES):
        cols = lanes(t)
        for b in range(batch):
            grad = jnp.zeros((SEGS, LANES), F32)
            for s in reversed(range(width // SEGS)):
                at = strided(b, width, s)
                grad = decay_ref[t, at] * (dstates_ref[t, at] + grad)
            gseg_ref[b * SEGS : (b + 1) * SEGS, cols] = grad
            whole = grad[SEGS - 1 :]
            for i in reversed(range(SEGS - 1)):
                whole = grad[i : i + 1] + pseg_ref[b * SEGS + i : b * SEGS + i + 1, cols] * whole
            gtot_ref[b : b + 1, cols] = whole

    @pl.when(step == pl.num_programs(0) - 1)
    def _():
        for half in range(2):
            pltpu.make_async_copy(stage.at[half], grad_ref.at[pl.ds(0, group), pl.ds(OUT_AT, orows)], sem.at[half]).wait()


def unproject(dlow, packed, gated, gate_pre, states, decay, pseg, batch):
    tokens, r = gated.shape
    depth = dlow.shape[1]
    width = tokens // batch
    n = packed.shape[0]
    orows = r // n
    group = n // 2
    wide = group * orows
    col = lambda count: pl.BlockSpec((count, wide), lambda j: (0, j))
    return pl.pallas_call(
        functools.partial(unproject_kernel, batch, width),
        grid=(n // group,),
        in_specs=[pl.BlockSpec((tokens, depth), lambda j: (0, 0)),
                  pl.BlockSpec((group, 2 * orows, W), lambda j: (j, OUT_AT // (2 * orows), 0)),
                  col(tokens)] + [tiled(tokens, wide, lambda j: j)] * 3 + [col(batch * SEGS)],
        out_specs=[tiled(tokens, wide, lambda j: j), col(tokens), col(batch * SEGS), col(8), pl.BlockSpec(memory_space=pl.ANY)],
        out_shape=[jax.ShapeDtypeStruct((r // LANES, tokens, LANES), F32), jax.ShapeDtypeStruct((tokens, r), BF16),
                   jax.ShapeDtypeStruct((batch * SEGS, r), F32), jax.ShapeDtypeStruct((8, r), F32),
                   jax.ShapeDtypeStruct((n, REC_ROWS, W), BF16)],
        scratch_shapes=[pltpu.VMEM((2, group, orows, W), BF16),
                        pltpu.SemaphoreType.DMA((2,))],
        compiler_params=pltpu.CompilerParams(vmem_limit_bytes=60 << 20),
    )(dlow, packed, gated, gate_pre, states, decay, pseg)


def recur_kernel(batch, width, n_seq, info_ref, mixed_ref, decay_ref, dstates_ref, states_ref, rate_ref, entry_ref,
                 pseg_ref, gseg_ref, sstart_ref, pall_ref, gall_ref, vec_ref, wr_ref, we_ref, _,
                 dmixed_ref, sums_ref, grad_ref, carried, across, gstart, rl, el, direct, stage, sem):
    step = pl.program_id(0)
    tokens, r = mixed_ref.shape
    n = grad_ref.shape[0]
    rows = r // n
    parts = r // W
    group = wr_ref.shape[0]
    wide = group * rows

    @pl.when(step < parts)
    def _():
        me = info_ref[batch]
        for b in range(batch):
            grad = jnp.zeros((1, W), F32)
            for k in reversed(range(n_seq)):
                new = pall_ref[k, b : b + 1] * grad + gall_ref[k, b : b + 1]
                grad = jnp.where(k > me, new, grad)
            for i in reversed(range(SEGS)):
                at = b * SEGS + i
                gstart[i : i + 1] = grad
                grad = pseg_ref[at : at + 1] * grad + gseg_ref[at : at + 1]
            for t in range(W // LANES):
                grad = gstart[:, lanes(t)]
                for s in reversed(range(width // SEGS)):
                    at = strided(b, width, s)
                    total = dstates_ref[t, at] + grad
                    carried[t, at] = total
                    grad = decay_ref[t, at] * total
                    before = states_ref[t, strided(b, width, s - 1)] if s else sstart_ref[b * SEGS : (b + 1) * SEGS, lanes(t)]
                    across[t, at] = grad * before
        j = jnp.minimum(step, parts - 1)
        here = pl.ds(pl.multiple_of(j * W, W), W)

        def gating(t, b, spot, at, cols, sums):
            tile = pl.ds(pl.multiple_of(j * W + t * LANES, LANES), LANES)
            coef = vec_ref[COEF : COEF + 1, cols]
            rate, entry = rate_ref[t, at], entry_ref[t, at]
            valid = in_row(spot, width, rate.shape) < info_ref[b]
            grad = jnp.where(valid, carried[t, at], 0.0)
            z = 2.0 * coef * rate
            exp_z = jnp.exp(z)
            under = one_less_exp(z, exp_z)
            inverse = lax.rsqrt(under)
            root = under * inverse
            mixed = mixed_ref[at, tile].astype(F32)
            part = grad * entry
            d_log = jnp.where(valid, across[t, at], 0.0) - part * mixed * exp_z * inverse
            d_rate = coef * d_log * rate * (1.0 - rate)
            straight = part * root
            d_entry = straight * mixed * (1.0 - entry)
            direct[at, tile] = straight
            rl[at, tile] = d_rate.astype(BF16)
            el[at, tile] = d_entry.astype(BF16)
            return (sums[0] + fold8(d_log * rate), sums[1] + fold8(d_rate), sums[2] + fold8(d_entry))
        zero = jnp.zeros((8, LANES), F32)
        sums = each_tile(batch, width, W // LANES, gating, (zero, zero, zero))
        sums_ref[...] = jnp.zeros_like(sums_ref)
        for t, kept in enumerate(sums):
            for line in range(3):
                factor = 8.0 * vec_ref[SIG : SIG + 1, lanes(t)] if line == 0 else 1.0
                sums_ref[line : line + 1, lanes(t)] = factor * jnp.sum(kept[line], axis=0, keepdims=True)
        for which, low_grad, base in ((0, rl, RATE_AT), (1, el, ENTRY_AT)):
            value = dot_outer(mixed_ref[...], low_grad[:, here]).astype(BF16).reshape(n, rows, W)
            dst = grad_ref.at[:, pl.ds(pl.multiple_of(base + j * rows, 16), rows)]
            put(stage, sem, which, dst, value, step > 0)

    @pl.when(step >= parts)
    def _():
        k = jnp.maximum(step - parts, 0)
        here = pl.ds(pl.multiple_of(k * wide, wide), wide)
        total = direct[:, here]
        for p in range(parts):
            cols = slice(p * W, (p + 1) * W)
            total = total + dot_back(rl[:, cols], wr_ref[:, p * rows : (p + 1) * rows].reshape(wide, W))
            total = total + dot_back(el[:, cols], we_ref[:, p * rows : (p + 1) * rows].reshape(wide, W))
        dmixed_ref[...] = total

    @pl.when(step == pl.num_programs(0) - 1)
    def _():
        for which in range(2):
            pltpu.make_async_copy(stage.at[which], grad_ref.at[:, pl.ds(0, rows)], sem.at[which]).wait()


def recur_back(info, mixed, decay, dstates, states, rate, entry, pseg, gseg, sstart, pall, gall, vec, packed, grad, batch):
    tokens, r = mixed.shape
    width = tokens // batch
    n = packed.shape[0]
    rows = r // n
    parts = r // W
    group = n // 2
    wide = group * rows
    n_seq = pall.shape[0]
    col = lambda count: pl.BlockSpec((count, W), lambda j: (0, jnp.minimum(j, parts - 1)))
    over = pl.BlockSpec((n_seq, 8, W), lambda j: (0, 0, jnp.minimum(j, parts - 1)))
    later = lambda j: jnp.maximum(j - parts, 0)
    vm = pltpu.VMEM
    return pl.pallas_call(
        functools.partial(recur_kernel, batch, width, n_seq),
        grid=(parts + n // group,),
        in_specs=[pl.BlockSpec(memory_space=pltpu.SMEM), pl.BlockSpec((tokens, r), lambda j: (0, 0))]
        + [tiled(tokens, W, lambda j: jnp.minimum(j, parts - 1))] * 5 + [col(batch * SEGS)] * 3 + [over, over, col(vec.shape[0]),
            pl.BlockSpec((group, parts * rows, W), lambda j: (later(j), RATE_AT // (parts * rows), 0)),
            pl.BlockSpec((group, parts * rows, W), lambda j: (later(j), ENTRY_AT // (parts * rows), 0)),
            pl.BlockSpec(memory_space=pl.ANY)],
        out_specs=[pl.BlockSpec((tokens, wide), lambda j: (0, later(j))), col(8), pl.BlockSpec(memory_space=pl.ANY)],
        out_shape=[jax.ShapeDtypeStruct((tokens, r), F32), jax.ShapeDtypeStruct((8, r), F32),
                   jax.ShapeDtypeStruct(grad.shape, grad.dtype)],
        input_output_aliases={15: 2},
        scratch_shapes=[vm((W // LANES, tokens, LANES), F32), vm((W // LANES, tokens, LANES), F32), vm((SEGS, W), F32), vm((tokens, r), BF16),
                        vm((tokens, r), BF16), vm((tokens, r), F32), vm((2, n, rows, W), BF16),
                        pltpu.SemaphoreType.DMA((2,))],
        compiler_params=pltpu.CompilerParams(vmem_limit_bytes=60 << 20),
    )(info, mixed, decay, dstates, states, rate, entry, pseg, gseg, sstart, pall, gall, vec, packed, packed, grad)


def entry_kernel(batch, width, dmixed_ref, rim_ref, inner_ref, dgate_ref, normed_ref, wg_ref, wi_ref, vec_ref,
                 x_ref, dfirst_ref, gain_ref, _, sums_ref, token_ref, ggain_ref, grad_ref, ext, di, dn, stage, sem):
    step = pl.program_id(0)
    tokens, depth = x_ref.shape
    n = grad_ref.shape[0]
    rows = depth // n
    span = width + 8
    sums_ref[...] = jnp.zeros_like(sums_ref)
    for b in range(batch):
        ext[b * span : b * span + width] = dmixed_ref[b * width : (b + 1) * width]
        ext[b * span + width : (b + 1) * span] = rim_ref[b * 8 : (b + 1) * 8]
    for b in range(batch):
        total = jnp.zeros((width, W), F32)
        for lag in range(4):
            total = total + vec_ref[lag : lag + 1] * ext[b * span + lag : b * span + lag + width]
        di[b * width : (b + 1) * width] = total.astype(BF16)
        d_mixed = dmixed_ref[b * width : (b + 1) * width]
        for lag in range(4):
            product = d_mixed * inner_ref[b * span + 8 - lag : (b + 1) * span - lag]
            sums_ref[lag : lag + 1] += jnp.sum(product, axis=0, keepdims=True)
        sums_ref[4:5] += jnp.sum(d_mixed, axis=0, keepdims=True)
    wg = wg_ref[...].reshape(depth, W)
    wi = wi_ref[...].reshape(depth, W)
    more = dot_back(dgate_ref[...], wg) + dot_back(di[...], wi)

    @pl.when(step == 0)
    def _():
        dn[...] = more

    @pl.when(step > 0)
    def _():
        dn[...] += more
    for which, low_grad, base in ((0, dgate_ref, GATE_AT), (1, di, INPUT_AT)):
        value = dot_outer(normed_ref[...], low_grad[...]).astype(BF16).reshape(n, rows, W)
        dst = grad_ref.at[:, pl.ds(pl.multiple_of(base + step * rows, 16), rows)]
        put(stage, sem, which, dst, value, step > 0)

    @pl.when(step == pl.num_programs(0) - 1)
    def _():
        def finish(i, total):
            at = rows_at(i * CHUNK)
            value, grad = x_ref[at].astype(F32), dn[at]
            scale = inverse_norm(value, depth)
            weighted = grad * gain_ref[:1]
            spread = jnp.sum(weighted * value, axis=-1, keepdims=True) * (1.0 / depth)
            token_ref[at] = dfirst_ref[at] + scale * weighted - value * (scale * scale * scale * spread)
            return total + fold8(grad * value * scale)
        ggain_ref[...] = lax.fori_loop(0, tokens // CHUNK, finish, jnp.zeros((8, depth), F32))
        for which in range(2):
            pltpu.make_async_copy(stage.at[which], grad_ref.at[:, pl.ds(0, rows)], sem.at[which]).wait()


def entry_back(dmixed, rim, inner, dgate, normed, packed, vec, tokens2, dfirst, gain, grad, batch):
    tokens, r = dmixed.shape
    depth = tokens2.shape[1]
    width = tokens // batch
    n = packed.shape[0]
    rows = depth // n
    col = lambda count: pl.BlockSpec((count, W), lambda j: (0, j))
    full = lambda shape: pl.BlockSpec(shape, lambda j: (0,) * len(shape))
    vm = pltpu.VMEM
    return pl.pallas_call(
        functools.partial(entry_kernel, batch, width),
        grid=(r // W,),
        in_specs=[col(tokens), col(rim.shape[0]), col(inner.shape[0]), col(tokens), full(normed.shape),
                  pl.BlockSpec((n, rows, W), lambda j: (0, GATE_AT // rows + j, 0)),
                  pl.BlockSpec((n, rows, W), lambda j: (0, INPUT_AT // rows + j, 0)),
                  col(vec.shape[0]), full(tokens2.shape), full(dfirst.shape), full(gain.shape),
                  pl.BlockSpec(memory_space=pl.ANY)],
        out_specs=[col(8), full((tokens, depth)), full((8, depth)), pl.BlockSpec(memory_space=pl.ANY)],
        out_shape=[jax.ShapeDtypeStruct((8, r), F32), jax.ShapeDtypeStruct((tokens, depth), F32),
                   jax.ShapeDtypeStruct((8, depth), F32), jax.ShapeDtypeStruct(grad.shape, grad.dtype)],
        input_output_aliases={11: 3},
        scratch_shapes=[vm((tokens + 8 * batch, W), F32), vm((tokens, W), BF16), vm((tokens, depth), F32),
                        vm((2, n, rows, W), BF16), pltpu.SemaphoreType.DMA((2,))],
        compiler_params=pltpu.CompilerParams(vmem_limit_bytes=60 << 20),
    )(dmixed, rim, inner, dgate, normed, packed, packed, vec, tokens2, dfirst, gain, grad)


MESH = pl.DeviceIdType.MESH
ROUTES = (("z", "x", "y"), ("z", "y", "x"), ("x", "z", "y"), ("y", "z", "x"))
ZN = 4
STG = 4
SEM = pltpu.SemaphoreType.DMA


def place():
    s = lax.axis_index("seq")
    return lax.rem(s, 2), lax.rem(lax.div(s, 2), 2), lax.div(s, 4), lax.axis_index("batch")


def flip(value, by):
    return 1 - value if by else value


def seq_of(y, x, c):
    return (y * 2 + x) * 2 + c


def far(z, j):
    if j == ZN - 1:
        return z
    found = None
    for here in range(ZN):
        others = sorted((q for q in range(ZN) if q != here), key=lambda q: (-abs(q - here), q))
        found = jnp.int32(others[j]) if found is None else jnp.where(z == here, others[j], found)
    return found


class Links:
    def __init__(self):
        self.c, self.x, self.y, self.z = c, x, y, z = place()
        self.beside = {
            "x": (seq_of(y, 1 - x, c), z),
            "y": (seq_of(1 - y, x, c), z),
            "up": (seq_of(y, x, c), z + 1),
            "dn": (seq_of(y, x, c), z - 1),
            "core": (seq_of(y, x, 1 - c), z),
        }
        self.spots = [far(z, j) for j in range(ZN)]
        self.above, self.below = z < ZN - 1, z > 0

    def greet(self):
        bar = pltpu.get_barrier_semaphore()

        def signal(d):
            pl.semaphore_signal(bar, inc=1, device_id=self.beside[d], device_id_type=MESH)
        for d in ("x", "y", "core"):
            signal(d)
        pl.when(self.above)(lambda: signal("up"))
        pl.when(self.below)(lambda: signal("dn"))
        pl.semaphore_wait(bar, 3 + self.above.astype(jnp.int32) + self.below.astype(jnp.int32))

    def slot(self, dx, dy, z, core):
        return seq_of(flip(self.y, dy), flip(self.x, dx), core) * ZN + z

    def copy(self, src, dst, send, recv, d):
        return pltpu.make_async_remote_copy(src, dst, send, recv, device_id=self.beside[d], device_id_type=MESH)


def onward(order, dx, dy, same):
    off = {"x": dx, "y": dy, "z": 0 if same else 1}
    return [
        d for i, d in enumerate(order)
        if not any(off[e] for e in order[i + 1 :]) and not (d != "z" and off[d])
    ]


def arrival(order, dx, dy, same):
    off = {"x": dx, "y": dy, "z": 0 if same else 1}
    return [d for d in order if off[d]][-1]


def blocks(parts):
    found = [
        (dx + dy + ZN - 1 - j, r, dx, dy, j)
        for dx in range(2) for dy in range(2) for j in range(ZN) for r in range(len(parts))
    ]
    return found


class Gather:
    def __init__(self, parts, ins, outs, send, recv, csend, crecv, lsem):
        self.parts, self.ins, self.outs = parts, ins, outs
        self.send, self.recv, self.csend, self.crecv, self.lsem = send, recv, csend, crecv, lsem
        self.links = Links()
        self.events = sorted(blocks(parts), key=lambda e: e[0])

    @staticmethod
    def scratch(parts):
        n = len(parts)
        return [SEM((n, 4, 4, ZN)), SEM((n, 4, ZN)), SEM((n, 4, ZN)), SEM((n, 4, ZN)), SEM((n,))]

    def window(self, r):
        return pl.ds(self.parts[r][2], self.parts[r][3])

    def dst(self, r, dx, dy, zs):
        return self.outs[self.parts[r][1]].at[self.links.slot(dx, dy, zs, self.links.c), self.window(r)]

    def src(self, r, dx, dy, zs, own):
        return self.ins[self.parts[r][0]].at[self.window(r)] if own else self.dst(r, dx, dy, zs)

    def hop(self, r, dx, dy, zs, d, own):
        to = (1 if d == "x" else dx) * 2 + (1 if d == "y" else dy)
        which = ("x", "y", "up", "dn").index(d)
        return self.links.copy(self.src(r, dx, dy, zs, own), self.dst(r, dx, dy, zs),
                               self.send.at[r, which, dx * 2 + dy, zs], self.recv.at[r, to, zs], d)

    def across(self, r, dx, dy, zs, own):
        return self.links.copy(self.src(r, dx, dy, zs, own), self.dst(r, dx, dy, zs),
                               self.csend.at[r, dx * 2 + dy, zs], self.crecv.at[r, dx * 2 + dy, zs], "core")

    def hops(self, r, dx, dy, j, act):
        links, zs = self.links, self.links.spots[j]
        z, same = links.z, j == ZN - 1
        own = same and not dx and not dy
        for d in onward(ROUTES[self.parts[r][4]], dx, dy, same):
            if d != "z":
                act(self.hop(r, dx, dy, zs, d, own))
                continue
            up = links.above if same else jnp.logical_and(z > zs, links.above)
            down = links.below if same else jnp.logical_and(z < zs, links.below)
            pl.when(up)(lambda: act(self.hop(r, dx, dy, zs, "up", own)))
            pl.when(down)(lambda: act(self.hop(r, dx, dy, zs, "dn", own)))

    def forward(self, event):
        _, r, dx, dy, j = event
        zs, own = self.links.spots[j], j == ZN - 1 and not dx and not dy
        if not own:
            self.links.copy(self.dst(r, dx, dy, zs), self.dst(r, dx, dy, zs), self.send.at[r, 0, 0, 0],
                            self.recv.at[r, dx * 2 + dy, zs], "core").wait_recv()
        self.hops(r, dx, dy, j, lambda copy: copy.start())
        self.across(r, dx, dy, zs, own).start()
        if own:
            self.local(r).start()

    def local(self, r):
        return pltpu.make_async_copy(self.ins[self.parts[r][0]].at[self.window(r)],
                                     self.dst(r, 0, 0, self.links.z), self.lsem.at[r])

    def finish(self):
        for _, r, dx, dy, j in self.events:
            own = j == ZN - 1 and not dx and not dy
            self.hops(r, dx, dy, j, lambda copy: copy.wait_send())
            copy = self.across(r, dx, dy, self.links.spots[j], own)
            copy.wait_send()
            copy.wait_recv()
            if own:
                self.local(r).wait()


def gather(parts, ins, rows):
    n = len(ins)

    def kernel(*refs):
        job = Gather(parts, refs[:n], refs[n : n + len(rows)], *refs[n + len(rows) :])
        job.links.greet()
        for event in job.events:
            job.forward(event)
        job.finish()
    anywhere = pl.BlockSpec(memory_space=pl.ANY)
    return pl.pallas_call(
        kernel,
        out_shape=[jax.ShapeDtypeStruct((8 * ZN, count, W), jnp.bfloat16) for count in rows],
        in_specs=[anywhere] * n,
        out_specs=[anywhere] * len(rows),
        scratch_shapes=Gather.scratch(parts),
        compiler_params=pltpu.CompilerParams(collective_id=1, has_side_effects=True),
    )(*ins)


def layout(order):
    base, count = {}, 0
    for i, d in enumerate(order):
        base[d] = count
        free = 1
        for e in order[:i]:
            free *= ZN if e == "z" else 2
        count += free * ((ZN + 1) if d == "z" else 1)
    return base, count


class Scatter:
    def __init__(self, parts, ins, out, sib, stage, send, csend, crecv, lsem, *rest):
        self.parts, self.ins, self.out, self.sib, self.stage = parts, ins, out, sib, stage
        self.send, self.csend, self.crecv, self.lsem = send, csend, crecv, lsem
        self.bufs, self.recv = rest[: len(parts)], rest[len(parts) :]
        self.links = Links()
        self.events = sorted(blocks(parts), key=lambda e: -e[0])
        self.lay = [layout(ROUTES[part[3]]) for part in parts]
        self.starts = [sum(part[2] for part in parts[:r]) for r in range(len(parts))]

    @staticmethod
    def scratch(parts):
        n, total = len(parts), sum(part[2] for part in parts)
        counts = [layout(ROUTES[part[3]])[1] for part in parts]
        most = max(part[2] for part in parts)
        return [pltpu.VMEM((4, ZN, total, W), jnp.bfloat16), pltpu.VMEM((STG, most, W), jnp.bfloat16), SEM((n, 4, ZN)),
                SEM((n, 4, ZN)), SEM((n, 4, ZN)), SEM((STG,))] + [
            pltpu.VMEM((count, part[2], W), jnp.bfloat16) for count, part in zip(counts, parts)
        ] + [SEM((count,)) for count in counts]

    def mine(self, r):
        return pl.ds(self.starts[r], self.parts[r][2])

    def source(self, r, dx, dy, zd, core):
        which, start, rows, _ = self.parts[r]
        return self.ins[which].at[self.links.slot(dx, dy, zd, core), pl.ds(start, rows)]

    def child(self, r, d, dx, dy, zd):
        order = ROUTES[self.parts[r][3]]
        dim = d if d in "xy" else "z"
        index = 0
        for e in order[: order.index(dim)]:
            index = index * ZN + zd if e == "z" else index * 2 + (dx if e == "x" else dy)
        if dim == "z":
            index = index * (ZN + 1) + (zd if d == "up" else zd + 1)
        return self.lay[r][0][dim] + index

    def across(self, event):
        _, r, dx, dy, j = event
        zd = self.links.spots[j]
        return self.links.copy(self.source(r, dx, dy, zd, 1 - self.links.c), self.sib.at[dx * 2 + dy, zd, self.mine(r)],
                               self.csend.at[r, dx * 2 + dy, zd], self.crecv.at[r, dx * 2 + dy, zd], "core")

    def load(self, i):
        _, r, dx, dy, j = self.events[i]
        return pltpu.make_async_copy(self.source(r, dx, dy, self.links.spots[j], self.links.c),
                                     self.stage.at[i % STG, pl.ds(0, self.parts[r][2])], self.lsem.at[i % STG])

    def hop(self, r, dx, dy, zd, d):
        came = {"x": "x", "y": "y", "up": "dn", "dn": "up"}[d]
        at = self.child(r, came, 0 if d == "x" else dx, 0 if d == "y" else dy, zd)
        return self.links.copy(self.sib.at[dx * 2 + dy, zd, self.mine(r)], self.bufs[r].at[at],
                               self.send.at[r, dx * 2 + dy, zd], self.recv[r].at[at], d)

    def add(self, i, dirs):
        _, r, dx, dy, j = self.events[i]
        zd = self.links.spots[j]
        final = j == ZN - 1 and not dx and not dy
        at = [self.child(r, d, dx, dy, zd) for d in dirs]
        for k in at:
            self.links.copy(self.bufs[r].at[k], self.bufs[r].at[k], self.send.at[r, 0, 0], self.recv[r].at[k], "core").wait_recv()

        def body(q, _):
            low = pl.ds(pl.multiple_of(q * 16, 16), 16)
            here = pl.ds(pl.multiple_of(self.starts[r] + q * 16, 16), 16)
            total = self.stage[i % STG, low].astype(jnp.float32) + self.sib[dx * 2 + dy, zd, here].astype(jnp.float32)
            for k in at:
                total = total + self.bufs[r][k, low].astype(jnp.float32)
            if final:
                self.out[here] = total
            else:
                self.sib[dx * 2 + dy, zd, here] = total.astype(jnp.bfloat16)
            return 0
        lax.fori_loop(0, self.parts[r][2] // 16, body, 0)

    def begin(self):
        for event in self.events:
            self.across(event).start()
        for i in range(STG - 1):
            self.load(i).start()

    def step(self, i):
        links = self.links
        _, r, dx, dy, j = self.events[i]
        zd, z, same = links.spots[j], links.z, j == ZN - 1
        order = ROUTES[self.parts[r][3]]
        if i + STG - 1 < len(self.events):
            self.load(i + STG - 1).start()
        self.load(i).wait()
        self.across(self.events[i]).wait_recv()
        kids = onward(order, dx, dy, same)
        fixed = [d for d in kids if d != "z"]
        if "z" not in kids:
            self.add(i, fixed)
        elif same:
            pl.when(z == 0)(lambda: self.add(i, fixed + ["up"]))
            pl.when(z == ZN - 1)(lambda: self.add(i, fixed + ["dn"]))
            pl.when(jnp.logical_and(links.below, links.above))(lambda: self.add(i, fixed + ["up", "dn"]))
        else:
            pl.when(jnp.logical_and(z > zd, links.above))(lambda: self.add(i, fixed + ["up"]))
            pl.when(jnp.logical_and(z < zd, links.below))(lambda: self.add(i, fixed + ["dn"]))
            pl.when(jnp.logical_or(z == 0, z == ZN - 1))(lambda: self.add(i, fixed))
        if not (same and not dx and not dy):
            d = arrival(order, dx, dy, same)
            if d == "z":
                pl.when(zd > z)(lambda: self.hop(r, dx, dy, zd, "up").start())
                pl.when(zd < z)(lambda: self.hop(r, dx, dy, zd, "dn").start())
            else:
                self.hop(r, dx, dy, zd, d).start()

    def finish(self):
        for event in self.events:
            _, r, dx, dy, j = event
            self.across(event).wait_send()
            if not (j == ZN - 1 and not dx and not dy):
                self.hop(r, dx, dy, self.links.spots[j], "x").wait_send()


def scatter(parts, ins):
    n, total = len(ins), sum(part[2] for part in parts)

    def kernel(*refs):
        job = Scatter(parts, refs[:n], *refs[n:])
        job.links.greet()
        job.begin()
        for i in range(len(job.events)):
            job.step(i)
        job.finish()
    return pl.pallas_call(
        kernel,
        out_shape=jax.ShapeDtypeStruct((total, W), jnp.float32),
        in_specs=[pl.BlockSpec(memory_space=pl.ANY)] * n,
        out_specs=pl.BlockSpec(memory_space=pltpu.VMEM),
        scratch_shapes=Scatter.scratch(parts),
        compiler_params=pltpu.CompilerParams(collective_id=2, has_side_effects=True, vmem_limit_bytes=62 << 20),
    )(*ins)


RATE_AT, ENTRY_AT, OUT_AT, GATE_AT, INPUT_AT, REC_ROWS = 0, 144, 288, 384, 480, 576
FFN_GATE_AT, FFN_UP_AT, FFN_DOWN_AT, SMALL_AT, SMALL_ROWS = 576, 768, 960, 1152, 16
GATHER_PARTS = ((0, 0, 0, 288, 0), (0, 0, 288, 288, 1), (0, 0, 576, 288, 2), (0, 0, 864, 304, 3))
SCATTER_PARTS = ((0, 0, 288, 0), (0, 288, 288, 1), (1, 0, 288, 2), (1, 288, 288, 3), (2, 0, 16, 0))


def pack_blocks(item):
    rows, cols = item.shape
    return item.reshape(rows, cols // W, W).transpose(1, 0, 2).reshape(rows * cols // W, W)


def unpack_blocks(item, rows, cols):
    return item.reshape(cols // W, rows, W).transpose(1, 0, 2).reshape(rows, cols)


def pad_rows(item, before, count):
    batch, rows, cols = item.shape
    item = jnp.pad(item, ((0, 0), (before, count - rows - before), (0, 0)))
    return item.reshape(batch * count, cols)


def per_device_packed(tokens, cotangent, lengths, *shards):
    (gate_proj, input_proj, rate_proj, entry_proj, out_proj, ffn_gate, ffn_up, ffn_down) = shards[:8]
    small = shards[8:]
    batch, width, depth = tokens.shape
    r, f = gate_proj.shape[1], ffn_gate.shape[1]
    n_seq = lax.axis_size("seq")
    me = lax.axis_index("seq")
    rim = pad_rows(from_behind(tokens[:, width - 3 :], "seq", 1), 5, 8)
    flat = jnp.concatenate([item.reshape(-1) for item in small])
    flat = jnp.pad(flat, (0, SMALL_ROWS * W - flat.shape[0])).reshape(SMALL_ROWS, W)
    order = (rate_proj, entry_proj, out_proj, gate_proj, input_proj, ffn_gate, ffn_up, ffn_down)
    packed = gather(GATHER_PARTS, [jnp.concatenate([pack_blocks(item) for item in order] + [flat], axis=0)], [SMALL_AT + SMALL_ROWS])[0]
    flats = packed[:, SMALL_AT].astype(jnp.float32)
    lo, vectors = 0, []
    for item in small:
        part = flats[:, lo : lo + item.size]
        lo += item.size
        if item.ndim == 2:
            part = part.reshape(-1, *item.shape).transpose(1, 0, 2).reshape(item.shape[0], -1)
        else:
            part = part.reshape(1, -1)
        vectors.append(part)
    norm_gain, ffn_gain, taps, conv_bias, rate_bias, entry_bias, logit = vectors
    vec = jnp.concatenate([taps, conv_bias, rate_bias, entry_bias, -lru_scale * jax.nn.softplus(-logit),
                           jax.nn.sigmoid(-logit), jnp.zeros((7, r), jnp.float32)], axis=0)
    norm_gain = jnp.broadcast_to(norm_gain, (8, depth))
    ffn_gain = jnp.broadcast_to(ffn_gain, (8, depth))
    info = jnp.concatenate([jnp.clip(lengths - me * width, 0, width), me[None]]).astype(jnp.int32)
    tokens2 = tokens.reshape(batch * width, depth)
    cot2 = cotangent.reshape(batch * width, depth)

    gate_pre, inner, mixed, normed = branch(tokens2, rim, norm_gain, packed, vec, batch)
    rate, entry, decay, drive, pseg, hseg, ends = gates(info, mixed, packed, vec, batch)
    pall = exchange(ends, n_seq, 3)
    states, sstart, gated, first, normed_two = states_and_first(
        info, decay, drive, gate_pre, pseg, hseg, pall, tokens2, packed, ffn_gain, batch)
    block_out, d_first, d_low, g_ffn_gain, grad_ffn = feed_forward(info, first, normed_two, cot2, ffn_gain, packed, f, batch)
    d_states, d_gate, gseg, gtot, grad_rec = unproject(d_low, packed, gated, gate_pre, states, decay, pseg, batch)
    gall = exchange(gtot, n_seq, 4)
    d_mixed, sums, grad_rec = recur_back(
        info, mixed, decay, d_states, states, rate, entry, pseg, gseg, sstart, pall, gall, vec, packed, grad_rec, batch)
    rim_back = from_behind(d_mixed.reshape(batch, width, r)[:, :3].astype(jnp.bfloat16), "seq", -1)
    rim_back = pad_rows(rim_back.astype(jnp.float32), 0, 8)
    csums, token_grad, g_norm_gain, grad_rec = entry_back(
        d_mixed, rim_back, inner, d_gate, normed, packed, vec, tokens2, d_first, norm_gain, grad_rec, batch)

    n = packed.shape[0]
    lines = [jnp.sum(g_norm_gain, axis=0).reshape(n, -1), jnp.sum(g_ffn_gain, axis=0).reshape(n, -1),
             csums[:4].reshape(4, n, -1).transpose(1, 0, 2).reshape(n, -1), csums[4].reshape(n, -1),
             sums[1].reshape(n, -1), sums[2].reshape(n, -1), sums[0].reshape(n, -1)]
    lines = jnp.concatenate(lines, axis=1).astype(jnp.bfloat16)
    lines = jnp.pad(lines, ((0, 0), (0, SMALL_ROWS * W - lines.shape[1]))).reshape(n, SMALL_ROWS, W)
    total = scatter(SCATTER_PARTS, [grad_ffn, grad_rec, lines])
    fr = REC_ROWS
    at = {"rate": fr + RATE_AT, "entry": fr + ENTRY_AT, "out": fr + OUT_AT, "gate": fr + GATE_AT, "input": fr + INPUT_AT}
    result = [(at["gate"], gate_proj), (at["input"], input_proj), (at["rate"], rate_proj), (at["entry"], entry_proj),
              (at["out"], out_proj), (0, ffn_gate), (FFN_UP_AT - FFN_GATE_AT, ffn_up), (FFN_DOWN_AT - FFN_GATE_AT, ffn_down)]
    result = [unpack_blocks(total[lo : lo + item.size // W], *item.shape) for lo, item in result]
    flat = total[SMALL_AT]
    lo = 0
    for item in small:
        result.append(flat[lo : lo + item.size].reshape(item.shape))
        lo += item.size
    return (block_out.reshape(tokens.shape), token_grad.reshape(tokens.shape), *result)


def solution(mesh):
    packs = mesh.shape["seq"] == 8 and mesh.shape["batch"] == ZN
    placed = (
        P("batch", "seq", None),
        P("batch", "seq", None),
        P("batch"),
        P(("seq", "batch"), None),
        P(("seq", "batch"), None),
        P(("seq", "batch"), None),
        P(("seq", "batch"), None),
        P(("seq", "batch"), None),
        P(("seq", "batch"), None),
        P(("seq", "batch"), None),
        P(("seq", "batch"), None),
        P(("seq", "batch")),
        P(("seq", "batch")),
        P(None, ("seq", "batch")),
        P(("seq", "batch")),
        P(("seq", "batch")),
        P(("seq", "batch")),
        P(("seq", "batch")),
    )
    return jax.shard_map(
        per_device_packed if packs else per_device,
        mesh=mesh,
        in_specs=placed,
        out_specs=(
            P("batch", "seq", None),
            P("batch", "seq", None),
            P(("seq", "batch"), None),
            P(("seq", "batch"), None),
            P(("seq", "batch"), None),
            P(("seq", "batch"), None),
            P(("seq", "batch"), None),
            P(("seq", "batch"), None),
            P(("seq", "batch"), None),
            P(("seq", "batch"), None),
            P(("seq", "batch")),
            P(("seq", "batch")),
            P(None, ("seq", "batch")),
            P(("seq", "batch")),
            P(("seq", "batch")),
            P(("seq", "batch")),
            P(("seq", "batch")),
        ),
        check_vma=False,
    )
```

```python
import functools

import jax
import jax.numpy as jnp
from jax import lax
from jax.experimental import pallas as pl
from jax.experimental.pallas import tpu as pltpu
from jax.sharding import PartitionSpec as P

MICRO = 2


eps = 1e-06
lru_scale = 8.0


def from_behind(value, axis, steps):
    count = lax.axis_size(axis)
    initial, last = (max(0, -steps), min(count, count - steps))
    return lax.ppermute(value, axis, [(source, source + steps) for source in range(initial, last)])


def entering(array, axis, combine, identity):
    size, place = (lax.axis_size(axis), lax.axis_index(axis))
    everything = jax.tree.map(lambda part: lax.all_gather(part, axis), array)
    start = jax.tree.map(
        lambda part, zero: jnp.broadcast_to(jnp.asarray(zero, part.dtype), part.shape),
        array,
        identity,
    )

    def entering_turn(k, before):
        reached = k < place
        new = combine(before, jax.tree.map(lambda part: part[k], everything))
        return jax.tree.map(lambda a, b: jnp.where(reached, a, b), new, before)

    return lax.fori_loop(0, size, entering_turn, start)


def carried_in(array, axis, combine, identity):
    size, place = (lax.axis_size(axis), lax.axis_index(axis))
    everything = jax.tree.map(
        lambda part, kind: lax.all_gather(part.astype(kind), axis),
        array,
        (jnp.bfloat16, jnp.bfloat16),
    )
    start = jax.tree.map(
        lambda part, zero: jnp.broadcast_to(jnp.asarray(zero, part.dtype), part.shape),
        array,
        identity,
    )

    def carried_turn(k, before):
        at = size - 1 - k
        reached = at > place
        new = combine(
            before, jax.tree.map(lambda part, own: part[at].astype(own.dtype), everything, array)
        )
        return jax.tree.map(lambda a, b: jnp.where(reached, a, b), new, before)

    return lax.fori_loop(0, size, carried_turn, start)


def for_sending(array):

    def short(part):
        return part.astype(jnp.bfloat16) if part.dtype == jnp.float32 else part

    return jax.tree.map(short, array)


def project(left, right):
    return jnp.einsum("btd,de->bte", left, right, preferred_element_type=jnp.float32)


def project_back(left, right):
    return jnp.einsum("bte,de->btd", left, right, preferred_element_type=jnp.float32)


def outer_sum(left, right):
    return jnp.einsum("btd,bte->de", left, right, preferred_element_type=jnp.float32)


def link(earlier, later):
    return (earlier[0] * later[0], later[0] * earlier[1] + later[1])


def norm_back(value, scale, gain, grad):
    weighted = grad * gain
    gain_grad = jnp.sum(grad * value * scale, axis=(0, 1))
    spread = jnp.mean(weighted * value, axis=-1, keepdims=True)
    return (scale * weighted - value * scale**3 * spread, gain_grad)


def fetch(shards):
    (
        gate_proj,
        input_proj,
        rate_proj,
        entry_proj,
        out_proj,
        ffn_gate,
        ffn_up,
        ffn_down,
        norm_gain,
        ffn_gain,
        conv_taps,
        conv_bias,
        rate_bias,
        entry_bias,
        decay_logit,
    ) = shards
    return (
        lax.all_gather(gate_proj, ("seq", "batch"), axis=0, tiled=True),
        lax.all_gather(input_proj, ("seq", "batch"), axis=0, tiled=True),
        lax.all_gather(rate_proj, ("seq", "batch"), axis=0, tiled=True),
        lax.all_gather(entry_proj, ("seq", "batch"), axis=0, tiled=True),
        lax.all_gather(out_proj, ("seq", "batch"), axis=0, tiled=True),
        lax.all_gather(ffn_gate, ("seq", "batch"), axis=0, tiled=True),
        lax.all_gather(ffn_up, ("seq", "batch"), axis=0, tiled=True),
        lax.all_gather(ffn_down, ("seq", "batch"), axis=0, tiled=True),
        lax.all_gather(norm_gain, ("seq", "batch"), axis=0, tiled=True),
        lax.all_gather(ffn_gain, ("seq", "batch"), axis=0, tiled=True),
        lax.all_gather(conv_taps, ("seq", "batch"), axis=1, tiled=True),
        lax.all_gather(conv_bias, ("seq", "batch"), axis=0, tiled=True),
        lax.all_gather(rate_bias, ("seq", "batch"), axis=0, tiled=True),
        lax.all_gather(entry_bias, ("seq", "batch"), axis=0, tiled=True),
        lax.all_gather(decay_logit, ("seq", "batch"), axis=0, tiled=True),
    )


def forward_part(tokens, mask, weights):
    (
        gate_proj,
        input_proj,
        rate_proj,
        entry_proj,
        out_proj,
        ffn_gate,
        ffn_up,
        ffn_down,
        norm_gain,
        ffn_gain,
        conv_taps,
        conv_bias,
        rate_bias,
        entry_bias,
        decay_logit,
    ) = weights
    width = tokens.shape[1]
    taps_count = conv_taps.shape[0]
    values = tokens.astype(jnp.float32)
    scale_one = lax.rsqrt(jnp.mean(values * values, axis=-1, keepdims=True) + eps)
    normed = (values * scale_one * norm_gain).astype(jnp.bfloat16)
    gate_pre = project(normed, gate_proj)
    inner = project(normed, input_proj)
    rim = from_behind(inner[:, width - (taps_count - 1) :], "seq", 1)
    extended = jnp.concatenate([rim, inner], axis=1)
    conv = jnp.zeros_like(inner) + conv_bias
    for lag in range(taps_count):
        start = taps_count - 1 - lag
        conv = conv + conv_taps[lag] * extended[:, start : start + width]
    mixed = conv.astype(jnp.bfloat16)
    mixed_full = mixed.astype(jnp.float32)
    rate = jax.nn.sigmoid(project(mixed, rate_proj) + rate_bias)
    entry = jax.nn.sigmoid(project(mixed, entry_proj) + entry_bias)
    logit = decay_logit.astype(jnp.float32)
    log_decay = -lru_scale * jax.nn.softplus(-logit) * rate
    decay = jnp.exp(mask * log_decay)
    root = jnp.sqrt(-jnp.expm1(2.0 * log_decay))
    drive = mask * root * entry * mixed_full
    reach, local = lax.associative_scan(link, (decay, drive), axis=1)
    unit_state = (jnp.ones_like(reach[:, -1]), jnp.zeros_like(local[:, -1]))
    start_state = entering((reach[:, -1], local[:, -1]), "seq", link, unit_state)[1]
    states = local + reach * start_state[:, None]
    gated = (states * jax.nn.gelu(gate_pre)).astype(jnp.bfloat16)
    first = values + project(gated, out_proj)
    scale_two = lax.rsqrt(jnp.mean(first * first, axis=-1, keepdims=True) + eps)
    normed_two = (first * scale_two * ffn_gain).astype(jnp.bfloat16)
    up_pre = project(normed_two, ffn_gate)
    mix_pre = project(normed_two, ffn_up)
    hidden = (jax.nn.gelu(up_pre) * mix_pre).astype(jnp.bfloat16)
    block_out = mask * (first + project(hidden, ffn_down))
    saved = (
        values,
        scale_one,
        normed,
        gate_pre,
        extended,
        mixed,
        mixed_full,
        rate,
        entry,
        log_decay,
        decay,
        root,
        start_state,
        states,
        gated,
        first,
        scale_two,
        normed_two,
        up_pre,
        mix_pre,
        hidden,
    )
    return (block_out, saved)


def backward_part(cotangent, mask, weights, saved):
    (
        gate_proj,
        input_proj,
        rate_proj,
        entry_proj,
        out_proj,
        ffn_gate,
        ffn_up,
        ffn_down,
        norm_gain,
        ffn_gain,
        conv_taps,
        conv_bias,
        rate_bias,
        entry_bias,
        decay_logit,
    ) = weights
    (
        values,
        scale_one,
        normed,
        gate_pre,
        extended,
        mixed,
        mixed_full,
        rate,
        entry,
        log_decay,
        decay,
        root,
        start_state,
        states,
        gated,
        first,
        scale_two,
        normed_two,
        up_pre,
        mix_pre,
        hidden,
    ) = saved
    width = values.shape[1]
    taps_count = conv_taps.shape[0]
    cot_full = mask * cotangent.astype(jnp.float32)
    cot_low = cot_full.astype(jnp.bfloat16)
    grad_ffn_down = outer_sum(hidden, cot_low)
    d_hidden = project_back(cot_low, ffn_down)
    gelu_up, gelu_pull = jax.vjp(jax.nn.gelu, up_pre)
    d_up = gelu_pull(d_hidden * mix_pre)[0].astype(jnp.bfloat16)
    d_mix = (d_hidden * gelu_up).astype(jnp.bfloat16)
    grad_ffn_gate = outer_sum(normed_two, d_up)
    grad_ffn_up = outer_sum(normed_two, d_mix)
    d_normed_two = project_back(d_up, ffn_gate) + project_back(d_mix, ffn_up)
    back_two, grad_ffn_gain = norm_back(first, scale_two, ffn_gain, d_normed_two)
    d_first = cot_full + back_two
    d_first_low = d_first.astype(jnp.bfloat16)
    grad_out_proj = outer_sum(gated, d_first_low)
    d_gated = project_back(d_first_low, out_proj)
    gate, gate_pull = jax.vjp(jax.nn.gelu, gate_pre)
    d_states = d_gated * gate
    d_gate_pre = gate_pull(d_gated * states)[0].astype(jnp.bfloat16)
    following = jnp.concatenate([decay[:, 1:], jnp.ones_like(decay[:, :1])], axis=1)
    reach_back, local_back = lax.associative_scan(link, (following, d_states), reverse=True, axis=1)
    unit_grad = (jnp.ones_like(decay[:, 0]), jnp.zeros_like(decay[:, 0]))
    end_grad = carried_in(
        (decay[:, 0] * reach_back[:, 0], decay[:, 0] * local_back[:, 0]), "seq", link, unit_grad
    )[1]
    carried = local_back + reach_back * end_grad[:, None]
    previous = jnp.concatenate([start_state[:, None], states[:, :-1]], axis=1)
    masked_grad = mask * carried
    d_log = (
        masked_grad * previous * decay
        - masked_grad * entry * mixed_full * jnp.exp(2.0 * log_decay) / root
    )
    logit = decay_logit.astype(jnp.float32)
    grad_decay_logit = jnp.sum(lru_scale * d_log * rate * jax.nn.sigmoid(-logit), axis=(0, 1))
    d_rate_pre = -lru_scale * jax.nn.softplus(-logit) * d_log * rate * (1.0 - rate)
    d_entry_pre = masked_grad * root * mixed_full * entry * (1.0 - entry)
    grad_rate_bias = jnp.sum(d_rate_pre, axis=(0, 1))
    grad_entry_bias = jnp.sum(d_entry_pre, axis=(0, 1))
    rate_low = d_rate_pre.astype(jnp.bfloat16)
    entry_low = d_entry_pre.astype(jnp.bfloat16)
    grad_rate_proj = outer_sum(mixed, rate_low)
    grad_entry_proj = outer_sum(mixed, entry_low)
    d_mixed = (
        masked_grad * root * entry
        + project_back(rate_low, rate_proj)
        + project_back(entry_low, entry_proj)
    )
    grad_conv_bias = jnp.sum(d_mixed, axis=(0, 1))
    tap_grads = []
    for lag in range(taps_count):
        start = taps_count - 1 - lag
        tap_grads.append(jnp.sum(d_mixed * extended[:, start : start + width], axis=(0, 1)))
    grad_conv_taps = jnp.stack(tap_grads, axis=0)
    rim_back = from_behind(for_sending(d_mixed[:, : taps_count - 1]), "seq", -1)
    later = jnp.concatenate([d_mixed, rim_back], axis=1)
    d_inner = jnp.zeros_like(d_mixed)
    for lag in range(taps_count):
        d_inner = d_inner + conv_taps[lag] * later[:, lag : lag + width]
    d_inner = d_inner.astype(jnp.bfloat16)
    grad_input_proj = outer_sum(normed, d_inner)
    grad_gate_proj = outer_sum(normed, d_gate_pre)
    d_normed = project_back(d_gate_pre, gate_proj) + project_back(d_inner, input_proj)
    back_one, grad_norm_gain = norm_back(values, scale_one, norm_gain, d_normed)
    token_grad = d_first + back_one
    grads = (
        grad_gate_proj,
        grad_input_proj,
        grad_rate_proj,
        grad_entry_proj,
        grad_out_proj,
        grad_ffn_gate,
        grad_ffn_up,
        grad_ffn_down,
        grad_norm_gain,
        grad_ffn_gain,
        grad_conv_taps,
        grad_conv_bias,
        grad_rate_bias,
        grad_entry_bias,
        grad_decay_logit,
    )
    return (token_grad, grads)


def reduce_grads(totals):
    shaped = []
    for index, item in enumerate(totals):
        if index == 10:
            item = item.T
        if item.ndim == 1:
            item = item[:, None]
        shaped.append(item[None])
    spread = (
        lax.all_to_all(
            shaped[0].astype(jnp.bfloat16), "seq", split_axis=1, concat_axis=0, tiled=True
        ).astype(jnp.float32),
        lax.all_to_all(
            shaped[1].astype(jnp.bfloat16), "seq", split_axis=1, concat_axis=0, tiled=True
        ).astype(jnp.float32),
        lax.all_to_all(
            shaped[2].astype(jnp.bfloat16), "seq", split_axis=1, concat_axis=0, tiled=True
        ).astype(jnp.float32),
        lax.all_to_all(
            shaped[3].astype(jnp.bfloat16), "seq", split_axis=1, concat_axis=0, tiled=True
        ).astype(jnp.float32),
        lax.all_to_all(
            shaped[4].astype(jnp.bfloat16), "seq", split_axis=1, concat_axis=0, tiled=True
        ).astype(jnp.float32),
        lax.all_to_all(
            shaped[5].astype(jnp.bfloat16), "seq", split_axis=1, concat_axis=0, tiled=True
        ).astype(jnp.float32),
        lax.all_to_all(
            shaped[6].astype(jnp.bfloat16), "seq", split_axis=1, concat_axis=0, tiled=True
        ).astype(jnp.float32),
        lax.all_to_all(
            shaped[7].astype(jnp.bfloat16), "seq", split_axis=1, concat_axis=0, tiled=True
        ).astype(jnp.float32),
        lax.all_to_all(
            shaped[8].astype(jnp.bfloat16), "seq", split_axis=1, concat_axis=0, tiled=True
        ).astype(jnp.float32),
        lax.all_to_all(
            shaped[9].astype(jnp.bfloat16), "seq", split_axis=1, concat_axis=0, tiled=True
        ).astype(jnp.float32),
        lax.all_to_all(for_sending(shaped[10]), "seq", split_axis=1, concat_axis=0, tiled=True),
        lax.all_to_all(for_sending(shaped[11]), "seq", split_axis=1, concat_axis=0, tiled=True),
        lax.all_to_all(for_sending(shaped[12]), "seq", split_axis=1, concat_axis=0, tiled=True),
        lax.all_to_all(for_sending(shaped[13]), "seq", split_axis=1, concat_axis=0, tiled=True),
        lax.all_to_all(for_sending(shaped[14]), "seq", split_axis=1, concat_axis=0, tiled=True),
    )
    folded = [jnp.sum(piece, axis=0) for piece in spread]
    summed = (
        lax.psum_scatter(
            folded[0].astype(jnp.bfloat16), "batch", scatter_dimension=0, tiled=True
        ).astype(jnp.float32),
        lax.psum_scatter(
            folded[1].astype(jnp.bfloat16), "batch", scatter_dimension=0, tiled=True
        ).astype(jnp.float32),
        lax.psum_scatter(
            folded[2].astype(jnp.bfloat16), "batch", scatter_dimension=0, tiled=True
        ).astype(jnp.float32),
        lax.psum_scatter(
            folded[3].astype(jnp.bfloat16), "batch", scatter_dimension=0, tiled=True
        ).astype(jnp.float32),
        lax.psum_scatter(
            folded[4].astype(jnp.bfloat16), "batch", scatter_dimension=0, tiled=True
        ).astype(jnp.float32),
        lax.psum_scatter(
            folded[5].astype(jnp.bfloat16), "batch", scatter_dimension=0, tiled=True
        ).astype(jnp.float32),
        lax.psum_scatter(
            folded[6].astype(jnp.bfloat16), "batch", scatter_dimension=0, tiled=True
        ).astype(jnp.float32),
        lax.psum_scatter(
            folded[7].astype(jnp.bfloat16), "batch", scatter_dimension=0, tiled=True
        ).astype(jnp.float32),
        lax.psum_scatter(
            folded[8].astype(jnp.bfloat16), "batch", scatter_dimension=0, tiled=True
        ).astype(jnp.float32),
        lax.psum_scatter(
            folded[9].astype(jnp.bfloat16), "batch", scatter_dimension=0, tiled=True
        ).astype(jnp.float32),
        lax.psum_scatter(
            folded[10].astype(jnp.bfloat16), "batch", scatter_dimension=0, tiled=True
        ).astype(jnp.float32),
        lax.psum_scatter(
            folded[11].astype(jnp.bfloat16), "batch", scatter_dimension=0, tiled=True
        ).astype(jnp.float32),
        lax.psum_scatter(
            folded[12].astype(jnp.bfloat16), "batch", scatter_dimension=0, tiled=True
        ).astype(jnp.float32),
        lax.psum_scatter(
            folded[13].astype(jnp.bfloat16), "batch", scatter_dimension=0, tiled=True
        ).astype(jnp.float32),
        lax.psum_scatter(
            folded[14].astype(jnp.bfloat16), "batch", scatter_dimension=0, tiled=True
        ).astype(jnp.float32),
    )
    result = []
    for index, item in enumerate(summed):
        if index == 10:
            result.append(item.T)
        elif totals[index].ndim == 1:
            result.append(item[:, 0])
        else:
            result.append(item)
    return tuple(result)


def per_device(
    tokens,
    cotangent,
    lengths,
    gate_proj,
    input_proj,
    rate_proj,
    entry_proj,
    out_proj,
    ffn_gate,
    ffn_up,
    ffn_down,
    norm_gain,
    ffn_gain,
    conv_taps,
    conv_bias,
    rate_bias,
    entry_bias,
    decay_logit,
):
    shards = (
        gate_proj,
        input_proj,
        rate_proj,
        entry_proj,
        out_proj,
        ffn_gate,
        ffn_up,
        ffn_down,
        norm_gain,
        ffn_gain,
        conv_taps,
        conv_bias,
        rate_bias,
        entry_bias,
        decay_logit,
    )
    rows, width = (tokens.shape[0], tokens.shape[1])
    place = lax.axis_index("seq") * width + lax.iota(jnp.int32, width)
    mask_all = (place[None, :] < lengths[:, None]).astype(jnp.float32)[:, :, None]
    group = rows // MICRO
    totals = None
    block_parts = []
    grad_parts = []
    for part in range(MICRO):
        lower = part * group
        mask = mask_all[lower : lower + group]
        weights = fetch(shards)
        block_out, saved = forward_part(tokens[lower : lower + group], mask, weights)
        weights = fetch(shards)
        token_grad, grads = backward_part(cotangent[lower : lower + group], mask, weights, saved)
        totals = grads if part == 0 else jax.tree.map(jnp.add, totals, grads)
        block_parts.append(block_out)
        grad_parts.append(token_grad)
    summed = reduce_grads(totals)
    return (jnp.concatenate(block_parts, axis=0), jnp.concatenate(grad_parts, axis=0)) + summed


F32 = jnp.float32
BF16 = jnp.bfloat16
W = 512
SEGS = 8
CHUNK = 16
TALL = 64
LANES = 128
GELU_A = 0.7978845608028654
GELU_B = 0.044715
TAPS, CONV_BIAS, RATE_BIAS, ENTRY_BIAS, COEF, SIG = 0, 4, 5, 6, 7, 8


def dot(left, right):
    return lax.dot_general(left, right, (((1,), (0,)), ((), ())), preferred_element_type=F32)


def dot_back(left, right):
    return lax.dot_general(left, right, (((1,), (1,)), ((), ())), preferred_element_type=F32)


def dot_outer(left, right):
    return lax.dot_general(left, right, (((0,), (0,)), ((), ())), preferred_element_type=F32)


def rows_at(start, count=CHUNK):
    return pl.ds(pl.multiple_of(start, CHUNK), count)


def gelu_both(value):
    square = value * value
    inside = GELU_A * value * (1.0 + GELU_B * square)
    tanh = jnp.tanh(inside)
    half = 0.5 + 0.5 * tanh
    slope = half + 0.5 * value * (1.0 - tanh * tanh) * (GELU_A * (1.0 + 3.0 * GELU_B * square))
    return value * half, slope


def sigmoid(value):
    return 1.0 / (1.0 + jnp.exp(-value))


def one_less_exp(z, exp_z):
    series = 1.0 + z * (1 / 2 + z * (1 / 6 + z * (1 / 24 + z * (1 / 120 + z * (1 / 720)))))
    return jnp.where(z > -0.25, -z * series, 1.0 - exp_z)


def in_row(row, width, shape):
    return row + lax.broadcasted_iota(jnp.int32, shape, 0)


def each_chunk(batch, width, body, carry=0):
    per = width // CHUNK
    for b in range(batch):
        carry = lax.fori_loop(0, per, lambda i, c, b=b: body(b, i * CHUNK, b * width + i * CHUNK, c), carry)
    return carry


def each_tile(batch, width, tiles, body, carry=None):
    carries = []
    for t in range(tiles):
        kept = carry
        for b in range(batch):
            def one(i, c, t=t, b=b):
                return body(t, b, i * TALL, rows_at(b * width + i * TALL, TALL), slice(t * LANES, (t + 1) * LANES), c)
            kept = lax.fori_loop(0, width // TALL, one, 0 if kept is None else kept)
        carries.append(kept)
    return carries


def strided(b, width, step):
    return pl.ds(b * width + step, SEGS, stride=width // SEGS)


def lanes(t):
    return slice(t * LANES, (t + 1) * LANES)


def spread(ref, value):
    for t in range(ref.shape[0]):
        ref[t] = value[:, lanes(t)]


def tiled(tokens, block, index):
    return pl.BlockSpec((block // LANES, tokens, LANES), lambda j: (index(j), 0, 0))


def inverse_norm(value, depth):
    return lax.rsqrt(jnp.sum(value * value, axis=-1, keepdims=True) * (1.0 / depth) + eps)


def fold8(value):
    total = value[:8]
    for i in range(8, value.shape[0], 8):
        total = total + value[i : i + 8]
    return total


def put(stage, sem, slot, dst, value, used):
    copy = pltpu.make_async_copy(stage.at[slot], dst, sem.at[slot])
    if used is True:
        copy.wait()
    elif used is not False:
        pl.when(used)(copy.wait)
    stage[slot] = value
    copy.start()


def ffn_kernel(batch, width, info_ref, first_ref, normed_ref, cot_ref, gain_ref, wg_ref, wu_ref, wd_ref,
               out_ref, dfirst_ref, dlow_ref, ggain_ref, grad_ref,
               low, dh, hid, acc, dn, up_s, mix_s, du, dm, nt, ltr, stage, dstage, sem, dsem):
    step = pl.program_id(0)
    tokens, depth = first_ref.shape
    n = grad_ref.shape[0]
    f = hid.shape[1]
    wide = wd_ref.shape[0] * wd_ref.shape[1] // 2
    nd, nw = f // wide, f // W
    rows = depth // n
    drows = wd_ref.shape[1] // 2

    @pl.when(step == 0)
    def _():
        def masked(b, spot, row, _):
            at = rows_at(row)
            value = cot_ref[at]
            valid = in_row(spot, width, value.shape) < info_ref[b]
            low[at] = jnp.where(valid, value.astype(F32), 0.0).astype(BF16)
            return 0
        each_chunk(batch, width, masked)

    @pl.when(step < nd)
    def _():
        here = pl.ds(pl.multiple_of(jnp.minimum(step, nd - 1) * wide, wide), wide)
        total = dot_back(low[:, :W], wd_ref[:, :drows].reshape(wide, W))
        dh[:, here] = total + dot_back(low[:, W:], wd_ref[:, drows:].reshape(wide, W))

    @pl.when(jnp.logical_and(step >= nd, step < nd + nw))
    def _():
        j = step - nd
        here = pl.ds(pl.multiple_of(j * W, W), W)
        wg = wg_ref[...].reshape(depth, W)
        wu = wu_ref[...].reshape(depth, W)
        up_s[...] = dot(normed_ref[...], wg)
        mix_s[...] = dot(normed_ref[...], wu)

        def gating(i, _):
            at = rows_at(i * CHUNK)
            gate, slope = gelu_both(up_s[at])
            mix, d = mix_s[at], dh[at, here]
            hid[at, here] = (gate * mix).astype(BF16)
            du[at] = (d * mix * slope).astype(BF16)
            dm[at] = (d * gate).astype(BF16)
            return 0
        lax.fori_loop(0, tokens // CHUNK, gating, 0)
        more = dot_back(du[...], wg) + dot_back(dm[...], wu)

        @pl.when(j == 0)
        def _():
            dn[...] = more

        @pl.when(j > 0)
        def _():
            dn[...] += more
        for which, low_grad in ((0, du), (1, dm)):
            value = dot_outer(normed_ref[...], low_grad[...]).astype(BF16).reshape(n, rows, W)
            dst = grad_ref.at[:, pl.ds(pl.multiple_of(which * nw * rows + j * rows, rows), rows)]
            put(stage, sem, which, dst, value, j > 0)

    @pl.when(step >= nd + nw)
    def _():
        k = step - nd - nw
        here = pl.ds(pl.multiple_of(k * wide, wide), wide)
        block = hid[:, here]
        for half in range(2):
            cols = slice(half * W, (half + 1) * W)
            more = dot(block, wd_ref[:, half * drows : (half + 1) * drows].reshape(wide, W))

            @pl.when(k == 0)
            def _():
                acc[:, cols] = more

            @pl.when(k > 0)
            def _():
                acc[:, cols] += more
            value = dot_outer(block, low[:, cols]).astype(BF16).reshape(wide // drows, drows, W)
            dst = grad_ref.at[pl.ds(k * (wide // drows), wide // drows),
                              pl.ds(2 * nw * rows + half * drows, drows)]
            put(dstage, dsem, half, dst, value, k > 0)

    @pl.when(step == pl.num_programs(0) - 1)
    def _():
        def finish(b, spot, row, total):
            at = rows_at(row)
            first, cot = first_ref[at], low[at].astype(F32)
            valid = in_row(spot, width, first.shape) < info_ref[b]
            out_ref[at] = jnp.where(valid, first + acc[at], 0.0)
            grad = dn[at]
            scale = inverse_norm(first, depth)
            weighted = grad * gain_ref[:1]
            spread = jnp.sum(weighted * first, axis=-1, keepdims=True) * (1.0 / depth)
            back = cot + scale * weighted - first * (scale * scale * scale * spread)
            dfirst_ref[at] = back
            dlow_ref[at] = back.astype(BF16)
            return total + fold8(grad * first * scale)
        total = each_chunk(batch, width, finish, jnp.zeros((8, depth), F32))
        ggain_ref[...] = total
        for which in range(2):
            pltpu.make_async_copy(stage.at[which], grad_ref.at[:, pl.ds(0, rows)], sem.at[which]).wait()
            pltpu.make_async_copy(dstage.at[which], grad_ref.at[pl.ds(0, wide // drows), pl.ds(0, drows)], dsem.at[which]).wait()


def feed_forward(info, first, normed_two, cot, gain, packed, f, batch):
    tokens, depth = first.shape
    width = tokens // batch
    n = packed.shape[0]
    rows, drows = depth // n, f // n
    group = 8
    wide = group * drows
    nd, nw = f // wide, f // W
    full = lambda shape: pl.BlockSpec(shape, lambda j: (0,) * len(shape))
    clamp = lambda j, low, count: jnp.clip(j - low, 0, count - 1)
    down = FFN_DOWN_AT // (2 * drows)

    def down_block(j):
        return (jnp.where(j < nd, jnp.minimum(j, nd - 1), clamp(j, nd + nw, nd)), down, 0)
    vm = pltpu.VMEM
    return pl.pallas_call(
        functools.partial(ffn_kernel, batch, width),
        grid=(nd + nw + nd,),
        in_specs=[pl.BlockSpec(memory_space=pltpu.SMEM), full(first.shape), full(normed_two.shape), full(cot.shape),
                  full(gain.shape),
                  pl.BlockSpec((n, rows, W), lambda j: (0, FFN_GATE_AT // rows + clamp(j, nd, nw), 0)),
                  pl.BlockSpec((n, rows, W), lambda j: (0, FFN_UP_AT // rows + clamp(j, nd, nw), 0)),
                  pl.BlockSpec((group, 2 * drows, W), down_block)],
        out_specs=[full((tokens, depth))] * 3 + [full((8, depth)), pl.BlockSpec(memory_space=pl.ANY)],
        out_shape=[jax.ShapeDtypeStruct((tokens, depth), F32), jax.ShapeDtypeStruct((tokens, depth), F32),
                   jax.ShapeDtypeStruct((tokens, depth), BF16), jax.ShapeDtypeStruct((8, depth), F32),
                   jax.ShapeDtypeStruct((n, 2 * nw * rows + 2 * drows, W), BF16)],
        scratch_shapes=[vm((tokens, depth), BF16), vm((tokens, f), F32), vm((tokens, f), BF16), vm((tokens, depth), F32),
                        vm((tokens, depth), F32), vm((tokens, W), F32), vm((tokens, W), F32), vm((tokens, W), BF16),
                        vm((tokens, W), BF16), vm((8, 128), BF16), vm((8, 128), BF16),
                        vm((2, n, rows, W), BF16), vm((2, group, drows, W), BF16),
                        pltpu.SemaphoreType.DMA((2,)), pltpu.SemaphoreType.DMA((2,))],
        compiler_params=pltpu.CompilerParams(vmem_limit_bytes=60 << 20),
    )(info, first, normed_two, cot, gain, packed, packed, packed)


def unproject_kernel(batch, width, dlow_ref, wo_ref, gated_ref, gate_ref, states_ref, decay_ref, pseg_ref,
                     dstates_ref, dgate_ref, gseg_ref, all_ref, grad_ref, stage, sem, gtot_ref, *rest):
    step = pl.program_id(0)
    swap = Exchange(all_ref.shape[0], gtot_ref, *rest)
    pl.when(step == 0)(lambda: greet(None, swap))
    tokens, depth = dlow_ref.shape
    orows = wo_ref.shape[1] // 2
    group = wo_ref.shape[0]
    wide = group * orows
    dg = dot_back(dlow_ref[:, :W], wo_ref[:, :orows].reshape(wide, W))
    spread(dstates_ref, dg + dot_back(dlow_ref[:, W:], wo_ref[:, orows:].reshape(wide, W)))

    def gating(t, b, spot, at, cols, _):
        gate, slope = gelu_both(gate_ref[t, at])
        d = dstates_ref[t, at]
        dstates_ref[t, at] = d * gate
        dgate_ref[at, cols] = (d * states_ref[t, at] * slope).astype(BF16)
        return 0
    each_tile(batch, width, wide // LANES, gating)
    for half in range(2):
        value = dot_outer(gated_ref[...], dlow_ref[:, half * W : (half + 1) * W]).astype(BF16)
        dst = grad_ref.at[pl.ds(step * group, group), pl.ds(OUT_AT + half * orows, orows)]
        put(stage, sem, half, dst, value.reshape(group, orows, W), step > 0)
    for t in range(wide // LANES):
        cols = lanes(t)
        for b in range(batch):
            grad = jnp.zeros((SEGS, LANES), F32)
            for s in reversed(range(width // SEGS)):
                at = strided(b, width, s)
                grad = decay_ref[t, at] * (dstates_ref[t, at] + grad)
            gseg_ref[b * SEGS : (b + 1) * SEGS, cols] = grad
            whole = grad[SEGS - 1 :]
            for i in reversed(range(SEGS - 1)):
                whole = grad[i : i + 1] + pseg_ref[b * SEGS + i : b * SEGS + i + 1, cols] * whole
            gtot_ref[step * (wide // LANES) + t, b : b + 1] = whole

    @pl.when(step == pl.num_programs(0) - 1)
    def _():
        for half in range(2):
            pltpu.make_async_copy(stage.at[half], grad_ref.at[pl.ds(0, group), pl.ds(OUT_AT, orows)], sem.at[half]).wait()
        swap.begin()
        swap.finish()
        all_ref[...] = swap.land[...]


def unproject(dlow, packed, gated, gate_pre, states, decay, pseg, batch, n_seq):
    tokens, r = gated.shape
    depth = dlow.shape[1]
    width = tokens // batch
    n = packed.shape[0]
    orows = r // n
    group = n // 2
    wide = group * orows
    col = lambda count: pl.BlockSpec((count, wide), lambda j: (0, j))
    return pl.pallas_call(
        functools.partial(unproject_kernel, batch, width),
        grid=(n // group,),
        in_specs=[pl.BlockSpec((tokens, depth), lambda j: (0, 0)),
                  pl.BlockSpec((group, 2 * orows, W), lambda j: (j, OUT_AT // (2 * orows), 0)),
                  col(tokens)] + [tiled(tokens, wide, lambda j: j)] * 3 + [col(batch * SEGS)],
        out_specs=[tiled(tokens, wide, lambda j: j), col(tokens), col(batch * SEGS),
                   pl.BlockSpec((n_seq, r // LANES, batch, LANES), lambda j: (0, 0, 0, 0)), pl.BlockSpec(memory_space=pl.ANY)],
        out_shape=[jax.ShapeDtypeStruct((r // LANES, tokens, LANES), F32), jax.ShapeDtypeStruct((tokens, r), BF16),
                   jax.ShapeDtypeStruct((batch * SEGS, r), F32), jax.ShapeDtypeStruct((n_seq, r // LANES, batch, LANES), F32),
                   jax.ShapeDtypeStruct((n, REC_ROWS, W), BF16)],
        scratch_shapes=[pltpu.VMEM((2, group, orows, W), BF16),
                        pltpu.SemaphoreType.DMA((2,))] + Exchange.scratch(n_seq, (r // LANES, batch, LANES)),
        compiler_params=pltpu.CompilerParams(collective_id=4, has_side_effects=True, vmem_limit_bytes=60 << 20),
    )(dlow, packed, gated, gate_pre, states, decay, pseg)


def recur_kernel(batch, width, n_seq, info_ref, mixed_ref, decay_ref, dstates_ref, states_ref, rate_ref, entry_ref,
                 pseg_ref, gseg_ref, sstart_ref, pall_ref, gall_ref, vec_ref, wr_ref, we_ref, _,
                 dmixed_ref, sums_ref, grad_ref, carried, across, gstart, rl, el, direct, stage, sem):
    step = pl.program_id(0)
    tokens, r = mixed_ref.shape
    n = grad_ref.shape[0]
    rows = r // n
    parts = r // W
    group = wr_ref.shape[0]
    wide = group * rows

    @pl.when(step < parts)
    def _():
        me = info_ref[batch]
        for b in range(batch):
            for t in range(W // LANES):
                cols = lanes(t)
                grad = jnp.zeros((1, LANES), F32)
                for k in reversed(range(n_seq)):
                    new = pall_ref[k, t, b : b + 1] * grad + gall_ref[k, t, b : b + 1]
                    grad = jnp.where(k > me, new, grad)
                for i in reversed(range(SEGS)):
                    at = b * SEGS + i
                    gstart[i : i + 1, cols] = grad
                    grad = pseg_ref[at : at + 1, cols] * grad + gseg_ref[at : at + 1, cols]
                grad = gstart[:, cols]
                for s in reversed(range(width // SEGS)):
                    at = strided(b, width, s)
                    total = dstates_ref[t, at] + grad
                    carried[t, at] = total
                    grad = decay_ref[t, at] * total
                    before = states_ref[t, strided(b, width, s - 1)] if s else sstart_ref[b * SEGS : (b + 1) * SEGS, lanes(t)]
                    across[t, at] = grad * before
        j = jnp.minimum(step, parts - 1)
        here = pl.ds(pl.multiple_of(j * W, W), W)

        def gating(t, b, spot, at, cols, sums):
            tile = pl.ds(pl.multiple_of(j * W + t * LANES, LANES), LANES)
            coef = vec_ref[COEF : COEF + 1, cols]
            rate, entry = rate_ref[t, at], entry_ref[t, at]
            valid = in_row(spot, width, rate.shape) < info_ref[b]
            grad = jnp.where(valid, carried[t, at], 0.0)
            z = 2.0 * coef * rate
            exp_z = jnp.exp(z)
            under = one_less_exp(z, exp_z)
            inverse = lax.rsqrt(under)
            root = under * inverse
            mixed = mixed_ref[at, tile].astype(F32)
            part = grad * entry
            d_log = jnp.where(valid, across[t, at], 0.0) - part * mixed * exp_z * inverse
            d_rate = coef * d_log * rate * (1.0 - rate)
            straight = part * root
            d_entry = straight * mixed * (1.0 - entry)
            direct[at, tile] = straight
            rl[at, tile] = d_rate.astype(BF16)
            el[at, tile] = d_entry.astype(BF16)
            return (sums[0] + fold8(d_log * rate), sums[1] + fold8(d_rate), sums[2] + fold8(d_entry))
        zero = jnp.zeros((8, LANES), F32)
        sums = each_tile(batch, width, W // LANES, gating, (zero, zero, zero))
        sums_ref[...] = jnp.zeros_like(sums_ref)
        for t, kept in enumerate(sums):
            for line in range(3):
                factor = 8.0 * vec_ref[SIG : SIG + 1, lanes(t)] if line == 0 else 1.0
                sums_ref[line : line + 1, lanes(t)] = factor * jnp.sum(kept[line], axis=0, keepdims=True)
        for which, low_grad, base in ((0, rl, RATE_AT), (1, el, ENTRY_AT)):
            value = dot_outer(mixed_ref[...], low_grad[:, here]).astype(BF16).reshape(n, rows, W)
            dst = grad_ref.at[:, pl.ds(pl.multiple_of(base + j * rows, 16), rows)]
            put(stage, sem, which, dst, value, step > 0)

    @pl.when(step >= parts)
    def _():
        k = jnp.maximum(step - parts, 0)
        here = pl.ds(pl.multiple_of(k * wide, wide), wide)
        total = direct[:, here]
        for p in range(parts):
            cols = slice(p * W, (p + 1) * W)
            total = total + dot_back(rl[:, cols], wr_ref[:, p * rows : (p + 1) * rows].reshape(wide, W))
            total = total + dot_back(el[:, cols], we_ref[:, p * rows : (p + 1) * rows].reshape(wide, W))
        dmixed_ref[...] = total

    @pl.when(step == pl.num_programs(0) - 1)
    def _():
        for which in range(2):
            pltpu.make_async_copy(stage.at[which], grad_ref.at[:, pl.ds(0, rows)], sem.at[which]).wait()


def recur_back(info, mixed, decay, dstates, states, rate, entry, pseg, gseg, sstart, pall, gall, vec, packed, grad, batch):
    tokens, r = mixed.shape
    width = tokens // batch
    n = packed.shape[0]
    rows = r // n
    parts = r // W
    group = n // 2
    wide = group * rows
    n_seq = pall.shape[0]
    col = lambda count: pl.BlockSpec((count, W), lambda j: (0, jnp.minimum(j, parts - 1)))
    over = lambda a: pl.BlockSpec((n_seq, W // LANES) + a.shape[2:], lambda j: (0, jnp.minimum(j, parts - 1), 0, 0))
    later = lambda j: jnp.maximum(j - parts, 0)
    vm = pltpu.VMEM
    return pl.pallas_call(
        functools.partial(recur_kernel, batch, width, n_seq),
        grid=(parts + n // group,),
        in_specs=[pl.BlockSpec(memory_space=pltpu.SMEM), pl.BlockSpec((tokens, r), lambda j: (0, 0))]
        + [tiled(tokens, W, lambda j: jnp.minimum(j, parts - 1))] * 5 + [col(batch * SEGS)] * 3 + [over(pall), over(gall), col(vec.shape[0]),
            pl.BlockSpec((group, parts * rows, W), lambda j: (later(j), RATE_AT // (parts * rows), 0)),
            pl.BlockSpec((group, parts * rows, W), lambda j: (later(j), ENTRY_AT // (parts * rows), 0)),
            pl.BlockSpec(memory_space=pl.ANY)],
        out_specs=[pl.BlockSpec((tokens, wide), lambda j: (0, later(j))), col(8), pl.BlockSpec(memory_space=pl.ANY)],
        out_shape=[jax.ShapeDtypeStruct((tokens, r), F32), jax.ShapeDtypeStruct((8, r), F32),
                   jax.ShapeDtypeStruct(grad.shape, grad.dtype)],
        input_output_aliases={15: 2},
        scratch_shapes=[vm((W // LANES, tokens, LANES), F32), vm((W // LANES, tokens, LANES), F32), vm((SEGS, W), F32), vm((tokens, r), BF16),
                        vm((tokens, r), BF16), vm((tokens, r), F32), vm((2, n, rows, W), BF16),
                        pltpu.SemaphoreType.DMA((2,))],
        compiler_params=pltpu.CompilerParams(vmem_limit_bytes=60 << 20),
    )(info, mixed, decay, dstates, states, rate, entry, pseg, gseg, sstart, pall, gall, vec, packed, packed, grad)


def entry_kernel(batch, width, dmixed_ref, rim_ref, inner_ref, dgate_ref, normed_ref, wg_ref, wi_ref, vec_ref,
                 x_ref, dfirst_ref, gain_ref, _, sums_ref, token_ref, ggain_ref, grad_ref, ext, di, dn, stage, sem):
    step = pl.program_id(0)
    tokens, depth = x_ref.shape
    n = grad_ref.shape[0]
    rows = depth // n
    span = width + 8
    sums_ref[...] = jnp.zeros_like(sums_ref)
    for b in range(batch):
        ext[b * span : b * span + width] = dmixed_ref[b * width : (b + 1) * width]
        ext[b * span + width : (b + 1) * span] = rim_ref[b * 8 : (b + 1) * 8]
    for b in range(batch):
        total = jnp.zeros((width, W), F32)
        for lag in range(4):
            total = total + vec_ref[lag : lag + 1] * ext[b * span + lag : b * span + lag + width]
        di[b * width : (b + 1) * width] = total.astype(BF16)
        d_mixed = dmixed_ref[b * width : (b + 1) * width]
        for lag in range(4):
            product = d_mixed * inner_ref[b * span + 8 - lag : (b + 1) * span - lag]
            sums_ref[lag : lag + 1] += jnp.sum(product, axis=0, keepdims=True)
        sums_ref[4:5] += jnp.sum(d_mixed, axis=0, keepdims=True)
    wg = wg_ref[...].reshape(depth, W)
    wi = wi_ref[...].reshape(depth, W)
    more = dot_back(dgate_ref[...], wg) + dot_back(di[...], wi)

    @pl.when(step == 0)
    def _():
        dn[...] = more

    @pl.when(step > 0)
    def _():
        dn[...] += more
    for which, low_grad, base in ((0, dgate_ref, GATE_AT), (1, di, INPUT_AT)):
        value = dot_outer(normed_ref[...], low_grad[...]).astype(BF16).reshape(n, rows, W)
        dst = grad_ref.at[:, pl.ds(pl.multiple_of(base + step * rows, 16), rows)]
        put(stage, sem, which, dst, value, step > 0)

    @pl.when(step == pl.num_programs(0) - 1)
    def _():
        def finish(i, total):
            at = rows_at(i * CHUNK)
            value, grad = x_ref[at].astype(F32), dn[at]
            scale = inverse_norm(value, depth)
            weighted = grad * gain_ref[:1]
            spread = jnp.sum(weighted * value, axis=-1, keepdims=True) * (1.0 / depth)
            token_ref[at] = dfirst_ref[at] + scale * weighted - value * (scale * scale * scale * spread)
            return total + fold8(grad * value * scale)
        ggain_ref[...] = lax.fori_loop(0, tokens // CHUNK, finish, jnp.zeros((8, depth), F32))
        for which in range(2):
            pltpu.make_async_copy(stage.at[which], grad_ref.at[:, pl.ds(0, rows)], sem.at[which]).wait()


def entry_back(dmixed, rim, inner, dgate, normed, packed, vec, tokens2, dfirst, gain, grad, batch):
    tokens, r = dmixed.shape
    depth = tokens2.shape[1]
    width = tokens // batch
    n = packed.shape[0]
    rows = depth // n
    col = lambda count: pl.BlockSpec((count, W), lambda j: (0, j))
    full = lambda shape: pl.BlockSpec(shape, lambda j: (0,) * len(shape))
    vm = pltpu.VMEM
    return pl.pallas_call(
        functools.partial(entry_kernel, batch, width),
        grid=(r // W,),
        in_specs=[col(tokens), col(rim.shape[0]), col(inner.shape[0]), col(tokens), full(normed.shape),
                  pl.BlockSpec((n, rows, W), lambda j: (0, GATE_AT // rows + j, 0)),
                  pl.BlockSpec((n, rows, W), lambda j: (0, INPUT_AT // rows + j, 0)),
                  col(vec.shape[0]), full(tokens2.shape), full(dfirst.shape), full(gain.shape),
                  pl.BlockSpec(memory_space=pl.ANY)],
        out_specs=[col(8), full((tokens, depth)), full((8, depth)), pl.BlockSpec(memory_space=pl.ANY)],
        out_shape=[jax.ShapeDtypeStruct((8, r), F32), jax.ShapeDtypeStruct((tokens, depth), F32),
                   jax.ShapeDtypeStruct((8, depth), F32), jax.ShapeDtypeStruct(grad.shape, grad.dtype)],
        input_output_aliases={11: 3},
        scratch_shapes=[vm((tokens + 8 * batch, W), F32), vm((tokens, W), BF16), vm((tokens, depth), F32),
                        vm((2, n, rows, W), BF16), pltpu.SemaphoreType.DMA((2,))],
        compiler_params=pltpu.CompilerParams(vmem_limit_bytes=60 << 20),
    )(dmixed, rim, inner, dgate, normed, packed, packed, vec, tokens2, dfirst, gain, grad)


MESH = pl.DeviceIdType.MESH
ROUTES = (("z", "x", "y"), ("z", "y", "x"), ("x", "z", "y"), ("y", "z", "x"))
ZN = 4
STG = 4
SEM = pltpu.SemaphoreType.DMA


def place():
    s = lax.axis_index("seq")
    return lax.rem(s, 2), lax.rem(lax.div(s, 2), 2), lax.div(s, 4), lax.axis_index("batch")


def flip(value, by):
    return 1 - value if by else value


def seq_of(y, x, c):
    return (y * 2 + x) * 2 + c


def far(z, j):
    if j == ZN - 1:
        return z
    found = None
    for here in range(ZN):
        others = sorted((q for q in range(ZN) if q != here), key=lambda q: (-abs(q - here), q))
        found = jnp.int32(others[j]) if found is None else jnp.where(z == here, others[j], found)
    return found


class Links:
    def __init__(self):
        self.c, self.x, self.y, self.z = c, x, y, z = place()
        self.beside = {
            "x": (seq_of(y, 1 - x, c), z),
            "y": (seq_of(1 - y, x, c), z),
            "up": (seq_of(y, x, c), z + 1),
            "dn": (seq_of(y, x, c), z - 1),
            "core": (seq_of(y, x, 1 - c), z),
        }
        self.spots = [far(z, j) for j in range(ZN)]
        self.above, self.below = z < ZN - 1, z > 0

    def slot(self, dx, dy, z, core):
        return seq_of(flip(self.y, dy), flip(self.x, dx), core) * ZN + z

    def copy(self, src, dst, send, recv, d):
        return pltpu.make_async_remote_copy(src, dst, send, recv, device_id=self.beside[d], device_id_type=MESH)


def greet(links, swap):
    bar = pltpu.get_barrier_semaphore()
    count = 0
    if swap is not None:
        count = swap.n - 1
        for k in range(1, swap.n):
            pl.semaphore_signal(bar, inc=1, device_id=swap.peer(k), device_id_type=MESH)
    if links is not None:
        def signal(d):
            pl.semaphore_signal(bar, inc=1, device_id=links.beside[d], device_id_type=MESH)
        if swap is None:
            count = 3
            for d in ("x", "y", "core"):
                signal(d)
        pl.when(links.above)(lambda: signal("up"))
        pl.when(links.below)(lambda: signal("dn"))
        count = count + links.above.astype(jnp.int32) + links.below.astype(jnp.int32)
    pl.semaphore_wait(bar, count)


class Exchange:
    def __init__(self, n, rows, land, send, recv, own):
        self.n, self.rows, self.land, self.send, self.recv, self.own = n, rows, land, send, recv, own
        self.me, self.z = lax.axis_index("seq"), lax.axis_index("batch")

    @staticmethod
    def scratch(n, shape):
        return [pltpu.VMEM(shape, F32), pltpu.VMEM((n,) + shape, F32), SEM((n,)), SEM((n,)), SEM]

    def peer(self, k):
        return (lax.rem(self.me + k, self.n), self.z)

    def copies(self):
        return [
            pltpu.make_async_remote_copy(self.rows, self.land.at[self.me], self.send.at[k], self.recv.at[k],
                                         device_id=self.peer(k), device_id_type=MESH)
            for k in range(1, self.n)
        ]

    def mine(self):
        return pltpu.make_async_copy(self.rows, self.land.at[self.me], self.own)

    def begin(self):
        self.mine().start()
        for copy in self.copies():
            copy.start()

    def finish(self):
        self.mine().wait()
        for copy in self.copies():
            copy.wait()


def onward(order, dx, dy, same):
    off = {"x": dx, "y": dy, "z": 0 if same else 1}
    return [
        d for i, d in enumerate(order)
        if not any(off[e] for e in order[i + 1 :]) and not (d != "z" and off[d])
    ]


def arrival(order, dx, dy, same):
    off = {"x": dx, "y": dy, "z": 0 if same else 1}
    return [d for d in order if off[d]][-1]


def blocks(parts):
    found = [
        (dx + dy + ZN - 1 - j, r, dx, dy, j)
        for dx in range(2) for dy in range(2) for j in range(ZN) for r in range(len(parts))
    ]
    return found


class Gather:
    def __init__(self, parts, ins, outs, send, recv, csend, crecv, lsem):
        self.parts, self.ins, self.outs = parts, ins, outs
        self.send, self.recv, self.csend, self.crecv, self.lsem = send, recv, csend, crecv, lsem
        self.links = Links()
        self.events = sorted(blocks(parts), key=lambda e: e[0])

    @staticmethod
    def scratch(parts):
        n = len(parts)
        return [SEM((n, 4, 4, ZN)), SEM((n, 4, ZN)), SEM((n, 4, ZN)), SEM((n, 4, ZN)), SEM((n,))]

    def window(self, r):
        return pl.ds(self.parts[r][2], self.parts[r][3])

    def dst(self, r, dx, dy, zs):
        return self.outs[self.parts[r][1]].at[self.links.slot(dx, dy, zs, self.links.c), self.window(r)]

    def src(self, r, dx, dy, zs, own):
        return self.ins[self.parts[r][0]].at[self.window(r)] if own else self.dst(r, dx, dy, zs)

    def hop(self, r, dx, dy, zs, d, own):
        to = (1 if d == "x" else dx) * 2 + (1 if d == "y" else dy)
        which = ("x", "y", "up", "dn").index(d)
        return self.links.copy(self.src(r, dx, dy, zs, own), self.dst(r, dx, dy, zs),
                               self.send.at[r, which, dx * 2 + dy, zs], self.recv.at[r, to, zs], d)

    def across(self, r, dx, dy, zs, own):
        return self.links.copy(self.src(r, dx, dy, zs, own), self.dst(r, dx, dy, zs),
                               self.csend.at[r, dx * 2 + dy, zs], self.crecv.at[r, dx * 2 + dy, zs], "core")

    def hops(self, r, dx, dy, j, act):
        links, zs = self.links, self.links.spots[j]
        z, same = links.z, j == ZN - 1
        own = same and not dx and not dy
        for d in onward(ROUTES[self.parts[r][4]], dx, dy, same):
            if d != "z":
                act(self.hop(r, dx, dy, zs, d, own))
                continue
            up = links.above if same else jnp.logical_and(z > zs, links.above)
            down = links.below if same else jnp.logical_and(z < zs, links.below)
            pl.when(up)(lambda: act(self.hop(r, dx, dy, zs, "up", own)))
            pl.when(down)(lambda: act(self.hop(r, dx, dy, zs, "dn", own)))

    def forward(self, event):
        _, r, dx, dy, j = event
        zs, own = self.links.spots[j], j == ZN - 1 and not dx and not dy
        if not own:
            self.links.copy(self.dst(r, dx, dy, zs), self.dst(r, dx, dy, zs), self.send.at[r, 0, 0, 0],
                            self.recv.at[r, dx * 2 + dy, zs], "core").wait_recv()
        self.hops(r, dx, dy, j, lambda copy: copy.start())
        self.across(r, dx, dy, zs, own).start()
        if own:
            self.local(r).start()

    def local(self, r):
        return pltpu.make_async_copy(self.ins[self.parts[r][0]].at[self.window(r)],
                                     self.dst(r, 0, 0, self.links.z), self.lsem.at[r])

    def finish(self):
        for _, r, dx, dy, j in self.events:
            own = j == ZN - 1 and not dx and not dy
            self.hops(r, dx, dy, j, lambda copy: copy.wait_send())
            copy = self.across(r, dx, dy, self.links.spots[j], own)
            copy.wait_send()
            copy.wait_recv()
            if own:
                self.local(r).wait()


def gather(parts, ins, rows):
    n = len(ins)

    def kernel(*refs):
        job = Gather(parts, refs[:n], refs[n : n + len(rows)], *refs[n + len(rows) :])
        greet(job.links, None)
        for event in job.events:
            job.forward(event)
        job.finish()
    anywhere = pl.BlockSpec(memory_space=pl.ANY)
    return pl.pallas_call(
        kernel,
        out_shape=[jax.ShapeDtypeStruct((8 * ZN, count, W), jnp.bfloat16) for count in rows],
        in_specs=[anywhere] * n,
        out_specs=[anywhere] * len(rows),
        scratch_shapes=Gather.scratch(parts),
        compiler_params=pltpu.CompilerParams(collective_id=1, has_side_effects=True),
    )(*ins)


def layout(order):
    base, count = {}, 0
    for i, d in enumerate(order):
        base[d] = count
        free = 1
        for e in order[:i]:
            free *= ZN if e == "z" else 2
        count += free * ((ZN + 1) if d == "z" else 1)
    return base, count


class Scatter:
    def __init__(self, parts, ins, out, sib, stage, send, csend, crecv, lsem, *rest):
        self.parts, self.ins, self.out, self.sib, self.stage = parts, ins, out, sib, stage
        self.send, self.csend, self.crecv, self.lsem = send, csend, crecv, lsem
        self.bufs, self.recv = rest[: len(parts)], rest[len(parts) :]
        self.links = Links()
        self.events = sorted(blocks(parts), key=lambda e: -e[0])
        self.lay = [layout(ROUTES[part[3]]) for part in parts]
        self.starts = [sum(part[2] for part in parts[:r]) for r in range(len(parts))]

    @staticmethod
    def scratch(parts):
        n, total = len(parts), sum(part[2] for part in parts)
        counts = [layout(ROUTES[part[3]])[1] for part in parts]
        most = max(part[2] for part in parts)
        return [pltpu.VMEM((4, ZN, total, W), jnp.bfloat16), pltpu.VMEM((STG, most, W), jnp.bfloat16), SEM((n, 4, ZN)),
                SEM((n, 4, ZN)), SEM((n, 4, ZN)), SEM((STG,))] + [
            pltpu.VMEM((count, part[2], W), jnp.bfloat16) for count, part in zip(counts, parts)
        ] + [SEM((count,)) for count in counts]

    def mine(self, r):
        return pl.ds(self.starts[r], self.parts[r][2])

    def source(self, r, dx, dy, zd, core):
        which, start, rows, _ = self.parts[r]
        return self.ins[which].at[self.links.slot(dx, dy, zd, core), pl.ds(start, rows)]

    def child(self, r, d, dx, dy, zd):
        order = ROUTES[self.parts[r][3]]
        dim = d if d in "xy" else "z"
        index = 0
        for e in order[: order.index(dim)]:
            index = index * ZN + zd if e == "z" else index * 2 + (dx if e == "x" else dy)
        if dim == "z":
            index = index * (ZN + 1) + (zd if d == "up" else zd + 1)
        return self.lay[r][0][dim] + index

    def across(self, event):
        _, r, dx, dy, j = event
        zd = self.links.spots[j]
        return self.links.copy(self.source(r, dx, dy, zd, 1 - self.links.c), self.sib.at[dx * 2 + dy, zd, self.mine(r)],
                               self.csend.at[r, dx * 2 + dy, zd], self.crecv.at[r, dx * 2 + dy, zd], "core")

    def load(self, i):
        _, r, dx, dy, j = self.events[i]
        return pltpu.make_async_copy(self.source(r, dx, dy, self.links.spots[j], self.links.c),
                                     self.stage.at[i % STG, pl.ds(0, self.parts[r][2])], self.lsem.at[i % STG])

    def hop(self, r, dx, dy, zd, d):
        came = {"x": "x", "y": "y", "up": "dn", "dn": "up"}[d]
        at = self.child(r, came, 0 if d == "x" else dx, 0 if d == "y" else dy, zd)
        return self.links.copy(self.sib.at[dx * 2 + dy, zd, self.mine(r)], self.bufs[r].at[at],
                               self.send.at[r, dx * 2 + dy, zd], self.recv[r].at[at], d)

    def add(self, i, dirs):
        _, r, dx, dy, j = self.events[i]
        zd = self.links.spots[j]
        final = j == ZN - 1 and not dx and not dy
        at = [self.child(r, d, dx, dy, zd) for d in dirs]
        for k in at:
            self.links.copy(self.bufs[r].at[k], self.bufs[r].at[k], self.send.at[r, 0, 0], self.recv[r].at[k], "core").wait_recv()

        def body(q, _):
            low = pl.ds(pl.multiple_of(q * 16, 16), 16)
            here = pl.ds(pl.multiple_of(self.starts[r] + q * 16, 16), 16)
            total = self.stage[i % STG, low].astype(jnp.float32) + self.sib[dx * 2 + dy, zd, here].astype(jnp.float32)
            for k in at:
                total = total + self.bufs[r][k, low].astype(jnp.float32)
            if final:
                self.out[here] = total
            else:
                self.sib[dx * 2 + dy, zd, here] = total.astype(jnp.bfloat16)
            return 0
        lax.fori_loop(0, self.parts[r][2] // 16, body, 0)

    def begin(self):
        for event in self.events:
            self.across(event).start()
        for i in range(STG - 1):
            self.load(i).start()

    def step(self, i):
        links = self.links
        _, r, dx, dy, j = self.events[i]
        zd, z, same = links.spots[j], links.z, j == ZN - 1
        order = ROUTES[self.parts[r][3]]
        if i + STG - 1 < len(self.events):
            self.load(i + STG - 1).start()
        self.load(i).wait()
        self.across(self.events[i]).wait_recv()
        kids = onward(order, dx, dy, same)
        fixed = [d for d in kids if d != "z"]
        if "z" not in kids:
            self.add(i, fixed)
        elif same:
            pl.when(z == 0)(lambda: self.add(i, fixed + ["up"]))
            pl.when(z == ZN - 1)(lambda: self.add(i, fixed + ["dn"]))
            pl.when(jnp.logical_and(links.below, links.above))(lambda: self.add(i, fixed + ["up", "dn"]))
        else:
            pl.when(jnp.logical_and(z > zd, links.above))(lambda: self.add(i, fixed + ["up"]))
            pl.when(jnp.logical_and(z < zd, links.below))(lambda: self.add(i, fixed + ["dn"]))
            pl.when(jnp.logical_or(z == 0, z == ZN - 1))(lambda: self.add(i, fixed))
        if not (same and not dx and not dy):
            d = arrival(order, dx, dy, same)
            if d == "z":
                pl.when(zd > z)(lambda: self.hop(r, dx, dy, zd, "up").start())
                pl.when(zd < z)(lambda: self.hop(r, dx, dy, zd, "dn").start())
            else:
                self.hop(r, dx, dy, zd, d).start()

    def finish(self):
        for event in self.events:
            _, r, dx, dy, j = event
            self.across(event).wait_send()
            if not (j == ZN - 1 and not dx and not dy):
                self.hop(r, dx, dy, self.links.spots[j], "x").wait_send()


def scatter(parts, ins):
    n, total = len(ins), sum(part[2] for part in parts)

    def kernel(*refs):
        job = Scatter(parts, refs[:n], *refs[n:])
        greet(job.links, None)
        job.begin()
        for i in range(len(job.events)):
            job.step(i)
        job.finish()
    return pl.pallas_call(
        kernel,
        out_shape=jax.ShapeDtypeStruct((total, W), jnp.float32),
        in_specs=[pl.BlockSpec(memory_space=pl.ANY)] * n,
        out_specs=pl.BlockSpec(memory_space=pltpu.VMEM),
        scratch_shapes=Scatter.scratch(parts),
        compiler_params=pltpu.CompilerParams(collective_id=2, has_side_effects=True, vmem_limit_bytes=62 << 20),
    )(*ins)


class Sends:
    def __init__(self, sems):
        self.sems, self.used = sems, []

    def add(self, src, dst):
        copy = pltpu.make_async_copy(src, dst, self.sems.at[len(self.used)])
        self.used.append(copy)
        return copy

    def finish(self):
        for copy in self.used:
            copy.wait()


def spaced(events, slots):
    bounds = [len(events) * i // slots for i in range(slots + 1)]
    return [events[bounds[i] : bounds[i + 1]] for i in range(slots)]


FORWARD_OUTS = 13


def forward_kernel(batch, width, n_seq, info_ref, x_ref, rim_ref, gain_ref, gain2_ref, vec_ref,
                   wg_ref, wi_ref, wr_ref, we_ref, wo_ref, shard_ref, *refs):
    outs, refs = refs[:FORWARD_OUTS], refs[FORWARD_OUTS:]
    (gate_o, inner_o, mixed_o, normed_o, rate_o, entry_o, decay_o, states_o, pseg_o, sstart_o, all_o,
     gated_o, first_o) = outs
    normed2_o, weights_o = refs[:2]
    (ext, gate, inner, mixed, rate, entry, decay, drive, states, pseg, hseg, sstart, gated, first, normed2,
     sems) = refs[2:18]
    swap = Exchange(n_seq, *refs[18:23])
    job = Gather(FFN_GATHER, [shard_ref], [weights_o], *refs[23:])
    step = pl.program_id(0)
    tokens, depth = x_ref.shape
    r = mixed.shape[1]
    parts, tiles, halves = r // W, W // LANES, depth // W
    steps = 3 * parts + halves
    span = width + 8
    plan = spaced(job.events[len(FFN_GATHER) :], 2 * steps)

    def pump(half, low, high):
        for s in range(low, high):
            if plan[2 * s + half]:
                @pl.when(step == s)
                def _():
                    for event in plan[2 * s + half]:
                        job.forward(event)
    sends = Sends(sems)
    branch_sends = [sends.add(gate, gate_o), sends.add(inner, inner_o), sends.add(mixed, mixed_o),
                    sends.add(ext.at[pl.ds(0, tokens)], normed_o)]
    gate_sends = [sends.add(rate, rate_o), sends.add(entry, entry_o), sends.add(decay, decay_o), sends.add(pseg, pseg_o)]
    state_sends = [sends.add(states, states_o), sends.add(sstart, sstart_o), sends.add(swap.land, all_o),
                   sends.add(gated, gated_o)]
    last_sends = [sends.add(first, first_o), sends.add(normed2, normed2_o)]

    def start(copies):
        for copy in copies:
            copy.start()

    @pl.when(step == 0)
    def _():
        greet(job.links, swap)
        for event in job.events[: len(FFN_GATHER)]:
            job.forward(event)
        gain = gain_ref[:1]

        def norm(i, _):
            at = rows_at(i * CHUNK)
            value = x_ref[at].astype(F32)
            ext[at] = (value * inverse_norm(value, depth) * gain).astype(BF16)
            return 0
        lax.fori_loop(0, tokens // CHUNK, norm, 0)
        rim = rim_ref[...].astype(F32)
        ext[pl.ds(tokens, rim.shape[0])] = (rim * inverse_norm(rim, depth) * gain).astype(BF16)

    @pl.when(step < parts)
    def _():
        j = jnp.minimum(step, parts - 1)
        here = pl.ds(pl.multiple_of(j * W, W), W)
        pump(0, 0, parts)
        got = dot(ext[:tokens], wg_ref[...].reshape(depth, W))
        for t in range(tiles):
            gate[j * tiles + t] = got[:, lanes(t)]
        got = dot(ext[...], wi_ref[...].reshape(depth, W))
        for b in range(batch):
            inner[b * span : b * span + 8, here] = got[tokens + 8 * b : tokens + 8 * b + 8]
            inner[b * span + 8 : (b + 1) * span, here] = got[b * width : (b + 1) * width]
        pump(1, 0, parts)
        for b in range(batch):
            conv = vec_ref[CONV_BIAS : CONV_BIAS + 1, here]
            for lag in range(4):
                conv = conv + vec_ref[lag : lag + 1, here] * inner[b * span + 8 - lag : (b + 1) * span - lag, here]
            mixed[b * width : (b + 1) * width, here] = conv.astype(BF16)

    @pl.when(step == parts - 1)
    def _():
        start(branch_sends)

    @pl.when(jnp.logical_and(step >= parts, step < 2 * parts))
    def _():
        j = jnp.clip(step - parts, 0, parts - 1)
        pump(0, parts, 2 * parts)
        for w_ref, to in ((wr_ref, rate), (we_ref, entry)):
            got = dot(mixed[...], w_ref[...].reshape(r, W))
            for t in range(tiles):
                to[j * tiles + t] = got[:, lanes(t)]
        pump(1, parts, 2 * parts)

        def gating(t, b, spot, at, cols, _):
            g = j * tiles + t
            tile = pl.ds(pl.multiple_of(j * W + t * LANES, LANES), LANES)
            a_rate = sigmoid(rate[g, at] + vec_ref[RATE_BIAS : RATE_BIAS + 1, tile])
            an_entry = sigmoid(entry[g, at] + vec_ref[ENTRY_BIAS : ENTRY_BIAS + 1, tile])
            log_decay = vec_ref[COEF : COEF + 1, tile] * a_rate
            z = 2.0 * log_decay
            root = jnp.sqrt(one_less_exp(z, jnp.exp(z)))
            valid = in_row(spot, width, a_rate.shape) < info_ref[b]
            rate[g, at] = a_rate
            entry[g, at] = an_entry
            decay[g, at] = jnp.where(valid, jnp.exp(log_decay), 1.0)
            drive[g, at] = jnp.where(valid, root * an_entry * mixed[at, tile].astype(F32), 0.0)
            return 0
        each_tile(batch, width, tiles, gating)
        for t in range(tiles):
            g = j * tiles + t
            tile = pl.ds(pl.multiple_of(j * W + t * LANES, LANES), LANES)
            for b in range(batch):
                prod = jnp.ones((SEGS, LANES), F32)
                state = jnp.zeros((SEGS, LANES), F32)
                for s in range(width // SEGS):
                    at = strided(b, width, s)
                    a = decay[g, at]
                    state = a * state + drive[g, at]
                    prod = prod * a
                pseg[b * SEGS : (b + 1) * SEGS, tile] = prod
                hseg[b * SEGS : (b + 1) * SEGS, tile] = state
                whole, end = prod[:1], state[:1]
                for i in range(1, SEGS):
                    whole = whole * prod[i : i + 1]
                    end = prod[i : i + 1] * end + state[i : i + 1]
                swap.rows[g, b : b + 1] = whole
                swap.rows[g, batch + b : batch + b + 1] = end

    @pl.when(step == 2 * parts - 1)
    def _():
        start(gate_sends)
        swap.begin()

    @pl.when(step == 2 * parts)
    def _():
        swap.finish()

    @pl.when(jnp.logical_and(step >= 2 * parts, step < 3 * parts))
    def _():
        j = jnp.clip(step - 2 * parts, 0, parts - 1)
        me = lax.axis_index("seq")
        pump(0, 2 * parts, 3 * parts)
        for t in range(tiles):
            g = j * tiles + t
            tile = pl.ds(pl.multiple_of(j * W + t * LANES, LANES), LANES)
            for b in range(batch):
                begin = jnp.zeros((1, LANES), F32)
                for k in range(n_seq):
                    new = swap.land[k, g, b : b + 1] * begin + swap.land[k, g, batch + b : batch + b + 1]
                    begin = jnp.where(k < me, new, begin)
                for i in range(SEGS):
                    at = b * SEGS + i
                    sstart[at : at + 1, tile] = begin
                    begin = pseg[at : at + 1, tile] * begin + hseg[at : at + 1, tile]
                state = sstart[b * SEGS : (b + 1) * SEGS, tile]
                for s in range(width // SEGS):
                    at = strided(b, width, s)
                    state = decay[g, at] * state + drive[g, at]
                    states[g, at] = state
        pump(1, 2 * parts, 3 * parts)

        def gating(t, b, spot, at, cols, _):
            g = j * tiles + t
            tile = pl.ds(pl.multiple_of(j * W + t * LANES, LANES), LANES)
            gated[at, tile] = (states[g, at] * gelu_both(gate[g, at])[0]).astype(BF16)
            return 0
        each_tile(batch, width, tiles, gating)

    @pl.when(step == 3 * parts - 1)
    def _():
        start(state_sends)

    @pl.when(step >= 3 * parts)
    def _():
        half = jnp.clip(step - 3 * parts, 0, halves - 1)
        here = pl.ds(pl.multiple_of(half * W, W), W)
        pump(0, 3 * parts, steps)
        first[:, here] = x_ref[:, here].astype(F32) + dot(gated[...], wo_ref[...].reshape(r, W))
        pump(1, 3 * parts, steps)

    @pl.when(step == steps - 1)
    def _():
        def norm(i, _):
            at = rows_at(i * CHUNK)
            value = first[at]
            normed2[at] = (value * inverse_norm(value, depth) * gain2_ref[:1]).astype(BF16)
            return 0
        lax.fori_loop(0, tokens // CHUNK, norm, 0)
        start(last_sends)
        job.finish()
        sends.finish()


def forward(info, tokens2, rim, gain, gain2, vec, packed, shard, batch, n_seq):
    tokens, depth = tokens2.shape
    width = tokens // batch
    n = packed.shape[0]
    r = vec.shape[1]
    parts, halves, tiles = r // W, depth // W, r // LANES
    rows, rrows = depth // n, r // n
    full = lambda a: pl.BlockSpec(a.shape, lambda j: (0,) * a.ndim)
    anywhere = pl.BlockSpec(memory_space=pl.ANY)
    clamp = lambda j, low, count: jnp.clip(j - low, 0, count - 1)

    def block(count, at, low, number):
        return pl.BlockSpec((n, count, W), lambda j: (0, at // count + clamp(j, low, number), 0))
    S = jax.ShapeDtypeStruct
    flat, tall, segs = S((tokens, r), BF16), S((tiles, tokens, LANES), F32), S((batch * SEGS, r), F32)
    inner, ends = S((tokens + 8 * batch, r), F32), S((n_seq, tiles, 2 * batch, LANES), F32)
    first, normed = S((tokens, depth), F32), S((tokens, depth), BF16)
    outs = [tall, inner, flat, normed, tall, tall, tall, tall, segs, segs, ends, flat, first, normed,
            S((n, shard.shape[0], W), BF16)]
    vm = lambda s: pltpu.VMEM(s.shape, s.dtype)
    scratch = [pltpu.VMEM((tokens + 8 * batch, depth), BF16)] + [
        vm(s) for s in (tall, inner, flat, tall, tall, tall, tall, tall, segs, segs, segs, flat, first, normed)]
    return pl.pallas_call(
        functools.partial(forward_kernel, batch, width, n_seq),
        grid=(3 * parts + halves,),
        in_specs=[pl.BlockSpec(memory_space=pltpu.SMEM), full(tokens2), full(rim), full(gain), full(gain2), full(vec),
                  block(rows, GATE_AT, 0, parts), block(rows, INPUT_AT, 0, parts),
                  block(rrows, RATE_AT, parts, parts), block(rrows, ENTRY_AT, parts, parts),
                  block(rrows, OUT_AT, 3 * parts, halves), anywhere],
        out_specs=[anywhere] * len(outs),
        out_shape=outs,
        scratch_shapes=scratch + [SEM((FORWARD_OUTS + 1,))] + Exchange.scratch(n_seq, (tiles, 2 * batch, LANES))
        + Gather.scratch(FFN_GATHER),
        compiler_params=pltpu.CompilerParams(collective_id=3, has_side_effects=True, vmem_limit_bytes=62 << 20),
    )(info, tokens2, rim, gain, gain2, vec, packed, packed, packed, packed, packed, shard)


RATE_AT, ENTRY_AT, OUT_AT, GATE_AT, INPUT_AT, REC_ROWS = 0, 144, 288, 384, 480, 576
FFN_GATE_AT, FFN_UP_AT, FFN_DOWN_AT, FFN_ROWS, SMALL_ROWS = 0, 192, 384, 576, 16
REC_GATHER = ((0, 0, 0, 144, 0), (0, 0, 144, 144, 1), (0, 0, 288, 144, 2), (0, 0, 432, 160, 3))
FFN_GATHER = ((0, 0, 0, 144, 0), (0, 0, 144, 144, 1), (0, 0, 288, 144, 2), (0, 0, 432, 144, 3))
SCATTER_PARTS = ((0, 0, 288, 0), (0, 288, 288, 1), (1, 0, 288, 2), (1, 288, 288, 3), (2, 0, 16, 0))


def pack_blocks(item):
    rows, cols = item.shape
    return item.reshape(rows, cols // W, W).transpose(1, 0, 2).reshape(rows * cols // W, W)


def unpack_blocks(item, rows, cols):
    return item.reshape(cols // W, rows, W).transpose(1, 0, 2).reshape(rows, cols)


def pad_rows(item, before, count):
    batch, rows, cols = item.shape
    item = jnp.pad(item, ((0, 0), (before, count - rows - before), (0, 0)))
    return item.reshape(batch * count, cols)


def per_device_packed(tokens, cotangent, lengths, *shards):
    (gate_proj, input_proj, rate_proj, entry_proj, out_proj, ffn_gate, ffn_up, ffn_down) = shards[:8]
    small = shards[8:]
    batch, width, depth = tokens.shape
    r, f = gate_proj.shape[1], ffn_gate.shape[1]
    n_seq = lax.axis_size("seq")
    me = lax.axis_index("seq")
    rim = pad_rows(from_behind(tokens[:, width - 3 :], "seq", 1), 5, 8)
    flat = jnp.concatenate([item.reshape(-1) for item in small])
    flat = jnp.pad(flat, (0, SMALL_ROWS * W - flat.shape[0])).reshape(SMALL_ROWS, W)
    order = (rate_proj, entry_proj, out_proj, gate_proj, input_proj)
    shard = jnp.concatenate([pack_blocks(item) for item in order] + [flat], axis=0)
    packed = gather(REC_GATHER, [shard], [REC_ROWS + SMALL_ROWS])[0]
    shard = jnp.concatenate([pack_blocks(item) for item in (ffn_gate, ffn_up, ffn_down)], axis=0)
    flats = packed[:, REC_ROWS].astype(jnp.float32)
    lo, vectors = 0, []
    for item in small:
        part = flats[:, lo : lo + item.size]
        lo += item.size
        if item.ndim == 2:
            part = part.reshape(-1, *item.shape).transpose(1, 0, 2).reshape(item.shape[0], -1)
        else:
            part = part.reshape(1, -1)
        vectors.append(part)
    norm_gain, ffn_gain, taps, conv_bias, rate_bias, entry_bias, logit = vectors
    vec = jnp.concatenate([taps, conv_bias, rate_bias, entry_bias, -lru_scale * jax.nn.softplus(-logit),
                           jax.nn.sigmoid(-logit), jnp.zeros((7, r), jnp.float32)], axis=0)
    norm_gain = jnp.broadcast_to(norm_gain, (8, depth))
    ffn_gain = jnp.broadcast_to(ffn_gain, (8, depth))
    info = jnp.concatenate([jnp.clip(lengths - me * width, 0, width), me[None]]).astype(jnp.int32)
    tokens2 = tokens.reshape(batch * width, depth)
    cot2 = cotangent.reshape(batch * width, depth)

    (gate_pre, inner, mixed, normed, rate, entry, decay, states, pseg, sstart, pall, gated, first, normed_two,
     packed_ffn) = forward(info, tokens2, rim, norm_gain, ffn_gain, vec, packed, shard, batch, n_seq)
    block_out, d_first, d_low, g_ffn_gain, grad_ffn = feed_forward(info, first, normed_two, cot2, ffn_gain, packed_ffn, f, batch)
    d_states, d_gate, gseg, gall, grad_rec = unproject(d_low, packed, gated, gate_pre, states, decay, pseg, batch, n_seq)
    d_mixed, sums, grad_rec = recur_back(
        info, mixed, decay, d_states, states, rate, entry, pseg, gseg, sstart, pall, gall, vec, packed, grad_rec, batch)
    rim_back = from_behind(d_mixed.reshape(batch, width, r)[:, :3].astype(jnp.bfloat16), "seq", -1)
    rim_back = pad_rows(rim_back.astype(jnp.float32), 0, 8)
    csums, token_grad, g_norm_gain, grad_rec = entry_back(
        d_mixed, rim_back, inner, d_gate, normed, packed, vec, tokens2, d_first, norm_gain, grad_rec, batch)

    n = packed.shape[0]
    lines = [jnp.sum(g_norm_gain, axis=0).reshape(n, -1), jnp.sum(g_ffn_gain, axis=0).reshape(n, -1),
             csums[:4].reshape(4, n, -1).transpose(1, 0, 2).reshape(n, -1), csums[4].reshape(n, -1),
             sums[1].reshape(n, -1), sums[2].reshape(n, -1), sums[0].reshape(n, -1)]
    lines = jnp.concatenate(lines, axis=1).astype(jnp.bfloat16)
    lines = jnp.pad(lines, ((0, 0), (0, SMALL_ROWS * W - lines.shape[1]))).reshape(n, SMALL_ROWS, W)
    total = scatter(SCATTER_PARTS, [grad_ffn, grad_rec, lines])
    fr = REC_ROWS
    at = {"rate": fr + RATE_AT, "entry": fr + ENTRY_AT, "out": fr + OUT_AT, "gate": fr + GATE_AT, "input": fr + INPUT_AT}
    result = [(at["gate"], gate_proj), (at["input"], input_proj), (at["rate"], rate_proj), (at["entry"], entry_proj),
              (at["out"], out_proj), (0, ffn_gate), (FFN_UP_AT - FFN_GATE_AT, ffn_up), (FFN_DOWN_AT - FFN_GATE_AT, ffn_down)]
    result = [unpack_blocks(total[lo : lo + item.size // W], *item.shape) for lo, item in result]
    flat = total[FFN_ROWS + REC_ROWS]
    lo = 0
    for item in small:
        result.append(flat[lo : lo + item.size].reshape(item.shape))
        lo += item.size
    return (block_out.reshape(tokens.shape), token_grad.reshape(tokens.shape), *result)


def solution(mesh):
    packs = mesh.shape["seq"] == 8 and mesh.shape["batch"] == ZN
    placed = (
        P("batch", "seq", None),
        P("batch", "seq", None),
        P("batch"),
        P(("seq", "batch"), None),
        P(("seq", "batch"), None),
        P(("seq", "batch"), None),
        P(("seq", "batch"), None),
        P(("seq", "batch"), None),
        P(("seq", "batch"), None),
        P(("seq", "batch"), None),
        P(("seq", "batch"), None),
        P(("seq", "batch")),
        P(("seq", "batch")),
        P(None, ("seq", "batch")),
        P(("seq", "batch")),
        P(("seq", "batch")),
        P(("seq", "batch")),
        P(("seq", "batch")),
    )
    return jax.shard_map(
        per_device_packed if packs else per_device,
        mesh=mesh,
        in_specs=placed,
        out_specs=(
            P("batch", "seq", None),
            P("batch", "seq", None),
            P(("seq", "batch"), None),
            P(("seq", "batch"), None),
            P(("seq", "batch"), None),
            P(("seq", "batch"), None),
            P(("seq", "batch"), None),
            P(("seq", "batch"), None),
            P(("seq", "batch"), None),
            P(("seq", "batch"), None),
            P(("seq", "batch")),
            P(("seq", "batch")),
            P(None, ("seq", "batch")),
            P(("seq", "batch")),
            P(("seq", "batch")),
            P(("seq", "batch")),
            P(("seq", "batch")),
        ),
        check_vma=False,
    )
```

```python
import functools

import jax
import jax.numpy as jnp
import numpy as np
from jax import lax
from jax.experimental import pallas as pl
from jax.experimental.pallas import tpu as pltpu
from jax.sharding import PartitionSpec as P

MICRO = 2


eps = 1e-06
lru_scale = 8.0


def from_behind(value, axis, steps):
    count = lax.axis_size(axis)
    initial, last = (max(0, -steps), min(count, count - steps))
    return lax.ppermute(value, axis, [(source, source + steps) for source in range(initial, last)])


def entering(array, axis, combine, identity):
    size, place = (lax.axis_size(axis), lax.axis_index(axis))
    everything = jax.tree.map(lambda part: lax.all_gather(part, axis), array)
    start = jax.tree.map(
        lambda part, zero: jnp.broadcast_to(jnp.asarray(zero, part.dtype), part.shape),
        array,
        identity,
    )

    def entering_turn(k, before):
        reached = k < place
        new = combine(before, jax.tree.map(lambda part: part[k], everything))
        return jax.tree.map(lambda a, b: jnp.where(reached, a, b), new, before)

    return lax.fori_loop(0, size, entering_turn, start)


def carried_in(array, axis, combine, identity):
    size, place = (lax.axis_size(axis), lax.axis_index(axis))
    everything = jax.tree.map(
        lambda part, kind: lax.all_gather(part.astype(kind), axis),
        array,
        (jnp.bfloat16, jnp.bfloat16),
    )
    start = jax.tree.map(
        lambda part, zero: jnp.broadcast_to(jnp.asarray(zero, part.dtype), part.shape),
        array,
        identity,
    )

    def carried_turn(k, before):
        at = size - 1 - k
        reached = at > place
        new = combine(
            before, jax.tree.map(lambda part, own: part[at].astype(own.dtype), everything, array)
        )
        return jax.tree.map(lambda a, b: jnp.where(reached, a, b), new, before)

    return lax.fori_loop(0, size, carried_turn, start)


def for_sending(array):

    def short(part):
        return part.astype(jnp.bfloat16) if part.dtype == jnp.float32 else part

    return jax.tree.map(short, array)


def project(left, right):
    return jnp.einsum("btd,de->bte", left, right, preferred_element_type=jnp.float32)


def project_back(left, right):
    return jnp.einsum("bte,de->btd", left, right, preferred_element_type=jnp.float32)


def outer_sum(left, right):
    return jnp.einsum("btd,bte->de", left, right, preferred_element_type=jnp.float32)


def link(earlier, later):
    return (earlier[0] * later[0], later[0] * earlier[1] + later[1])


def norm_back(value, scale, gain, grad):
    weighted = grad * gain
    gain_grad = jnp.sum(grad * value * scale, axis=(0, 1))
    spread = jnp.mean(weighted * value, axis=-1, keepdims=True)
    return (scale * weighted - value * scale**3 * spread, gain_grad)


def fetch(shards):
    (
        gate_proj,
        input_proj,
        rate_proj,
        entry_proj,
        out_proj,
        ffn_gate,
        ffn_up,
        ffn_down,
        norm_gain,
        ffn_gain,
        conv_taps,
        conv_bias,
        rate_bias,
        entry_bias,
        decay_logit,
    ) = shards
    return (
        lax.all_gather(gate_proj, ("seq", "batch"), axis=0, tiled=True),
        lax.all_gather(input_proj, ("seq", "batch"), axis=0, tiled=True),
        lax.all_gather(rate_proj, ("seq", "batch"), axis=0, tiled=True),
        lax.all_gather(entry_proj, ("seq", "batch"), axis=0, tiled=True),
        lax.all_gather(out_proj, ("seq", "batch"), axis=0, tiled=True),
        lax.all_gather(ffn_gate, ("seq", "batch"), axis=0, tiled=True),
        lax.all_gather(ffn_up, ("seq", "batch"), axis=0, tiled=True),
        lax.all_gather(ffn_down, ("seq", "batch"), axis=0, tiled=True),
        lax.all_gather(norm_gain, ("seq", "batch"), axis=0, tiled=True),
        lax.all_gather(ffn_gain, ("seq", "batch"), axis=0, tiled=True),
        lax.all_gather(conv_taps, ("seq", "batch"), axis=1, tiled=True),
        lax.all_gather(conv_bias, ("seq", "batch"), axis=0, tiled=True),
        lax.all_gather(rate_bias, ("seq", "batch"), axis=0, tiled=True),
        lax.all_gather(entry_bias, ("seq", "batch"), axis=0, tiled=True),
        lax.all_gather(decay_logit, ("seq", "batch"), axis=0, tiled=True),
    )


def forward_part(tokens, mask, weights):
    (
        gate_proj,
        input_proj,
        rate_proj,
        entry_proj,
        out_proj,
        ffn_gate,
        ffn_up,
        ffn_down,
        norm_gain,
        ffn_gain,
        conv_taps,
        conv_bias,
        rate_bias,
        entry_bias,
        decay_logit,
    ) = weights
    width = tokens.shape[1]
    taps_count = conv_taps.shape[0]
    values = tokens.astype(jnp.float32)
    scale_one = lax.rsqrt(jnp.mean(values * values, axis=-1, keepdims=True) + eps)
    normed = (values * scale_one * norm_gain).astype(jnp.bfloat16)
    gate_pre = project(normed, gate_proj)
    inner = project(normed, input_proj)
    rim = from_behind(inner[:, width - (taps_count - 1) :], "seq", 1)
    extended = jnp.concatenate([rim, inner], axis=1)
    conv = jnp.zeros_like(inner) + conv_bias
    for lag in range(taps_count):
        start = taps_count - 1 - lag
        conv = conv + conv_taps[lag] * extended[:, start : start + width]
    mixed = conv.astype(jnp.bfloat16)
    mixed_full = mixed.astype(jnp.float32)
    rate = jax.nn.sigmoid(project(mixed, rate_proj) + rate_bias)
    entry = jax.nn.sigmoid(project(mixed, entry_proj) + entry_bias)
    logit = decay_logit.astype(jnp.float32)
    log_decay = -lru_scale * jax.nn.softplus(-logit) * rate
    decay = jnp.exp(mask * log_decay)
    root = jnp.sqrt(-jnp.expm1(2.0 * log_decay))
    drive = mask * root * entry * mixed_full
    reach, local = lax.associative_scan(link, (decay, drive), axis=1)
    unit_state = (jnp.ones_like(reach[:, -1]), jnp.zeros_like(local[:, -1]))
    start_state = entering((reach[:, -1], local[:, -1]), "seq", link, unit_state)[1]
    states = local + reach * start_state[:, None]
    gated = (states * jax.nn.gelu(gate_pre)).astype(jnp.bfloat16)
    first = values + project(gated, out_proj)
    scale_two = lax.rsqrt(jnp.mean(first * first, axis=-1, keepdims=True) + eps)
    normed_two = (first * scale_two * ffn_gain).astype(jnp.bfloat16)
    up_pre = project(normed_two, ffn_gate)
    mix_pre = project(normed_two, ffn_up)
    hidden = (jax.nn.gelu(up_pre) * mix_pre).astype(jnp.bfloat16)
    block_out = mask * (first + project(hidden, ffn_down))
    saved = (
        values,
        scale_one,
        normed,
        gate_pre,
        extended,
        mixed,
        mixed_full,
        rate,
        entry,
        log_decay,
        decay,
        root,
        start_state,
        states,
        gated,
        first,
        scale_two,
        normed_two,
        up_pre,
        mix_pre,
        hidden,
    )
    return (block_out, saved)


def backward_part(cotangent, mask, weights, saved):
    (
        gate_proj,
        input_proj,
        rate_proj,
        entry_proj,
        out_proj,
        ffn_gate,
        ffn_up,
        ffn_down,
        norm_gain,
        ffn_gain,
        conv_taps,
        conv_bias,
        rate_bias,
        entry_bias,
        decay_logit,
    ) = weights
    (
        values,
        scale_one,
        normed,
        gate_pre,
        extended,
        mixed,
        mixed_full,
        rate,
        entry,
        log_decay,
        decay,
        root,
        start_state,
        states,
        gated,
        first,
        scale_two,
        normed_two,
        up_pre,
        mix_pre,
        hidden,
    ) = saved
    width = values.shape[1]
    taps_count = conv_taps.shape[0]
    cot_full = mask * cotangent.astype(jnp.float32)
    cot_low = cot_full.astype(jnp.bfloat16)
    grad_ffn_down = outer_sum(hidden, cot_low)
    d_hidden = project_back(cot_low, ffn_down)
    gelu_up, gelu_pull = jax.vjp(jax.nn.gelu, up_pre)
    d_up = gelu_pull(d_hidden * mix_pre)[0].astype(jnp.bfloat16)
    d_mix = (d_hidden * gelu_up).astype(jnp.bfloat16)
    grad_ffn_gate = outer_sum(normed_two, d_up)
    grad_ffn_up = outer_sum(normed_two, d_mix)
    d_normed_two = project_back(d_up, ffn_gate) + project_back(d_mix, ffn_up)
    back_two, grad_ffn_gain = norm_back(first, scale_two, ffn_gain, d_normed_two)
    d_first = cot_full + back_two
    d_first_low = d_first.astype(jnp.bfloat16)
    grad_out_proj = outer_sum(gated, d_first_low)
    d_gated = project_back(d_first_low, out_proj)
    gate, gate_pull = jax.vjp(jax.nn.gelu, gate_pre)
    d_states = d_gated * gate
    d_gate_pre = gate_pull(d_gated * states)[0].astype(jnp.bfloat16)
    following = jnp.concatenate([decay[:, 1:], jnp.ones_like(decay[:, :1])], axis=1)
    reach_back, local_back = lax.associative_scan(link, (following, d_states), reverse=True, axis=1)
    unit_grad = (jnp.ones_like(decay[:, 0]), jnp.zeros_like(decay[:, 0]))
    end_grad = carried_in(
        (decay[:, 0] * reach_back[:, 0], decay[:, 0] * local_back[:, 0]), "seq", link, unit_grad
    )[1]
    carried = local_back + reach_back * end_grad[:, None]
    previous = jnp.concatenate([start_state[:, None], states[:, :-1]], axis=1)
    masked_grad = mask * carried
    d_log = (
        masked_grad * previous * decay
        - masked_grad * entry * mixed_full * jnp.exp(2.0 * log_decay) / root
    )
    logit = decay_logit.astype(jnp.float32)
    grad_decay_logit = jnp.sum(lru_scale * d_log * rate * jax.nn.sigmoid(-logit), axis=(0, 1))
    d_rate_pre = -lru_scale * jax.nn.softplus(-logit) * d_log * rate * (1.0 - rate)
    d_entry_pre = masked_grad * root * mixed_full * entry * (1.0 - entry)
    grad_rate_bias = jnp.sum(d_rate_pre, axis=(0, 1))
    grad_entry_bias = jnp.sum(d_entry_pre, axis=(0, 1))
    rate_low = d_rate_pre.astype(jnp.bfloat16)
    entry_low = d_entry_pre.astype(jnp.bfloat16)
    grad_rate_proj = outer_sum(mixed, rate_low)
    grad_entry_proj = outer_sum(mixed, entry_low)
    d_mixed = (
        masked_grad * root * entry
        + project_back(rate_low, rate_proj)
        + project_back(entry_low, entry_proj)
    )
    grad_conv_bias = jnp.sum(d_mixed, axis=(0, 1))
    tap_grads = []
    for lag in range(taps_count):
        start = taps_count - 1 - lag
        tap_grads.append(jnp.sum(d_mixed * extended[:, start : start + width], axis=(0, 1)))
    grad_conv_taps = jnp.stack(tap_grads, axis=0)
    rim_back = from_behind(for_sending(d_mixed[:, : taps_count - 1]), "seq", -1)
    later = jnp.concatenate([d_mixed, rim_back], axis=1)
    d_inner = jnp.zeros_like(d_mixed)
    for lag in range(taps_count):
        d_inner = d_inner + conv_taps[lag] * later[:, lag : lag + width]
    d_inner = d_inner.astype(jnp.bfloat16)
    grad_input_proj = outer_sum(normed, d_inner)
    grad_gate_proj = outer_sum(normed, d_gate_pre)
    d_normed = project_back(d_gate_pre, gate_proj) + project_back(d_inner, input_proj)
    back_one, grad_norm_gain = norm_back(values, scale_one, norm_gain, d_normed)
    token_grad = d_first + back_one
    grads = (
        grad_gate_proj,
        grad_input_proj,
        grad_rate_proj,
        grad_entry_proj,
        grad_out_proj,
        grad_ffn_gate,
        grad_ffn_up,
        grad_ffn_down,
        grad_norm_gain,
        grad_ffn_gain,
        grad_conv_taps,
        grad_conv_bias,
        grad_rate_bias,
        grad_entry_bias,
        grad_decay_logit,
    )
    return (token_grad, grads)


def reduce_grads(totals):
    shaped = []
    for index, item in enumerate(totals):
        if index == 10:
            item = item.T
        if item.ndim == 1:
            item = item[:, None]
        shaped.append(item[None])
    spread = (
        lax.all_to_all(
            shaped[0].astype(jnp.bfloat16), "seq", split_axis=1, concat_axis=0, tiled=True
        ).astype(jnp.float32),
        lax.all_to_all(
            shaped[1].astype(jnp.bfloat16), "seq", split_axis=1, concat_axis=0, tiled=True
        ).astype(jnp.float32),
        lax.all_to_all(
            shaped[2].astype(jnp.bfloat16), "seq", split_axis=1, concat_axis=0, tiled=True
        ).astype(jnp.float32),
        lax.all_to_all(
            shaped[3].astype(jnp.bfloat16), "seq", split_axis=1, concat_axis=0, tiled=True
        ).astype(jnp.float32),
        lax.all_to_all(
            shaped[4].astype(jnp.bfloat16), "seq", split_axis=1, concat_axis=0, tiled=True
        ).astype(jnp.float32),
        lax.all_to_all(
            shaped[5].astype(jnp.bfloat16), "seq", split_axis=1, concat_axis=0, tiled=True
        ).astype(jnp.float32),
        lax.all_to_all(
            shaped[6].astype(jnp.bfloat16), "seq", split_axis=1, concat_axis=0, tiled=True
        ).astype(jnp.float32),
        lax.all_to_all(
            shaped[7].astype(jnp.bfloat16), "seq", split_axis=1, concat_axis=0, tiled=True
        ).astype(jnp.float32),
        lax.all_to_all(
            shaped[8].astype(jnp.bfloat16), "seq", split_axis=1, concat_axis=0, tiled=True
        ).astype(jnp.float32),
        lax.all_to_all(
            shaped[9].astype(jnp.bfloat16), "seq", split_axis=1, concat_axis=0, tiled=True
        ).astype(jnp.float32),
        lax.all_to_all(for_sending(shaped[10]), "seq", split_axis=1, concat_axis=0, tiled=True),
        lax.all_to_all(for_sending(shaped[11]), "seq", split_axis=1, concat_axis=0, tiled=True),
        lax.all_to_all(for_sending(shaped[12]), "seq", split_axis=1, concat_axis=0, tiled=True),
        lax.all_to_all(for_sending(shaped[13]), "seq", split_axis=1, concat_axis=0, tiled=True),
        lax.all_to_all(for_sending(shaped[14]), "seq", split_axis=1, concat_axis=0, tiled=True),
    )
    folded = [jnp.sum(piece, axis=0) for piece in spread]
    summed = (
        lax.psum_scatter(
            folded[0].astype(jnp.bfloat16), "batch", scatter_dimension=0, tiled=True
        ).astype(jnp.float32),
        lax.psum_scatter(
            folded[1].astype(jnp.bfloat16), "batch", scatter_dimension=0, tiled=True
        ).astype(jnp.float32),
        lax.psum_scatter(
            folded[2].astype(jnp.bfloat16), "batch", scatter_dimension=0, tiled=True
        ).astype(jnp.float32),
        lax.psum_scatter(
            folded[3].astype(jnp.bfloat16), "batch", scatter_dimension=0, tiled=True
        ).astype(jnp.float32),
        lax.psum_scatter(
            folded[4].astype(jnp.bfloat16), "batch", scatter_dimension=0, tiled=True
        ).astype(jnp.float32),
        lax.psum_scatter(
            folded[5].astype(jnp.bfloat16), "batch", scatter_dimension=0, tiled=True
        ).astype(jnp.float32),
        lax.psum_scatter(
            folded[6].astype(jnp.bfloat16), "batch", scatter_dimension=0, tiled=True
        ).astype(jnp.float32),
        lax.psum_scatter(
            folded[7].astype(jnp.bfloat16), "batch", scatter_dimension=0, tiled=True
        ).astype(jnp.float32),
        lax.psum_scatter(
            folded[8].astype(jnp.bfloat16), "batch", scatter_dimension=0, tiled=True
        ).astype(jnp.float32),
        lax.psum_scatter(
            folded[9].astype(jnp.bfloat16), "batch", scatter_dimension=0, tiled=True
        ).astype(jnp.float32),
        lax.psum_scatter(
            folded[10].astype(jnp.bfloat16), "batch", scatter_dimension=0, tiled=True
        ).astype(jnp.float32),
        lax.psum_scatter(
            folded[11].astype(jnp.bfloat16), "batch", scatter_dimension=0, tiled=True
        ).astype(jnp.float32),
        lax.psum_scatter(
            folded[12].astype(jnp.bfloat16), "batch", scatter_dimension=0, tiled=True
        ).astype(jnp.float32),
        lax.psum_scatter(
            folded[13].astype(jnp.bfloat16), "batch", scatter_dimension=0, tiled=True
        ).astype(jnp.float32),
        lax.psum_scatter(
            folded[14].astype(jnp.bfloat16), "batch", scatter_dimension=0, tiled=True
        ).astype(jnp.float32),
    )
    result = []
    for index, item in enumerate(summed):
        if index == 10:
            result.append(item.T)
        elif totals[index].ndim == 1:
            result.append(item[:, 0])
        else:
            result.append(item)
    return tuple(result)


def per_device(
    tokens,
    cotangent,
    lengths,
    gate_proj,
    input_proj,
    rate_proj,
    entry_proj,
    out_proj,
    ffn_gate,
    ffn_up,
    ffn_down,
    norm_gain,
    ffn_gain,
    conv_taps,
    conv_bias,
    rate_bias,
    entry_bias,
    decay_logit,
):
    shards = (
        gate_proj,
        input_proj,
        rate_proj,
        entry_proj,
        out_proj,
        ffn_gate,
        ffn_up,
        ffn_down,
        norm_gain,
        ffn_gain,
        conv_taps,
        conv_bias,
        rate_bias,
        entry_bias,
        decay_logit,
    )
    rows, width = (tokens.shape[0], tokens.shape[1])
    place = lax.axis_index("seq") * width + lax.iota(jnp.int32, width)
    mask_all = (place[None, :] < lengths[:, None]).astype(jnp.float32)[:, :, None]
    group = rows // MICRO
    totals = None
    block_parts = []
    grad_parts = []
    for part in range(MICRO):
        lower = part * group
        mask = mask_all[lower : lower + group]
        weights = fetch(shards)
        block_out, saved = forward_part(tokens[lower : lower + group], mask, weights)
        weights = fetch(shards)
        token_grad, grads = backward_part(cotangent[lower : lower + group], mask, weights, saved)
        totals = grads if part == 0 else jax.tree.map(jnp.add, totals, grads)
        block_parts.append(block_out)
        grad_parts.append(token_grad)
    summed = reduce_grads(totals)
    return (jnp.concatenate(block_parts, axis=0), jnp.concatenate(grad_parts, axis=0)) + summed


F32 = jnp.float32
BF16 = jnp.bfloat16
W = 512
SEGS = 8
CHUNK = 16
TALL = 64
LANES = 128
GELU_A = 0.7978845608028654
GELU_B = 0.044715
TAPS, CONV_BIAS, RATE_BIAS, ENTRY_BIAS, COEF, SIG = 0, 4, 5, 6, 7, 8


def dot(left, right):
    return lax.dot_general(left, right, (((1,), (0,)), ((), ())), preferred_element_type=F32)


def dot_back(left, right):
    return lax.dot_general(left, right, (((1,), (1,)), ((), ())), preferred_element_type=F32)


def dot_outer(left, right):
    return lax.dot_general(left, right, (((0,), (0,)), ((), ())), preferred_element_type=F32)


def rows_at(start, count=CHUNK):
    return pl.ds(pl.multiple_of(start, CHUNK), count)


def gelu_both(value):
    square = value * value
    inside = GELU_A * value * (1.0 + GELU_B * square)
    tanh = jnp.tanh(inside)
    half = 0.5 + 0.5 * tanh
    slope = half + 0.5 * value * (1.0 - tanh * tanh) * (GELU_A * (1.0 + 3.0 * GELU_B * square))
    return value * half, slope


def sigmoid(value):
    return 1.0 / (1.0 + jnp.exp(-value))


def one_less_exp(z, exp_z):
    series = 1.0 + z * (1 / 2 + z * (1 / 6 + z * (1 / 24 + z * (1 / 120 + z * (1 / 720)))))
    return jnp.where(z > -0.25, -z * series, 1.0 - exp_z)


def in_row(row, width, shape):
    return row + lax.broadcasted_iota(jnp.int32, shape, 0)


def each_chunk(batch, width, body, carry=0):
    per = width // CHUNK
    for b in range(batch):
        carry = lax.fori_loop(0, per, lambda i, c, b=b: body(b, i * CHUNK, b * width + i * CHUNK, c), carry)
    return carry


def each_tile(batch, width, tiles, body, carry=None):
    carries = []
    for t in range(tiles):
        kept = carry
        for b in range(batch):
            def one(i, c, t=t, b=b):
                return body(t, b, i * TALL, rows_at(b * width + i * TALL, TALL), slice(t * LANES, (t + 1) * LANES), c)
            kept = lax.fori_loop(0, width // TALL, one, 0 if kept is None else kept)
        carries.append(kept)
    return carries


def strided(b, width, step):
    return pl.ds(b * width + step, SEGS, stride=width // SEGS)


def lanes(t):
    return slice(t * LANES, (t + 1) * LANES)


def spread(ref, value):
    for t in range(ref.shape[0]):
        ref[t] = value[:, lanes(t)]


def tiled(tokens, block, index):
    return pl.BlockSpec((block // LANES, tokens, LANES), lambda j: (index(j), 0, 0))


def inverse_norm(value, depth):
    return lax.rsqrt(jnp.sum(value * value, axis=-1, keepdims=True) * (1.0 / depth) + eps)


def fold8(value):
    total = value[:8]
    for i in range(8, value.shape[0], 8):
        total = total + value[i : i + 8]
    return total


def put(stage, sem, slot, dst, value, used):
    copy = pltpu.make_async_copy(stage.at[slot], dst, sem.at[slot])
    if used is True:
        copy.wait()
    elif used is not False:
        pl.when(used)(copy.wait)
    stage[slot] = value
    copy.start()


def ffn_kernel(batch, width, info_ref, first_ref, normed_ref, cot_ref, gain_ref, wg_ref, wu_ref, wd_ref,
               out_ref, dfirst_ref, dlow_ref, ggain_ref, grad_ref,
               low, dh, hid, acc, dn, up_s, mix_s, du, dm, nt, ltr, stage, dstage, sem, dsem):
    step = pl.program_id(0)
    tokens, depth = first_ref.shape
    n = grad_ref.shape[0]
    f = hid.shape[1]
    wide = wd_ref.shape[0] * wd_ref.shape[1] // 2
    nd, nw = f // wide, f // W
    rows = depth // n
    drows = wd_ref.shape[1] // 2

    @pl.when(step == 0)
    def _():
        def masked(b, spot, row, _):
            at = rows_at(row)
            value = cot_ref[at]
            valid = in_row(spot, width, value.shape) < info_ref[b]
            low[at] = jnp.where(valid, value.astype(F32), 0.0).astype(BF16)
            return 0
        each_chunk(batch, width, masked)

    @pl.when(step < nd)
    def _():
        here = pl.ds(pl.multiple_of(jnp.minimum(step, nd - 1) * wide, wide), wide)
        total = dot_back(low[:, :W], wd_ref[:, :drows].reshape(wide, W))
        dh[:, here] = total + dot_back(low[:, W:], wd_ref[:, drows:].reshape(wide, W))

    @pl.when(jnp.logical_and(step >= nd, step < nd + nw))
    def _():
        j = step - nd
        here = pl.ds(pl.multiple_of(j * W, W), W)
        wg = wg_ref[...].reshape(depth, W)
        wu = wu_ref[...].reshape(depth, W)
        up_s[...] = dot(normed_ref[...], wg)
        mix_s[...] = dot(normed_ref[...], wu)

        def gating(i, _):
            at = rows_at(i * CHUNK)
            gate, slope = gelu_both(up_s[at])
            mix, d = mix_s[at], dh[at, here]
            hid[at, here] = (gate * mix).astype(BF16)
            du[at] = (d * mix * slope).astype(BF16)
            dm[at] = (d * gate).astype(BF16)
            return 0
        lax.fori_loop(0, tokens // CHUNK, gating, 0)
        more = dot_back(du[...], wg) + dot_back(dm[...], wu)

        @pl.when(j == 0)
        def _():
            dn[...] = more

        @pl.when(j > 0)
        def _():
            dn[...] += more
        for which, low_grad in ((0, du), (1, dm)):
            value = dot_outer(normed_ref[...], low_grad[...]).astype(BF16).reshape(n, rows, W)
            dst = grad_ref.at[:, pl.ds(pl.multiple_of(which * nw * rows + j * rows, rows), rows)]
            put(stage, sem, which, dst, value, j > 0)

    @pl.when(step >= nd + nw)
    def _():
        k = step - nd - nw
        here = pl.ds(pl.multiple_of(k * wide, wide), wide)
        block = hid[:, here]
        for half in range(2):
            cols = slice(half * W, (half + 1) * W)
            more = dot(block, wd_ref[:, half * drows : (half + 1) * drows].reshape(wide, W))

            @pl.when(k == 0)
            def _():
                acc[:, cols] = more

            @pl.when(k > 0)
            def _():
                acc[:, cols] += more
            value = dot_outer(block, low[:, cols]).astype(BF16).reshape(wide // drows, drows, W)
            dst = grad_ref.at[pl.ds(k * (wide // drows), wide // drows),
                              pl.ds(2 * nw * rows + half * drows, drows)]
            put(dstage, dsem, half, dst, value, k > 0)

    @pl.when(step == pl.num_programs(0) - 1)
    def _():
        def finish(b, spot, row, total):
            at = rows_at(row)
            first, cot = first_ref[at], low[at].astype(F32)
            valid = in_row(spot, width, first.shape) < info_ref[b]
            out_ref[at] = jnp.where(valid, first + acc[at], 0.0)
            grad = dn[at]
            scale = inverse_norm(first, depth)
            weighted = grad * gain_ref[:1]
            spread = jnp.sum(weighted * first, axis=-1, keepdims=True) * (1.0 / depth)
            back = cot + scale * weighted - first * (scale * scale * scale * spread)
            dfirst_ref[at] = back
            dlow_ref[at] = back.astype(BF16)
            return total + fold8(grad * first * scale)
        total = each_chunk(batch, width, finish, jnp.zeros((8, depth), F32))
        ggain_ref[...] = total
        for which in range(2):
            pltpu.make_async_copy(stage.at[which], grad_ref.at[:, pl.ds(0, rows)], sem.at[which]).wait()
            pltpu.make_async_copy(dstage.at[which], grad_ref.at[pl.ds(0, wide // drows), pl.ds(0, drows)], dsem.at[which]).wait()


def feed_forward(info, first, normed_two, cot, gain, packed, f, batch):
    tokens, depth = first.shape
    width = tokens // batch
    n = packed.shape[0]
    rows, drows = depth // n, f // n
    group = 8
    wide = group * drows
    nd, nw = f // wide, f // W
    full = lambda shape: pl.BlockSpec(shape, lambda j: (0,) * len(shape))
    clamp = lambda j, low, count: jnp.clip(j - low, 0, count - 1)
    down = FFN_DOWN_AT // (2 * drows)

    def down_block(j):
        return (jnp.where(j < nd, jnp.minimum(j, nd - 1), clamp(j, nd + nw, nd)), down, 0)
    vm = pltpu.VMEM
    return pl.pallas_call(
        functools.partial(ffn_kernel, batch, width),
        grid=(nd + nw + nd,),
        in_specs=[pl.BlockSpec(memory_space=pltpu.SMEM), full(first.shape), full(normed_two.shape), full(cot.shape),
                  full(gain.shape),
                  pl.BlockSpec((n, rows, W), lambda j: (0, FFN_GATE_AT // rows + clamp(j, nd, nw), 0)),
                  pl.BlockSpec((n, rows, W), lambda j: (0, FFN_UP_AT // rows + clamp(j, nd, nw), 0)),
                  pl.BlockSpec((group, 2 * drows, W), down_block)],
        out_specs=[full((tokens, depth))] * 3 + [full((8, depth)), pl.BlockSpec(memory_space=pl.ANY)],
        out_shape=[jax.ShapeDtypeStruct((tokens, depth), F32), jax.ShapeDtypeStruct((tokens, depth), F32),
                   jax.ShapeDtypeStruct((tokens, depth), BF16), jax.ShapeDtypeStruct((8, depth), F32),
                   jax.ShapeDtypeStruct((n, 2 * nw * rows + 2 * drows, W), BF16)],
        scratch_shapes=[vm((tokens, depth), BF16), vm((tokens, f), F32), vm((tokens, f), BF16), vm((tokens, depth), F32),
                        vm((tokens, depth), F32), vm((tokens, W), F32), vm((tokens, W), F32), vm((tokens, W), BF16),
                        vm((tokens, W), BF16), vm((8, 128), BF16), vm((8, 128), BF16),
                        vm((2, n, rows, W), BF16), vm((2, group, drows, W), BF16),
                        pltpu.SemaphoreType.DMA((2,)), pltpu.SemaphoreType.DMA((2,))],
        compiler_params=pltpu.CompilerParams(vmem_limit_bytes=60 << 20),
    )(info, first, normed_two, cot, gain, packed, packed, packed)


MESH = pl.DeviceIdType.MESH
ROUTES = (("z", "x", "y"), ("z", "y", "x"), ("x", "z", "y"), ("y", "z", "x"))
ZN = 4
STG = 4
SEM = pltpu.SemaphoreType.DMA


def place():
    s = lax.axis_index("seq")
    return lax.rem(s, 2), lax.rem(lax.div(s, 2), 2), lax.div(s, 4), lax.axis_index("batch")


def flip(value, by):
    return 1 - value if by else value


def seq_of(y, x, c):
    return (y * 2 + x) * 2 + c


def far(z, j):
    if j == ZN - 1:
        return z
    found = None
    for here in range(ZN):
        others = sorted((q for q in range(ZN) if q != here), key=lambda q: (-abs(q - here), q))
        found = jnp.int32(others[j]) if found is None else jnp.where(z == here, others[j], found)
    return found


class Links:
    def __init__(self):
        self.c, self.x, self.y, self.z = c, x, y, z = place()
        self.beside = {
            "x": (seq_of(y, 1 - x, c), z),
            "y": (seq_of(1 - y, x, c), z),
            "up": (seq_of(y, x, c), z + 1),
            "dn": (seq_of(y, x, c), z - 1),
            "core": (seq_of(y, x, 1 - c), z),
        }
        self.spots = [far(z, j) for j in range(ZN)]
        self.above, self.below = z < ZN - 1, z > 0

    def slot(self, dx, dy, z, core):
        return seq_of(flip(self.y, dy), flip(self.x, dx), core) * ZN + z

    def copy(self, src, dst, send, recv, d):
        return pltpu.make_async_remote_copy(src, dst, send, recv, device_id=self.beside[d], device_id_type=MESH)


def greet(links, swap):
    bar = pltpu.get_barrier_semaphore()
    count = 0
    if swap is not None:
        count = swap.n - 1
        for k in range(1, swap.n):
            pl.semaphore_signal(bar, inc=1, device_id=swap.peer(k), device_id_type=MESH)
    if links is not None:
        def signal(d):
            pl.semaphore_signal(bar, inc=1, device_id=links.beside[d], device_id_type=MESH)
        if swap is None:
            count = 3
            for d in ("x", "y", "core"):
                signal(d)
        pl.when(links.above)(lambda: signal("up"))
        pl.when(links.below)(lambda: signal("dn"))
        count = count + links.above.astype(jnp.int32) + links.below.astype(jnp.int32)
    pl.semaphore_wait(bar, count)


class Exchange:
    def __init__(self, n, rows, land, send, recv, own):
        self.n, self.rows, self.land, self.send, self.recv, self.own = n, rows, land, send, recv, own
        self.me, self.z = lax.axis_index("seq"), lax.axis_index("batch")

    @staticmethod
    def scratch(n, shape):
        return [pltpu.VMEM(shape, F32), pltpu.VMEM((n,) + shape, F32), SEM((n,)), SEM((n,)), SEM]

    def peer(self, k):
        return (lax.rem(self.me + k, self.n), self.z)

    def copies(self):
        return [
            pltpu.make_async_remote_copy(self.rows, self.land.at[self.me], self.send.at[k], self.recv.at[k],
                                         device_id=self.peer(k), device_id_type=MESH)
            for k in range(1, self.n)
        ]

    def mine(self):
        return pltpu.make_async_copy(self.rows, self.land.at[self.me], self.own)

    def begin(self):
        self.mine().start()
        for copy in self.copies():
            copy.start()

    def finish(self):
        self.mine().wait()
        for copy in self.copies():
            copy.wait()


def onward(order, dx, dy, same):
    off = {"x": dx, "y": dy, "z": 0 if same else 1}
    return [
        d for i, d in enumerate(order)
        if not any(off[e] for e in order[i + 1 :]) and not (d != "z" and off[d])
    ]


def arrival(order, dx, dy, same):
    off = {"x": dx, "y": dy, "z": 0 if same else 1}
    return [d for d in order if off[d]][-1]


def blocks(parts):
    found = [
        (dx + dy + ZN - 1 - j, r, dx, dy, j)
        for dx in range(2) for dy in range(2) for j in range(ZN) for r in range(len(parts))
    ]
    return found


class Gather:
    def __init__(self, parts, ins, outs, send, recv, csend, crecv, lsem):
        self.parts, self.ins, self.outs = parts, ins, outs
        self.send, self.recv, self.csend, self.crecv, self.lsem = send, recv, csend, crecv, lsem
        self.links = Links()
        self.events = sorted(blocks(parts), key=lambda e: e[0])

    @staticmethod
    def scratch(parts):
        n = len(parts)
        return [SEM((n, 4, 4, ZN)), SEM((n, 4, ZN)), SEM((n, 4, ZN)), SEM((n, 4, ZN)), SEM((n,))]

    def window(self, r):
        return pl.ds(self.parts[r][2], self.parts[r][3])

    def dst(self, r, dx, dy, zs):
        return self.outs[self.parts[r][1]].at[self.links.slot(dx, dy, zs, self.links.c), self.window(r)]

    def src(self, r, dx, dy, zs, own):
        return self.ins[self.parts[r][0]].at[self.window(r)] if own else self.dst(r, dx, dy, zs)

    def hop(self, r, dx, dy, zs, d, own):
        to = (1 if d == "x" else dx) * 2 + (1 if d == "y" else dy)
        which = ("x", "y", "up", "dn").index(d)
        return self.links.copy(self.src(r, dx, dy, zs, own), self.dst(r, dx, dy, zs),
                               self.send.at[r, which, dx * 2 + dy, zs], self.recv.at[r, to, zs], d)

    def across(self, r, dx, dy, zs, own):
        return self.links.copy(self.src(r, dx, dy, zs, own), self.dst(r, dx, dy, zs),
                               self.csend.at[r, dx * 2 + dy, zs], self.crecv.at[r, dx * 2 + dy, zs], "core")

    def hops(self, r, dx, dy, j, act):
        links, zs = self.links, self.links.spots[j]
        z, same = links.z, j == ZN - 1
        own = same and not dx and not dy
        for d in onward(ROUTES[self.parts[r][4]], dx, dy, same):
            if d != "z":
                act(self.hop(r, dx, dy, zs, d, own))
                continue
            up = links.above if same else jnp.logical_and(z > zs, links.above)
            down = links.below if same else jnp.logical_and(z < zs, links.below)
            pl.when(up)(lambda: act(self.hop(r, dx, dy, zs, "up", own)))
            pl.when(down)(lambda: act(self.hop(r, dx, dy, zs, "dn", own)))

    def forward(self, event):
        _, r, dx, dy, j = event
        zs, own = self.links.spots[j], j == ZN - 1 and not dx and not dy
        if not own:
            self.links.copy(self.dst(r, dx, dy, zs), self.dst(r, dx, dy, zs), self.send.at[r, 0, 0, 0],
                            self.recv.at[r, dx * 2 + dy, zs], "core").wait_recv()
        self.hops(r, dx, dy, j, lambda copy: copy.start())
        self.across(r, dx, dy, zs, own).start()
        if own:
            self.local(r).start()

    def local(self, r):
        return pltpu.make_async_copy(self.ins[self.parts[r][0]].at[self.window(r)],
                                     self.dst(r, 0, 0, self.links.z), self.lsem.at[r])

    def finish(self):
        for _, r, dx, dy, j in self.events:
            own = j == ZN - 1 and not dx and not dy
            self.hops(r, dx, dy, j, lambda copy: copy.wait_send())
            copy = self.across(r, dx, dy, self.links.spots[j], own)
            copy.wait_send()
            copy.wait_recv()
            if own:
                self.local(r).wait()


def gather(parts, ins, rows):
    n = len(ins)

    def kernel(*refs):
        job = Gather(parts, refs[:n], refs[n : n + len(rows)], *refs[n + len(rows) :])
        greet(job.links, None)
        for event in job.events:
            job.forward(event)
        job.finish()
    anywhere = pl.BlockSpec(memory_space=pl.ANY)
    return pl.pallas_call(
        kernel,
        out_shape=[jax.ShapeDtypeStruct((8 * ZN, count, W), jnp.bfloat16) for count in rows],
        in_specs=[anywhere] * n,
        out_specs=[anywhere] * len(rows),
        scratch_shapes=Gather.scratch(parts),
        compiler_params=pltpu.CompilerParams(collective_id=1, has_side_effects=True),
    )(*ins)


def layout(order):
    base, count = {}, 0
    for i, d in enumerate(order):
        base[d] = count
        free = 1
        for e in order[:i]:
            free *= ZN if e == "z" else 2
        count += free * ((ZN + 1) if d == "z" else 1)
    return base, count


class Scatter:
    AHEAD, RING = 4, 6

    def __init__(self, parts, ins, out, sib, stage, ring, fin, csend, crecv, lsem, send, fsem, *rest):
        self.parts, self.ins, self.out, self.sib = parts, ins, out, sib
        self.stage, self.ring, self.fin = stage, ring, fin
        self.csend, self.crecv, self.lsem, self.send, self.fsem = csend, crecv, lsem, send, fsem
        self.bufs, self.recv = rest[: len(parts)], rest[len(parts) :]
        self.links = Links()
        self.lay = [layout(ROUTES[part[3]]) for part in parts]
        rows = [part[2] for part in parts]
        self.starts = [sum(rows[:r]) for r in range(len(parts))]
        self.events = sorted(blocks(parts), key=lambda e: -e[0])
        self.in_slot, self.in_fin, self.finals = {}, {}, 0

    @staticmethod
    def buffers(parts):
        total = sum(part[2] for part in parts)
        S = jax.ShapeDtypeStruct
        return [S((total, W), jnp.float32), S((4 * ZN * total, W), jnp.bfloat16)]

    @classmethod
    def scratch(cls, parts):
        n, most = len(parts), max(part[2] for part in parts)
        counts = [layout(ROUTES[part[3]])[1] for part in parts]
        return [pltpu.VMEM((cls.AHEAD, 2, most, W), jnp.bfloat16), pltpu.VMEM((cls.RING, most, W), jnp.bfloat16),
                pltpu.VMEM((2, most, W), jnp.float32), SEM((n,)), SEM((n, 4, ZN)), SEM((cls.AHEAD, 2)), SEM((cls.RING,)),
                SEM((2,))] + [
            pltpu.VMEM((count, part[2], W), jnp.bfloat16) for count, part in zip(counts, parts)
        ] + [SEM((count,)) for count in counts]

    def source(self, r, dx, dy, zd, core):
        which, start, rows, _ = self.parts[r]
        return self.ins[which].at[self.links.slot(dx, dy, zd, core), pl.ds(start, rows)]

    def sibling(self, r, dx, dy, zd):
        count = self.parts[r][2]
        start = 4 * ZN * self.starts[r] + ((dx * 2 + dy) * ZN + zd) * count
        return self.sib.at[pl.ds(pl.multiple_of(start, 16), count)]

    def child(self, r, d, dx, dy, zd):
        order = ROUTES[self.parts[r][3]]
        dim = d if d in "xy" else "z"
        index = 0
        for e in order[: order.index(dim)]:
            index = index * ZN + zd if e == "z" else index * 2 + (dx if e == "x" else dy)
        if dim == "z":
            index = index * (ZN + 1) + (zd if d == "up" else zd + 1)
        return self.lay[r][0][dim] + index

    def across(self, i):
        _, r, dx, dy, j = self.events[i]
        zd = self.links.spots[j]
        return self.links.copy(self.source(r, dx, dy, zd, 1 - self.links.c), self.sibling(r, dx, dy, zd),
                               self.csend.at[r], self.crecv.at[r, dx * 2 + dy, zd], "core")

    def begin(self):
        for i in range(len(self.events)):
            self.across(i).start()
        for i in range(self.AHEAD - 1):
            self.prefetch(i)

    def loads(self, i):
        _, r, dx, dy, j = self.events[i]
        zd, s, count = self.links.spots[j], i % self.AHEAD, self.parts[r][2]
        return [
            pltpu.make_async_copy(ref, self.stage.at[s, k, pl.ds(0, count)], self.lsem.at[s, k])
            for k, ref in enumerate((self.source(r, dx, dy, zd, self.links.c), self.sibling(r, dx, dy, zd)))
        ]

    def prefetch(self, i):
        own, other = self.loads(i)
        own.start()
        self.across(i).wait_recv()
        other.start()

    def terms(self, i):
        _, r, dx, dy, j = self.events[i]
        same = j == ZN - 1
        kids = onward(ROUTES[self.parts[r][3]], dx, dy, same)
        z, zd = self.links.z, self.links.spots[j]
        found = [(self.child(r, d, dx, dy, zd), None) for d in kids if d != "z"]
        if "z" in kids:
            up, down = self.child(r, "up", dx, dy, zd), self.child(r, "dn", dx, dy, zd)
            if same:
                found += [(up, self.links.above), (down, self.links.below)]
            else:
                found.append((jnp.where(z > zd, up, down), jnp.logical_and(self.links.above, self.links.below)))
        return found

    def hop(self, i, d):
        _, r, dx, dy, j = self.events[i]
        zd, q = self.links.spots[j], i % self.RING
        came = {"x": "x", "y": "y", "up": "dn", "dn": "up"}[d]
        at = self.child(r, came, 0 if d == "x" else dx, 0 if d == "y" else dy, zd)
        return self.links.copy(self.ring.at[q, pl.ds(0, self.parts[r][2])], self.bufs[r].at[at],
                               self.send.at[q], self.recv[r].at[at], d)

    def result(self, i, slot):
        r = self.events[i][1]
        count = self.parts[r][2]
        return pltpu.make_async_copy(self.fin.at[slot, pl.ds(0, count)], self.out.at[pl.ds(self.starts[r], count)],
                                     self.fsem.at[slot])

    def step(self, i):
        _, r, dx, dy, j = self.events[i]
        zd, z, s, q = self.links.spots[j], self.links.z, i % self.AHEAD, i % self.RING
        if i + self.AHEAD - 1 < len(self.events):
            self.prefetch(i + self.AHEAD - 1)
        leaves = j != ZN - 1 or dx or dy
        if leaves:
            if q in self.in_slot:
                self.hop(self.in_slot[q], "x").wait_send()
            self.in_slot[q] = i
        else:
            slot = self.finals % 2
            if slot in self.in_fin:
                self.result(self.in_fin[slot], slot).wait()
            self.in_fin[slot] = i
            self.finals += 1
        for load in self.loads(i):
            load.wait()
        terms = self.terms(i)
        for at, cond in terms:
            slab = self.bufs[r].at[at]
            arrived = self.links.copy(slab, slab, self.send.at[0], self.recv[r].at[at], "core")
            if cond is None:
                arrived.wait_recv()
            else:
                pl.when(cond)(arrived.wait_recv)

        def body(k, _):
            rows = pl.ds(pl.multiple_of(k * 16, 16), 16)
            total = self.stage[s, 0, rows].astype(jnp.float32) + self.stage[s, 1, rows].astype(jnp.float32)
            for at, cond in terms:
                more = self.bufs[r][at, rows].astype(jnp.float32)
                total = total + (more if cond is None else jnp.where(cond, more, 0.0))
            if leaves:
                self.ring[q, rows] = total.astype(jnp.bfloat16)
            else:
                self.fin[slot, rows] = total
            return 0
        lax.fori_loop(0, self.parts[r][2] // 16, body, 0)
        if not leaves:
            self.result(i, slot).start()
            return
        d = arrival(ROUTES[self.parts[r][3]], dx, dy, j == ZN - 1)
        if d == "z":
            pl.when(zd > z)(lambda: self.hop(i, "up").start())
            pl.when(zd < z)(lambda: self.hop(i, "dn").start())
        else:
            self.hop(i, d).start()

    def finish(self):
        for i in self.in_slot.values():
            self.hop(i, "x").wait_send()
        for slot, i in self.in_fin.items():
            self.result(i, slot).wait()
        for r, part in enumerate(self.parts):
            whole = self.sib.at[pl.ds(4 * ZN * self.starts[r], 4 * ZN * part[2])]
            self.links.copy(whole, whole, self.csend.at[r], self.crecv.at[r, 0, 0], "core").wait_send()


def scatter(parts, ins):
    n = len(ins)

    def kernel(*refs):
        job = Scatter(parts, refs[:n], *refs[n:])
        greet(job.links, None)
        job.begin()
        for i in range(len(job.events)):
            job.step(i)
        job.finish()
    anywhere = pl.BlockSpec(memory_space=pl.ANY)
    outs = Scatter.buffers(parts)
    return pl.pallas_call(
        kernel,
        out_shape=outs,
        in_specs=[anywhere] * n,
        out_specs=[anywhere] * len(outs),
        scratch_shapes=Scatter.scratch(parts),
        compiler_params=pltpu.CompilerParams(collective_id=2, has_side_effects=True, vmem_limit_bytes=60 << 20),
    )(*ins)[0]


class Sends:
    def __init__(self, sems):
        self.sems, self.used = sems, []

    def add(self, src, dst):
        copy = pltpu.make_async_copy(src, dst, self.sems.at[len(self.used)])
        self.used.append(copy)
        return copy

    def finish(self):
        for copy in self.used:
            copy.wait()


def spaced(events, slots):
    bounds = [len(events) * i // slots for i in range(slots + 1)]
    return [events[bounds[i] : bounds[i + 1]] for i in range(slots)]


FORWARD_OUTS = 13


def forward_kernel(batch, width, n_seq, info_ref, x_ref, rim_ref, gain_ref, gain2_ref, vec_ref,
                   wg_ref, wi_ref, wr_ref, we_ref, wo_ref, shard_ref, *refs):
    outs, refs = refs[:FORWARD_OUTS], refs[FORWARD_OUTS:]
    (gate_o, inner_o, mixed_o, normed_o, rate_o, entry_o, decay_o, states_o, pseg_o, sstart_o, all_o,
     gated_o, first_o) = outs
    normed2_o, weights_o = refs[:2]
    (ext, gate, inner, mixed, rate, entry, decay, drive, states, pseg, hseg, sstart, gated, first, normed2,
     sems) = refs[2:18]
    swap = Exchange(n_seq, *refs[18:23])
    job = Gather(FFN_GATHER, [shard_ref], [weights_o], *refs[23:])
    step = pl.program_id(0)
    tokens, depth = x_ref.shape
    r = mixed.shape[1]
    parts, tiles, halves = r // W, W // LANES, depth // W
    steps = 3 * parts + halves
    span = width + 8
    plan = spaced(job.events[len(FFN_GATHER) :], 2 * steps)

    def pump(half, low, high):
        for s in range(low, high):
            if plan[2 * s + half]:
                @pl.when(step == s)
                def _():
                    for event in plan[2 * s + half]:
                        job.forward(event)
    sends = Sends(sems)
    branch_sends = [sends.add(gate, gate_o), sends.add(inner, inner_o), sends.add(mixed, mixed_o),
                    sends.add(ext.at[pl.ds(0, tokens)], normed_o)]
    gate_sends = [sends.add(rate, rate_o), sends.add(entry, entry_o), sends.add(decay, decay_o), sends.add(pseg, pseg_o)]
    state_sends = [sends.add(states, states_o), sends.add(sstart, sstart_o), sends.add(swap.land, all_o),
                   sends.add(gated, gated_o)]
    last_sends = [sends.add(first, first_o), sends.add(normed2, normed2_o)]

    def start(copies):
        for copy in copies:
            copy.start()

    @pl.when(step == 0)
    def _():
        greet(job.links, swap)
        for event in job.events[: len(FFN_GATHER)]:
            job.forward(event)
        gain = gain_ref[:1]

        def norm(i, _):
            at = rows_at(i * CHUNK)
            value = x_ref[at].astype(F32)
            ext[at] = (value * inverse_norm(value, depth) * gain).astype(BF16)
            return 0
        lax.fori_loop(0, tokens // CHUNK, norm, 0)
        rim = rim_ref[...].astype(F32)
        ext[pl.ds(tokens, rim.shape[0])] = (rim * inverse_norm(rim, depth) * gain).astype(BF16)

    @pl.when(step < parts)
    def _():
        j = jnp.minimum(step, parts - 1)
        here = pl.ds(pl.multiple_of(j * W, W), W)
        pump(0, 0, parts)
        got = dot(ext[:tokens], wg_ref[...].reshape(depth, W))
        for t in range(tiles):
            gate[j * tiles + t] = got[:, lanes(t)]
        got = dot(ext[...], wi_ref[...].reshape(depth, W))
        for b in range(batch):
            inner[b * span : b * span + 8, here] = got[tokens + 8 * b : tokens + 8 * b + 8]
            inner[b * span + 8 : (b + 1) * span, here] = got[b * width : (b + 1) * width]
        pump(1, 0, parts)
        for b in range(batch):
            conv = vec_ref[CONV_BIAS : CONV_BIAS + 1, here]
            for lag in range(4):
                conv = conv + vec_ref[lag : lag + 1, here] * inner[b * span + 8 - lag : (b + 1) * span - lag, here]
            mixed[b * width : (b + 1) * width, here] = conv.astype(BF16)

    @pl.when(step == parts - 1)
    def _():
        start(branch_sends)

    @pl.when(jnp.logical_and(step >= parts, step < 2 * parts))
    def _():
        j = jnp.clip(step - parts, 0, parts - 1)
        pump(0, parts, 2 * parts)
        for w_ref, to in ((wr_ref, rate), (we_ref, entry)):
            got = dot(mixed[...], w_ref[...].reshape(r, W))
            for t in range(tiles):
                to[j * tiles + t] = got[:, lanes(t)]
        pump(1, parts, 2 * parts)

        def gating(t, b, spot, at, cols, _):
            g = j * tiles + t
            tile = pl.ds(pl.multiple_of(j * W + t * LANES, LANES), LANES)
            a_rate = sigmoid(rate[g, at] + vec_ref[RATE_BIAS : RATE_BIAS + 1, tile])
            an_entry = sigmoid(entry[g, at] + vec_ref[ENTRY_BIAS : ENTRY_BIAS + 1, tile])
            log_decay = vec_ref[COEF : COEF + 1, tile] * a_rate
            z = 2.0 * log_decay
            root = jnp.sqrt(one_less_exp(z, jnp.exp(z)))
            valid = in_row(spot, width, a_rate.shape) < info_ref[b]
            rate[g, at] = a_rate
            entry[g, at] = an_entry
            decay[g, at] = jnp.where(valid, jnp.exp(log_decay), 1.0)
            drive[g, at] = jnp.where(valid, root * an_entry * mixed[at, tile].astype(F32), 0.0)
            return 0
        each_tile(batch, width, tiles, gating)
        for t in range(tiles):
            g = j * tiles + t
            tile = pl.ds(pl.multiple_of(j * W + t * LANES, LANES), LANES)
            for b in range(batch):
                prod = jnp.ones((SEGS, LANES), F32)
                state = jnp.zeros((SEGS, LANES), F32)
                for s in range(width // SEGS):
                    at = strided(b, width, s)
                    a = decay[g, at]
                    state = a * state + drive[g, at]
                    prod = prod * a
                pseg[b * SEGS : (b + 1) * SEGS, tile] = prod
                hseg[b * SEGS : (b + 1) * SEGS, tile] = state
                whole, end = prod[:1], state[:1]
                for i in range(1, SEGS):
                    whole = whole * prod[i : i + 1]
                    end = prod[i : i + 1] * end + state[i : i + 1]
                swap.rows[g, b : b + 1] = whole
                swap.rows[g, batch + b : batch + b + 1] = end

    @pl.when(step == 2 * parts - 1)
    def _():
        start(gate_sends)
        swap.begin()

    @pl.when(step == 2 * parts)
    def _():
        swap.finish()

    @pl.when(jnp.logical_and(step >= 2 * parts, step < 3 * parts))
    def _():
        j = jnp.clip(step - 2 * parts, 0, parts - 1)
        me = lax.axis_index("seq")
        pump(0, 2 * parts, 3 * parts)
        for t in range(tiles):
            g = j * tiles + t
            tile = pl.ds(pl.multiple_of(j * W + t * LANES, LANES), LANES)
            for b in range(batch):
                begin = jnp.zeros((1, LANES), F32)
                for k in range(n_seq):
                    new = swap.land[k, g, b : b + 1] * begin + swap.land[k, g, batch + b : batch + b + 1]
                    begin = jnp.where(k < me, new, begin)
                for i in range(SEGS):
                    at = b * SEGS + i
                    sstart[at : at + 1, tile] = begin
                    begin = pseg[at : at + 1, tile] * begin + hseg[at : at + 1, tile]
                state = sstart[b * SEGS : (b + 1) * SEGS, tile]
                for s in range(width // SEGS):
                    at = strided(b, width, s)
                    state = decay[g, at] * state + drive[g, at]
                    states[g, at] = state
        pump(1, 2 * parts, 3 * parts)

        def gating(t, b, spot, at, cols, _):
            g = j * tiles + t
            tile = pl.ds(pl.multiple_of(j * W + t * LANES, LANES), LANES)
            gated[at, tile] = (states[g, at] * gelu_both(gate[g, at])[0]).astype(BF16)
            return 0
        each_tile(batch, width, tiles, gating)

    @pl.when(step == 3 * parts - 1)
    def _():
        start(state_sends)

    @pl.when(step >= 3 * parts)
    def _():
        half = jnp.clip(step - 3 * parts, 0, halves - 1)
        here = pl.ds(pl.multiple_of(half * W, W), W)
        pump(0, 3 * parts, steps)
        first[:, here] = x_ref[:, here].astype(F32) + dot(gated[...], wo_ref[...].reshape(r, W))
        pump(1, 3 * parts, steps)

    @pl.when(step == steps - 1)
    def _():
        def norm(i, _):
            at = rows_at(i * CHUNK)
            value = first[at]
            normed2[at] = (value * inverse_norm(value, depth) * gain2_ref[:1]).astype(BF16)
            return 0
        lax.fori_loop(0, tokens // CHUNK, norm, 0)
        start(last_sends)
        job.finish()
        sends.finish()


def forward(info, tokens2, rim, gain, gain2, vec, packed, shard, batch, n_seq):
    tokens, depth = tokens2.shape
    width = tokens // batch
    n = packed.shape[0]
    r = vec.shape[1]
    parts, halves, tiles = r // W, depth // W, r // LANES
    rows, rrows = depth // n, r // n
    full = lambda a: pl.BlockSpec(a.shape, lambda j: (0,) * a.ndim)
    anywhere = pl.BlockSpec(memory_space=pl.ANY)
    clamp = lambda j, low, count: jnp.clip(j - low, 0, count - 1)

    def block(count, at, low, number):
        return pl.BlockSpec((n, count, W), lambda j: (0, at // count + clamp(j, low, number), 0))
    S = jax.ShapeDtypeStruct
    flat, tall, segs = S((tokens, r), BF16), S((tiles, tokens, LANES), F32), S((batch * SEGS, r), F32)
    inner, ends = S((tokens + 8 * batch, r), F32), S((n_seq, tiles, 2 * batch, LANES), F32)
    first, normed = S((tokens, depth), F32), S((tokens, depth), BF16)
    outs = [tall, inner, flat, normed, tall, tall, tall, tall, segs, segs, ends, flat, first, normed,
            S((n, shard.shape[0], W), BF16)]
    vm = lambda s: pltpu.VMEM(s.shape, s.dtype)
    scratch = [pltpu.VMEM((tokens + 8 * batch, depth), BF16)] + [
        vm(s) for s in (tall, inner, flat, tall, tall, tall, tall, tall, segs, segs, segs, flat, first, normed)]
    return pl.pallas_call(
        functools.partial(forward_kernel, batch, width, n_seq),
        grid=(3 * parts + halves,),
        in_specs=[pl.BlockSpec(memory_space=pltpu.SMEM), full(tokens2), full(rim), full(gain), full(gain2), full(vec),
                  block(rows, GATE_AT, 0, parts), block(rows, INPUT_AT, 0, parts),
                  block(rrows, RATE_AT, parts, parts), block(rrows, ENTRY_AT, parts, parts),
                  block(rrows, OUT_AT, 3 * parts, halves), anywhere],
        out_specs=[anywhere] * len(outs),
        out_shape=outs,
        scratch_shapes=scratch + [SEM((FORWARD_OUTS + 1,))] + Exchange.scratch(n_seq, (tiles, 2 * batch, LANES))
        + Gather.scratch(FFN_GATHER),
        compiler_params=pltpu.CompilerParams(collective_id=3, has_side_effects=True, vmem_limit_bytes=62 << 20),
    )(info, tokens2, rim, gain, gain2, vec, packed, packed, packed, packed, packed, shard)


FFN_SCATTER = ((0, 0, 144, 0), (0, 144, 144, 1), (0, 288, 144, 2), (0, 432, 144, 3))
REC_SCATTER = ((0, 0, 144, 0), (0, 144, 144, 1), (0, 288, 144, 2), (0, 432, 144, 3), (1, 0, 16, 0))


def backward_kernel(batch, width, n_seq, pump_plan, *refs):
    (info_ref, gain_ref, ggain2_ref, vec_ref, pseg_ref, sstart_ref, pall_ref, wo_ref, wr_ref, we_ref, we1_ref,
     states_ref, decay_ref, gate_ref, rate_ref, entry_ref, gated_ref, inner_ref,
     dlow_h, dfirst_h, mixed_h, normed_h, x_h, gf, token_h, gr, gs, total_h, sib_h,
     low, tall, hid, dn, one, two, du, dgate, ext, stage, first, mixed, normed, x,
     gseg, gstart, sums, csums, ggain, rims, rim_land, sem, lsem, osem, rimsem) = refs[:54]
    swap = Exchange(n_seq, *refs[54:59])
    job = Scatter(FFN_SCATTER, (gf,), total_h, sib_h, *refs[59:])
    step = pl.program_id(0)
    tokens, depth = first.shape
    n = gf.shape[0]
    r = dgate.shape[1]
    rows, rrows = depth // n, r // n
    group = wo_ref.shape[0]
    thin = group * rrows
    tiles, few, rt = W // LANES, thin // LANES, r // LANES
    counts = backward_steps(n, r, group)
    at, total_steps = {}, 0
    for name, count in counts:
        at[name] = total_steps
        total_steps += count
    size = dict(counts)
    span = width + 8
    me = lax.axis_index("seq")

    def phase(name):
        return jnp.logical_and(step >= at[name], step < at[name] + size[name])

    def index(name):
        return jnp.clip(step - at[name], 0, size[name] - 1)

    def cols(start, count):
        return pl.ds(pl.multiple_of(start, LANES), count)

    def when_step(s, act):
        pl.when(step == s)(act)

    def outgoing(slot, dst, value, count, over=None):
        src = stage.at[slot, pl.ds(0, value.shape[0]), pl.ds(0, count)]
        stage[slot, : value.shape[0], :count] = value
        pltpu.make_async_copy(src, dst, sem.at[slot]).start()

    def wait_out(slot, devices, count):
        src = stage.at[slot, pl.ds(0, devices), pl.ds(0, count)]
        pltpu.make_async_copy(src, gr.at[pl.ds(0, devices), pl.ds(0, count)], sem.at[slot]).wait()

    inputs = [pltpu.make_async_copy(src, dst, lsem.at[k]) for k, (src, dst) in enumerate(
        ((dlow_h, low), (dfirst_h, first), (mixed_h, mixed), (normed_h, normed), (x_h, x)))]
    rim_copy = pltpu.make_async_remote_copy(rims, rim_land, rimsem.at[0], rimsem.at[1],
                                            device_id=(lax.rem(me + n_seq - 1, n_seq), swap.z), device_id_type=MESH)

    @pl.when(step == 0)
    def _():
        for copy in inputs:
            copy.start()
        greet(job.links, swap)
        job.begin()

        @pl.when(me == n_seq - 1)
        def _():
            rim_land[...] = jnp.zeros_like(rim_land)
        inputs[0].wait()

    @pl.when(step == at["V"])
    def _():
        for slot in range(2):
            wait_out(slot, group, rrows)
        inputs[3].wait()

    @pl.when(step == at["E"])
    def _():
        wait_out(0, n, rows)
        inputs[2].wait()
        swap.finish()

    @pl.when(step == at["M"])
    def _():
        for slot in range(2):
            wait_out(slot, n, rrows)

    for s, events in pump_plan:
        if events:
            @pl.when(step == s)
            def _():
                for i in events:
                    job.step(i)

    @pl.when(phase("U"))
    def _():
        k = index("U")
        total = dot_back(low[:, :W], wo_ref[:, :rrows].reshape(thin, W))
        total = total + dot_back(low[:, W:], wo_ref[:, rrows:].reshape(thin, W))
        for t in range(few):
            tall[k * few + t] = total[:, lanes(t)]

        def gating(t, b, spot, here, tile, _):
            gate, slope = gelu_both(gate_ref[t, here])
            d = tall[k * few + t, here]
            tall[k * few + t, here] = d * gate
            dgate[here, cols(k * thin + t * LANES, LANES)] = (d * states_ref[t, here] * slope).astype(BF16)
            return 0
        each_tile(batch, width, few, gating)
        for half in range(2):
            value = dot_outer(gated_ref[...], low[:, half * W : (half + 1) * W]).astype(BF16).reshape(group, rrows, W)
            pl.when(k > 0)(lambda: wait_out(half, group, rrows))
            outgoing(half, gr.at[pl.ds(k * group, group), pl.ds(OUT_AT + half * rrows, rrows)], value, rrows)
        for t in range(few):
            tile = cols(k * thin + t * LANES, LANES)
            for b in range(batch):
                grad = jnp.zeros((SEGS, LANES), F32)
                for s in reversed(range(width // SEGS)):
                    here = strided(b, width, s)
                    grad = decay_ref[t, here] * (tall[k * few + t, here] + grad)
                gseg[b * SEGS : (b + 1) * SEGS, tile] = grad
                whole = grad[SEGS - 1 :]
                for i in reversed(range(SEGS - 1)):
                    whole = grad[i : i + 1] + pseg_ref[b * SEGS + i : b * SEGS + i + 1, tile] * whole
                swap.rows[k * few + t, b : b + 1] = whole

    @pl.when(step == at["U"] + size["U"] - 1)
    def _():
        swap.begin()

    @pl.when(phase("V"))
    def _():
        j = index("V")
        grad = dgate[:, cols(j * W, W)]
        more = dot_back(grad, we1_ref[...].reshape(depth, W))

        @pl.when(j == 0)
        def _():
            dn[...] = more

        @pl.when(j > 0)
        def _():
            dn[...] += more
        value = dot_outer(normed[...], grad).astype(BF16).reshape(n, rows, W)
        pl.when(j > 0)(lambda: wait_out(0, n, rows))
        outgoing(0, gr.at[:, pl.ds(pl.multiple_of(GATE_AT + j * rows, 16), rows)], value, rows)

    @pl.when(phase("E"))
    def _():
        k = index("E")
        for t in range(few):
            g = k * few + t
            tile = cols(k * thin + t * LANES, LANES)
            for b in range(batch):
                grad = jnp.zeros((1, LANES), F32)
                for q in reversed(range(n_seq)):
                    new = pall_ref[q, g, b : b + 1] * grad + swap.land[q, g, b : b + 1]
                    grad = jnp.where(q > me, new, grad)
                for i in reversed(range(SEGS)):
                    line = b * SEGS + i
                    gstart[i : i + 1] = grad
                    grad = pseg_ref[line : line + 1, tile] * grad + gseg[line : line + 1, tile]
                grad = gstart[...]
                for s in reversed(range(width // SEGS)):
                    here = strided(b, width, s)
                    total = tall[g, here] + grad
                    one[t, here] = total
                    grad = decay_ref[t, here] * total
                    before = states_ref[t, strided(b, width, s - 1)] if s else sstart_ref[b * SEGS : (b + 1) * SEGS, tile]
                    two[t, here] = grad * before

        def gating(t, b, spot, here, _, kept):
            tile = cols(k * thin + t * LANES, LANES)
            coef = vec_ref[COEF : COEF + 1, tile]
            rate, entry = rate_ref[t, here], entry_ref[t, here]
            valid = in_row(spot, width, rate.shape) < info_ref[b]
            grad = jnp.where(valid, one[t, here], 0.0)
            z = 2.0 * coef * rate
            exp_z = jnp.exp(z)
            under = one_less_exp(z, exp_z)
            inverse = lax.rsqrt(under)
            root = under * inverse
            value = mixed[here, tile].astype(F32)
            part = grad * entry
            d_log = jnp.where(valid, two[t, here], 0.0) - part * value * exp_z * inverse
            d_rate = coef * d_log * rate * (1.0 - rate)
            straight = part * root
            d_entry = straight * value * (1.0 - entry)
            tall[rt + k * few + t, here] = straight
            hid[here, tile] = d_rate.astype(BF16)
            hid[here, cols(r + k * thin + t * LANES, LANES)] = d_entry.astype(BF16)
            return (kept[0] + fold8(d_log * rate), kept[1] + fold8(d_rate), kept[2] + fold8(d_entry))
        zero = jnp.zeros((8, LANES), F32)
        for t, kept in enumerate(each_tile(batch, width, few, gating, (zero, zero, zero))):
            tile = cols(k * thin + t * LANES, LANES)
            for line in range(3):
                factor = 8.0 * vec_ref[SIG : SIG + 1, tile] if line == 0 else 1.0
                sums[line : line + 1, tile] = factor * jnp.sum(kept[line], axis=0, keepdims=True)

    @pl.when(phase("R"))
    def _():
        j = index("R")
        for which, base in ((0, RATE_AT), (1, ENTRY_AT)):
            value = dot_outer(mixed[...], hid[:, cols(which * r + j * W, W)]).astype(BF16).reshape(n, rrows, W)
            pl.when(j > 0)(lambda: wait_out(which, n, rrows))
            outgoing(which, gr.at[:, pl.ds(pl.multiple_of(base + j * rrows, 16), rrows)], value, rrows)

    @pl.when(phase("M"))
    def _():
        k = index("M")
        total = jnp.zeros((tokens, thin), F32)
        for p in range(r // W):
            for which, w_ref in ((0, wr_ref), (1, we_ref)):
                there = slice(which * r + p * W, which * r + (p + 1) * W)
                total = total + dot_back(hid[:, there], w_ref[:, p * rrows : (p + 1) * rrows].reshape(thin, W))
        for t in range(few):
            tall[rt + k * few + t] += total[:, lanes(t)]

    @pl.when(step == at["M"] + size["M"] - 1)
    def _():
        for b in range(batch):
            rims[:, b * 4 : b * 4 + 4] = tall[rt : 2 * rt, b * width : b * width + 4]
        pl.when(me > 0)(rim_copy.start)

    @pl.when(step == at["I"])
    def _():
        pl.when(me < n_seq - 1)(rim_copy.wait_recv)
        pl.when(me > 0)(rim_copy.wait_send)

    @pl.when(phase("I"))
    def _():
        j = index("I")
        here = cols(j * W, W)
        for t in range(tiles):
            for b in range(batch):
                ext[b * span : b * span + width, lanes(t)] = tall[rt + j * tiles + t, b * width : (b + 1) * width]
                ext[b * span + width : b * span + width + 4, lanes(t)] = rim_land[j * tiles + t, b * 4 : b * 4 + 4]
        for b in range(batch):
            total = jnp.zeros((width, W), F32)
            for lag in range(4):
                total = total + vec_ref[lag : lag + 1, here] * ext[b * span + lag : b * span + lag + width]
            du[b * width : (b + 1) * width] = total.astype(BF16)
        for lag in range(5):
            total = jnp.zeros((1, W), F32)
            for b in range(batch):
                value = ext[b * span : b * span + width]
                if lag < 4:
                    value = value * inner_ref[b * span + 8 - lag : (b + 1) * span - lag]
                total = total + jnp.sum(value, axis=0, keepdims=True)
            csums[lag : lag + 1, here] = total
        dn[...] += dot_back(du[...], we1_ref[...].reshape(depth, W))
        value = dot_outer(normed[...], du[...]).astype(BF16).reshape(n, rows, W)
        pl.when(j > 0)(lambda: wait_out(0, n, rows))
        outgoing(0, gr.at[:, pl.ds(pl.multiple_of(INPUT_AT + j * rows, 16), rows)], value, rows)

    @pl.when(step == total_steps - 1)
    def _():
        inputs[1].wait()
        inputs[4].wait()

        def finish(i, total):
            here = rows_at(i * CHUNK)
            value, grad = x[here].astype(F32), dn[here]
            scale = inverse_norm(value, depth)
            weighted = grad * gain_ref[:1]
            mean = jnp.sum(weighted * value, axis=-1, keepdims=True) * (1.0 / depth)
            dn[here] = first[here] + scale * weighted - value * (scale * scale * scale * mean)
            return total + fold8(grad * value * scale)
        ggain[...] = lax.fori_loop(0, tokens // CHUNK, finish, jnp.zeros((8, depth), F32))
        pltpu.make_async_copy(dn, token_h, osem.at[0]).start()
        wait_out(0, n, rows)
        small = stage.at[0, :, pl.ds(0, SMALL_ROWS)]
        small[...] = jnp.zeros((n, SMALL_ROWS, W), BF16)
        lines = [(jnp.sum(ggain[...], axis=0, keepdims=True), rows), (jnp.sum(ggain2_ref[...], axis=0, keepdims=True), rows)]
        lines += [(csums[k : k + 1], rrows) for k in range(5)] + [(sums[k : k + 1], rrows) for k in (1, 2, 0)]
        for k, (line, count) in enumerate(lines):
            stage[0, :, k, :LANES] = deal(line, n, count)
        small_out = pltpu.make_async_copy(small, gs, osem.at[1])
        small_out.start()
        small_out.wait()
        done = sum(len(events) for _, events in pump_plan)
        for i in range(done, len(job.events)):
            job.step(i)
        job.finish()
        pltpu.make_async_copy(dn, token_h, osem.at[0]).wait()


def deal(line, n, count):
    length = n * count
    lane = lax.broadcasted_iota(jnp.int32, (n, length), 1)
    row = lax.broadcasted_iota(jnp.int32, (n, length), 0)
    own = jnp.where(jnp.logical_and(lane >= row * count, lane < (row + 1) * count), line, 0.0).astype(BF16)
    spot = lax.broadcasted_iota(jnp.int32, (length, LANES), 0)
    col = lax.broadcasted_iota(jnp.int32, (length, LANES), 1)
    pick = jnp.where(jnp.logical_and(lax.rem(spot, count) == col, col < count), 1.0, 0.0).astype(BF16)
    return dot(own, pick).astype(BF16)


def backward_steps(n, r, group):
    parts = n // group
    return (("U", parts), ("V", r // W), ("E", parts), ("R", r // W), ("M", parts), ("I", r // W))


STEP_US = {"U": 5.0, "V": 2.0, "E": 4.0, "R": 3.0, "M": 2.5, "I": 5.0}
ROW_US = 140 / (1168 * 16)


def pump_steps(counts):
    times, now = [], 0.0
    for name, count in counts:
        for _ in range(count):
            times.append(now)
            now += STEP_US[name]
    plan, free = [[] for _ in times], 4.0
    for number in range(16 * len(FFN_SCATTER)):
        free += ROW_US * FFN_SCATTER[number % len(FFN_SCATTER)][2]
        s = next((s for s, t in enumerate(times) if t >= free), None)
        if s is None:
            break
        plan[s].append(number)
    return list(enumerate(plan))


def backward(info, gain, ggain2, vec, pseg, sstart, pall, packed, states, decay, gate_pre, rate, entry, gated,
             inner, d_low, d_first, mixed, normed, x, grad_ffn, batch):
    tokens, depth = x.shape
    width = tokens // batch
    n, r = packed.shape[0], vec.shape[1]
    group = 8
    rows, rrows = depth // n, r // n
    thin = group * rrows
    few, tiles = thin // LANES, W // LANES
    n_seq = pall.shape[0]
    counts = backward_steps(n, r, group)
    at, steps = {}, 0
    for name, count in counts:
        at[name] = steps
        steps += count
    size = dict(counts)
    clamp = lambda j, name: jnp.clip(j - at[name], 0, size[name] - 1)
    full = lambda a: pl.BlockSpec(a.shape, lambda j: (0,) * a.ndim, pipeline_mode=pl.Buffered(buffer_count=1))
    anywhere = pl.BlockSpec(memory_space=pl.ANY)

    def two_phases(j, one, two):
        return jnp.where(j < at[two], clamp(j, one), clamp(j, two))
    both = pl.BlockSpec((few, tokens, LANES), lambda j: (two_phases(j, "U", "E"), 0, 0))
    early = pl.BlockSpec((few, tokens, LANES), lambda j: (clamp(j, "U"), 0, 0))
    late = pl.BlockSpec((few, tokens, LANES), lambda j: (clamp(j, "E"), 0, 0))
    in_specs = [pl.BlockSpec(memory_space=pltpu.SMEM)] + [full(a) for a in (gain, ggain2, vec, pseg, sstart, pall)] + [
        pl.BlockSpec((group, 2 * rrows, W), lambda j: (clamp(j, "U"), OUT_AT // (2 * rrows), 0)),
        pl.BlockSpec((group, r // W * rrows, W), lambda j: (clamp(j, "M"), RATE_AT // (r // W * rrows), 0)),
        pl.BlockSpec((group, r // W * rrows, W), lambda j: (clamp(j, "M"), ENTRY_AT // (r // W * rrows), 0)),
        pl.BlockSpec((n, rows, W), lambda j: (0, jnp.where(j < at["I"], GATE_AT // rows + clamp(j, "V"),
                                                           INPUT_AT // rows + clamp(j, "I")), 0)),
        both, both, early, late, late,
        pl.BlockSpec((tokens, thin), lambda j: (0, clamp(j, "U"))),
        pl.BlockSpec((inner.shape[0], W), lambda j: (0, clamp(j, "I"))),
    ] + [anywhere] * 6
    S = jax.ShapeDtypeStruct
    outs = [S((tokens, depth), F32), S((n, REC_ROWS, W), BF16), S((n, SMALL_ROWS, W), BF16)]
    outs += Scatter.buffers(FFN_SCATTER)
    vm = pltpu.VMEM
    scratch = [
        vm((tokens, depth), BF16), vm((2 * r // LANES, tokens, LANES), F32), vm((tokens, 2 * r), BF16),
        vm((tokens, depth), F32), vm((few, tokens, LANES), F32), vm((few, tokens, LANES), F32),
        vm((tokens, W), BF16), vm((tokens, r), BF16), vm((tokens + 8 * batch, W), F32),
        vm((2, n, rrows, W), BF16), vm((tokens, depth), F32), vm((tokens, r), BF16), vm((tokens, depth), BF16),
        vm((tokens, depth), BF16), vm((batch * SEGS, r), F32), vm((SEGS, LANES), F32), vm((8, r), F32), vm((8, r), F32),
        vm((8, depth), F32), vm((r // LANES, 4 * batch, LANES), F32), vm((r // LANES, 4 * batch, LANES), F32),
        SEM((2,)), SEM((5,)), SEM((2,)), SEM((2,)),
    ] + Exchange.scratch(n_seq, (r // LANES, batch, LANES)) + Scatter.scratch(FFN_SCATTER)
    got = pl.pallas_call(
        functools.partial(backward_kernel, batch, width, n_seq, pump_steps(counts)),
        grid=(steps,),
        in_specs=in_specs,
        out_specs=[anywhere] * len(outs),
        out_shape=outs,
        scratch_shapes=scratch,
        compiler_params=pltpu.CompilerParams(collective_id=4, has_side_effects=True, vmem_limit_bytes=64 << 20),
    )(info, gain, ggain2, vec, pseg, sstart, pall, packed, packed, packed, packed,
      states, decay, gate_pre, rate, entry, gated, inner, d_low, d_first, mixed, normed, x, grad_ffn)
    return got[0], got[1], got[2], got[3]


RATE_AT, ENTRY_AT, OUT_AT, GATE_AT, INPUT_AT, REC_ROWS = 0, 144, 288, 384, 480, 576
FFN_GATE_AT, FFN_UP_AT, FFN_DOWN_AT, FFN_ROWS, SMALL_ROWS = 0, 192, 384, 576, 16
REC_GATHER = ((0, 0, 0, 144, 0), (0, 0, 144, 144, 1), (0, 0, 288, 144, 2), (0, 0, 432, 160, 3))
FFN_GATHER = ((0, 0, 0, 144, 0), (0, 0, 144, 144, 1), (0, 0, 288, 144, 2), (0, 0, 432, 144, 3))


def pack_blocks(item):
    rows, cols = item.shape
    return item.reshape(rows, cols // W, W).transpose(1, 0, 2).reshape(rows * cols // W, W)


def unpack_blocks(item, rows, cols):
    return item.reshape(cols // W, rows, W).transpose(1, 0, 2).reshape(rows, cols)


def pad_rows(item, before, count):
    batch, rows, cols = item.shape
    item = jnp.pad(item, ((0, 0), (before, count - rows - before), (0, 0)))
    return item.reshape(batch * count, cols)


def per_device_packed(tokens, cotangent, lengths, *shards):
    (gate_proj, input_proj, rate_proj, entry_proj, out_proj, ffn_gate, ffn_up, ffn_down) = shards[:8]
    small = shards[8:]
    batch, width, depth = tokens.shape
    r, f = gate_proj.shape[1], ffn_gate.shape[1]
    n_seq = lax.axis_size("seq")
    me = lax.axis_index("seq")
    rim = pad_rows(from_behind(tokens[:, width - 3 :], "seq", 1), 5, 8)
    flat = jnp.concatenate([item.reshape(-1) for item in small])
    flat = jnp.pad(flat, (0, SMALL_ROWS * W - flat.shape[0])).reshape(SMALL_ROWS, W)
    order = (rate_proj, entry_proj, out_proj, gate_proj, input_proj)
    shard = jnp.concatenate([pack_blocks(item) for item in order] + [flat], axis=0)
    packed = gather(REC_GATHER, [shard], [REC_ROWS + SMALL_ROWS])[0]
    shard = jnp.concatenate([pack_blocks(item) for item in (ffn_gate, ffn_up, ffn_down)], axis=0)
    flats = packed[:, REC_ROWS].astype(jnp.float32)
    lo, vectors = 0, []
    for item in small:
        part = flats[:, lo : lo + item.size]
        lo += item.size
        if item.ndim == 2:
            part = part.reshape(-1, *item.shape).transpose(1, 0, 2).reshape(item.shape[0], -1)
        else:
            part = part.reshape(1, -1)
        vectors.append(part)
    norm_gain, ffn_gain, taps, conv_bias, rate_bias, entry_bias, logit = vectors
    vec = jnp.concatenate([taps, conv_bias, rate_bias, entry_bias, -lru_scale * jax.nn.softplus(-logit),
                           jax.nn.sigmoid(-logit), jnp.zeros((7, r), jnp.float32)], axis=0)
    norm_gain = jnp.broadcast_to(norm_gain, (8, depth))
    ffn_gain = jnp.broadcast_to(ffn_gain, (8, depth))
    info = jnp.concatenate([jnp.clip(lengths - me * width, 0, width), me[None]]).astype(jnp.int32)
    tokens2 = tokens.reshape(batch * width, depth)
    cot2 = cotangent.reshape(batch * width, depth)

    (gate_pre, inner, mixed, normed, rate, entry, decay, states, pseg, sstart, pall, gated, first, normed_two,
     packed_ffn) = forward(info, tokens2, rim, norm_gain, ffn_gain, vec, packed, shard, batch, n_seq)
    block_out, d_first, d_low, g_ffn_gain, grad_ffn = feed_forward(
        info, first, normed_two, cot2, ffn_gain, packed_ffn, f, batch)
    token_grad, grad_rec, grad_small, total_ffn = backward(
        info, norm_gain, g_ffn_gain, vec, pseg, sstart, pall, packed, states, decay, gate_pre, rate, entry, gated, inner,
        d_low, d_first, mixed, normed, tokens2, grad_ffn, batch)
    total = scatter(REC_SCATTER, [grad_rec, grad_small])
    result = [(total, GATE_AT, gate_proj), (total, INPUT_AT, input_proj), (total, RATE_AT, rate_proj),
              (total, ENTRY_AT, entry_proj), (total, OUT_AT, out_proj), (total_ffn, FFN_GATE_AT, ffn_gate),
              (total_ffn, FFN_UP_AT, ffn_up), (total_ffn, FFN_DOWN_AT, ffn_down)]
    result = [unpack_blocks(rows[lo : lo + item.size // W], *item.shape) for rows, lo, item in result]
    line = REC_ROWS
    for item in small:
        count = item.shape[0] if item.ndim == 2 else 1
        part = total[line : line + count, : item.shape[-1]]
        line += count
        result.append(part.reshape(item.shape))
    return (block_out.reshape(tokens.shape), token_grad.reshape(tokens.shape), *result)


def solution(mesh):
    packs = mesh.shape["seq"] == 8 and mesh.shape["batch"] == ZN
    placed = (
        P("batch", "seq", None),
        P("batch", "seq", None),
        P("batch"),
        P(("seq", "batch"), None),
        P(("seq", "batch"), None),
        P(("seq", "batch"), None),
        P(("seq", "batch"), None),
        P(("seq", "batch"), None),
        P(("seq", "batch"), None),
        P(("seq", "batch"), None),
        P(("seq", "batch"), None),
        P(("seq", "batch")),
        P(("seq", "batch")),
        P(None, ("seq", "batch")),
        P(("seq", "batch")),
        P(("seq", "batch")),
        P(("seq", "batch")),
        P(("seq", "batch")),
    )
    return jax.shard_map(
        per_device_packed if packs else per_device,
        mesh=mesh,
        in_specs=placed,
        out_specs=(
            P("batch", "seq", None),
            P("batch", "seq", None),
            P(("seq", "batch"), None),
            P(("seq", "batch"), None),
            P(("seq", "batch"), None),
            P(("seq", "batch"), None),
            P(("seq", "batch"), None),
            P(("seq", "batch"), None),
            P(("seq", "batch"), None),
            P(("seq", "batch"), None),
            P(("seq", "batch")),
            P(("seq", "batch")),
            P(None, ("seq", "batch")),
            P(("seq", "batch")),
            P(("seq", "batch")),
            P(("seq", "batch")),
            P(("seq", "batch")),
        ),
        check_vma=False,
    )
```

```python
import functools

import jax
import jax.numpy as jnp
import numpy as np
from jax import lax
from jax.experimental import pallas as pl
from jax.experimental.pallas import tpu as pltpu
from jax.sharding import PartitionSpec as P

MICRO = 2


eps = 1e-06
lru_scale = 8.0


def from_behind(value, axis, steps):
    count = lax.axis_size(axis)
    initial, last = (max(0, -steps), min(count, count - steps))
    return lax.ppermute(value, axis, [(source, source + steps) for source in range(initial, last)])


def entering(array, axis, combine, identity):
    size, place = (lax.axis_size(axis), lax.axis_index(axis))
    everything = jax.tree.map(lambda part: lax.all_gather(part, axis), array)
    start = jax.tree.map(
        lambda part, zero: jnp.broadcast_to(jnp.asarray(zero, part.dtype), part.shape),
        array,
        identity,
    )

    def entering_turn(k, before):
        reached = k < place
        new = combine(before, jax.tree.map(lambda part: part[k], everything))
        return jax.tree.map(lambda a, b: jnp.where(reached, a, b), new, before)

    return lax.fori_loop(0, size, entering_turn, start)


def carried_in(array, axis, combine, identity):
    size, place = (lax.axis_size(axis), lax.axis_index(axis))
    everything = jax.tree.map(
        lambda part, kind: lax.all_gather(part.astype(kind), axis),
        array,
        (jnp.bfloat16, jnp.bfloat16),
    )
    start = jax.tree.map(
        lambda part, zero: jnp.broadcast_to(jnp.asarray(zero, part.dtype), part.shape),
        array,
        identity,
    )

    def carried_turn(k, before):
        at = size - 1 - k
        reached = at > place
        new = combine(
            before, jax.tree.map(lambda part, own: part[at].astype(own.dtype), everything, array)
        )
        return jax.tree.map(lambda a, b: jnp.where(reached, a, b), new, before)

    return lax.fori_loop(0, size, carried_turn, start)


def for_sending(array):

    def short(part):
        return part.astype(jnp.bfloat16) if part.dtype == jnp.float32 else part

    return jax.tree.map(short, array)


def project(left, right):
    return jnp.einsum("btd,de->bte", left, right, preferred_element_type=jnp.float32)


def project_back(left, right):
    return jnp.einsum("bte,de->btd", left, right, preferred_element_type=jnp.float32)


def outer_sum(left, right):
    return jnp.einsum("btd,bte->de", left, right, preferred_element_type=jnp.float32)


def link(earlier, later):
    return (earlier[0] * later[0], later[0] * earlier[1] + later[1])


def norm_back(value, scale, gain, grad):
    weighted = grad * gain
    gain_grad = jnp.sum(grad * value * scale, axis=(0, 1))
    spread = jnp.mean(weighted * value, axis=-1, keepdims=True)
    return (scale * weighted - value * scale**3 * spread, gain_grad)


def fetch(shards):
    (
        gate_proj,
        input_proj,
        rate_proj,
        entry_proj,
        out_proj,
        ffn_gate,
        ffn_up,
        ffn_down,
        norm_gain,
        ffn_gain,
        conv_taps,
        conv_bias,
        rate_bias,
        entry_bias,
        decay_logit,
    ) = shards
    return (
        lax.all_gather(gate_proj, ("seq", "batch"), axis=0, tiled=True),
        lax.all_gather(input_proj, ("seq", "batch"), axis=0, tiled=True),
        lax.all_gather(rate_proj, ("seq", "batch"), axis=0, tiled=True),
        lax.all_gather(entry_proj, ("seq", "batch"), axis=0, tiled=True),
        lax.all_gather(out_proj, ("seq", "batch"), axis=0, tiled=True),
        lax.all_gather(ffn_gate, ("seq", "batch"), axis=0, tiled=True),
        lax.all_gather(ffn_up, ("seq", "batch"), axis=0, tiled=True),
        lax.all_gather(ffn_down, ("seq", "batch"), axis=0, tiled=True),
        lax.all_gather(norm_gain, ("seq", "batch"), axis=0, tiled=True),
        lax.all_gather(ffn_gain, ("seq", "batch"), axis=0, tiled=True),
        lax.all_gather(conv_taps, ("seq", "batch"), axis=1, tiled=True),
        lax.all_gather(conv_bias, ("seq", "batch"), axis=0, tiled=True),
        lax.all_gather(rate_bias, ("seq", "batch"), axis=0, tiled=True),
        lax.all_gather(entry_bias, ("seq", "batch"), axis=0, tiled=True),
        lax.all_gather(decay_logit, ("seq", "batch"), axis=0, tiled=True),
    )


def forward_part(tokens, mask, weights):
    (
        gate_proj,
        input_proj,
        rate_proj,
        entry_proj,
        out_proj,
        ffn_gate,
        ffn_up,
        ffn_down,
        norm_gain,
        ffn_gain,
        conv_taps,
        conv_bias,
        rate_bias,
        entry_bias,
        decay_logit,
    ) = weights
    width = tokens.shape[1]
    taps_count = conv_taps.shape[0]
    values = tokens.astype(jnp.float32)
    scale_one = lax.rsqrt(jnp.mean(values * values, axis=-1, keepdims=True) + eps)
    normed = (values * scale_one * norm_gain).astype(jnp.bfloat16)
    gate_pre = project(normed, gate_proj)
    inner = project(normed, input_proj)
    rim = from_behind(inner[:, width - (taps_count - 1) :], "seq", 1)
    extended = jnp.concatenate([rim, inner], axis=1)
    conv = jnp.zeros_like(inner) + conv_bias
    for lag in range(taps_count):
        start = taps_count - 1 - lag
        conv = conv + conv_taps[lag] * extended[:, start : start + width]
    mixed = conv.astype(jnp.bfloat16)
    mixed_full = mixed.astype(jnp.float32)
    rate = jax.nn.sigmoid(project(mixed, rate_proj) + rate_bias)
    entry = jax.nn.sigmoid(project(mixed, entry_proj) + entry_bias)
    logit = decay_logit.astype(jnp.float32)
    log_decay = -lru_scale * jax.nn.softplus(-logit) * rate
    decay = jnp.exp(mask * log_decay)
    root = jnp.sqrt(-jnp.expm1(2.0 * log_decay))
    drive = mask * root * entry * mixed_full
    reach, local = lax.associative_scan(link, (decay, drive), axis=1)
    unit_state = (jnp.ones_like(reach[:, -1]), jnp.zeros_like(local[:, -1]))
    start_state = entering((reach[:, -1], local[:, -1]), "seq", link, unit_state)[1]
    states = local + reach * start_state[:, None]
    gated = (states * jax.nn.gelu(gate_pre)).astype(jnp.bfloat16)
    first = values + project(gated, out_proj)
    scale_two = lax.rsqrt(jnp.mean(first * first, axis=-1, keepdims=True) + eps)
    normed_two = (first * scale_two * ffn_gain).astype(jnp.bfloat16)
    up_pre = project(normed_two, ffn_gate)
    mix_pre = project(normed_two, ffn_up)
    hidden = (jax.nn.gelu(up_pre) * mix_pre).astype(jnp.bfloat16)
    block_out = mask * (first + project(hidden, ffn_down))
    saved = (
        values,
        scale_one,
        normed,
        gate_pre,
        extended,
        mixed,
        mixed_full,
        rate,
        entry,
        log_decay,
        decay,
        root,
        start_state,
        states,
        gated,
        first,
        scale_two,
        normed_two,
        up_pre,
        mix_pre,
        hidden,
    )
    return (block_out, saved)


def backward_part(cotangent, mask, weights, saved):
    (
        gate_proj,
        input_proj,
        rate_proj,
        entry_proj,
        out_proj,
        ffn_gate,
        ffn_up,
        ffn_down,
        norm_gain,
        ffn_gain,
        conv_taps,
        conv_bias,
        rate_bias,
        entry_bias,
        decay_logit,
    ) = weights
    (
        values,
        scale_one,
        normed,
        gate_pre,
        extended,
        mixed,
        mixed_full,
        rate,
        entry,
        log_decay,
        decay,
        root,
        start_state,
        states,
        gated,
        first,
        scale_two,
        normed_two,
        up_pre,
        mix_pre,
        hidden,
    ) = saved
    width = values.shape[1]
    taps_count = conv_taps.shape[0]
    cot_full = mask * cotangent.astype(jnp.float32)
    cot_low = cot_full.astype(jnp.bfloat16)
    grad_ffn_down = outer_sum(hidden, cot_low)
    d_hidden = project_back(cot_low, ffn_down)
    gelu_up, gelu_pull = jax.vjp(jax.nn.gelu, up_pre)
    d_up = gelu_pull(d_hidden * mix_pre)[0].astype(jnp.bfloat16)
    d_mix = (d_hidden * gelu_up).astype(jnp.bfloat16)
    grad_ffn_gate = outer_sum(normed_two, d_up)
    grad_ffn_up = outer_sum(normed_two, d_mix)
    d_normed_two = project_back(d_up, ffn_gate) + project_back(d_mix, ffn_up)
    back_two, grad_ffn_gain = norm_back(first, scale_two, ffn_gain, d_normed_two)
    d_first = cot_full + back_two
    d_first_low = d_first.astype(jnp.bfloat16)
    grad_out_proj = outer_sum(gated, d_first_low)
    d_gated = project_back(d_first_low, out_proj)
    gate, gate_pull = jax.vjp(jax.nn.gelu, gate_pre)
    d_states = d_gated * gate
    d_gate_pre = gate_pull(d_gated * states)[0].astype(jnp.bfloat16)
    following = jnp.concatenate([decay[:, 1:], jnp.ones_like(decay[:, :1])], axis=1)
    reach_back, local_back = lax.associative_scan(link, (following, d_states), reverse=True, axis=1)
    unit_grad = (jnp.ones_like(decay[:, 0]), jnp.zeros_like(decay[:, 0]))
    end_grad = carried_in(
        (decay[:, 0] * reach_back[:, 0], decay[:, 0] * local_back[:, 0]), "seq", link, unit_grad
    )[1]
    carried = local_back + reach_back * end_grad[:, None]
    previous = jnp.concatenate([start_state[:, None], states[:, :-1]], axis=1)
    masked_grad = mask * carried
    d_log = (
        masked_grad * previous * decay
        - masked_grad * entry * mixed_full * jnp.exp(2.0 * log_decay) / root
    )
    logit = decay_logit.astype(jnp.float32)
    grad_decay_logit = jnp.sum(lru_scale * d_log * rate * jax.nn.sigmoid(-logit), axis=(0, 1))
    d_rate_pre = -lru_scale * jax.nn.softplus(-logit) * d_log * rate * (1.0 - rate)
    d_entry_pre = masked_grad * root * mixed_full * entry * (1.0 - entry)
    grad_rate_bias = jnp.sum(d_rate_pre, axis=(0, 1))
    grad_entry_bias = jnp.sum(d_entry_pre, axis=(0, 1))
    rate_low = d_rate_pre.astype(jnp.bfloat16)
    entry_low = d_entry_pre.astype(jnp.bfloat16)
    grad_rate_proj = outer_sum(mixed, rate_low)
    grad_entry_proj = outer_sum(mixed, entry_low)
    d_mixed = (
        masked_grad * root * entry
        + project_back(rate_low, rate_proj)
        + project_back(entry_low, entry_proj)
    )
    grad_conv_bias = jnp.sum(d_mixed, axis=(0, 1))
    tap_grads = []
    for lag in range(taps_count):
        start = taps_count - 1 - lag
        tap_grads.append(jnp.sum(d_mixed * extended[:, start : start + width], axis=(0, 1)))
    grad_conv_taps = jnp.stack(tap_grads, axis=0)
    rim_back = from_behind(for_sending(d_mixed[:, : taps_count - 1]), "seq", -1)
    later = jnp.concatenate([d_mixed, rim_back], axis=1)
    d_inner = jnp.zeros_like(d_mixed)
    for lag in range(taps_count):
        d_inner = d_inner + conv_taps[lag] * later[:, lag : lag + width]
    d_inner = d_inner.astype(jnp.bfloat16)
    grad_input_proj = outer_sum(normed, d_inner)
    grad_gate_proj = outer_sum(normed, d_gate_pre)
    d_normed = project_back(d_gate_pre, gate_proj) + project_back(d_inner, input_proj)
    back_one, grad_norm_gain = norm_back(values, scale_one, norm_gain, d_normed)
    token_grad = d_first + back_one
    grads = (
        grad_gate_proj,
        grad_input_proj,
        grad_rate_proj,
        grad_entry_proj,
        grad_out_proj,
        grad_ffn_gate,
        grad_ffn_up,
        grad_ffn_down,
        grad_norm_gain,
        grad_ffn_gain,
        grad_conv_taps,
        grad_conv_bias,
        grad_rate_bias,
        grad_entry_bias,
        grad_decay_logit,
    )
    return (token_grad, grads)


def reduce_grads(totals):
    shaped = []
    for index, item in enumerate(totals):
        if index == 10:
            item = item.T
        if item.ndim == 1:
            item = item[:, None]
        shaped.append(item[None])
    spread = (
        lax.all_to_all(
            shaped[0].astype(jnp.bfloat16), "seq", split_axis=1, concat_axis=0, tiled=True
        ).astype(jnp.float32),
        lax.all_to_all(
            shaped[1].astype(jnp.bfloat16), "seq", split_axis=1, concat_axis=0, tiled=True
        ).astype(jnp.float32),
        lax.all_to_all(
            shaped[2].astype(jnp.bfloat16), "seq", split_axis=1, concat_axis=0, tiled=True
        ).astype(jnp.float32),
        lax.all_to_all(
            shaped[3].astype(jnp.bfloat16), "seq", split_axis=1, concat_axis=0, tiled=True
        ).astype(jnp.float32),
        lax.all_to_all(
            shaped[4].astype(jnp.bfloat16), "seq", split_axis=1, concat_axis=0, tiled=True
        ).astype(jnp.float32),
        lax.all_to_all(
            shaped[5].astype(jnp.bfloat16), "seq", split_axis=1, concat_axis=0, tiled=True
        ).astype(jnp.float32),
        lax.all_to_all(
            shaped[6].astype(jnp.bfloat16), "seq", split_axis=1, concat_axis=0, tiled=True
        ).astype(jnp.float32),
        lax.all_to_all(
            shaped[7].astype(jnp.bfloat16), "seq", split_axis=1, concat_axis=0, tiled=True
        ).astype(jnp.float32),
        lax.all_to_all(
            shaped[8].astype(jnp.bfloat16), "seq", split_axis=1, concat_axis=0, tiled=True
        ).astype(jnp.float32),
        lax.all_to_all(
            shaped[9].astype(jnp.bfloat16), "seq", split_axis=1, concat_axis=0, tiled=True
        ).astype(jnp.float32),
        lax.all_to_all(for_sending(shaped[10]), "seq", split_axis=1, concat_axis=0, tiled=True),
        lax.all_to_all(for_sending(shaped[11]), "seq", split_axis=1, concat_axis=0, tiled=True),
        lax.all_to_all(for_sending(shaped[12]), "seq", split_axis=1, concat_axis=0, tiled=True),
        lax.all_to_all(for_sending(shaped[13]), "seq", split_axis=1, concat_axis=0, tiled=True),
        lax.all_to_all(for_sending(shaped[14]), "seq", split_axis=1, concat_axis=0, tiled=True),
    )
    folded = [jnp.sum(piece, axis=0) for piece in spread]
    summed = (
        lax.psum_scatter(
            folded[0].astype(jnp.bfloat16), "batch", scatter_dimension=0, tiled=True
        ).astype(jnp.float32),
        lax.psum_scatter(
            folded[1].astype(jnp.bfloat16), "batch", scatter_dimension=0, tiled=True
        ).astype(jnp.float32),
        lax.psum_scatter(
            folded[2].astype(jnp.bfloat16), "batch", scatter_dimension=0, tiled=True
        ).astype(jnp.float32),
        lax.psum_scatter(
            folded[3].astype(jnp.bfloat16), "batch", scatter_dimension=0, tiled=True
        ).astype(jnp.float32),
        lax.psum_scatter(
            folded[4].astype(jnp.bfloat16), "batch", scatter_dimension=0, tiled=True
        ).astype(jnp.float32),
        lax.psum_scatter(
            folded[5].astype(jnp.bfloat16), "batch", scatter_dimension=0, tiled=True
        ).astype(jnp.float32),
        lax.psum_scatter(
            folded[6].astype(jnp.bfloat16), "batch", scatter_dimension=0, tiled=True
        ).astype(jnp.float32),
        lax.psum_scatter(
            folded[7].astype(jnp.bfloat16), "batch", scatter_dimension=0, tiled=True
        ).astype(jnp.float32),
        lax.psum_scatter(
            folded[8].astype(jnp.bfloat16), "batch", scatter_dimension=0, tiled=True
        ).astype(jnp.float32),
        lax.psum_scatter(
            folded[9].astype(jnp.bfloat16), "batch", scatter_dimension=0, tiled=True
        ).astype(jnp.float32),
        lax.psum_scatter(
            folded[10].astype(jnp.bfloat16), "batch", scatter_dimension=0, tiled=True
        ).astype(jnp.float32),
        lax.psum_scatter(
            folded[11].astype(jnp.bfloat16), "batch", scatter_dimension=0, tiled=True
        ).astype(jnp.float32),
        lax.psum_scatter(
            folded[12].astype(jnp.bfloat16), "batch", scatter_dimension=0, tiled=True
        ).astype(jnp.float32),
        lax.psum_scatter(
            folded[13].astype(jnp.bfloat16), "batch", scatter_dimension=0, tiled=True
        ).astype(jnp.float32),
        lax.psum_scatter(
            folded[14].astype(jnp.bfloat16), "batch", scatter_dimension=0, tiled=True
        ).astype(jnp.float32),
    )
    result = []
    for index, item in enumerate(summed):
        if index == 10:
            result.append(item.T)
        elif totals[index].ndim == 1:
            result.append(item[:, 0])
        else:
            result.append(item)
    return tuple(result)


def per_device(
    tokens,
    cotangent,
    lengths,
    gate_proj,
    input_proj,
    rate_proj,
    entry_proj,
    out_proj,
    ffn_gate,
    ffn_up,
    ffn_down,
    norm_gain,
    ffn_gain,
    conv_taps,
    conv_bias,
    rate_bias,
    entry_bias,
    decay_logit,
):
    shards = (
        gate_proj,
        input_proj,
        rate_proj,
        entry_proj,
        out_proj,
        ffn_gate,
        ffn_up,
        ffn_down,
        norm_gain,
        ffn_gain,
        conv_taps,
        conv_bias,
        rate_bias,
        entry_bias,
        decay_logit,
    )
    rows, width = (tokens.shape[0], tokens.shape[1])
    place = lax.axis_index("seq") * width + lax.iota(jnp.int32, width)
    mask_all = (place[None, :] < lengths[:, None]).astype(jnp.float32)[:, :, None]
    group = rows // MICRO
    totals = None
    block_parts = []
    grad_parts = []
    for part in range(MICRO):
        lower = part * group
        mask = mask_all[lower : lower + group]
        weights = fetch(shards)
        block_out, saved = forward_part(tokens[lower : lower + group], mask, weights)
        weights = fetch(shards)
        token_grad, grads = backward_part(cotangent[lower : lower + group], mask, weights, saved)
        totals = grads if part == 0 else jax.tree.map(jnp.add, totals, grads)
        block_parts.append(block_out)
        grad_parts.append(token_grad)
    summed = reduce_grads(totals)
    return (jnp.concatenate(block_parts, axis=0), jnp.concatenate(grad_parts, axis=0)) + summed


F32 = jnp.float32
BF16 = jnp.bfloat16
W = 512
PACK = 2 * W
SEGS = 8
CHUNK = 32
TALL = 64
LANES = 128
GELU_A = 0.7978845608028654
GELU_B = 0.044715
TAPS, CONV_BIAS, RATE_BIAS, ENTRY_BIAS, COEF, SIG = 0, 4, 5, 6, 7, 8


def dot(left, right):
    return lax.dot_general(left, right, (((1,), (0,)), ((), ())), preferred_element_type=F32)


def dot_back(left, right):
    return lax.dot_general(left, right, (((1,), (1,)), ((), ())), preferred_element_type=F32)


def dot_outer(left, right):
    return lax.dot_general(left, right, (((0,), (0,)), ((), ())), preferred_element_type=F32)


def rows_at(start, count=CHUNK):
    return pl.ds(pl.multiple_of(start, CHUNK), count)


def gelu_both(value):
    square = value * value
    inside = GELU_A * value * (1.0 + GELU_B * square)
    tanh = jnp.tanh(inside)
    half = 0.5 + 0.5 * tanh
    slope = half + 0.5 * value * (1.0 - tanh * tanh) * (GELU_A * (1.0 + 3.0 * GELU_B * square))
    return value * half, slope


def sigmoid(value):
    return 1.0 / (1.0 + jnp.exp(-value))


def one_less_exp(z, exp_z):
    series = 1.0 + z * (1 / 2 + z * (1 / 6 + z * (1 / 24 + z * (1 / 120 + z * (1 / 720)))))
    return jnp.where(z > -0.25, -z * series, 1.0 - exp_z)


def in_row(row, width, shape):
    return row + lax.broadcasted_iota(jnp.int32, shape, 0)


def each_chunk(batch, width, body, carry=0):
    per = width // CHUNK
    for b in range(batch):
        carry = lax.fori_loop(0, per, lambda i, c, b=b: body(b, i * CHUNK, b * width + i * CHUNK, c), carry)
    return carry


def each_tile(batch, width, tiles, body, carry=None):
    carries = []
    for t in range(tiles):
        kept = carry
        for b in range(batch):
            def one(i, c, t=t, b=b):
                return body(t, b, i * TALL, rows_at(b * width + i * TALL, TALL), slice(t * LANES, (t + 1) * LANES), c)
            kept = lax.fori_loop(0, width // TALL, one, 0 if kept is None else kept)
        carries.append(kept)
    return carries


def strided(b, width, step):
    return pl.ds(b * width + step, SEGS, stride=width // SEGS)


def lanes(t):
    return slice(t * LANES, (t + 1) * LANES)


def spread(ref, value):
    for t in range(ref.shape[0]):
        ref[t] = value[:, lanes(t)]


def tiled(tokens, block, index):
    return pl.BlockSpec((block // LANES, tokens, LANES), lambda j: (index(j), 0, 0))


def pair_cols(tile, second):
    block = lax.div(tile, W // LANES)
    return pl.ds(pl.multiple_of(tile * LANES + (block + second) * W, LANES), LANES)


def inverse_norm(value, depth):
    return lax.rsqrt(jnp.sum(value * value, axis=-1, keepdims=True) * (1.0 / depth) + eps)


def fold8(value):
    total = value[:8]
    for i in range(8, value.shape[0], 8):
        total = total + value[i : i + 8]
    return total


def ffn_kernel(batch, width, info_ref, first_ref, normed_ref, cot_ref, gain_ref, wu_ref, wd_ref,
               out_ref, dfirst_ref, dlow_ref, ggain_ref, grad_ref,
               low, tall, hid, acc, dn, pair, du, stage, dstage, sem):
    step = pl.program_id(0)
    tokens, depth = first_ref.shape
    n = grad_ref.shape[0]
    group, drows = wd_ref.shape[:2]
    wide = group * drows
    rows = depth // n
    nd, nw = n // group, hid.shape[1] // W
    tiles = W // LANES

    def block_out(j):
        return pltpu.make_async_copy(stage, grad_ref.at[:, pl.ds(pl.multiple_of(UPS_AT + j * rows, rows), rows)], sem.at[0])

    def down_out(k):
        return pltpu.make_async_copy(dstage, grad_ref.at[pl.ds(k * group, group), pl.ds(DOWN_AT, drows)], sem.at[1])

    @pl.when(step == 0)
    def _():
        def masked(b, spot, row, _):
            at = rows_at(row)
            value = cot_ref[at]
            valid = in_row(spot, width, value.shape) < info_ref[b]
            low[at] = jnp.where(valid, value.astype(F32), 0.0).astype(BF16)
            return 0
        each_chunk(batch, width, masked)

    @pl.when(step < nd)
    def _():
        total = dot_back(low[...], wd_ref[...].reshape(wide, depth))
        for t in range(wide // LANES):
            tall[jnp.minimum(step, nd - 1) * (wide // LANES) + t] = total[:, lanes(t)]

    @pl.when(jnp.logical_and(step >= nd, step < nd + nw))
    def _():
        j = jnp.clip(step - nd, 0, nw - 1)
        weights = wu_ref[...].reshape(depth, PACK)
        spread(pair, dot(normed_ref[...], weights))

        def gating(t, b, spot, at, cols, _):
            gate, slope = gelu_both(pair[t, at])
            mix, d = pair[tiles + t, at], tall[j * tiles + t, at]
            hid[at, pl.ds(pl.multiple_of(j * W + t * LANES, LANES), LANES)] = (gate * mix).astype(BF16)
            du[at, cols] = (d * mix * slope).astype(BF16)
            du[at, lanes(tiles + t)] = (d * gate).astype(BF16)
            return 0
        each_tile(batch, width, tiles, gating)
        more = dot_back(du[...], weights)

        @pl.when(j == 0)
        def _():
            dn[...] = more

        @pl.when(j > 0)
        def _():
            dn[...] += more
        value = dot_outer(normed_ref[...], du[...]).astype(BF16).reshape(n, rows, PACK)
        pl.when(j > 0)(lambda: block_out(0).wait())
        stage[...] = value
        block_out(j).start()

    @pl.when(step >= nd + nw)
    def _():
        k = jnp.clip(step - nd - nw, 0, nd - 1)
        block = hid[:, pl.ds(pl.multiple_of(k * wide, wide), wide)]
        more = dot(block, wd_ref[...].reshape(wide, depth))

        @pl.when(k == 0)
        def _():
            acc[...] = more

        @pl.when(k > 0)
        def _():
            acc[...] += more
        value = dot_outer(block, low[...]).astype(BF16).reshape(group, drows, depth)
        pl.when(k > 0)(lambda: down_out(0).wait())
        dstage[...] = value
        down_out(k).start()

    @pl.when(step == pl.num_programs(0) - 1)
    def _():
        def finish(b, spot, row, total):
            at = rows_at(row)
            first, cot = first_ref[at], low[at].astype(F32)
            valid = in_row(spot, width, first.shape) < info_ref[b]
            out_ref[at] = jnp.where(valid, first + acc[at], 0.0)
            grad = dn[at]
            scale = inverse_norm(first, depth)
            weighted = grad * gain_ref[:1]
            mean = jnp.sum(weighted * first, axis=-1, keepdims=True) * (1.0 / depth)
            back = cot + scale * weighted - first * (scale * scale * scale * mean)
            for t in range(depth // LANES):
                dfirst_ref[t, at] = back[:, lanes(t)]
            dlow_ref[at] = back.astype(BF16)
            return total + fold8(grad * first * scale)
        ggain_ref[...] = each_chunk(batch, width, finish, jnp.zeros((8, depth), F32))
        block_out(0).wait()
        down_out(0).wait()


def feed_forward(info, first, normed_two, cot, gain, packed, f, batch):
    tokens, depth = first.shape
    width = tokens // batch
    n = packed.shape[0]
    rows, drows = depth // n, f // n
    group = 8
    wide = group * drows
    nd, nw = f // wide, f // W
    full = lambda shape: pl.BlockSpec(shape, lambda j: (0,) * len(shape))
    clamp = lambda j, low, count: jnp.clip(j - low, 0, count - 1)

    def down_block(j):
        return (jnp.where(j < nd, jnp.minimum(j, nd - 1), clamp(j, nd + nw, nd)), DOWN_AT // drows, 0)
    vm = pltpu.VMEM
    S = jax.ShapeDtypeStruct
    return pl.pallas_call(
        functools.partial(ffn_kernel, batch, width),
        grid=(nd + nw + nd,),
        in_specs=[pl.BlockSpec(memory_space=pltpu.SMEM), full(first.shape), full(normed_two.shape), full(cot.shape),
                  full(gain.shape), pl.BlockSpec((n, rows, PACK), lambda j: (0, UPS_AT // rows + clamp(j, nd, nw), 0)),
                  pl.BlockSpec((group, drows, depth), down_block)],
        out_specs=[full((tokens, depth)), full((depth // LANES, tokens, LANES)), full((tokens, depth)), full((8, depth)),
                   pl.BlockSpec(memory_space=pl.ANY)],
        out_shape=[S((tokens, depth), F32), S((depth // LANES, tokens, LANES), F32), S((tokens, depth), BF16),
                   S((8, depth), F32), S((n, FFN_ROWS, PACK), BF16)],
        scratch_shapes=[vm((tokens, depth), BF16), vm((f // LANES, tokens, LANES), F32), vm((tokens, f), BF16),
                        vm((tokens, depth), F32), vm((tokens, depth), F32), vm((PACK // LANES, tokens, LANES), F32),
                        vm((tokens, PACK), BF16), vm((n, rows, PACK), BF16), vm((group, drows, depth), BF16),
                        pltpu.SemaphoreType.DMA((2,))],
        compiler_params=pltpu.CompilerParams(vmem_limit_bytes=60 << 20),
    )(info, first, normed_two, cot, gain, packed, packed)


MESH = pl.DeviceIdType.MESH
ROUTES = (("z", "x", "y"), ("z", "y", "x"), ("x", "z", "y"), ("y", "z", "x"))
ZN = 4
STG = 4
SEM = pltpu.SemaphoreType.DMA


def place():
    s = lax.axis_index("seq")
    return lax.rem(s, 2), lax.rem(lax.div(s, 2), 2), lax.div(s, 4), lax.axis_index("batch")


def flip(value, by):
    return 1 - value if by else value


def seq_of(y, x, c):
    return (y * 2 + x) * 2 + c


def far(z, j):
    if j == ZN - 1:
        return z
    found = None
    for here in range(ZN):
        others = sorted((q for q in range(ZN) if q != here), key=lambda q: (-abs(q - here), q))
        found = jnp.int32(others[j]) if found is None else jnp.where(z == here, others[j], found)
    return found


class Links:
    def __init__(self):
        self.c, self.x, self.y, self.z = c, x, y, z = place()
        self.beside = {
            "x": (seq_of(y, 1 - x, c), z),
            "y": (seq_of(1 - y, x, c), z),
            "up": (seq_of(y, x, c), z + 1),
            "dn": (seq_of(y, x, c), z - 1),
            "core": (seq_of(y, x, 1 - c), z),
        }
        self.spots = [far(z, j) for j in range(ZN)]
        self.above, self.below = z < ZN - 1, z > 0

    def slot(self, dx, dy, z, core):
        return seq_of(flip(self.y, dy), flip(self.x, dx), core) * ZN + z

    def copy(self, src, dst, send, recv, d):
        return pltpu.make_async_remote_copy(src, dst, send, recv, device_id=self.beside[d], device_id_type=MESH)


def greet(links, swap):
    bar = pltpu.get_barrier_semaphore()
    count = 0
    if swap is not None:
        count = swap.n - 1
        for k in range(1, swap.n):
            pl.semaphore_signal(bar, inc=1, device_id=swap.peer(k), device_id_type=MESH)
    if links is not None:
        def signal(d):
            pl.semaphore_signal(bar, inc=1, device_id=links.beside[d], device_id_type=MESH)
        if swap is None:
            count = 3
            for d in ("x", "y", "core"):
                signal(d)
        pl.when(links.above)(lambda: signal("up"))
        pl.when(links.below)(lambda: signal("dn"))
        count = count + links.above.astype(jnp.int32) + links.below.astype(jnp.int32)
    pl.semaphore_wait(bar, count)


class Exchange:
    def __init__(self, n, rows, land, send, recv, own):
        self.n, self.rows, self.land, self.send, self.recv, self.own = n, rows, land, send, recv, own
        self.me, self.z = lax.axis_index("seq"), lax.axis_index("batch")

    @staticmethod
    def scratch(n, shape):
        return [pltpu.VMEM(shape, F32), pltpu.VMEM((n,) + shape, F32), SEM((n,)), SEM((n,)), SEM]

    def peer(self, k):
        return (lax.rem(self.me + k, self.n), self.z)

    def copies(self):
        return [
            pltpu.make_async_remote_copy(self.rows, self.land.at[self.me], self.send.at[k], self.recv.at[k],
                                         device_id=self.peer(k), device_id_type=MESH)
            for k in range(1, self.n)
        ]

    def mine(self):
        return pltpu.make_async_copy(self.rows, self.land.at[self.me], self.own)

    def begin(self):
        self.mine().start()
        for copy in self.copies():
            copy.start()

    def finish(self):
        self.mine().wait()
        for copy in self.copies():
            copy.wait()


def onward(order, dx, dy, same):
    off = {"x": dx, "y": dy, "z": 0 if same else 1}
    return [
        d for i, d in enumerate(order)
        if not any(off[e] for e in order[i + 1 :]) and not (d != "z" and off[d])
    ]


def arrival(order, dx, dy, same):
    off = {"x": dx, "y": dy, "z": 0 if same else 1}
    return [d for d in order if off[d]][-1]


def blocks(parts):
    found = [
        (dx + dy + ZN - 1 - j, r, dx, dy, j)
        for dx in range(2) for dy in range(2) for j in range(ZN) for r in range(len(parts))
    ]
    return found


class Gather:
    def __init__(self, parts, ins, outs, send, recv, csend, crecv, lsem):
        self.parts, self.ins, self.outs = parts, ins, outs
        self.send, self.recv, self.csend, self.crecv, self.lsem = send, recv, csend, crecv, lsem
        self.links = Links()
        self.events = blocks(parts)

    @staticmethod
    def scratch(parts):
        n = len(parts)
        return [SEM((n, 4, 4, ZN)), SEM((n, 4, ZN)), SEM((n, 4, ZN)), SEM((n, 4, ZN)), SEM((n,))]

    def window(self, r):
        return pl.ds(self.parts[r][2], self.parts[r][3])

    def dst(self, r, dx, dy, zs):
        return self.outs[self.parts[r][1]].at[self.links.slot(dx, dy, zs, self.links.c), self.window(r)]

    def src(self, r, dx, dy, zs, own):
        return self.ins[self.parts[r][0]].at[self.window(r)] if own else self.dst(r, dx, dy, zs)

    def hop(self, r, dx, dy, zs, d, own):
        to = (1 if d == "x" else dx) * 2 + (1 if d == "y" else dy)
        which = ("x", "y", "up", "dn").index(d)
        return self.links.copy(self.src(r, dx, dy, zs, own), self.dst(r, dx, dy, zs),
                               self.send.at[r, which, dx * 2 + dy, zs], self.recv.at[r, to, zs], d)

    def across(self, r, dx, dy, zs, own):
        return self.links.copy(self.src(r, dx, dy, zs, own), self.dst(r, dx, dy, zs),
                               self.csend.at[r, dx * 2 + dy, zs], self.crecv.at[r, dx * 2 + dy, zs], "core")

    def hops(self, r, dx, dy, j, act):
        links, zs = self.links, self.links.spots[j]
        z, same = links.z, j == ZN - 1
        own = same and not dx and not dy
        for d in onward(ROUTES[self.parts[r][4]], dx, dy, same):
            if d != "z":
                act(self.hop(r, dx, dy, zs, d, own))
                continue
            up = links.above if same else jnp.logical_and(z > zs, links.above)
            down = links.below if same else jnp.logical_and(z < zs, links.below)
            pl.when(up)(lambda: act(self.hop(r, dx, dy, zs, "up", own)))
            pl.when(down)(lambda: act(self.hop(r, dx, dy, zs, "dn", own)))

    def forward(self, event):
        _, r, dx, dy, j = event
        zs, own = self.links.spots[j], j == ZN - 1 and not dx and not dy
        if not own:
            self.links.copy(self.dst(r, dx, dy, zs), self.dst(r, dx, dy, zs), self.send.at[r, 0, 0, 0],
                            self.recv.at[r, dx * 2 + dy, zs], "core").wait_recv()
        self.hops(r, dx, dy, j, lambda copy: copy.start())
        self.across(r, dx, dy, zs, own).start()
        if own:
            self.local(r).start()

    def local(self, r):
        return pltpu.make_async_copy(self.ins[self.parts[r][0]].at[self.window(r)],
                                     self.dst(r, 0, 0, self.links.z), self.lsem.at[r])

    def arrived(self, parts):
        for _, r, dx, dy, j in self.events:
            if r in parts:
                own = j == ZN - 1 and not dx and not dy
                self.across(r, dx, dy, self.links.spots[j], own).wait_recv()
                if own:
                    self.local(r).wait()

    def sent(self):
        for _, r, dx, dy, j in self.events:
            own = j == ZN - 1 and not dx and not dy
            self.hops(r, dx, dy, j, lambda copy: copy.wait_send())
            self.across(r, dx, dy, self.links.spots[j], own).wait_send()


def layout(order):
    base, count = {}, 0
    for i, d in enumerate(order):
        base[d] = count
        free = 1
        for e in order[:i]:
            free *= ZN if e == "z" else 2
        count += free * ((ZN + 1) if d == "z" else 1)
    return base, count


class Scatter:
    def __init__(self, parts, order, ins, out, sib, stage, ring, fin, csend, crecv, lsem, send, fsem, *rest):
        self.parts, self.ins, self.out, self.sib = parts, ins, out, sib
        self.stage, self.ring, self.fin = stage, ring, fin
        self.ahead, self.slots = stage.shape[0], ring.shape[0]
        self.csend, self.crecv, self.lsem, self.send, self.fsem = csend, crecv, lsem, send, fsem
        self.bufs, self.recv = rest[: len(parts)], rest[len(parts) :]
        self.links = Links()
        self.lay = [layout(ROUTES[part[3]]) for part in parts]
        rows = [part[2] for part in parts]
        self.starts = [sum(rows[:r]) for r in range(len(parts))]
        every = blocks(parts)
        self.events = [every[number] for number in order]
        self.in_slot, self.in_fin, self.finals = {}, {}, 0

    @staticmethod
    def buffers(parts):
        total = sum(part[2] for part in parts)
        S = jax.ShapeDtypeStruct
        return [S((total, PACK), jnp.float32), S((4 * ZN * total, PACK), jnp.bfloat16)]

    @staticmethod
    def scratch(parts, ahead, slots):
        n, most = len(parts), max(part[2] for part in parts)
        counts = [layout(ROUTES[part[3]])[1] for part in parts]
        return [pltpu.VMEM((ahead, 2, most, PACK), jnp.bfloat16), pltpu.VMEM((slots, most, PACK), jnp.bfloat16),
                pltpu.VMEM((2, most, PACK), jnp.float32), SEM((n,)), SEM((n, 4, ZN)), SEM((ahead, 2)), SEM((slots,)),
                SEM((2,))] + [
            pltpu.VMEM((count, part[2], PACK), jnp.bfloat16) for count, part in zip(counts, parts)
        ] + [SEM((count,)) for count in counts]

    def source(self, r, dx, dy, zd, core):
        which, start, rows, _ = self.parts[r]
        return self.ins[which].at[self.links.slot(dx, dy, zd, core), pl.ds(start, rows)]

    def sibling(self, r, dx, dy, zd):
        count = self.parts[r][2]
        start = 4 * ZN * self.starts[r] + ((dx * 2 + dy) * ZN + zd) * count
        return self.sib.at[pl.ds(pl.multiple_of(start, 16), count)]

    def child(self, r, d, dx, dy, zd):
        order = ROUTES[self.parts[r][3]]
        dim = d if d in "xy" else "z"
        index = 0
        for e in order[: order.index(dim)]:
            index = index * ZN + zd if e == "z" else index * 2 + (dx if e == "x" else dy)
        if dim == "z":
            index = index * (ZN + 1) + (zd if d == "up" else zd + 1)
        return self.lay[r][0][dim] + index

    def across(self, i):
        _, r, dx, dy, j = self.events[i]
        zd = self.links.spots[j]
        return self.links.copy(self.source(r, dx, dy, zd, 1 - self.links.c), self.sibling(r, dx, dy, zd),
                               self.csend.at[r], self.crecv.at[r, dx * 2 + dy, zd], "core")

    def begin(self):
        for i in range(len(self.events)):
            self.across(i).start()
        for i in range(self.ahead - 1):
            self.prefetch(i)

    def loads(self, i):
        _, r, dx, dy, j = self.events[i]
        zd, s, count = self.links.spots[j], i % self.ahead, self.parts[r][2]
        return [
            pltpu.make_async_copy(ref, self.stage.at[s, k, pl.ds(0, count)], self.lsem.at[s, k])
            for k, ref in enumerate((self.source(r, dx, dy, zd, self.links.c), self.sibling(r, dx, dy, zd)))
        ]

    def prefetch(self, i):
        own, other = self.loads(i)
        own.start()
        self.across(i).wait_recv()
        other.start()

    def terms(self, i):
        _, r, dx, dy, j = self.events[i]
        same = j == ZN - 1
        kids = onward(ROUTES[self.parts[r][3]], dx, dy, same)
        z, zd = self.links.z, self.links.spots[j]
        found = [(self.child(r, d, dx, dy, zd), None) for d in kids if d != "z"]
        if "z" in kids:
            up, down = self.child(r, "up", dx, dy, zd), self.child(r, "dn", dx, dy, zd)
            if same:
                found += [(up, self.links.above), (down, self.links.below)]
            else:
                found.append((jnp.where(z > zd, up, down), jnp.logical_and(self.links.above, self.links.below)))
        return found

    def hop(self, i, d):
        _, r, dx, dy, j = self.events[i]
        zd, q = self.links.spots[j], i % self.slots
        came = {"x": "x", "y": "y", "up": "dn", "dn": "up"}[d]
        at = self.child(r, came, 0 if d == "x" else dx, 0 if d == "y" else dy, zd)
        return self.links.copy(self.ring.at[q, pl.ds(0, self.parts[r][2])], self.bufs[r].at[at],
                               self.send.at[q], self.recv[r].at[at], d)

    def result(self, i, slot):
        r = self.events[i][1]
        count = self.parts[r][2]
        return pltpu.make_async_copy(self.fin.at[slot, pl.ds(0, count)], self.out.at[pl.ds(self.starts[r], count)],
                                     self.fsem.at[slot])

    def step(self, i):
        _, r, dx, dy, j = self.events[i]
        zd, z, s, q = self.links.spots[j], self.links.z, i % self.ahead, i % self.slots
        if i + self.ahead - 1 < len(self.events):
            self.prefetch(i + self.ahead - 1)
        leaves = j != ZN - 1 or dx or dy
        if leaves:
            if q in self.in_slot:
                self.hop(self.in_slot[q], "x").wait_send()
            self.in_slot[q] = i
        else:
            slot = self.finals % 2
            if slot in self.in_fin:
                self.result(self.in_fin[slot], slot).wait()
            self.in_fin[slot] = i
            self.finals += 1
        for load in self.loads(i):
            load.wait()
        terms = self.terms(i)
        for at, cond in terms:
            slab = self.bufs[r].at[at]
            arrived = self.links.copy(slab, slab, self.send.at[0], self.recv[r].at[at], "core")
            if cond is None:
                arrived.wait_recv()
            else:
                pl.when(cond)(arrived.wait_recv)

        def body(k, _):
            rows = pl.ds(pl.multiple_of(k * 16, 16), 16)
            total = self.stage[s, 0, rows].astype(jnp.float32) + self.stage[s, 1, rows].astype(jnp.float32)
            for at, cond in terms:
                more = self.bufs[r][at, rows].astype(jnp.float32)
                total = total + (more if cond is None else jnp.where(cond, more, 0.0))
            if leaves:
                self.ring[q, rows] = total.astype(jnp.bfloat16)
            else:
                self.fin[slot, rows] = total
            return 0
        lax.fori_loop(0, self.parts[r][2] // 16, body, 0)
        if not leaves:
            self.result(i, slot).start()
            return
        d = arrival(ROUTES[self.parts[r][3]], dx, dy, j == ZN - 1)
        if d == "z":
            pl.when(zd > z)(lambda: self.hop(i, "up").start())
            pl.when(zd < z)(lambda: self.hop(i, "dn").start())
        else:
            self.hop(i, d).start()

    def finish(self):
        for i in self.in_slot.values():
            self.hop(i, "x").wait_send()
        for slot, i in self.in_fin.items():
            self.result(i, slot).wait()
        for r, part in enumerate(self.parts):
            whole = self.sib.at[pl.ds(4 * ZN * self.starts[r], 4 * ZN * part[2])]
            self.links.copy(whole, whole, self.csend.at[r], self.crecv.at[r, 0, 0], "core").wait_send()


def scatter(parts, order, ins):
    n = len(ins)

    def kernel(*refs):
        job = Scatter(parts, order, refs[:n], *refs[n:])
        greet(job.links, None)
        job.begin()
        for i in range(len(job.events)):
            job.step(i)
        job.finish()
    anywhere = pl.BlockSpec(memory_space=pl.ANY)
    outs = Scatter.buffers(parts)
    return pl.pallas_call(
        kernel,
        out_shape=outs,
        in_specs=[anywhere] * n,
        out_specs=[anywhere] * len(outs),
        scratch_shapes=Scatter.scratch(parts, 4, 24),
        compiler_params=pltpu.CompilerParams(collective_id=2, has_side_effects=True, vmem_limit_bytes=60 << 20),
    )(*ins)[0]


class Sends:
    def __init__(self, sems):
        self.sems, self.used = sems, []

    def add(self, src, dst):
        copy = pltpu.make_async_copy(src, dst, self.sems.at[len(self.used)])
        self.used.append(copy)
        return copy

    def finish(self):
        for copy in self.used:
            copy.wait()


def undeal(lines, n, count):
    length = n * count
    spot = lax.broadcasted_iota(jnp.int32, (LANES, length), 1)
    row = lax.broadcasted_iota(jnp.int32, (LANES, length), 0)
    pick = jnp.where(lax.rem(spot, count) == row, 1.0, 0.0).astype(BF16)
    lane = lax.broadcasted_iota(jnp.int32, (n, length), 1)
    owner = lax.broadcasted_iota(jnp.int32, (n, length), 0)
    own = jnp.logical_and(lane >= owner * count, lane < (owner + 1) * count)
    return jnp.sum(jnp.where(own, dot(lines, pick), 0.0), axis=0, keepdims=True)


def softplus(value):
    small = jnp.exp(-jnp.abs(value))
    series = small * (1.0 - small * (1 / 2 - small * (1 / 3 - small * (1 / 4 - small * (1 / 5 - small * (1 / 6))))))
    return jnp.maximum(value, 0.0) + jnp.where(small < 0.02, series, jnp.log(1.0 + small))


FORWARD_OUTS = 13
GATHER_PARTS = ((0, 0, 0, 64, 0), (0, 0, 64, 80, 1), (0, 0, 144, 80, 2), (0, 0, 224, 80, 3),
                (1, 1, 0, 64, 0), (1, 1, 64, 80, 1), (1, 1, 144, 64, 2), (1, 1, 208, 80, 3))
REC_PARTS = (0, 1, 2, 3)
FORWARD_PLAN = (
    (24, 25, 26, 27, 17, 9, 57, 18, 10, 88, 81, 1, 16, 8, 89, 90, 41, 91, 49, 59, 19, 43, 11, 0, 65, 51, 58, 72, 120, 48, 74, 82, 3, 121, 66, 80, 28, 122, 33, 56, 2, 83, 42, 30, 113, 31, 35, 67, 29, 97, 75, 64, 34, 115, 123, 112, 40, 22, 94, 60, 114, 98, 23, 63, 20, 95, 92, 21, 105, 106, 104, 32, 15, 61, 107, 50, 96, 73, 99, 14),
    (12,),
    (55,),
    (),
    (13,),
    (52,),
    (86,),
    (),
    (6,),
    (47,),
    (),
    (53, 4, 44, 76),
    (5,),
    (85,),
    (7, 79, 108, 111, 126, 54, 117, 125, 62, 38, 87, 78, 124, 84),
    (37, 36, 77, 45),
    (),
    (119, 68),
    (69, 39),
    (46,),
    (70, 118, 116, 71, 109, 127, 93, 102, 100, 103, 101, 110),
)


def forward_kernel(batch, width, n_seq, info_ref, x_ref, rim_ref, lines_ref, *refs):
    shards, refs = refs[:8], refs[8:]
    outs, refs = refs[:FORWARD_OUTS], refs[FORWARD_OUTS:]
    (gate_o, inner_o, mixed_o, normed_o, rate_o, entry_o, decay_o, states_o, pseg_o, sstart_o, all_o,
     gated_o, first_o) = outs
    normed2_o, vec_o, gain_o, gain2_o, weights, ffn_weights = refs[:6]
    (ext, gate, inner, mixed, rate, entry, decay, drive, states, pseg, hseg, sstart, gated, first, normed2,
     vec_ref, gain_ref, gain2_ref, small, wbuf, shard_ref, ffn_shard_ref, sems, wsem, psem) = refs[6:31]
    swap = Exchange(n_seq, *refs[31:36])
    job = Gather(GATHER_PARTS, [shard_ref, ffn_shard_ref], [weights, ffn_weights], *refs[36:])
    step = pl.program_id(0)
    tokens, depth = x_ref.shape
    r = mixed.shape[1]
    parts, tiles = r // W, W // LANES
    step = step - 1
    steps = 3 * parts + 1
    span = width + 8
    n = weights.shape[0]
    rows, rrows = depth // n, r // n

    def pump(half, low, high):
        for s in range(low, high):
            numbers = FORWARD_PLAN[1 + 2 * s + half]
            if numbers:
                @pl.when(step == s)
                def _():
                    for number in numbers:
                        job.forward(job.events[number])

    def pack():
        gate_w, input_w, rate_w, entry_w, out_w, ffn_gate_w, ffn_up_w, ffn_down_w = shards
        moves = ([], [])
        for which, one, two, base in ((0, rate_w, entry_w, GATES_AT), (0, gate_w, input_w, IN_AT), (1, ffn_gate_w, ffn_up_w, UPS_AT)):
            count, length = one.shape
            to = (shard_ref, ffn_shard_ref)[which]
            for j in range(length // W):
                for half, src in enumerate((one, two)):
                    moves[which].append((src.at[:, pl.ds(j * W, W)], to.at[pl.ds(base + j * count, count), pl.ds(half * W, W)]))
        moves[0].append((out_w, shard_ref.at[pl.ds(OUT_AT, rrows)]))
        moves[0].append((lines_ref, shard_ref.at[pl.ds(REC_ROWS, SMALL_ROWS)]))
        moves[1].append((ffn_down_w, ffn_shard_ref.at[pl.ds(DOWN_AT, ffn_down_w.shape[0])]))
        copies, k = ([], []), 0
        for which in range(2):
            for src, dst in moves[which]:
                copies[which].append(pltpu.make_async_copy(src, dst, psem.at[k]))
                k += 1
        return copies

    blocks_at = [(IN_AT + j * rows, rows) for j in range(parts)] + [(GATES_AT + j * rrows, rrows) for j in range(parts)]
    blocks_at += [(OUT_AT, rrows)]

    def load(k):
        start, count = blocks_at[k]
        return pltpu.make_async_copy(weights.at[:, pl.ds(start, count)], wbuf.at[k % 2, :, pl.ds(0, count)], wsem.at[k % 2])

    def next_block(k):
        if k + 1 < len(blocks_at):
            load(k + 1).start()
        load(k).wait()
    sends = Sends(sems)
    branch_sends = [sends.add(gate, gate_o), sends.add(inner, inner_o), sends.add(mixed, mixed_o),
                    sends.add(ext.at[pl.ds(0, tokens)], normed_o)]
    gate_sends = [sends.add(rate, rate_o), sends.add(entry, entry_o), sends.add(decay, decay_o), sends.add(pseg, pseg_o)]
    state_sends = [sends.add(states, states_o), sends.add(sstart, sstart_o), sends.add(swap.land, all_o),
                   sends.add(gated, gated_o)]
    last_sends = [sends.add(first, first_o), sends.add(normed2, normed2_o)]
    vector_sends = [sends.add(vec_ref, vec_o), sends.add(gain_ref, gain_o), sends.add(gain2_ref, gain2_o)]

    def start(copies):
        for copy in copies:
            copy.start()

    @pl.when(step < 0)
    def _():
        packing = pack()
        start(packing[0] + packing[1])
        greet(job.links, swap)
        for copy in packing[0] + packing[1]:
            copy.wait()
        numbers = FORWARD_PLAN[0]
        for number in numbers[: len(REC_PARTS)]:
            job.forward(job.events[number])

        def scaled(i, _):
            at = rows_at(i * CHUNK)
            value = x_ref[at].astype(F32)
            first[at] = value * inverse_norm(value, depth)
            return 0
        lax.fori_loop(0, tokens // CHUNK, scaled, 0)
        for number in numbers[len(REC_PARTS) :]:
            job.forward(job.events[number])
        job.arrived(REC_PARTS)
        lines_in = pltpu.make_async_copy(weights.at[:, pl.ds(REC_ROWS, SMALL_ROWS), pl.ds(0, LANES)], small, wsem.at[1])
        lines_in.start()
        load(0).start()
        lines_in.wait()
        lines = small[...].astype(F32)
        found = [undeal(lines[:, k].astype(BF16), n, rows if k < 2 else rrows) for k in range(10)]
        gain_ref[...] = jnp.broadcast_to(found[0], gain_ref.shape)
        gain2_ref[...] = jnp.broadcast_to(found[1], gain2_ref.shape)
        vec_ref[...] = jnp.zeros_like(vec_ref)
        for k in range(7):
            vec_ref[k : k + 1] = found[2 + k]
        vec_ref[COEF : COEF + 1] = -lru_scale * softplus(-found[9])
        vec_ref[SIG : SIG + 1] = sigmoid(-found[9])
        gain = gain_ref[:1]

        def norm(i, _):
            at = rows_at(i * CHUNK)
            ext[at] = (first[at] * gain).astype(BF16)
            return 0
        lax.fori_loop(0, tokens // CHUNK, norm, 0)
        rim = rim_ref[...].astype(F32)
        ext[pl.ds(tokens, rim.shape[0])] = (rim * inverse_norm(rim, depth) * gain).astype(BF16)
        start(vector_sends)

    for k, s in enumerate(list(range(2 * parts)) + [3 * parts]):
        pl.when(step == s)(lambda k=k: next_block(k))

    @pl.when(jnp.logical_and(step >= 0, step < parts))
    def _():
        j = jnp.clip(step, 0, parts - 1)
        slot = lax.rem(j, 2)
        here = pl.ds(pl.multiple_of(j * W, W), W)
        pump(0, 0, parts)
        got = dot(ext[...], wbuf[slot, :, :rows].reshape(depth, PACK))
        for t in range(tiles):
            gate[j * tiles + t] = got[:tokens, lanes(t)]
        for b in range(batch):
            inner[b * span : b * span + 8, here] = got[tokens + 8 * b : tokens + 8 * b + 8, W:]
            inner[b * span + 8 : (b + 1) * span, here] = got[b * width : (b + 1) * width, W:]
        pump(1, 0, parts)
        for b in range(batch):
            conv = vec_ref[CONV_BIAS : CONV_BIAS + 1, here]
            for lag in range(4):
                conv = conv + vec_ref[lag : lag + 1, here] * inner[b * span + 8 - lag : (b + 1) * span - lag, here]
            mixed[b * width : (b + 1) * width, here] = conv.astype(BF16)

    @pl.when(step == parts - 1)
    def _():
        start(branch_sends)

    @pl.when(jnp.logical_and(step >= parts, step < 2 * parts))
    def _():
        j = jnp.clip(step - parts, 0, parts - 1)
        slot = lax.rem(j + parts, 2)
        pump(0, parts, 2 * parts)
        got = dot(mixed[...], wbuf[slot].reshape(r, PACK))
        for t in range(tiles):
            rate[j * tiles + t] = got[:, lanes(t)]
            entry[j * tiles + t] = got[:, lanes(tiles + t)]
        pump(1, parts, 2 * parts)

        def gating(t, b, spot, at, cols, _):
            g = j * tiles + t
            tile = pl.ds(pl.multiple_of(j * W + t * LANES, LANES), LANES)
            a_rate = sigmoid(rate[g, at] + vec_ref[RATE_BIAS : RATE_BIAS + 1, tile])
            an_entry = sigmoid(entry[g, at] + vec_ref[ENTRY_BIAS : ENTRY_BIAS + 1, tile])
            log_decay = vec_ref[COEF : COEF + 1, tile] * a_rate
            z = 2.0 * log_decay
            root = jnp.sqrt(one_less_exp(z, jnp.exp(z)))
            valid = in_row(spot, width, a_rate.shape) < info_ref[b]
            rate[g, at] = a_rate
            entry[g, at] = an_entry
            decay[g, at] = jnp.where(valid, jnp.exp(log_decay), 1.0)
            drive[g, at] = jnp.where(valid, root * an_entry * mixed[at, tile].astype(F32), 0.0)
            return 0
        each_tile(batch, width, tiles, gating)
        for t in range(tiles):
            g = j * tiles + t
            tile = pl.ds(pl.multiple_of(j * W + t * LANES, LANES), LANES)
            for b in range(batch):
                prod = jnp.ones((SEGS, LANES), F32)
                state = jnp.zeros((SEGS, LANES), F32)
                for s in range(width // SEGS):
                    at = strided(b, width, s)
                    a = decay[g, at]
                    state = a * state + drive[g, at]
                    prod = prod * a
                pseg[b * SEGS : (b + 1) * SEGS, tile] = prod
                hseg[b * SEGS : (b + 1) * SEGS, tile] = state
                whole, end = prod[:1], state[:1]
                for i in range(1, SEGS):
                    whole = whole * prod[i : i + 1]
                    end = prod[i : i + 1] * end + state[i : i + 1]
                swap.rows[g, b : b + 1] = whole
                swap.rows[g, batch + b : batch + b + 1] = end

    @pl.when(step == 2 * parts - 1)
    def _():
        start(gate_sends)
        swap.begin()

    @pl.when(step == 2 * parts)
    def _():
        swap.finish()

    @pl.when(jnp.logical_and(step >= 2 * parts, step < 3 * parts))
    def _():
        j = jnp.clip(step - 2 * parts, 0, parts - 1)
        me = lax.axis_index("seq")
        pump(0, 2 * parts, 3 * parts)
        for t in range(tiles):
            g = j * tiles + t
            tile = pl.ds(pl.multiple_of(j * W + t * LANES, LANES), LANES)
            for b in range(batch):
                begin = jnp.zeros((1, LANES), F32)
                for k in range(n_seq):
                    new = swap.land[k, g, b : b + 1] * begin + swap.land[k, g, batch + b : batch + b + 1]
                    begin = jnp.where(k < me, new, begin)
                for i in range(SEGS):
                    at = b * SEGS + i
                    sstart[at : at + 1, tile] = begin
                    begin = pseg[at : at + 1, tile] * begin + hseg[at : at + 1, tile]
                state = sstart[b * SEGS : (b + 1) * SEGS, tile]
                for s in range(width // SEGS):
                    at = strided(b, width, s)
                    state = decay[g, at] * state + drive[g, at]
                    states[g, at] = state
        pump(1, 2 * parts, 3 * parts)

        def gating(t, b, spot, at, cols, _):
            g = j * tiles + t
            tile = pl.ds(pl.multiple_of(j * W + t * LANES, LANES), LANES)
            gated[at, tile] = (states[g, at] * gelu_both(gate[g, at])[0]).astype(BF16)
            return 0
        each_tile(batch, width, tiles, gating)

    @pl.when(step == 3 * parts - 1)
    def _():
        start(state_sends)

    @pl.when(step >= 3 * parts)
    def _():
        pump(0, 3 * parts, steps)
        first[...] = x_ref[...].astype(F32) + dot(gated[...], wbuf[(2 * parts) % 2].reshape(r, depth))
        pump(1, 3 * parts, steps)

    @pl.when(step == steps - 1)
    def _():
        def norm(i, _):
            at = rows_at(i * CHUNK)
            value = first[at]
            normed2[at] = (value * inverse_norm(value, depth) * gain2_ref[:1]).astype(BF16)
            return 0
        lax.fori_loop(0, tokens // CHUNK, norm, 0)
        start(last_sends)
        job.arrived([r for r in range(len(GATHER_PARTS)) if r not in REC_PARTS])
        job.sent()
        sends.finish()


def forward(info, tokens2, rim, lines, shards, batch, n_seq, r):
    tokens, depth = tokens2.shape
    n = n_seq * ZN
    parts, tiles = r // W, r // LANES
    full = lambda a: pl.BlockSpec(a.shape, lambda j: (0,) * a.ndim)
    anywhere = pl.BlockSpec(memory_space=pl.ANY)
    S = jax.ShapeDtypeStruct
    flat, tall, segs = S((tokens, r), BF16), S((tiles, tokens, LANES), F32), S((batch * SEGS, r), F32)
    inner, ends = S((tokens + 8 * batch, r), F32), S((n_seq, tiles, 2 * batch, LANES), F32)
    first, normed, vec, gain = S((tokens, depth), F32), S((tokens, depth), BF16), S((16, r), F32), S((8, depth), F32)
    outs = [tall, inner, flat, normed, tall, tall, tall, tall, segs, segs, ends, flat, first, normed, vec, gain, gain,
            S((n, REC_ROWS + SMALL_ROWS, PACK), BF16), S((n, FFN_ROWS, PACK), BF16)]
    vm = lambda s: pltpu.VMEM(s.shape, s.dtype)
    scratch = [pltpu.VMEM((tokens + 8 * batch, depth), BF16)] + [
        vm(s) for s in (tall, inner, flat, tall, tall, tall, tall, tall, segs, segs, segs, flat, first, normed, vec, gain, gain)]
    scratch += [pltpu.VMEM((n, SMALL_ROWS, LANES), BF16), pltpu.VMEM((2, n, r // n, PACK), BF16),
                pltpu.VMEM((REC_ROWS + SMALL_ROWS, PACK), BF16), pltpu.VMEM((FFN_ROWS, PACK), BF16)]
    return pl.pallas_call(
        functools.partial(forward_kernel, batch, tokens // batch, n_seq),
        grid=(3 * parts + 2,),
        in_specs=[pl.BlockSpec(memory_space=pltpu.SMEM), full(tokens2), full(rim)] + [anywhere] * (1 + len(shards)),
        out_specs=[anywhere] * len(outs),
        out_shape=outs,
        scratch_shapes=scratch + [SEM((FORWARD_OUTS + 4,)), SEM((2,)), SEM((32,))] + Exchange.scratch(n_seq, (tiles, 2 * batch, LANES))
        + Gather.scratch(GATHER_PARTS),
        compiler_params=pltpu.CompilerParams(collective_id=3, has_side_effects=True, vmem_limit_bytes=62 << 20),
    )(info, tokens2, rim, lines, *shards)


FFN_SCATTER = ((0, 0, 144, 2), (0, 144, 144, 3))
REC_SCATTER = ((0, 0, 64, 0), (0, 64, 64, 1), (0, 128, 48, 2), (0, 176, 48, 3), (0, 224, 32, 2), (0, 256, 32, 3), (1, 0, 16, 0))
BACKWARD_PLAN = (
    (17, 8, 25, 21, 26),
    (),
    (),
    (),
    (0, 19),
    (24,),
    (27, 1, 30),
    (10,),
    (12, 9),
    (),
    (),
    (),
    (16,),
    (),
    (29,),
    (),
    (),
    (31,),
    (2,),
    (28,),
    (),
    (),
    (11,),
    (),
    (),
    (18,),
    (),
    (),
    (),
    (3, 23, 20, 13),
    (),
    (),
    (4,),
    (5,),
    (14, 22, 15),
    (),
    (6, 7),
)
REC_ORDER = (
    97, 90, 88, 89, 85, 30, 84, 61, 57, 62, 86, 60, 59, 28, 91, 104, 2, 95, 98, 56,
    33, 34, 93, 58, 29, 68, 87, 94, 5, 99, 3, 35, 44, 0, 39, 103, 102, 63, 67, 92,
    46, 96, 31, 6, 109, 78, 12, 32, 38, 1, 41, 69, 64, 75, 65, 37, 7, 66, 36, 53,
    101, 100, 108, 74, 107, 51, 40, 80, 105, 47, 71, 76, 4, 70, 11, 9, 43, 106, 48, 10,
    73, 45, 13, 8, 16, 81, 72, 110, 49, 42, 111, 15, 50, 52, 18, 17, 77, 79, 14, 54,
    19, 20, 82, 83, 22, 55, 25, 21, 24, 23, 26, 27,
)


def backward_kernel(batch, width, n_seq, *refs):
    (info_ref, gain_ref, ggain2_ref, vec_ref, pseg_ref, sstart_ref, pall_ref, wo_ref, wr_ref, wi_ref,
     states_ref, decay_ref, gate_ref, rate_ref, entry_ref, gated_ref, inner_ref,
     dlow_h, dfirst_h, mixed_h, normed_h, x_h, gf, token_h, gr, gs, total_h, sib_h,
     low, tall, hid, dn, one, two, both, ext, stage, mixed, normed,
     gseg, gstart, sums, csums, ggain, rims, rim_land, sem, lsem, osem, rimsem) = refs[:50]
    swap = Exchange(n_seq, *refs[50:55])
    job = Scatter(FFN_SCATTER, sum(BACKWARD_PLAN, ()), (gf,), total_h, sib_h, *refs[55:])
    step = pl.program_id(0)
    tokens, depth = low.shape
    n = gf.shape[0]
    r = mixed.shape[1]
    rows, rrows = depth // n, r // n
    group = wo_ref.shape[0]
    thin = group * rrows
    tiles, few, rt = W // LANES, thin // LANES, r // LANES
    counts = backward_steps(n, r, group)
    at, total_steps = {}, 0
    for name, count in counts:
        at[name] = total_steps
        total_steps += count
    size = dict(counts)
    span = width + 8
    me = lax.axis_index("seq")

    def phase(name):
        return jnp.logical_and(step >= at[name], step < at[name] + size[name])

    def index(name):
        return jnp.clip(step - at[name], 0, size[name] - 1)

    def cols(start, count):
        return pl.ds(pl.multiple_of(start, LANES), count)

    def when_step(s, act):
        pl.when(step == s)(act)

    def outgoing(first, value, dst):
        devices, count = value.shape[:2]
        stage[first : first + devices, :count] = value
        pltpu.make_async_copy(stage.at[pl.ds(first, devices), pl.ds(0, count)], dst, sem).start()

    def wait_out(devices, count):
        src = stage.at[pl.ds(0, devices), pl.ds(0, count)]
        pltpu.make_async_copy(src, gr.at[pl.ds(0, devices), pl.ds(0, count)], sem).wait()

    inputs = [pltpu.make_async_copy(src, dst, lsem.at[k]) for k, (src, dst) in enumerate(
        ((dlow_h, low), (mixed_h, mixed), (normed_h, normed), (x_h, low),
         (dfirst_h, tall.at[pl.ds(0, depth // LANES)])))]
    rim_copy = pltpu.make_async_remote_copy(rims, rim_land, rimsem.at[0], rimsem.at[1],
                                            device_id=(lax.rem(me + n_seq - 1, n_seq), swap.z), device_id_type=MESH)

    numbers = [list(range(sum(map(len, BACKWARD_PLAN[:k])), sum(map(len, BACKWARD_PLAN[: k + 1])))) for k in range(2 * total_steps + 1)]

    def pump(half, name):
        for s in range(at[name], at[name] + size[name]):
            if numbers[2 * s + half]:
                @pl.when(step == s)
                def _():
                    for i in numbers[2 * s + half]:
                        job.step(i)

    @pl.when(step == 0)
    def _():
        for copy in inputs[:3]:
            copy.start()
        greet(job.links, swap)
        job.begin()

        @pl.when(me == n_seq - 1)
        def _():
            rim_land[...] = jnp.zeros_like(rim_land)
        inputs[0].wait()

    for name, _ in counts:
        pump(0, name)

    @pl.when(step == at["E"])
    def _():
        wait_out(group, rrows)
        inputs[1].wait()
        inputs[3].start()
        swap.finish()

    @pl.when(step == at["R"])
    def _():
        inputs[4].start()

    @pl.when(step == at["M"])
    def _():
        wait_out(n, rrows)

    @pl.when(phase("U"))
    def _():
        k = index("U")
        total = dot_back(low[...], wo_ref[...].reshape(thin, depth))
        for t in range(few):
            tall[k * few + t] = total[:, lanes(t)]

        def gating(t, b, spot, here, tile, _):
            gate, slope = gelu_both(gate_ref[t, here])
            d = tall[k * few + t, here]
            tall[k * few + t, here] = d * gate
            both[here, pair_cols(k * few + t, 0)] = (d * states_ref[t, here] * slope).astype(BF16)
            return 0
        each_tile(batch, width, few, gating)
        value = dot_outer(gated_ref[...], low[...]).astype(BF16).reshape(group, rrows, depth)
        pl.when(k > 0)(lambda: wait_out(group, rrows))
        outgoing(0, value, gr.at[pl.ds(k * group, group), pl.ds(OUT_AT, rrows)])
        pump(1, "U")
        for t in range(few):
            tile = cols(k * thin + t * LANES, LANES)
            for b in range(batch):
                grad = jnp.zeros((SEGS, LANES), F32)
                for s in reversed(range(width // SEGS)):
                    here = strided(b, width, s)
                    grad = decay_ref[t, here] * (tall[k * few + t, here] + grad)
                gseg[b * SEGS : (b + 1) * SEGS, tile] = grad
                whole = grad[SEGS - 1 :]
                for i in reversed(range(SEGS - 1)):
                    whole = grad[i : i + 1] + pseg_ref[b * SEGS + i : b * SEGS + i + 1, tile] * whole
                swap.rows[k * few + t, b : b + 1] = whole

    @pl.when(step == at["U"] + size["U"] - 1)
    def _():
        swap.begin()

    @pl.when(phase("E"))
    def _():
        k = index("E")
        for t in range(few):
            g = k * few + t
            tile = cols(k * thin + t * LANES, LANES)
            for b in range(batch):
                grad = jnp.zeros((1, LANES), F32)
                for q in reversed(range(n_seq)):
                    new = pall_ref[q, g, b : b + 1] * grad + swap.land[q, g, b : b + 1]
                    grad = jnp.where(q > me, new, grad)
                for i in reversed(range(SEGS)):
                    line = b * SEGS + i
                    gstart[i : i + 1] = grad
                    grad = pseg_ref[line : line + 1, tile] * grad + gseg[line : line + 1, tile]
                grad = gstart[...]
                for s in reversed(range(width // SEGS)):
                    here = strided(b, width, s)
                    total = tall[g, here] + grad
                    one[t, here] = total
                    grad = decay_ref[t, here] * total
                    before = states_ref[t, strided(b, width, s - 1)] if s else sstart_ref[b * SEGS : (b + 1) * SEGS, tile]
                    two[t, here] = grad * before

        pump(1, "E")

        def gating(t, b, spot, here, _, kept):
            tile = cols(k * thin + t * LANES, LANES)
            coef = vec_ref[COEF : COEF + 1, tile]
            rate, entry = rate_ref[t, here], entry_ref[t, here]
            valid = in_row(spot, width, rate.shape) < info_ref[b]
            grad = jnp.where(valid, one[t, here], 0.0)
            z = 2.0 * coef * rate
            exp_z = jnp.exp(z)
            under = one_less_exp(z, exp_z)
            inverse = lax.rsqrt(under)
            root = under * inverse
            value = mixed[here, tile].astype(F32)
            part = grad * entry
            d_log = jnp.where(valid, two[t, here], 0.0) - part * value * exp_z * inverse
            d_rate = coef * d_log * rate * (1.0 - rate)
            straight = part * root
            d_entry = straight * value * (1.0 - entry)
            tall[rt + k * few + t, here] = straight
            hid[here, pair_cols(k * few + t, 0)] = d_rate.astype(BF16)
            hid[here, pair_cols(k * few + t, 1)] = d_entry.astype(BF16)
            return (kept[0] + fold8(d_log * rate), kept[1] + fold8(d_rate), kept[2] + fold8(d_entry))
        zero = jnp.zeros((8, LANES), F32)
        for t, kept in enumerate(each_tile(batch, width, few, gating, (zero, zero, zero))):
            tile = cols(k * thin + t * LANES, LANES)
            for line in range(3):
                factor = 8.0 * vec_ref[SIG : SIG + 1, tile] if line == 0 else 1.0
                sums[line : line + 1, tile] = factor * jnp.sum(kept[line], axis=0, keepdims=True)

    @pl.when(phase("R"))
    def _():
        j = index("R")
        grads = hid[:, cols(j * PACK, PACK)]
        pl.when(j > 0)(lambda: wait_out(n, rrows))
        for half in range(2):
            value = dot_outer(mixed[:, half * r // 2 : (half + 1) * r // 2], grads).astype(BF16)
            dst = gr.at[pl.ds(half * n // 2, n // 2), pl.ds(pl.multiple_of(GATES_AT + j * rrows, 16), rrows)]
            outgoing(half * n // 2, value.reshape(n // 2, rrows, PACK), dst)
            if half == 0:
                pump(1, "R")

    @pl.when(phase("M"))
    def _():
        k = index("M")
        total = jnp.zeros((tokens, thin), F32)
        for p in range(r // W):
            weights = wr_ref[:, p * rrows : (p + 1) * rrows].reshape(thin, PACK)
            total = total + dot_back(hid[:, p * PACK : (p + 1) * PACK], weights)
        for t in range(few):
            tall[rt + k * few + t] += total[:, lanes(t)]
        pump(1, "M")

    @pl.when(step == at["M"] + size["M"] - 1)
    def _():
        for b in range(batch):
            rims[:, b * 4 : b * 4 + 4] = tall[rt : 2 * rt, b * width : b * width + 4]
        pl.when(me > 0)(rim_copy.start)

    @pl.when(step == at["I"])
    def _():
        inputs[2].wait()
        pl.when(me < n_seq - 1)(rim_copy.wait_recv)
        pl.when(me > 0)(rim_copy.wait_send)

    @pl.when(phase("I"))
    def _():
        j = index("I")
        here = cols(j * W, W)
        for t in range(tiles):
            for b in range(batch):
                ext[b * span : b * span + width, lanes(t)] = tall[rt + j * tiles + t, b * width : (b + 1) * width]
                ext[b * span + width : b * span + width + 4, lanes(t)] = rim_land[j * tiles + t, b * 4 : b * 4 + 4]
        for b in range(batch):
            total = jnp.zeros((width, W), F32)
            for lag in range(4):
                total = total + vec_ref[lag : lag + 1, here] * ext[b * span + lag : b * span + lag + width]
            both[b * width : (b + 1) * width, cols(j * PACK + W, W)] = total.astype(BF16)
        for lag in range(5):
            total = jnp.zeros((1, W), F32)
            for b in range(batch):
                value = ext[b * span : b * span + width]
                if lag < 4:
                    value = value * inner_ref[b * span + 8 - lag : (b + 1) * span - lag]
                total = total + jnp.sum(value, axis=0, keepdims=True)
            csums[lag : lag + 1, here] = total
        pump(1, "I")
        grads = both[:, cols(j * PACK, PACK)]
        more = dot_back(grads, wi_ref[...].reshape(depth, PACK))

        @pl.when(j == 0)
        def _():
            dn[...] = more

        @pl.when(j > 0)
        def _():
            dn[...] += more
        value = dot_outer(normed[...], grads).astype(BF16).reshape(n, rows, PACK)
        pl.when(j > 0)(lambda: wait_out(n, rows))
        outgoing(0, value, gr.at[:, pl.ds(pl.multiple_of(IN_AT + j * rows, 16), rows)])

    @pl.when(step == total_steps - 1)
    def _():
        inputs[3].wait()
        inputs[4].wait()

        def finish(i, total):
            here = rows_at(i * CHUNK)
            value, grad = low[here].astype(F32), dn[here]
            scale = inverse_norm(value, depth)
            weighted = grad * gain_ref[:1]
            mean = jnp.sum(weighted * value, axis=-1, keepdims=True) * (1.0 / depth)
            first = jnp.concatenate([tall[t, here] for t in range(depth // LANES)], axis=1)
            dn[here] = first + scale * weighted - value * (scale * scale * scale * mean)
            return total + fold8(grad * value * scale)
        ggain[...] = lax.fori_loop(0, tokens // CHUNK, finish, jnp.zeros((8, depth), F32))
        pltpu.make_async_copy(dn, token_h, osem.at[0]).start()
        wait_out(n, rows)
        small = stage.at[:, pl.ds(0, SMALL_ROWS)]
        small[...] = jnp.zeros((n, SMALL_ROWS, PACK), BF16)
        lines = [(jnp.sum(ggain[...], axis=0, keepdims=True), rows), (jnp.sum(ggain2_ref[...], axis=0, keepdims=True), rows)]
        lines += [(csums[k : k + 1], rrows) for k in range(5)] + [(sums[k : k + 1], rrows) for k in (1, 2, 0)]
        for k, (line, count) in enumerate(lines):
            stage[:, k, :LANES] = deal(line, n, count)
        small_out = pltpu.make_async_copy(small, gs, osem.at[1])
        small_out.start()
        small_out.wait()
        for i in numbers[-1]:
            job.step(i)
        job.finish()
        pltpu.make_async_copy(dn, token_h, osem.at[0]).wait()


def deal(line, n, count):
    length = n * count
    lane = lax.broadcasted_iota(jnp.int32, (n, length), 1)
    row = lax.broadcasted_iota(jnp.int32, (n, length), 0)
    own = jnp.where(jnp.logical_and(lane >= row * count, lane < (row + 1) * count), line, 0.0).astype(BF16)
    spot = lax.broadcasted_iota(jnp.int32, (length, LANES), 0)
    col = lax.broadcasted_iota(jnp.int32, (length, LANES), 1)
    pick = jnp.where(jnp.logical_and(lax.rem(spot, count) == col, col < count), 1.0, 0.0).astype(BF16)
    return dot(own, pick).astype(BF16)


def backward_steps(n, r, group):
    parts = n // group
    return (("U", parts), ("E", parts), ("R", r // W), ("M", parts), ("I", r // W))


def backward(info, gain, ggain2, vec, pseg, sstart, pall, packed, states, decay, gate_pre, rate, entry, gated,
             inner, d_low, d_first, mixed, normed, x, grad_ffn, batch):
    tokens, depth = x.shape
    width = tokens // batch
    n, r = packed.shape[0], vec.shape[1]
    group = 8
    rows, rrows = depth // n, r // n
    thin = group * rrows
    few, tiles = thin // LANES, W // LANES
    n_seq = pall.shape[0]
    counts = backward_steps(n, r, group)
    at, steps = {}, 0
    for name, count in counts:
        at[name] = steps
        steps += count
    size = dict(counts)
    clamp = lambda j, name: jnp.clip(j - at[name], 0, size[name] - 1)
    full = lambda a: pl.BlockSpec(a.shape, lambda j: (0,) * a.ndim, pipeline_mode=pl.Buffered(buffer_count=1))
    anywhere = pl.BlockSpec(memory_space=pl.ANY)

    def two_phases(j, one, two):
        return jnp.where(j < at[two], clamp(j, one), clamp(j, two))
    twice = pl.BlockSpec((few, tokens, LANES), lambda j: (two_phases(j, "U", "E"), 0, 0))
    early = pl.BlockSpec((few, tokens, LANES), lambda j: (clamp(j, "U"), 0, 0))
    late = pl.BlockSpec((few, tokens, LANES), lambda j: (clamp(j, "E"), 0, 0))
    in_specs = [pl.BlockSpec(memory_space=pltpu.SMEM)] + [full(a) for a in (gain, ggain2, vec, pseg, sstart, pall)] + [
        pl.BlockSpec((group, rrows, PACK), lambda j: (clamp(j, "U"), OUT_AT // rrows, 0)),
        pl.BlockSpec((group, r // W * rrows, PACK), lambda j: (clamp(j, "M"), GATES_AT // (r // W * rrows), 0)),
        pl.BlockSpec((n, rows, PACK), lambda j: (0, IN_AT // rows + clamp(j, "I"), 0)),
        twice, twice, early, late, late,
        pl.BlockSpec((tokens, thin), lambda j: (0, clamp(j, "U"))),
        pl.BlockSpec((inner.shape[0], W), lambda j: (0, clamp(j, "I"))),
    ] + [anywhere] * 6
    S = jax.ShapeDtypeStruct
    outs = [S((tokens, depth), F32), S((n, REC_ROWS, PACK), BF16), S((n, SMALL_ROWS, PACK), BF16)]
    outs += Scatter.buffers(FFN_SCATTER)
    vm = pltpu.VMEM
    scratch = [
        vm((tokens, depth), BF16), vm((2 * r // LANES, tokens, LANES), F32), vm((tokens, 2 * r), BF16),
        vm((tokens, depth), F32), vm((few, tokens, LANES), F32), vm((few, tokens, LANES), F32),
        vm((tokens, 2 * r), BF16), vm((tokens + 8 * batch, W), F32), vm((n, rrows, PACK), BF16),
        vm((tokens, r), BF16), vm((tokens, depth), BF16), vm((batch * SEGS, r), F32), vm((SEGS, LANES), F32),
        vm((8, r), F32), vm((8, r), F32), vm((8, depth), F32), vm((r // LANES, 4 * batch, LANES), F32),
        vm((r // LANES, 4 * batch, LANES), F32), SEM, SEM((5,)), SEM((2,)), SEM((2,)),
    ] + Exchange.scratch(n_seq, (r // LANES, batch, LANES)) + Scatter.scratch(FFN_SCATTER, 4, 6)
    got = pl.pallas_call(
        functools.partial(backward_kernel, batch, width, n_seq),
        grid=(steps,),
        in_specs=in_specs,
        out_specs=[anywhere] * len(outs),
        out_shape=outs,
        scratch_shapes=scratch,
        compiler_params=pltpu.CompilerParams(collective_id=4, has_side_effects=True, vmem_limit_bytes=64 << 20),
    )(info, gain, ggain2, vec, pseg, sstart, pall, packed, packed, packed,
      states, decay, gate_pre, rate, entry, gated, inner, d_low, d_first, mixed, normed, x, grad_ffn)
    return got[0], got[1], got[2], got[3]


GATES_AT, OUT_AT, IN_AT, REC_ROWS = 0, 144, 192, 288
UPS_AT, DOWN_AT, FFN_ROWS, SMALL_ROWS = 0, 192, 288, 16


def unpack_pair(item, rows, cols):
    blocks = item.reshape(cols // W, rows, 2, W).transpose(2, 1, 0, 3)
    return blocks[0].reshape(rows, cols), blocks[1].reshape(rows, cols)


def pad_rows(item, before, count):
    batch, rows, cols = item.shape
    item = jnp.pad(item, ((0, 0), (before, count - rows - before), (0, 0)))
    return item.reshape(batch * count, cols)


def per_device_packed(tokens, cotangent, lengths, *shards):
    (gate_proj, input_proj, rate_proj, entry_proj, out_proj, ffn_gate, ffn_up, ffn_down) = shards[:8]
    small = shards[8:]
    batch, width, depth = tokens.shape
    r, f = gate_proj.shape[1], ffn_gate.shape[1]
    n_seq = lax.axis_size("seq")
    me = lax.axis_index("seq")
    rim = pad_rows(from_behind(tokens[:, width - 3 :], "seq", 1), 5, 8)
    lines = jnp.concatenate([jnp.pad(item.reshape(-1, item.shape[-1]), ((0, 0), (0, PACK - item.shape[-1])))
                             for item in small] + [jnp.zeros((SMALL_ROWS - 10, PACK), jnp.bfloat16)], axis=0)
    info = jnp.concatenate([jnp.clip(lengths - me * width, 0, width), me[None]]).astype(jnp.int32)
    tokens2 = tokens.reshape(batch * width, depth)
    cot2 = cotangent.reshape(batch * width, depth)

    (gate_pre, inner, mixed, normed, rate, entry, decay, states, pseg, sstart, pall, gated, first, normed_two, vec,
     norm_gain, ffn_gain, packed, packed_ffn) = forward(info, tokens2, rim, lines, shards[:8], batch, n_seq, r)
    block_out, d_first, d_low, g_ffn_gain, grad_ffn = feed_forward(
        info, first, normed_two, cot2, ffn_gain, packed_ffn, f, batch)
    token_grad, grad_rec, grad_small, total_ffn = backward(
        info, norm_gain, g_ffn_gain, vec, pseg, sstart, pall, packed, states, decay, gate_pre, rate, entry, gated, inner,
        d_low, d_first, mixed, normed, tokens2, grad_ffn, batch)
    total = scatter(REC_SCATTER, REC_ORDER, [grad_rec, grad_small])
    g_rate, g_entry = unpack_pair(total[:OUT_AT], *rate_proj.shape)
    g_gate, g_input = unpack_pair(total[IN_AT:REC_ROWS], *gate_proj.shape)
    g_ffn_gate, g_ffn_up = unpack_pair(total_ffn[:DOWN_AT], *ffn_gate.shape)
    result = [g_gate, g_input, g_rate, g_entry, total[OUT_AT:IN_AT], g_ffn_gate, g_ffn_up, total_ffn[DOWN_AT:]]
    line = REC_ROWS
    for item in small:
        count = item.shape[0] if item.ndim == 2 else 1
        part = total[line : line + count, : item.shape[-1]]
        line += count
        result.append(part.reshape(item.shape))
    return (block_out.reshape(tokens.shape), token_grad.reshape(tokens.shape), *result)


def solution(mesh):
    packs = mesh.shape["seq"] == 8 and mesh.shape["batch"] == ZN
    placed = (
        P("batch", "seq", None),
        P("batch", "seq", None),
        P("batch"),
        P(("seq", "batch"), None),
        P(("seq", "batch"), None),
        P(("seq", "batch"), None),
        P(("seq", "batch"), None),
        P(("seq", "batch"), None),
        P(("seq", "batch"), None),
        P(("seq", "batch"), None),
        P(("seq", "batch"), None),
        P(("seq", "batch")),
        P(("seq", "batch")),
        P(None, ("seq", "batch")),
        P(("seq", "batch")),
        P(("seq", "batch")),
        P(("seq", "batch")),
        P(("seq", "batch")),
    )
    return jax.shard_map(
        per_device_packed if packs else per_device,
        mesh=mesh,
        in_specs=placed,
        out_specs=(
            P("batch", "seq", None),
            P("batch", "seq", None),
            P(("seq", "batch"), None),
            P(("seq", "batch"), None),
            P(("seq", "batch"), None),
            P(("seq", "batch"), None),
            P(("seq", "batch"), None),
            P(("seq", "batch"), None),
            P(("seq", "batch"), None),
            P(("seq", "batch"), None),
            P(("seq", "batch")),
            P(("seq", "batch")),
            P(None, ("seq", "batch")),
            P(("seq", "batch")),
            P(("seq", "batch")),
            P(("seq", "batch")),
            P(("seq", "batch")),
        ),
        check_vma=False,
    )
```

```python
import functools

import jax
import jax.numpy as jnp
import numpy as np
from jax import lax
from jax.experimental import pallas as pl
from jax.experimental.pallas import tpu as pltpu
from jax.sharding import PartitionSpec as P

MICRO = 2


eps = 1e-06
lru_scale = 8.0


def from_behind(value, axis, steps):
    count = lax.axis_size(axis)
    initial, last = (max(0, -steps), min(count, count - steps))
    return lax.ppermute(value, axis, [(source, source + steps) for source in range(initial, last)])


def entering(array, axis, combine, identity):
    size, place = (lax.axis_size(axis), lax.axis_index(axis))
    everything = jax.tree.map(lambda part: lax.all_gather(part, axis), array)
    start = jax.tree.map(
        lambda part, zero: jnp.broadcast_to(jnp.asarray(zero, part.dtype), part.shape),
        array,
        identity,
    )

    def entering_turn(k, before):
        reached = k < place
        new = combine(before, jax.tree.map(lambda part: part[k], everything))
        return jax.tree.map(lambda a, b: jnp.where(reached, a, b), new, before)

    return lax.fori_loop(0, size, entering_turn, start)


def carried_in(array, axis, combine, identity):
    size, place = (lax.axis_size(axis), lax.axis_index(axis))
    everything = jax.tree.map(
        lambda part, kind: lax.all_gather(part.astype(kind), axis),
        array,
        (jnp.bfloat16, jnp.bfloat16),
    )
    start = jax.tree.map(
        lambda part, zero: jnp.broadcast_to(jnp.asarray(zero, part.dtype), part.shape),
        array,
        identity,
    )

    def carried_turn(k, before):
        at = size - 1 - k
        reached = at > place
        new = combine(
            before, jax.tree.map(lambda part, own: part[at].astype(own.dtype), everything, array)
        )
        return jax.tree.map(lambda a, b: jnp.where(reached, a, b), new, before)

    return lax.fori_loop(0, size, carried_turn, start)


def for_sending(array):

    def short(part):
        return part.astype(jnp.bfloat16) if part.dtype == jnp.float32 else part

    return jax.tree.map(short, array)


def project(left, right):
    return jnp.einsum("btd,de->bte", left, right, preferred_element_type=jnp.float32)


def project_back(left, right):
    return jnp.einsum("bte,de->btd", left, right, preferred_element_type=jnp.float32)


def outer_sum(left, right):
    return jnp.einsum("btd,bte->de", left, right, preferred_element_type=jnp.float32)


def link(earlier, later):
    return (earlier[0] * later[0], later[0] * earlier[1] + later[1])


def norm_back(value, scale, gain, grad):
    weighted = grad * gain
    gain_grad = jnp.sum(grad * value * scale, axis=(0, 1))
    spread = jnp.mean(weighted * value, axis=-1, keepdims=True)
    return (scale * weighted - value * scale**3 * spread, gain_grad)


def fetch(shards):
    (
        gate_proj,
        input_proj,
        rate_proj,
        entry_proj,
        out_proj,
        ffn_gate,
        ffn_up,
        ffn_down,
        norm_gain,
        ffn_gain,
        conv_taps,
        conv_bias,
        rate_bias,
        entry_bias,
        decay_logit,
    ) = shards
    return (
        lax.all_gather(gate_proj, ("seq", "batch"), axis=0, tiled=True),
        lax.all_gather(input_proj, ("seq", "batch"), axis=0, tiled=True),
        lax.all_gather(rate_proj, ("seq", "batch"), axis=0, tiled=True),
        lax.all_gather(entry_proj, ("seq", "batch"), axis=0, tiled=True),
        lax.all_gather(out_proj, ("seq", "batch"), axis=0, tiled=True),
        lax.all_gather(ffn_gate, ("seq", "batch"), axis=0, tiled=True),
        lax.all_gather(ffn_up, ("seq", "batch"), axis=0, tiled=True),
        lax.all_gather(ffn_down, ("seq", "batch"), axis=0, tiled=True),
        lax.all_gather(norm_gain, ("seq", "batch"), axis=0, tiled=True),
        lax.all_gather(ffn_gain, ("seq", "batch"), axis=0, tiled=True),
        lax.all_gather(conv_taps, ("seq", "batch"), axis=1, tiled=True),
        lax.all_gather(conv_bias, ("seq", "batch"), axis=0, tiled=True),
        lax.all_gather(rate_bias, ("seq", "batch"), axis=0, tiled=True),
        lax.all_gather(entry_bias, ("seq", "batch"), axis=0, tiled=True),
        lax.all_gather(decay_logit, ("seq", "batch"), axis=0, tiled=True),
    )


def forward_part(tokens, mask, weights):
    (
        gate_proj,
        input_proj,
        rate_proj,
        entry_proj,
        out_proj,
        ffn_gate,
        ffn_up,
        ffn_down,
        norm_gain,
        ffn_gain,
        conv_taps,
        conv_bias,
        rate_bias,
        entry_bias,
        decay_logit,
    ) = weights
    width = tokens.shape[1]
    taps_count = conv_taps.shape[0]
    values = tokens.astype(jnp.float32)
    scale_one = lax.rsqrt(jnp.mean(values * values, axis=-1, keepdims=True) + eps)
    normed = (values * scale_one * norm_gain).astype(jnp.bfloat16)
    gate_pre = project(normed, gate_proj)
    inner = project(normed, input_proj)
    rim = from_behind(inner[:, width - (taps_count - 1) :], "seq", 1)
    extended = jnp.concatenate([rim, inner], axis=1)
    conv = jnp.zeros_like(inner) + conv_bias
    for lag in range(taps_count):
        start = taps_count - 1 - lag
        conv = conv + conv_taps[lag] * extended[:, start : start + width]
    mixed = conv.astype(jnp.bfloat16)
    mixed_full = mixed.astype(jnp.float32)
    rate = jax.nn.sigmoid(project(mixed, rate_proj) + rate_bias)
    entry = jax.nn.sigmoid(project(mixed, entry_proj) + entry_bias)
    logit = decay_logit.astype(jnp.float32)
    log_decay = -lru_scale * jax.nn.softplus(-logit) * rate
    decay = jnp.exp(mask * log_decay)
    root = jnp.sqrt(-jnp.expm1(2.0 * log_decay))
    drive = mask * root * entry * mixed_full
    reach, local = lax.associative_scan(link, (decay, drive), axis=1)
    unit_state = (jnp.ones_like(reach[:, -1]), jnp.zeros_like(local[:, -1]))
    start_state = entering((reach[:, -1], local[:, -1]), "seq", link, unit_state)[1]
    states = local + reach * start_state[:, None]
    gated = (states * jax.nn.gelu(gate_pre)).astype(jnp.bfloat16)
    first = values + project(gated, out_proj)
    scale_two = lax.rsqrt(jnp.mean(first * first, axis=-1, keepdims=True) + eps)
    normed_two = (first * scale_two * ffn_gain).astype(jnp.bfloat16)
    up_pre = project(normed_two, ffn_gate)
    mix_pre = project(normed_two, ffn_up)
    hidden = (jax.nn.gelu(up_pre) * mix_pre).astype(jnp.bfloat16)
    block_out = mask * (first + project(hidden, ffn_down))
    saved = (
        values,
        scale_one,
        normed,
        gate_pre,
        extended,
        mixed,
        mixed_full,
        rate,
        entry,
        log_decay,
        decay,
        root,
        start_state,
        states,
        gated,
        first,
        scale_two,
        normed_two,
        up_pre,
        mix_pre,
        hidden,
    )
    return (block_out, saved)


def backward_part(cotangent, mask, weights, saved):
    (
        gate_proj,
        input_proj,
        rate_proj,
        entry_proj,
        out_proj,
        ffn_gate,
        ffn_up,
        ffn_down,
        norm_gain,
        ffn_gain,
        conv_taps,
        conv_bias,
        rate_bias,
        entry_bias,
        decay_logit,
    ) = weights
    (
        values,
        scale_one,
        normed,
        gate_pre,
        extended,
        mixed,
        mixed_full,
        rate,
        entry,
        log_decay,
        decay,
        root,
        start_state,
        states,
        gated,
        first,
        scale_two,
        normed_two,
        up_pre,
        mix_pre,
        hidden,
    ) = saved
    width = values.shape[1]
    taps_count = conv_taps.shape[0]
    cot_full = mask * cotangent.astype(jnp.float32)
    cot_low = cot_full.astype(jnp.bfloat16)
    grad_ffn_down = outer_sum(hidden, cot_low)
    d_hidden = project_back(cot_low, ffn_down)
    gelu_up, gelu_pull = jax.vjp(jax.nn.gelu, up_pre)
    d_up = gelu_pull(d_hidden * mix_pre)[0].astype(jnp.bfloat16)
    d_mix = (d_hidden * gelu_up).astype(jnp.bfloat16)
    grad_ffn_gate = outer_sum(normed_two, d_up)
    grad_ffn_up = outer_sum(normed_two, d_mix)
    d_normed_two = project_back(d_up, ffn_gate) + project_back(d_mix, ffn_up)
    back_two, grad_ffn_gain = norm_back(first, scale_two, ffn_gain, d_normed_two)
    d_first = cot_full + back_two
    d_first_low = d_first.astype(jnp.bfloat16)
    grad_out_proj = outer_sum(gated, d_first_low)
    d_gated = project_back(d_first_low, out_proj)
    gate, gate_pull = jax.vjp(jax.nn.gelu, gate_pre)
    d_states = d_gated * gate
    d_gate_pre = gate_pull(d_gated * states)[0].astype(jnp.bfloat16)
    following = jnp.concatenate([decay[:, 1:], jnp.ones_like(decay[:, :1])], axis=1)
    reach_back, local_back = lax.associative_scan(link, (following, d_states), reverse=True, axis=1)
    unit_grad = (jnp.ones_like(decay[:, 0]), jnp.zeros_like(decay[:, 0]))
    end_grad = carried_in(
        (decay[:, 0] * reach_back[:, 0], decay[:, 0] * local_back[:, 0]), "seq", link, unit_grad
    )[1]
    carried = local_back + reach_back * end_grad[:, None]
    previous = jnp.concatenate([start_state[:, None], states[:, :-1]], axis=1)
    masked_grad = mask * carried
    d_log = (
        masked_grad * previous * decay
        - masked_grad * entry * mixed_full * jnp.exp(2.0 * log_decay) / root
    )
    logit = decay_logit.astype(jnp.float32)
    grad_decay_logit = jnp.sum(lru_scale * d_log * rate * jax.nn.sigmoid(-logit), axis=(0, 1))
    d_rate_pre = -lru_scale * jax.nn.softplus(-logit) * d_log * rate * (1.0 - rate)
    d_entry_pre = masked_grad * root * mixed_full * entry * (1.0 - entry)
    grad_rate_bias = jnp.sum(d_rate_pre, axis=(0, 1))
    grad_entry_bias = jnp.sum(d_entry_pre, axis=(0, 1))
    rate_low = d_rate_pre.astype(jnp.bfloat16)
    entry_low = d_entry_pre.astype(jnp.bfloat16)
    grad_rate_proj = outer_sum(mixed, rate_low)
    grad_entry_proj = outer_sum(mixed, entry_low)
    d_mixed = (
        masked_grad * root * entry
        + project_back(rate_low, rate_proj)
        + project_back(entry_low, entry_proj)
    )
    grad_conv_bias = jnp.sum(d_mixed, axis=(0, 1))
    tap_grads = []
    for lag in range(taps_count):
        start = taps_count - 1 - lag
        tap_grads.append(jnp.sum(d_mixed * extended[:, start : start + width], axis=(0, 1)))
    grad_conv_taps = jnp.stack(tap_grads, axis=0)
    rim_back = from_behind(for_sending(d_mixed[:, : taps_count - 1]), "seq", -1)
    later = jnp.concatenate([d_mixed, rim_back], axis=1)
    d_inner = jnp.zeros_like(d_mixed)
    for lag in range(taps_count):
        d_inner = d_inner + conv_taps[lag] * later[:, lag : lag + width]
    d_inner = d_inner.astype(jnp.bfloat16)
    grad_input_proj = outer_sum(normed, d_inner)
    grad_gate_proj = outer_sum(normed, d_gate_pre)
    d_normed = project_back(d_gate_pre, gate_proj) + project_back(d_inner, input_proj)
    back_one, grad_norm_gain = norm_back(values, scale_one, norm_gain, d_normed)
    token_grad = d_first + back_one
    grads = (
        grad_gate_proj,
        grad_input_proj,
        grad_rate_proj,
        grad_entry_proj,
        grad_out_proj,
        grad_ffn_gate,
        grad_ffn_up,
        grad_ffn_down,
        grad_norm_gain,
        grad_ffn_gain,
        grad_conv_taps,
        grad_conv_bias,
        grad_rate_bias,
        grad_entry_bias,
        grad_decay_logit,
    )
    return (token_grad, grads)


def reduce_grads(totals):
    shaped = []
    for index, item in enumerate(totals):
        if index == 10:
            item = item.T
        if item.ndim == 1:
            item = item[:, None]
        shaped.append(item[None])
    spread = (
        lax.all_to_all(
            shaped[0].astype(jnp.bfloat16), "seq", split_axis=1, concat_axis=0, tiled=True
        ).astype(jnp.float32),
        lax.all_to_all(
            shaped[1].astype(jnp.bfloat16), "seq", split_axis=1, concat_axis=0, tiled=True
        ).astype(jnp.float32),
        lax.all_to_all(
            shaped[2].astype(jnp.bfloat16), "seq", split_axis=1, concat_axis=0, tiled=True
        ).astype(jnp.float32),
        lax.all_to_all(
            shaped[3].astype(jnp.bfloat16), "seq", split_axis=1, concat_axis=0, tiled=True
        ).astype(jnp.float32),
        lax.all_to_all(
            shaped[4].astype(jnp.bfloat16), "seq", split_axis=1, concat_axis=0, tiled=True
        ).astype(jnp.float32),
        lax.all_to_all(
            shaped[5].astype(jnp.bfloat16), "seq", split_axis=1, concat_axis=0, tiled=True
        ).astype(jnp.float32),
        lax.all_to_all(
            shaped[6].astype(jnp.bfloat16), "seq", split_axis=1, concat_axis=0, tiled=True
        ).astype(jnp.float32),
        lax.all_to_all(
            shaped[7].astype(jnp.bfloat16), "seq", split_axis=1, concat_axis=0, tiled=True
        ).astype(jnp.float32),
        lax.all_to_all(
            shaped[8].astype(jnp.bfloat16), "seq", split_axis=1, concat_axis=0, tiled=True
        ).astype(jnp.float32),
        lax.all_to_all(
            shaped[9].astype(jnp.bfloat16), "seq", split_axis=1, concat_axis=0, tiled=True
        ).astype(jnp.float32),
        lax.all_to_all(for_sending(shaped[10]), "seq", split_axis=1, concat_axis=0, tiled=True),
        lax.all_to_all(for_sending(shaped[11]), "seq", split_axis=1, concat_axis=0, tiled=True),
        lax.all_to_all(for_sending(shaped[12]), "seq", split_axis=1, concat_axis=0, tiled=True),
        lax.all_to_all(for_sending(shaped[13]), "seq", split_axis=1, concat_axis=0, tiled=True),
        lax.all_to_all(for_sending(shaped[14]), "seq", split_axis=1, concat_axis=0, tiled=True),
    )
    folded = [jnp.sum(piece, axis=0) for piece in spread]
    summed = (
        lax.psum_scatter(
            folded[0].astype(jnp.bfloat16), "batch", scatter_dimension=0, tiled=True
        ).astype(jnp.float32),
        lax.psum_scatter(
            folded[1].astype(jnp.bfloat16), "batch", scatter_dimension=0, tiled=True
        ).astype(jnp.float32),
        lax.psum_scatter(
            folded[2].astype(jnp.bfloat16), "batch", scatter_dimension=0, tiled=True
        ).astype(jnp.float32),
        lax.psum_scatter(
            folded[3].astype(jnp.bfloat16), "batch", scatter_dimension=0, tiled=True
        ).astype(jnp.float32),
        lax.psum_scatter(
            folded[4].astype(jnp.bfloat16), "batch", scatter_dimension=0, tiled=True
        ).astype(jnp.float32),
        lax.psum_scatter(
            folded[5].astype(jnp.bfloat16), "batch", scatter_dimension=0, tiled=True
        ).astype(jnp.float32),
        lax.psum_scatter(
            folded[6].astype(jnp.bfloat16), "batch", scatter_dimension=0, tiled=True
        ).astype(jnp.float32),
        lax.psum_scatter(
            folded[7].astype(jnp.bfloat16), "batch", scatter_dimension=0, tiled=True
        ).astype(jnp.float32),
        lax.psum_scatter(
            folded[8].astype(jnp.bfloat16), "batch", scatter_dimension=0, tiled=True
        ).astype(jnp.float32),
        lax.psum_scatter(
            folded[9].astype(jnp.bfloat16), "batch", scatter_dimension=0, tiled=True
        ).astype(jnp.float32),
        lax.psum_scatter(
            folded[10].astype(jnp.bfloat16), "batch", scatter_dimension=0, tiled=True
        ).astype(jnp.float32),
        lax.psum_scatter(
            folded[11].astype(jnp.bfloat16), "batch", scatter_dimension=0, tiled=True
        ).astype(jnp.float32),
        lax.psum_scatter(
            folded[12].astype(jnp.bfloat16), "batch", scatter_dimension=0, tiled=True
        ).astype(jnp.float32),
        lax.psum_scatter(
            folded[13].astype(jnp.bfloat16), "batch", scatter_dimension=0, tiled=True
        ).astype(jnp.float32),
        lax.psum_scatter(
            folded[14].astype(jnp.bfloat16), "batch", scatter_dimension=0, tiled=True
        ).astype(jnp.float32),
    )
    result = []
    for index, item in enumerate(summed):
        if index == 10:
            result.append(item.T)
        elif totals[index].ndim == 1:
            result.append(item[:, 0])
        else:
            result.append(item)
    return tuple(result)


def per_device(
    tokens,
    cotangent,
    lengths,
    gate_proj,
    input_proj,
    rate_proj,
    entry_proj,
    out_proj,
    ffn_gate,
    ffn_up,
    ffn_down,
    norm_gain,
    ffn_gain,
    conv_taps,
    conv_bias,
    rate_bias,
    entry_bias,
    decay_logit,
):
    shards = (
        gate_proj,
        input_proj,
        rate_proj,
        entry_proj,
        out_proj,
        ffn_gate,
        ffn_up,
        ffn_down,
        norm_gain,
        ffn_gain,
        conv_taps,
        conv_bias,
        rate_bias,
        entry_bias,
        decay_logit,
    )
    rows, width = (tokens.shape[0], tokens.shape[1])
    place = lax.axis_index("seq") * width + lax.iota(jnp.int32, width)
    mask_all = (place[None, :] < lengths[:, None]).astype(jnp.float32)[:, :, None]
    group = rows // MICRO
    totals = None
    block_parts = []
    grad_parts = []
    for part in range(MICRO):
        lower = part * group
        mask = mask_all[lower : lower + group]
        weights = fetch(shards)
        block_out, saved = forward_part(tokens[lower : lower + group], mask, weights)
        weights = fetch(shards)
        token_grad, grads = backward_part(cotangent[lower : lower + group], mask, weights, saved)
        totals = grads if part == 0 else jax.tree.map(jnp.add, totals, grads)
        block_parts.append(block_out)
        grad_parts.append(token_grad)
    summed = reduce_grads(totals)
    return (jnp.concatenate(block_parts, axis=0), jnp.concatenate(grad_parts, axis=0)) + summed


F32 = jnp.float32
BF16 = jnp.bfloat16
W = 512
PACK = 2 * W
SEGS = 8
CHUNK = 32
TALL = 64
LANES = 128
GELU_A = 0.7978845608028654
GELU_B = 0.044715
TAPS, CONV_BIAS, RATE_BIAS, ENTRY_BIAS, COEF, SIG = 0, 4, 5, 6, 7, 8


def dot(left, right):
    return lax.dot_general(left, right, (((1,), (0,)), ((), ())), preferred_element_type=F32)


def dot_back(left, right):
    return lax.dot_general(left, right, (((1,), (1,)), ((), ())), preferred_element_type=F32)


def dot_outer(left, right):
    return lax.dot_general(left, right, (((0,), (0,)), ((), ())), preferred_element_type=F32)


def rows_at(start, count=CHUNK):
    return pl.ds(pl.multiple_of(start, CHUNK), count)


def gelu_both(value):
    square = value * value
    inside = GELU_A * value * (1.0 + GELU_B * square)
    tanh = jnp.tanh(inside)
    half = 0.5 + 0.5 * tanh
    slope = half + 0.5 * value * (1.0 - tanh * tanh) * (GELU_A * (1.0 + 3.0 * GELU_B * square))
    return value * half, slope


def sigmoid(value):
    return 1.0 / (1.0 + jnp.exp(-value))


def one_less_exp(z, exp_z):
    series = 1.0 + z * (1 / 2 + z * (1 / 6 + z * (1 / 24 + z * (1 / 120 + z * (1 / 720)))))
    return jnp.where(z > -0.25, -z * series, 1.0 - exp_z)


def in_row(row, width, shape):
    return row + lax.broadcasted_iota(jnp.int32, shape, 0)


def each_chunk(batch, width, body, carry=0):
    per = width // CHUNK
    for b in range(batch):
        carry = lax.fori_loop(0, per, lambda i, c, b=b: body(b, i * CHUNK, b * width + i * CHUNK, c), carry)
    return carry


def each_tile(batch, width, tiles, body, carry=None):
    carries = []
    for t in range(tiles):
        kept = carry
        for b in range(batch):
            def one(i, c, t=t, b=b):
                return body(t, b, i * TALL, rows_at(b * width + i * TALL, TALL), slice(t * LANES, (t + 1) * LANES), c)
            kept = lax.fori_loop(0, width // TALL, one, 0 if kept is None else kept)
        carries.append(kept)
    return carries


def strided(b, width, step):
    return pl.ds(b * width + step, SEGS, stride=width // SEGS)


def lanes(t):
    return slice(t * LANES, (t + 1) * LANES)


def spread(ref, value):
    for t in range(ref.shape[0]):
        ref[t] = value[:, lanes(t)]


def tiled(tokens, block, index):
    return pl.BlockSpec((block // LANES, tokens, LANES), lambda j: (index(j), 0, 0))


def pair_cols(tile, second):
    block = lax.div(tile, W // LANES)
    return pl.ds(pl.multiple_of(tile * LANES + (block + second) * W, LANES), LANES)


def inverse_norm(value, depth):
    return lax.rsqrt(jnp.sum(value * value, axis=-1, keepdims=True) * (1.0 / depth) + eps)


def fold8(value):
    total = value[:8]
    for i in range(8, value.shape[0], 8):
        total = total + value[i : i + 8]
    return total


def ffn_kernel(batch, width, info_ref, first_ref, normed_ref, cot_ref, gain_ref, wu_ref, wd_ref,
               out_ref, dfirst_ref, dlow_ref, ggain_ref, grad_ref,
               low, tall, hid, acc, dn, pair, du, stage, dstage, sem):
    step = pl.program_id(0)
    tokens, depth = first_ref.shape
    n = grad_ref.shape[0]
    group, drows = wd_ref.shape[:2]
    wide = group * drows
    rows = depth // n
    nd, nw = n // group, hid.shape[1] // W
    tiles = W // LANES

    def block_out(j):
        return pltpu.make_async_copy(stage, grad_ref.at[:, pl.ds(pl.multiple_of(UPS_AT + j * rows, rows), rows)], sem.at[0])

    def down_out(k):
        return pltpu.make_async_copy(dstage, grad_ref.at[pl.ds(k * group, group), pl.ds(DOWN_AT, drows)], sem.at[1])

    @pl.when(step == 0)
    def _():
        def masked(b, spot, row, _):
            at = rows_at(row)
            value = cot_ref[at]
            valid = in_row(spot, width, value.shape) < info_ref[b]
            low[at] = jnp.where(valid, value.astype(F32), 0.0).astype(BF16)
            return 0
        each_chunk(batch, width, masked)

    @pl.when(step < nd)
    def _():
        total = dot_back(low[...], wd_ref[...].reshape(wide, depth))
        for t in range(wide // LANES):
            tall[jnp.minimum(step, nd - 1) * (wide // LANES) + t] = total[:, lanes(t)]

    @pl.when(jnp.logical_and(step >= nd, step < nd + nw))
    def _():
        j = jnp.clip(step - nd, 0, nw - 1)
        weights = wu_ref[...].reshape(depth, PACK)
        spread(pair, dot(normed_ref[...], weights))

        def gating(t, b, spot, at, cols, _):
            gate, slope = gelu_both(pair[t, at])
            mix, d = pair[tiles + t, at], tall[j * tiles + t, at]
            hid[at, pl.ds(pl.multiple_of(j * W + t * LANES, LANES), LANES)] = (gate * mix).astype(BF16)
            du[at, cols] = (d * mix * slope).astype(BF16)
            du[at, lanes(tiles + t)] = (d * gate).astype(BF16)
            return 0
        each_tile(batch, width, tiles, gating)
        more = dot_back(du[...], weights)

        @pl.when(j == 0)
        def _():
            dn[...] = more

        @pl.when(j > 0)
        def _():
            dn[...] += more
        value = dot_outer(normed_ref[...], du[...]).astype(BF16).reshape(n, rows, PACK)
        pl.when(j > 0)(lambda: block_out(0).wait())
        stage[...] = value
        block_out(j).start()

    @pl.when(step >= nd + nw)
    def _():
        k = jnp.clip(step - nd - nw, 0, nd - 1)
        block = hid[:, pl.ds(pl.multiple_of(k * wide, wide), wide)]
        more = dot(block, wd_ref[...].reshape(wide, depth))

        @pl.when(k == 0)
        def _():
            acc[...] = more

        @pl.when(k > 0)
        def _():
            acc[...] += more
        value = dot_outer(block, low[...]).astype(BF16).reshape(group, drows, depth)
        pl.when(k > 0)(lambda: down_out(0).wait())
        dstage[...] = value
        down_out(k).start()

    @pl.when(step == pl.num_programs(0) - 1)
    def _():
        def finish(b, spot, row, total):
            at = rows_at(row)
            first, cot = first_ref[at], low[at].astype(F32)
            valid = in_row(spot, width, first.shape) < info_ref[b]
            out_ref[at] = jnp.where(valid, first + acc[at], 0.0)
            grad = dn[at]
            scale = inverse_norm(first, depth)
            weighted = grad * gain_ref[:1]
            mean = jnp.sum(weighted * first, axis=-1, keepdims=True) * (1.0 / depth)
            back = cot + scale * weighted - first * (scale * scale * scale * mean)
            for t in range(depth // LANES):
                dfirst_ref[t, at] = back[:, lanes(t)]
            dlow_ref[at] = back.astype(BF16)
            return total + fold8(grad * first * scale)
        ggain_ref[...] = each_chunk(batch, width, finish, jnp.zeros((8, depth), F32))
        block_out(0).wait()
        down_out(0).wait()


def feed_forward(info, first, normed_two, cot, gain, packed, f, batch):
    tokens, depth = first.shape
    width = tokens // batch
    n = packed.shape[0]
    rows, drows = depth // n, f // n
    group = 8
    wide = group * drows
    nd, nw = f // wide, f // W
    full = lambda shape: pl.BlockSpec(shape, lambda j: (0,) * len(shape))
    clamp = lambda j, low, count: jnp.clip(j - low, 0, count - 1)

    def down_block(j):
        return (jnp.where(j < nd, jnp.minimum(j, nd - 1), clamp(j, nd + nw, nd)), DOWN_AT // drows, 0)
    vm = pltpu.VMEM
    S = jax.ShapeDtypeStruct
    return pl.pallas_call(
        functools.partial(ffn_kernel, batch, width),
        grid=(nd + nw + nd,),
        in_specs=[pl.BlockSpec(memory_space=pltpu.SMEM), full(first.shape), full(normed_two.shape), full(cot.shape),
                  full(gain.shape), pl.BlockSpec((n, rows, PACK), lambda j: (0, UPS_AT // rows + clamp(j, nd, nw), 0)),
                  pl.BlockSpec((group, drows, depth), down_block)],
        out_specs=[full((tokens, depth)), full((depth // LANES, tokens, LANES)), full((tokens, depth)), full((8, depth)),
                   pl.BlockSpec(memory_space=pl.ANY)],
        out_shape=[S((tokens, depth), F32), S((depth // LANES, tokens, LANES), F32), S((tokens, depth), BF16),
                   S((8, depth), F32), S((n, FFN_ROWS, PACK), BF16)],
        scratch_shapes=[vm((tokens, depth), BF16), vm((f // LANES, tokens, LANES), F32), vm((tokens, f), BF16),
                        vm((tokens, depth), F32), vm((tokens, depth), F32), vm((PACK // LANES, tokens, LANES), F32),
                        vm((tokens, PACK), BF16), vm((n, rows, PACK), BF16), vm((group, drows, depth), BF16),
                        pltpu.SemaphoreType.DMA((2,))],
        compiler_params=pltpu.CompilerParams(vmem_limit_bytes=60 << 20),
    )(info, first, normed_two, cot, gain, packed, packed)


MESH = pl.DeviceIdType.MESH
ROUTES = (("z", "x", "y"), ("z", "y", "x"), ("x", "z", "y"), ("y", "z", "x"))
ZN = 4
STG = 4
SEM = pltpu.SemaphoreType.DMA


def place():
    s = lax.axis_index("seq")
    return lax.rem(s, 2), lax.rem(lax.div(s, 2), 2), lax.div(s, 4), lax.axis_index("batch")


def flip(value, by):
    return 1 - value if by else value


def seq_of(y, x, c):
    return (y * 2 + x) * 2 + c


def far(z, j):
    if j == ZN - 1:
        return z
    found = None
    for here in range(ZN):
        others = sorted((q for q in range(ZN) if q != here), key=lambda q: (-abs(q - here), q))
        found = jnp.int32(others[j]) if found is None else jnp.where(z == here, others[j], found)
    return found


class Links:
    def __init__(self):
        self.c, self.x, self.y, self.z = c, x, y, z = place()
        self.beside = {
            "x": (seq_of(y, 1 - x, c), z),
            "y": (seq_of(1 - y, x, c), z),
            "up": (seq_of(y, x, c), z + 1),
            "dn": (seq_of(y, x, c), z - 1),
            "core": (seq_of(y, x, 1 - c), z),
        }
        self.spots = [far(z, j) for j in range(ZN)]
        self.above, self.below = z < ZN - 1, z > 0

    def slot(self, dx, dy, z, core):
        return seq_of(flip(self.y, dy), flip(self.x, dx), core) * ZN + z

    def copy(self, src, dst, send, recv, d):
        return pltpu.make_async_remote_copy(src, dst, send, recv, device_id=self.beside[d], device_id_type=MESH)


def greet(links, swap):
    bar = pltpu.get_barrier_semaphore()
    count = 0
    if swap is not None:
        count = swap.n - 1
        for k in range(1, swap.n):
            pl.semaphore_signal(bar, inc=1, device_id=swap.peer(k), device_id_type=MESH)
    if links is not None:
        def signal(d):
            pl.semaphore_signal(bar, inc=1, device_id=links.beside[d], device_id_type=MESH)
        if swap is None:
            count = 3
            for d in ("x", "y", "core"):
                signal(d)
        pl.when(links.above)(lambda: signal("up"))
        pl.when(links.below)(lambda: signal("dn"))
        count = count + links.above.astype(jnp.int32) + links.below.astype(jnp.int32)
    pl.semaphore_wait(bar, count)


class Exchange:
    def __init__(self, n, rows, land, send, recv, own):
        self.n, self.rows, self.land, self.send, self.recv, self.own = n, rows, land, send, recv, own
        self.me, self.z = lax.axis_index("seq"), lax.axis_index("batch")

    @staticmethod
    def scratch(n, shape):
        return [pltpu.VMEM(shape, F32), pltpu.VMEM((n,) + shape, F32), SEM((n,)), SEM((n,)), SEM]

    def peer(self, k):
        return (lax.rem(self.me + k, self.n), self.z)

    def copies(self):
        return [
            pltpu.make_async_remote_copy(self.rows, self.land.at[self.me], self.send.at[k], self.recv.at[k],
                                         device_id=self.peer(k), device_id_type=MESH)
            for k in range(1, self.n)
        ]

    def mine(self):
        return pltpu.make_async_copy(self.rows, self.land.at[self.me], self.own)

    def begin(self):
        self.mine().start()
        for copy in self.copies():
            copy.start()

    def finish(self):
        self.mine().wait()
        for copy in self.copies():
            copy.wait()


def onward(order, dx, dy, same):
    off = {"x": dx, "y": dy, "z": 0 if same else 1}
    return [
        d for i, d in enumerate(order)
        if not any(off[e] for e in order[i + 1 :]) and not (d != "z" and off[d])
    ]


def arrival(order, dx, dy, same):
    off = {"x": dx, "y": dy, "z": 0 if same else 1}
    return [d for d in order if off[d]][-1]


def blocks(parts):
    found = [
        (dx + dy + ZN - 1 - j, r, dx, dy, j)
        for dx in range(2) for dy in range(2) for j in range(ZN) for r in range(len(parts))
    ]
    return found


class Gather:
    def __init__(self, parts, ins, outs, send, recv, csend, crecv, lsem):
        self.parts, self.ins, self.outs = parts, ins, outs
        self.send, self.recv, self.csend, self.crecv, self.lsem = send, recv, csend, crecv, lsem
        self.links = Links()
        self.events = blocks(parts)

    @staticmethod
    def scratch(parts):
        n = len(parts)
        return [SEM((n, 4, 4, ZN)), SEM((n, 4, ZN)), SEM((n, 4, ZN)), SEM((n, 4, ZN)), SEM((n,))]

    def window(self, r):
        return pl.ds(self.parts[r][2], self.parts[r][3])

    def dst(self, r, dx, dy, zs):
        return self.outs[self.parts[r][1]].at[self.links.slot(dx, dy, zs, self.links.c), self.window(r)]

    def src(self, r, dx, dy, zs, own):
        return self.ins[self.parts[r][0]].at[self.window(r)] if own else self.dst(r, dx, dy, zs)

    def hop(self, r, dx, dy, zs, d, own):
        to = (1 if d == "x" else dx) * 2 + (1 if d == "y" else dy)
        which = ("x", "y", "up", "dn").index(d)
        return self.links.copy(self.src(r, dx, dy, zs, own), self.dst(r, dx, dy, zs),
                               self.send.at[r, which, dx * 2 + dy, zs], self.recv.at[r, to, zs], d)

    def across(self, r, dx, dy, zs, own):
        return self.links.copy(self.src(r, dx, dy, zs, own), self.dst(r, dx, dy, zs),
                               self.csend.at[r, dx * 2 + dy, zs], self.crecv.at[r, dx * 2 + dy, zs], "core")

    def hops(self, r, dx, dy, j, act):
        links, zs = self.links, self.links.spots[j]
        z, same = links.z, j == ZN - 1
        own = same and not dx and not dy
        for d in onward(ROUTES[self.parts[r][4]], dx, dy, same):
            if d != "z":
                act(self.hop(r, dx, dy, zs, d, own))
                continue
            up = links.above if same else jnp.logical_and(z > zs, links.above)
            down = links.below if same else jnp.logical_and(z < zs, links.below)
            pl.when(up)(lambda: act(self.hop(r, dx, dy, zs, "up", own)))
            pl.when(down)(lambda: act(self.hop(r, dx, dy, zs, "dn", own)))

    def forward(self, event):
        _, r, dx, dy, j = event
        zs, own = self.links.spots[j], j == ZN - 1 and not dx and not dy
        if not own:
            self.links.copy(self.dst(r, dx, dy, zs), self.dst(r, dx, dy, zs), self.send.at[r, 0, 0, 0],
                            self.recv.at[r, dx * 2 + dy, zs], "core").wait_recv()
        self.hops(r, dx, dy, j, lambda copy: copy.start())
        self.across(r, dx, dy, zs, own).start()
        if own:
            self.local(r).start()

    def local(self, r):
        return pltpu.make_async_copy(self.ins[self.parts[r][0]].at[self.window(r)],
                                     self.dst(r, 0, 0, self.links.z), self.lsem.at[r])

    def arrived(self, parts):
        for _, r, dx, dy, j in self.events:
            if r in parts:
                own = j == ZN - 1 and not dx and not dy
                self.across(r, dx, dy, self.links.spots[j], own).wait_recv()
                if own:
                    self.local(r).wait()

    def sent(self):
        for _, r, dx, dy, j in self.events:
            own = j == ZN - 1 and not dx and not dy
            self.hops(r, dx, dy, j, lambda copy: copy.wait_send())
            self.across(r, dx, dy, self.links.spots[j], own).wait_send()


def layout(order):
    base, count = {}, 0
    for i, d in enumerate(order):
        base[d] = count
        free = 1
        for e in order[:i]:
            free *= ZN if e == "z" else 2
        count += free * ((ZN + 1) if d == "z" else 1)
    return base, count


class Scatter:
    def __init__(self, parts, order, ins, out, sib, stage, ring, fin, csend, crecv, lsem, send, fsem, *rest):
        self.parts, self.ins, self.out, self.sib = parts, ins, out, sib
        self.stage, self.ring, self.fin = stage, ring, fin
        self.ahead, self.slots = stage.shape[0], ring.shape[0]
        self.csend, self.crecv, self.lsem, self.send, self.fsem = csend, crecv, lsem, send, fsem
        self.bufs, self.recv = rest[: len(parts)], rest[len(parts) :]
        self.links = Links()
        self.lay = [layout(ROUTES[part[3]]) for part in parts]
        rows = [part[2] for part in parts]
        self.starts = [sum(rows[:r]) for r in range(len(parts))]
        every = blocks(parts)
        self.events = [every[number] for number in order]
        self.leaves = [bool(j != ZN - 1 or dx or dy) for _, _, dx, dy, j in self.events]

    def sent_before(self, i):
        return {k % self.slots: k for k in range(i) if self.leaves[k]}

    def finals_before(self, i):
        return [k for k in range(i) if not self.leaves[k]]

    @staticmethod
    def buffers(parts):
        total = sum(part[2] for part in parts)
        S = jax.ShapeDtypeStruct
        return [S((total, PACK), jnp.float32), S((4 * ZN * total, PACK), jnp.bfloat16)]

    @staticmethod
    def scratch(parts, ahead, slots):
        n, most = len(parts), max(part[2] for part in parts)
        counts = [layout(ROUTES[part[3]])[1] for part in parts]
        return [pltpu.VMEM((ahead, 2, most, PACK), jnp.bfloat16), pltpu.VMEM((slots, most, PACK), jnp.bfloat16),
                pltpu.VMEM((2, most, PACK), jnp.float32), SEM((n,)), SEM((n, 4, ZN)), SEM((ahead, 2)), SEM((slots,)),
                SEM((2,))] + [
            pltpu.VMEM((count, part[2], PACK), jnp.bfloat16) for count, part in zip(counts, parts)
        ] + [SEM((count,)) for count in counts]

    def source(self, r, dx, dy, zd, core):
        which, start, rows, _ = self.parts[r]
        return self.ins[which].at[self.links.slot(dx, dy, zd, core), pl.ds(start, rows)]

    def sibling(self, r, dx, dy, zd):
        count = self.parts[r][2]
        start = 4 * ZN * self.starts[r] + ((dx * 2 + dy) * ZN + zd) * count
        return self.sib.at[pl.ds(pl.multiple_of(start, 16), count)]

    def child(self, r, d, dx, dy, zd):
        order = ROUTES[self.parts[r][3]]
        dim = d if d in "xy" else "z"
        index = 0
        for e in order[: order.index(dim)]:
            index = index * ZN + zd if e == "z" else index * 2 + (dx if e == "x" else dy)
        if dim == "z":
            index = index * (ZN + 1) + (zd if d == "up" else zd + 1)
        return self.lay[r][0][dim] + index

    def across(self, i):
        _, r, dx, dy, j = self.events[i]
        zd = self.links.spots[j]
        return self.links.copy(self.source(r, dx, dy, zd, 1 - self.links.c), self.sibling(r, dx, dy, zd),
                               self.csend.at[r], self.crecv.at[r, dx * 2 + dy, zd], "core")

    def begin(self):
        for i in range(len(self.events)):
            self.across(i).start()
        for i in range(self.ahead - 1):
            self.prefetch(i)

    def loads(self, i):
        _, r, dx, dy, j = self.events[i]
        zd, s, count = self.links.spots[j], i % self.ahead, self.parts[r][2]
        return [
            pltpu.make_async_copy(ref, self.stage.at[s, k, pl.ds(0, count)], self.lsem.at[s, k])
            for k, ref in enumerate((self.source(r, dx, dy, zd, self.links.c), self.sibling(r, dx, dy, zd)))
        ]

    def prefetch(self, i):
        own, other = self.loads(i)
        own.start()
        self.across(i).wait_recv()
        other.start()

    def terms(self, i):
        _, r, dx, dy, j = self.events[i]
        same = j == ZN - 1
        kids = onward(ROUTES[self.parts[r][3]], dx, dy, same)
        z, zd = self.links.z, self.links.spots[j]
        found = [(self.child(r, d, dx, dy, zd), None) for d in kids if d != "z"]
        if "z" in kids:
            up, down = self.child(r, "up", dx, dy, zd), self.child(r, "dn", dx, dy, zd)
            if same:
                found += [(up, self.links.above), (down, self.links.below)]
            else:
                found.append((jnp.where(z > zd, up, down), jnp.logical_and(self.links.above, self.links.below)))
        return found

    def hop(self, i, d):
        _, r, dx, dy, j = self.events[i]
        zd, q = self.links.spots[j], i % self.slots
        came = {"x": "x", "y": "y", "up": "dn", "dn": "up"}[d]
        at = self.child(r, came, 0 if d == "x" else dx, 0 if d == "y" else dy, zd)
        return self.links.copy(self.ring.at[q, pl.ds(0, self.parts[r][2])], self.bufs[r].at[at],
                               self.send.at[q], self.recv[r].at[at], d)

    def result(self, i, slot):
        r = self.events[i][1]
        count = self.parts[r][2]
        return pltpu.make_async_copy(self.fin.at[slot, pl.ds(0, count)], self.out.at[pl.ds(self.starts[r], count)],
                                     self.fsem.at[slot])

    def step(self, i):
        _, r, dx, dy, j = self.events[i]
        zd, z, s, q = self.links.spots[j], self.links.z, i % self.ahead, i % self.slots
        if i + self.ahead - 1 < len(self.events):
            self.prefetch(i + self.ahead - 1)
        leaves, finals = self.leaves[i], self.finals_before(i)
        slot = len(finals) % 2
        if leaves and q in self.sent_before(i):
            self.hop(self.sent_before(i)[q], "x").wait_send()
        if not leaves and len(finals) > 1:
            self.result(finals[-2], slot).wait()
        for load in self.loads(i):
            load.wait()
        terms = self.terms(i)
        for at, cond in terms:
            slab = self.bufs[r].at[at]
            arrived = self.links.copy(slab, slab, self.send.at[0], self.recv[r].at[at], "core")
            if cond is None:
                arrived.wait_recv()
            else:
                pl.when(cond)(arrived.wait_recv)

        def body(k, _):
            rows = pl.ds(pl.multiple_of(k * 16, 16), 16)
            total = self.stage[s, 0, rows].astype(jnp.float32) + self.stage[s, 1, rows].astype(jnp.float32)
            for at, cond in terms:
                more = self.bufs[r][at, rows].astype(jnp.float32)
                total = total + (more if cond is None else jnp.where(cond, more, 0.0))
            if leaves:
                self.ring[q, rows] = total.astype(jnp.bfloat16)
            else:
                self.fin[slot, rows] = total
            return 0
        lax.fori_loop(0, self.parts[r][2] // 16, body, 0, unroll=3 if self.parts[r][2] % 48 == 0 else 1)
        if not leaves:
            self.result(i, slot).start()
            return
        d = arrival(ROUTES[self.parts[r][3]], dx, dy, j == ZN - 1)
        if d == "z":
            pl.when(zd > z)(lambda: self.hop(i, "up").start())
            pl.when(zd < z)(lambda: self.hop(i, "dn").start())
        else:
            self.hop(i, d).start()

    def finish(self):
        for i in self.sent_before(len(self.events)).values():
            self.hop(i, "x").wait_send()
        finals = self.finals_before(len(self.events))
        for k in range(max(0, len(finals) - 2), len(finals)):
            self.result(finals[k], k % 2).wait()
        for r, part in enumerate(self.parts):
            whole = self.sib.at[pl.ds(4 * ZN * self.starts[r], 4 * ZN * part[2])]
            self.links.copy(whole, whole, self.csend.at[r], self.crecv.at[r, 0, 0], "core").wait_send()


def scatter(parts, order, ins):
    n = len(ins)

    def kernel(*refs):
        job = Scatter(parts, order, refs[:n], *refs[n:])
        greet(job.links, None)
        job.begin()
        for i in range(len(job.events)):
            job.step(i)
        job.finish()
    anywhere = pl.BlockSpec(memory_space=pl.ANY)
    outs = Scatter.buffers(parts)
    return pl.pallas_call(
        kernel,
        out_shape=outs,
        in_specs=[anywhere] * n,
        out_specs=[anywhere] * len(outs),
        scratch_shapes=Scatter.scratch(parts, 4, 24),
        compiler_params=pltpu.CompilerParams(collective_id=2, has_side_effects=True, vmem_limit_bytes=60 << 20),
    )(*ins)[0]


class Sends:
    def __init__(self, sems):
        self.sems, self.used = sems, []

    def add(self, src, dst):
        copy = pltpu.make_async_copy(src, dst, self.sems.at[len(self.used)])
        self.used.append(copy)
        return copy

    def finish(self):
        for copy in self.used:
            copy.wait()


def undeal(lines, n, count):
    length = n * count
    spot = lax.broadcasted_iota(jnp.int32, (LANES, length), 1)
    row = lax.broadcasted_iota(jnp.int32, (LANES, length), 0)
    pick = jnp.where(lax.rem(spot, count) == row, 1.0, 0.0).astype(BF16)
    lane = lax.broadcasted_iota(jnp.int32, (n, length), 1)
    owner = lax.broadcasted_iota(jnp.int32, (n, length), 0)
    own = jnp.logical_and(lane >= owner * count, lane < (owner + 1) * count)
    return jnp.sum(jnp.where(own, dot(lines, pick), 0.0), axis=0, keepdims=True)


def softplus(value):
    small = jnp.exp(-jnp.abs(value))
    series = small * (1.0 - small * (1 / 2 - small * (1 / 3 - small * (1 / 4 - small * (1 / 5 - small * (1 / 6))))))
    return jnp.maximum(value, 0.0) + jnp.where(small < 0.02, series, jnp.log(1.0 + small))


FORWARD_OUTS = 13
GATHER_PARTS = ((0, 0, 0, 64, 0), (0, 0, 64, 80, 1), (0, 0, 144, 80, 2), (0, 0, 224, 80, 3),
                (1, 1, 0, 64, 0), (1, 1, 64, 80, 1), (1, 1, 144, 64, 2), (1, 1, 208, 80, 3))
REC_PARTS = (0, 1, 2, 3)
FORWARD_PLAN = (
    (24, 25, 26, 27, 89, 17, 9, 59, 1, 18, 16, 8, 19, 90, 49, 11, 91, 48, 58, 10, 2, 57, 88, 28, 0, 82, 51, 56, 3, 65, 73, 121, 113, 75, 43, 42, 74, 41, 50, 30, 33, 115, 80, 31, 123, 66, 72, 60, 35, 29, 112, 64, 81, 106, 67, 32, 120, 34, 22, 23, 105, 94, 114, 107, 122, 14, 97, 95, 98, 15, 62, 104, 83, 63, 20, 92, 21, 40, 61, 96, 99),
    (),
    (),
    (12,),
    (13,),
    (55,),
    (87,),
    (6,),
    (84,),
    (47,),
    (86,),
    (125, 4),
    (45,),
    (38,),
    (),
    (119, 7),
    (36, 5),
    (53, 124, 79, 126, 78),
    (68,),
    (),
    (111, 116, 46, 118),
    (69, 37, 76, 85, 93, 39),
    (117,),
    (77, 54, 70),
    (108, 71, 52, 109, 102, 127, 110, 44, 101, 100, 103),
)


def forward_kernel(batch, width, n_seq, info_ref, x_ref, rim_ref, lines_ref, *refs):
    shards, refs = refs[:8], refs[8:]
    outs, refs = refs[:FORWARD_OUTS], refs[FORWARD_OUTS:]
    (gate_o, inner_o, mixed_o, normed_o, rate_o, entry_o, decay_o, states_o, pseg_o, sstart_o, all_o,
     gated_o, first_o) = outs
    normed2_o, vec_o, gain_o, gain2_o, weights, ffn_weights = refs[:6]
    (ext, gate, inner, mixed, rate, entry, decay, drive, states, pseg, hseg, sstart, gated, first, normed2,
     vec_ref, gain_ref, gain2_ref, small, wbuf, shard_ref, ffn_shard_ref, sems, wsem, psem) = refs[6:31]
    swap = Exchange(n_seq, *refs[31:36])
    job = Gather(GATHER_PARTS, [shard_ref, ffn_shard_ref], [weights, ffn_weights], *refs[36:])
    step = pl.program_id(0)
    tokens, depth = x_ref.shape
    r = mixed.shape[1]
    parts, tiles = r // W, W // LANES
    step = step - 1
    steps = 3 * parts + 1
    span = width + 8
    n = weights.shape[0]
    rows, rrows = depth // n, r // n

    def pump(half, low, high):
        for s in range(low, high):
            numbers = FORWARD_PLAN[4 + 2 * s + half]
            if numbers:
                @pl.when(step == s)
                def _():
                    for number in numbers:
                        job.forward(job.events[number])

    def pack():
        gate_w, input_w, rate_w, entry_w, out_w, ffn_gate_w, ffn_up_w, ffn_down_w = shards
        moves = ([], [])
        for which, one, two, base in ((0, rate_w, entry_w, GATES_AT), (0, gate_w, input_w, IN_AT), (1, ffn_gate_w, ffn_up_w, UPS_AT)):
            count, length = one.shape
            to = (shard_ref, ffn_shard_ref)[which]
            for j in range(length // W):
                for half, src in enumerate((one, two)):
                    moves[which].append((src.at[:, pl.ds(j * W, W)], to.at[pl.ds(base + j * count, count), pl.ds(half * W, W)]))
        moves[0].append((out_w, shard_ref.at[pl.ds(OUT_AT, rrows)]))
        moves[0].append((lines_ref, shard_ref.at[pl.ds(REC_ROWS, SMALL_ROWS)]))
        moves[1].append((ffn_down_w, ffn_shard_ref.at[pl.ds(DOWN_AT, ffn_down_w.shape[0])]))
        copies, k = ([], []), 0
        for which in range(2):
            for src, dst in moves[which]:
                copies[which].append(pltpu.make_async_copy(src, dst, psem.at[k]))
                k += 1
        return copies

    blocks_at = [(IN_AT + j * rows, rows) for j in range(parts)] + [(GATES_AT + j * rrows, rrows) for j in range(parts)]
    blocks_at += [(OUT_AT, rrows)]

    def load(k):
        start, count = blocks_at[k]
        return pltpu.make_async_copy(weights.at[:, pl.ds(start, count)], wbuf.at[k % 2, :, pl.ds(0, count)], wsem.at[k % 2])

    def next_block(k):
        if k + 1 < len(blocks_at):
            load(k + 1).start()
        load(k).wait()
    sends = Sends(sems)
    branch_sends = [sends.add(gate, gate_o), sends.add(inner, inner_o), sends.add(mixed, mixed_o),
                    sends.add(ext.at[pl.ds(0, tokens)], normed_o)]
    gate_sends = [sends.add(rate, rate_o), sends.add(entry, entry_o), sends.add(decay, decay_o), sends.add(pseg, pseg_o)]
    state_sends = [sends.add(states, states_o), sends.add(sstart, sstart_o), sends.add(swap.land, all_o),
                   sends.add(gated, gated_o)]
    last_sends = [sends.add(first, first_o), sends.add(normed2, normed2_o)]
    vector_sends = [sends.add(vec_ref, vec_o), sends.add(gain_ref, gain_o), sends.add(gain2_ref, gain2_o)]

    def start(copies):
        for copy in copies:
            copy.start()

    @pl.when(step < 0)
    def _():
        packing = pack()
        start(packing[0] + packing[1])
        greet(job.links, swap)
        for copy in packing[0]:
            copy.wait()
        numbers = FORWARD_PLAN[0]
        for number in numbers[: len(REC_PARTS)]:
            job.forward(job.events[number])
        for copy in packing[1]:
            copy.wait()

        def scaled(i, _):
            at = rows_at(i * CHUNK)
            value = x_ref[at].astype(F32)
            first[at] = value * inverse_norm(value, depth)
            return 0
        lax.fori_loop(0, tokens // CHUNK, scaled, 0)
        for number in numbers[len(REC_PARTS) :]:
            job.forward(job.events[number])
        job.arrived(REC_PARTS)
        lines_in = pltpu.make_async_copy(weights.at[:, pl.ds(REC_ROWS, SMALL_ROWS), pl.ds(0, LANES)], small, wsem.at[1])
        lines_in.start()
        load(0).start()
        for number in FORWARD_PLAN[1]:
            job.forward(job.events[number])
        lines_in.wait()
        lines = small[...].astype(F32)
        found = [undeal(lines[:, k].astype(BF16), n, rows if k < 2 else rrows) for k in range(10)]
        gain_ref[...] = jnp.broadcast_to(found[0], gain_ref.shape)
        gain2_ref[...] = jnp.broadcast_to(found[1], gain2_ref.shape)
        vec_ref[...] = jnp.zeros_like(vec_ref)
        for k in range(7):
            vec_ref[k : k + 1] = found[2 + k]
        vec_ref[COEF : COEF + 1] = -lru_scale * softplus(-found[9])
        vec_ref[SIG : SIG + 1] = sigmoid(-found[9])
        for number in FORWARD_PLAN[2]:
            job.forward(job.events[number])
        gain = gain_ref[:1]

        def norm(i, _):
            at = rows_at(i * CHUNK)
            ext[at] = (first[at] * gain).astype(BF16)
            return 0
        lax.fori_loop(0, tokens // CHUNK, norm, 0)
        rim = rim_ref[...].astype(F32)
        ext[pl.ds(tokens, rim.shape[0])] = (rim * inverse_norm(rim, depth) * gain).astype(BF16)
        start(vector_sends)
        for number in FORWARD_PLAN[3]:
            job.forward(job.events[number])

    for k, s in enumerate(list(range(2 * parts)) + [3 * parts]):
        pl.when(step == s)(lambda k=k: next_block(k))

    @pl.when(jnp.logical_and(step >= 0, step < parts))
    def _():
        j = jnp.clip(step, 0, parts - 1)
        slot = lax.rem(j, 2)
        here = pl.ds(pl.multiple_of(j * W, W), W)
        pump(0, 0, parts)
        got = dot(ext[...], wbuf[slot, :, :rows].reshape(depth, PACK))
        for t in range(tiles):
            gate[j * tiles + t] = got[:tokens, lanes(t)]
        for b in range(batch):
            inner[b * span : b * span + 8, here] = got[tokens + 8 * b : tokens + 8 * b + 8, W:]
            inner[b * span + 8 : (b + 1) * span, here] = got[b * width : (b + 1) * width, W:]
        pump(1, 0, parts)
        for b in range(batch):
            conv = vec_ref[CONV_BIAS : CONV_BIAS + 1, here]
            for lag in range(4):
                conv = conv + vec_ref[lag : lag + 1, here] * inner[b * span + 8 - lag : (b + 1) * span - lag, here]
            mixed[b * width : (b + 1) * width, here] = conv.astype(BF16)

    @pl.when(step == parts - 1)
    def _():
        start(branch_sends)

    @pl.when(jnp.logical_and(step >= parts, step < 2 * parts))
    def _():
        j = jnp.clip(step - parts, 0, parts - 1)
        slot = lax.rem(j + parts, 2)
        pump(0, parts, 2 * parts)
        got = dot(mixed[...], wbuf[slot].reshape(r, PACK))
        for t in range(tiles):
            rate[j * tiles + t] = got[:, lanes(t)]
            entry[j * tiles + t] = got[:, lanes(tiles + t)]
        pump(1, parts, 2 * parts)

        def gating(t, b, spot, at, cols, _):
            g = j * tiles + t
            tile = pl.ds(pl.multiple_of(j * W + t * LANES, LANES), LANES)
            a_rate = sigmoid(rate[g, at] + vec_ref[RATE_BIAS : RATE_BIAS + 1, tile])
            an_entry = sigmoid(entry[g, at] + vec_ref[ENTRY_BIAS : ENTRY_BIAS + 1, tile])
            log_decay = vec_ref[COEF : COEF + 1, tile] * a_rate
            z = 2.0 * log_decay
            root = jnp.sqrt(one_less_exp(z, jnp.exp(z)))
            valid = in_row(spot, width, a_rate.shape) < info_ref[b]
            rate[g, at] = a_rate
            entry[g, at] = an_entry
            decay[g, at] = jnp.where(valid, jnp.exp(log_decay), 1.0)
            drive[g, at] = jnp.where(valid, root * an_entry * mixed[at, tile].astype(F32), 0.0)
            return 0
        each_tile(batch, width, tiles, gating)
        for t in range(tiles):
            g = j * tiles + t
            tile = pl.ds(pl.multiple_of(j * W + t * LANES, LANES), LANES)
            for b in range(batch):
                prod = jnp.ones((SEGS, LANES), F32)
                state = jnp.zeros((SEGS, LANES), F32)
                for s in range(width // SEGS):
                    at = strided(b, width, s)
                    a = decay[g, at]
                    state = a * state + drive[g, at]
                    prod = prod * a
                pseg[b * SEGS : (b + 1) * SEGS, tile] = prod
                hseg[b * SEGS : (b + 1) * SEGS, tile] = state
                whole, end = prod[:1], state[:1]
                for i in range(1, SEGS):
                    whole = whole * prod[i : i + 1]
                    end = prod[i : i + 1] * end + state[i : i + 1]
                swap.rows[g, b : b + 1] = whole
                swap.rows[g, batch + b : batch + b + 1] = end

    @pl.when(step == 2 * parts - 1)
    def _():
        start(gate_sends)
        swap.begin()

    @pl.when(step == 2 * parts)
    def _():
        swap.finish()

    @pl.when(jnp.logical_and(step >= 2 * parts, step < 3 * parts))
    def _():
        j = jnp.clip(step - 2 * parts, 0, parts - 1)
        me = lax.axis_index("seq")
        pump(0, 2 * parts, 3 * parts)
        for t in range(tiles):
            g = j * tiles + t
            tile = pl.ds(pl.multiple_of(j * W + t * LANES, LANES), LANES)
            for b in range(batch):
                begin = jnp.zeros((1, LANES), F32)
                for k in range(n_seq):
                    new = swap.land[k, g, b : b + 1] * begin + swap.land[k, g, batch + b : batch + b + 1]
                    begin = jnp.where(k < me, new, begin)
                for i in range(SEGS):
                    at = b * SEGS + i
                    sstart[at : at + 1, tile] = begin
                    begin = pseg[at : at + 1, tile] * begin + hseg[at : at + 1, tile]
                state = sstart[b * SEGS : (b + 1) * SEGS, tile]
                for s in range(width // SEGS):
                    at = strided(b, width, s)
                    state = decay[g, at] * state + drive[g, at]
                    states[g, at] = state
        pump(1, 2 * parts, 3 * parts)

        def gating(t, b, spot, at, cols, _):
            g = j * tiles + t
            tile = pl.ds(pl.multiple_of(j * W + t * LANES, LANES), LANES)
            gated[at, tile] = (states[g, at] * gelu_both(gate[g, at])[0]).astype(BF16)
            return 0
        each_tile(batch, width, tiles, gating)

    @pl.when(step == 3 * parts - 1)
    def _():
        start(state_sends)

    @pl.when(step >= 3 * parts)
    def _():
        pump(0, 3 * parts, steps)
        first[...] = x_ref[...].astype(F32) + dot(gated[...], wbuf[(2 * parts) % 2].reshape(r, depth))
        pump(1, 3 * parts, steps)

    @pl.when(step == steps - 1)
    def _():
        def norm(i, _):
            at = rows_at(i * CHUNK)
            value = first[at]
            normed2[at] = (value * inverse_norm(value, depth) * gain2_ref[:1]).astype(BF16)
            return 0
        lax.fori_loop(0, tokens // CHUNK, norm, 0)
        start(last_sends)
        for number in FORWARD_PLAN[-1]:
            job.forward(job.events[number])
        job.arrived([r for r in range(len(GATHER_PARTS)) if r not in REC_PARTS])
        job.sent()
        sends.finish()


def forward(info, tokens2, rim, lines, shards, batch, n_seq, r):
    tokens, depth = tokens2.shape
    n = n_seq * ZN
    parts, tiles = r // W, r // LANES
    full = lambda a: pl.BlockSpec(a.shape, lambda j: (0,) * a.ndim)
    anywhere = pl.BlockSpec(memory_space=pl.ANY)
    S = jax.ShapeDtypeStruct
    flat, tall, segs = S((tokens, r), BF16), S((tiles, tokens, LANES), F32), S((batch * SEGS, r), F32)
    inner, ends = S((tokens + 8 * batch, r), F32), S((n_seq, tiles, 2 * batch, LANES), F32)
    first, normed, vec, gain = S((tokens, depth), F32), S((tokens, depth), BF16), S((16, r), F32), S((8, depth), F32)
    outs = [tall, inner, flat, normed, tall, tall, tall, tall, segs, segs, ends, flat, first, normed, vec, gain, gain,
            S((n, REC_ROWS + SMALL_ROWS, PACK), BF16), S((n, FFN_ROWS, PACK), BF16)]
    vm = lambda s: pltpu.VMEM(s.shape, s.dtype)
    scratch = [pltpu.VMEM((tokens + 8 * batch, depth), BF16)] + [
        vm(s) for s in (tall, inner, flat, tall, tall, tall, tall, tall, segs, segs, segs, flat, first, normed, vec, gain, gain)]
    scratch += [pltpu.VMEM((n, SMALL_ROWS, LANES), BF16), pltpu.VMEM((2, n, r // n, PACK), BF16),
                pltpu.VMEM((REC_ROWS + SMALL_ROWS, PACK), BF16), pltpu.VMEM((FFN_ROWS, PACK), BF16)]
    return pl.pallas_call(
        functools.partial(forward_kernel, batch, tokens // batch, n_seq),
        grid=(3 * parts + 2,),
        in_specs=[pl.BlockSpec(memory_space=pltpu.SMEM), full(tokens2), full(rim)] + [anywhere] * (1 + len(shards)),
        out_specs=[anywhere] * len(outs),
        out_shape=outs,
        scratch_shapes=scratch + [SEM((FORWARD_OUTS + 4,)), SEM((2,)), SEM((32,))] + Exchange.scratch(n_seq, (tiles, 2 * batch, LANES))
        + Gather.scratch(GATHER_PARTS),
        compiler_params=pltpu.CompilerParams(collective_id=3, has_side_effects=True, vmem_limit_bytes=62 << 20),
    )(info, tokens2, rim, lines, *shards)


FFN_SCATTER = ((0, 0, 144, 2), (0, 144, 144, 3))
REC_SCATTER = ((0, 0, 64, 0), (0, 64, 64, 1), (0, 128, 48, 2), (0, 176, 48, 3), (0, 224, 32, 2), (0, 256, 32, 3), (1, 0, 16, 0))
BACKWARD_PLAN = (
    (17, 8, 25, 21, 26),
    (),
    (),
    (),
    (0, 19),
    (24,),
    (27, 1, 30),
    (10,),
    (12, 9),
    (),
    (),
    (),
    (16,),
    (),
    (29,),
    (),
    (),
    (31,),
    (2,),
    (28,),
    (),
    (),
    (11,),
    (),
    (),
    (18,),
    (),
    (),
    (),
    (3, 23, 20, 13),
    (),
    (),
    (4,),
    (5,),
    (14, 22, 15),
    (),
    (6, 7),
)
REC_ORDER = (
    97, 90, 88, 89, 85, 30, 84, 61, 57, 62, 86, 60, 59, 28, 91, 104, 2, 95, 98, 56,
    33, 34, 93, 58, 29, 68, 87, 94, 5, 99, 3, 35, 44, 0, 39, 103, 102, 63, 67, 92,
    46, 96, 31, 6, 109, 78, 12, 32, 38, 1, 41, 69, 64, 75, 65, 37, 7, 66, 36, 53,
    101, 100, 108, 74, 107, 51, 40, 80, 105, 47, 71, 76, 4, 70, 11, 9, 43, 106, 48, 10,
    73, 45, 13, 8, 16, 81, 72, 110, 49, 42, 111, 15, 50, 52, 18, 17, 77, 79, 14, 54,
    19, 20, 82, 83, 22, 55, 25, 21, 24, 23, 26, 27,
)


def backward_kernel(batch, width, n_seq, *refs):
    (info_ref, gain_ref, ggain2_ref, vec_ref, pseg_ref, sstart_ref, pall_ref, wo_ref, wr_ref, wi_ref,
     states_ref, decay_ref, gate_ref, rate_ref, entry_ref, gated_ref, inner_ref,
     dlow_h, dfirst_h, mixed_h, normed_h, x_h, gf, token_h, gr, gs, total_h, sib_h,
     low, tall, hid, dn, one, two, both, ext, stage, mixed, normed,
     gseg, gstart, sums, csums, ggain, rims, rim_land, ends, sem, lsem, osem, rimsem) = refs[:51]
    swap = Exchange(n_seq, *refs[51:56])
    job = Scatter(FFN_SCATTER, sum(BACKWARD_PLAN, ()), (gf,), total_h, sib_h, *refs[56:])
    step = pl.program_id(0)
    tokens, depth = low.shape
    n = gf.shape[0]
    r = mixed.shape[1]
    rows, rrows = depth // n, r // n
    group = wo_ref.shape[0]
    thin = group * rrows
    tiles, few, rt = W // LANES, thin // LANES, r // LANES
    counts = backward_steps(n, r, group)
    at, total_steps = {}, 0
    for name, count in counts:
        at[name] = total_steps
        total_steps += count
    size = dict(counts)
    span = width + 8
    me = lax.axis_index("seq")

    def phase(name):
        return jnp.logical_and(step >= at[name], step < at[name] + size[name])

    def index(name):
        return jnp.clip(step - at[name], 0, size[name] - 1)

    def cols(start, count):
        return pl.ds(pl.multiple_of(start, LANES), count)

    def when_step(s, act):
        pl.when(step == s)(act)

    def outgoing(first, value, dst):
        devices, count = value.shape[:2]
        stage[first : first + devices, :count] = value
        pltpu.make_async_copy(stage.at[pl.ds(first, devices), pl.ds(0, count)], dst, sem).start()

    def wait_out(devices, count):
        src = stage.at[pl.ds(0, devices), pl.ds(0, count)]
        pltpu.make_async_copy(src, gr.at[pl.ds(0, devices), pl.ds(0, count)], sem).wait()

    inputs = [pltpu.make_async_copy(src, dst, lsem.at[k]) for k, (src, dst) in enumerate(
        ((dlow_h, low), (mixed_h, mixed), (normed_h, normed), (x_h, low),
         (dfirst_h, tall.at[pl.ds(0, depth // LANES)])))]
    rim_copy = pltpu.make_async_remote_copy(rims, rim_land, rimsem.at[0], rimsem.at[1],
                                            device_id=(lax.rem(me + n_seq - 1, n_seq), swap.z), device_id_type=MESH)

    numbers = [list(range(sum(map(len, BACKWARD_PLAN[:k])), sum(map(len, BACKWARD_PLAN[: k + 1])))) for k in range(2 * total_steps + 1)]

    def pump(half, name):
        for s in range(at[name], at[name] + size[name]):
            if numbers[2 * s + half]:
                @pl.when(step == s)
                def _():
                    for i in numbers[2 * s + half]:
                        job.step(i)

    @pl.when(step == 0)
    def _():
        for copy in inputs[:3]:
            copy.start()
        greet(job.links, swap)
        job.begin()

        @pl.when(me == n_seq - 1)
        def _():
            rim_land[...] = jnp.zeros_like(rim_land)
        inputs[0].wait()

    for name, _ in counts:
        pump(0, name)

    @pl.when(step == at["E"])
    def _():
        wait_out(group, rrows)
        inputs[1].wait()
        inputs[3].start()
        swap.finish()
        for b in range(batch):
            grad = jnp.zeros((rt, LANES), F32)
            for q in reversed(range(n_seq)):
                new = pall_ref[q][:, b] * grad + swap.land[q][:, b]
                grad = jnp.where(q > me, new, grad)
            ends[b] = grad

    @pl.when(step == at["R"])
    def _():
        inputs[4].start()

    @pl.when(step == at["M"])
    def _():
        wait_out(n, rrows)

    @pl.when(phase("U"))
    def _():
        k = index("U")
        total = dot_back(low[...], wo_ref[...].reshape(thin, depth))
        for t in range(few):
            tall[k * few + t] = total[:, lanes(t)]

        def gating(t, b, spot, here, tile, _):
            gate, slope = gelu_both(gate_ref[t, here])
            d = tall[k * few + t, here]
            tall[k * few + t, here] = d * gate
            both[here, pair_cols(k * few + t, 0)] = (d * states_ref[t, here] * slope).astype(BF16)
            return 0
        each_tile(batch, width, few, gating)
        value = dot_outer(gated_ref[...], low[...]).astype(BF16).reshape(group, rrows, depth)
        pl.when(k > 0)(lambda: wait_out(group, rrows))
        outgoing(0, value, gr.at[pl.ds(k * group, group), pl.ds(OUT_AT, rrows)])
        pump(1, "U")
        for t in range(few):
            tile = cols(k * thin + t * LANES, LANES)
            for b in range(batch):
                grad = jnp.zeros((SEGS, LANES), F32)
                for s in reversed(range(width // SEGS)):
                    here = strided(b, width, s)
                    grad = decay_ref[t, here] * (tall[k * few + t, here] + grad)
                gseg[b * SEGS : (b + 1) * SEGS, tile] = grad
                whole = grad[SEGS - 1 :]
                for i in reversed(range(SEGS - 1)):
                    whole = grad[i : i + 1] + pseg_ref[b * SEGS + i : b * SEGS + i + 1, tile] * whole
                swap.rows[k * few + t, b : b + 1] = whole

    @pl.when(step == at["U"] + size["U"] - 1)
    def _():
        swap.begin()

    @pl.when(phase("E"))
    def _():
        k = index("E")
        for t in range(few):
            g = k * few + t
            tile = cols(k * thin + t * LANES, LANES)
            for b in range(batch):
                grad = ends[b, pl.ds(g, 1)]
                for i in reversed(range(SEGS)):
                    line = b * SEGS + i
                    gstart[i : i + 1] = grad
                    grad = pseg_ref[line : line + 1, tile] * grad + gseg[line : line + 1, tile]
                grad = gstart[...]
                for s in reversed(range(width // SEGS)):
                    here = strided(b, width, s)
                    total = tall[g, here] + grad
                    one[t, here] = total
                    grad = decay_ref[t, here] * total
                    before = states_ref[t, strided(b, width, s - 1)] if s else sstart_ref[b * SEGS : (b + 1) * SEGS, tile]
                    two[t, here] = grad * before

        pump(1, "E")

        def gating(t, b, spot, here, _, kept):
            tile = cols(k * thin + t * LANES, LANES)
            coef = vec_ref[COEF : COEF + 1, tile]
            rate, entry = rate_ref[t, here], entry_ref[t, here]
            valid = in_row(spot, width, rate.shape) < info_ref[b]
            grad = jnp.where(valid, one[t, here], 0.0)
            z = 2.0 * coef * rate
            exp_z = jnp.exp(z)
            under = one_less_exp(z, exp_z)
            inverse = lax.rsqrt(under)
            root = under * inverse
            value = mixed[here, tile].astype(F32)
            part = grad * entry
            d_log = jnp.where(valid, two[t, here], 0.0) - part * value * exp_z * inverse
            d_rate = coef * d_log * rate * (1.0 - rate)
            straight = part * root
            d_entry = straight * value * (1.0 - entry)
            tall[rt + k * few + t, here] = straight
            hid[here, pair_cols(k * few + t, 0)] = d_rate.astype(BF16)
            hid[here, pair_cols(k * few + t, 1)] = d_entry.astype(BF16)
            return (kept[0] + fold8(d_log * rate), kept[1] + fold8(d_rate), kept[2] + fold8(d_entry))
        zero = jnp.zeros((8, LANES), F32)
        for t, kept in enumerate(each_tile(batch, width, few, gating, (zero, zero, zero))):
            tile = cols(k * thin + t * LANES, LANES)
            for line in range(3):
                factor = 8.0 * vec_ref[SIG : SIG + 1, tile] if line == 0 else 1.0
                sums[line : line + 1, tile] = factor * jnp.sum(kept[line], axis=0, keepdims=True)

    @pl.when(phase("R"))
    def _():
        j = index("R")
        grads = hid[:, cols(j * PACK, PACK)]
        pl.when(j > 0)(lambda: wait_out(n, rrows))
        for half in range(2):
            value = dot_outer(mixed[:, half * r // 2 : (half + 1) * r // 2], grads).astype(BF16)
            dst = gr.at[pl.ds(half * n // 2, n // 2), pl.ds(pl.multiple_of(GATES_AT + j * rrows, 16), rrows)]
            outgoing(half * n // 2, value.reshape(n // 2, rrows, PACK), dst)
            if half == 0:
                pump(1, "R")

    @pl.when(phase("M"))
    def _():
        k = index("M")
        total = jnp.zeros((tokens, thin), F32)
        for p in range(r // W):
            weights = wr_ref[:, p * rrows : (p + 1) * rrows].reshape(thin, PACK)
            total = total + dot_back(hid[:, p * PACK : (p + 1) * PACK], weights)
        for t in range(few):
            tall[rt + k * few + t] += total[:, lanes(t)]
        pump(1, "M")

    @pl.when(step == at["M"] + size["M"] - 1)
    def _():
        for b in range(batch):
            rims[:, b * 4 : b * 4 + 4] = tall[rt : 2 * rt, b * width : b * width + 4]
        pl.when(me > 0)(rim_copy.start)

    @pl.when(step == at["I"])
    def _():
        inputs[2].wait()
        pl.when(me < n_seq - 1)(rim_copy.wait_recv)
        pl.when(me > 0)(rim_copy.wait_send)

    @pl.when(phase("I"))
    def _():
        j = index("I")
        here = cols(j * W, W)
        for t in range(tiles):
            for b in range(batch):
                ext[b * span : b * span + width, lanes(t)] = tall[rt + j * tiles + t, b * width : (b + 1) * width]
                ext[b * span + width : b * span + width + 4, lanes(t)] = rim_land[j * tiles + t, b * 4 : b * 4 + 4]
        for b in range(batch):
            total = jnp.zeros((width, W), F32)
            for lag in range(4):
                total = total + vec_ref[lag : lag + 1, here] * ext[b * span + lag : b * span + lag + width]
            both[b * width : (b + 1) * width, cols(j * PACK + W, W)] = total.astype(BF16)
        for lag in range(5):
            total = jnp.zeros((1, W), F32)
            for b in range(batch):
                value = ext[b * span : b * span + width]
                if lag < 4:
                    value = value * inner_ref[b * span + 8 - lag : (b + 1) * span - lag]
                total = total + jnp.sum(value, axis=0, keepdims=True)
            csums[lag : lag + 1, here] = total
        pump(1, "I")
        grads = both[:, cols(j * PACK, PACK)]
        more = dot_back(grads, wi_ref[...].reshape(depth, PACK))

        @pl.when(j == 0)
        def _():
            dn[...] = more

        @pl.when(j > 0)
        def _():
            dn[...] += more
        value = dot_outer(normed[...], grads).astype(BF16).reshape(n, rows, PACK)
        pl.when(j > 0)(lambda: wait_out(n, rows))
        outgoing(0, value, gr.at[:, pl.ds(pl.multiple_of(IN_AT + j * rows, 16), rows)])

    @pl.when(step == total_steps - 1)
    def _():
        inputs[3].wait()
        inputs[4].wait()

        def finish(i, total):
            here = rows_at(i * CHUNK)
            value, grad = low[here].astype(F32), dn[here]
            scale = inverse_norm(value, depth)
            weighted = grad * gain_ref[:1]
            mean = jnp.sum(weighted * value, axis=-1, keepdims=True) * (1.0 / depth)
            first = jnp.concatenate([tall[t, here] for t in range(depth // LANES)], axis=1)
            dn[here] = first + scale * weighted - value * (scale * scale * scale * mean)
            return total + fold8(grad * value * scale)
        ggain[...] = lax.fori_loop(0, tokens // CHUNK, finish, jnp.zeros((8, depth), F32))
        pltpu.make_async_copy(dn, token_h, osem.at[0]).start()
        wait_out(n, rows)
        small = stage.at[:, pl.ds(0, SMALL_ROWS)]
        small[...] = jnp.zeros((n, SMALL_ROWS, PACK), BF16)
        lines = [(jnp.sum(ggain[...], axis=0, keepdims=True), rows), (jnp.sum(ggain2_ref[...], axis=0, keepdims=True), rows)]
        lines += [(csums[k : k + 1], rrows) for k in range(5)] + [(sums[k : k + 1], rrows) for k in (1, 2, 0)]
        for k, (line, count) in enumerate(lines):
            stage[:, k, :LANES] = deal(line, n, count)
        small_out = pltpu.make_async_copy(small, gs, osem.at[1])
        small_out.start()
        small_out.wait()
        for i in numbers[-1]:
            job.step(i)
        job.finish()
        pltpu.make_async_copy(dn, token_h, osem.at[0]).wait()


def deal(line, n, count):
    length = n * count
    lane = lax.broadcasted_iota(jnp.int32, (n, length), 1)
    row = lax.broadcasted_iota(jnp.int32, (n, length), 0)
    own = jnp.where(jnp.logical_and(lane >= row * count, lane < (row + 1) * count), line, 0.0).astype(BF16)
    spot = lax.broadcasted_iota(jnp.int32, (length, LANES), 0)
    col = lax.broadcasted_iota(jnp.int32, (length, LANES), 1)
    pick = jnp.where(jnp.logical_and(lax.rem(spot, count) == col, col < count), 1.0, 0.0).astype(BF16)
    return dot(own, pick).astype(BF16)


def backward_steps(n, r, group):
    parts = n // group
    return (("U", parts), ("E", parts), ("R", r // W), ("M", parts), ("I", r // W))


def backward(info, gain, ggain2, vec, pseg, sstart, pall, packed, states, decay, gate_pre, rate, entry, gated,
             inner, d_low, d_first, mixed, normed, x, grad_ffn, batch):
    tokens, depth = x.shape
    width = tokens // batch
    n, r = packed.shape[0], vec.shape[1]
    group = 8
    rows, rrows = depth // n, r // n
    thin = group * rrows
    few, tiles = thin // LANES, W // LANES
    n_seq = pall.shape[0]
    counts = backward_steps(n, r, group)
    at, steps = {}, 0
    for name, count in counts:
        at[name] = steps
        steps += count
    size = dict(counts)
    clamp = lambda j, name: jnp.clip(j - at[name], 0, size[name] - 1)
    full = lambda a: pl.BlockSpec(a.shape, lambda j: (0,) * a.ndim, pipeline_mode=pl.Buffered(buffer_count=1))
    anywhere = pl.BlockSpec(memory_space=pl.ANY)

    def two_phases(j, one, two):
        return jnp.where(j < at[two], clamp(j, one), clamp(j, two))
    twice = pl.BlockSpec((few, tokens, LANES), lambda j: (two_phases(j, "U", "E"), 0, 0))
    early = pl.BlockSpec((few, tokens, LANES), lambda j: (clamp(j, "U"), 0, 0))
    late = pl.BlockSpec((few, tokens, LANES), lambda j: (clamp(j, "E"), 0, 0))
    in_specs = [pl.BlockSpec(memory_space=pltpu.SMEM)] + [full(a) for a in (gain, ggain2, vec, pseg, sstart, pall)] + [
        pl.BlockSpec((group, rrows, PACK), lambda j: (clamp(j, "U"), OUT_AT // rrows, 0)),
        pl.BlockSpec((group, r // W * rrows, PACK), lambda j: (clamp(j, "M"), GATES_AT // (r // W * rrows), 0)),
        pl.BlockSpec((n, rows, PACK), lambda j: (0, IN_AT // rows + clamp(j, "I"), 0)),
        twice, twice, early, late, late,
        pl.BlockSpec((tokens, thin), lambda j: (0, clamp(j, "U"))),
        pl.BlockSpec((inner.shape[0], W), lambda j: (0, clamp(j, "I"))),
    ] + [anywhere] * 6
    S = jax.ShapeDtypeStruct
    outs = [S((tokens, depth), F32), S((n, REC_ROWS, PACK), BF16), S((n, SMALL_ROWS, PACK), BF16)]
    outs += Scatter.buffers(FFN_SCATTER)
    vm = pltpu.VMEM
    scratch = [
        vm((tokens, depth), BF16), vm((2 * r // LANES, tokens, LANES), F32), vm((tokens, 2 * r), BF16),
        vm((tokens, depth), F32), vm((few, tokens, LANES), F32), vm((few, tokens, LANES), F32),
        vm((tokens, 2 * r), BF16), vm((tokens + 8 * batch, W), F32), vm((n, rrows, PACK), BF16),
        vm((tokens, r), BF16), vm((tokens, depth), BF16), vm((batch * SEGS, r), F32), vm((SEGS, LANES), F32),
        vm((8, r), F32), vm((8, r), F32), vm((8, depth), F32), vm((r // LANES, 4 * batch, LANES), F32),
        vm((r // LANES, 4 * batch, LANES), F32), vm((batch, r // LANES, LANES), F32), SEM, SEM((5,)), SEM((2,)), SEM((2,)),
    ] + Exchange.scratch(n_seq, (r // LANES, batch, LANES)) + Scatter.scratch(FFN_SCATTER, 3, 8)
    got = pl.pallas_call(
        functools.partial(backward_kernel, batch, width, n_seq),
        grid=(steps,),
        in_specs=in_specs,
        out_specs=[anywhere] * len(outs),
        out_shape=outs,
        scratch_shapes=scratch,
        compiler_params=pltpu.CompilerParams(collective_id=4, has_side_effects=True, vmem_limit_bytes=64 << 20),
    )(info, gain, ggain2, vec, pseg, sstart, pall, packed, packed, packed,
      states, decay, gate_pre, rate, entry, gated, inner, d_low, d_first, mixed, normed, x, grad_ffn)
    return got[0], got[1], got[2], got[3]


GATES_AT, OUT_AT, IN_AT, REC_ROWS = 0, 144, 192, 288
UPS_AT, DOWN_AT, FFN_ROWS, SMALL_ROWS = 0, 192, 288, 16


def unpack_pair(item, rows, cols):
    blocks = item.reshape(cols // W, rows, 2, W).transpose(2, 1, 0, 3)
    return blocks[0].reshape(rows, cols), blocks[1].reshape(rows, cols)


def pad_rows(item, before, count):
    batch, rows, cols = item.shape
    item = jnp.pad(item, ((0, 0), (before, count - rows - before), (0, 0)))
    return item.reshape(batch * count, cols)


def per_device_packed(tokens, cotangent, lengths, *shards):
    (gate_proj, input_proj, rate_proj, entry_proj, out_proj, ffn_gate, ffn_up, ffn_down) = shards[:8]
    small = shards[8:]
    batch, width, depth = tokens.shape
    r, f = gate_proj.shape[1], ffn_gate.shape[1]
    n_seq = lax.axis_size("seq")
    me = lax.axis_index("seq")
    rim = pad_rows(from_behind(tokens[:, width - 3 :], "seq", 1), 5, 8)
    lines = jnp.concatenate([jnp.pad(item.reshape(-1, item.shape[-1]), ((0, 0), (0, PACK - item.shape[-1])))
                             for item in small] + [jnp.zeros((SMALL_ROWS - 10, PACK), jnp.bfloat16)], axis=0)
    info = jnp.concatenate([jnp.clip(lengths - me * width, 0, width), me[None]]).astype(jnp.int32)
    tokens2 = tokens.reshape(batch * width, depth)
    cot2 = cotangent.reshape(batch * width, depth)

    (gate_pre, inner, mixed, normed, rate, entry, decay, states, pseg, sstart, pall, gated, first, normed_two, vec,
     norm_gain, ffn_gain, packed, packed_ffn) = forward(info, tokens2, rim, lines, shards[:8], batch, n_seq, r)
    block_out, d_first, d_low, g_ffn_gain, grad_ffn = feed_forward(
        info, first, normed_two, cot2, ffn_gain, packed_ffn, f, batch)
    token_grad, grad_rec, grad_small, total_ffn = backward(
        info, norm_gain, g_ffn_gain, vec, pseg, sstart, pall, packed, states, decay, gate_pre, rate, entry, gated, inner,
        d_low, d_first, mixed, normed, tokens2, grad_ffn, batch)
    total = scatter(REC_SCATTER, REC_ORDER, [grad_rec, grad_small])
    g_rate, g_entry = unpack_pair(total[:OUT_AT], *rate_proj.shape)
    g_gate, g_input = unpack_pair(total[IN_AT:REC_ROWS], *gate_proj.shape)
    g_ffn_gate, g_ffn_up = unpack_pair(total_ffn[:DOWN_AT], *ffn_gate.shape)
    result = [g_gate, g_input, g_rate, g_entry, total[OUT_AT:IN_AT], g_ffn_gate, g_ffn_up, total_ffn[DOWN_AT:]]
    line = REC_ROWS
    for item in small:
        count = item.shape[0] if item.ndim == 2 else 1
        part = total[line : line + count, : item.shape[-1]]
        line += count
        result.append(part.reshape(item.shape))
    return (block_out.reshape(tokens.shape), token_grad.reshape(tokens.shape), *result)


def solution(mesh):
    packs = mesh.shape["seq"] == 8 and mesh.shape["batch"] == ZN
    placed = (
        P("batch", "seq", None),
        P("batch", "seq", None),
        P("batch"),
        P(("seq", "batch"), None),
        P(("seq", "batch"), None),
        P(("seq", "batch"), None),
        P(("seq", "batch"), None),
        P(("seq", "batch"), None),
        P(("seq", "batch"), None),
        P(("seq", "batch"), None),
        P(("seq", "batch"), None),
        P(("seq", "batch")),
        P(("seq", "batch")),
        P(None, ("seq", "batch")),
        P(("seq", "batch")),
        P(("seq", "batch")),
        P(("seq", "batch")),
        P(("seq", "batch")),
    )
    return jax.shard_map(
        per_device_packed if packs else per_device,
        mesh=mesh,
        in_specs=placed,
        out_specs=(
            P("batch", "seq", None),
            P("batch", "seq", None),
            P(("seq", "batch"), None),
            P(("seq", "batch"), None),
            P(("seq", "batch"), None),
            P(("seq", "batch"), None),
            P(("seq", "batch"), None),
            P(("seq", "batch"), None),
            P(("seq", "batch"), None),
            P(("seq", "batch"), None),
            P(("seq", "batch")),
            P(("seq", "batch")),
            P(None, ("seq", "batch")),
            P(("seq", "batch")),
            P(("seq", "batch")),
            P(("seq", "batch")),
            P(("seq", "batch")),
        ),
        check_vma=False,
    )
```

```python
import functools

import jax
import jax.numpy as jnp
import numpy as np
from jax import lax
from jax.experimental import pallas as pl
from jax.experimental.pallas import tpu as pltpu
from jax.sharding import PartitionSpec as P

MICRO = 2


eps = 1e-06
lru_scale = 8.0


def from_behind(value, axis, steps):
    count = lax.axis_size(axis)
    initial, last = (max(0, -steps), min(count, count - steps))
    return lax.ppermute(value, axis, [(source, source + steps) for source in range(initial, last)])


def entering(array, axis, combine, identity):
    size, place = (lax.axis_size(axis), lax.axis_index(axis))
    everything = jax.tree.map(lambda part: lax.all_gather(part, axis), array)
    start = jax.tree.map(
        lambda part, zero: jnp.broadcast_to(jnp.asarray(zero, part.dtype), part.shape),
        array,
        identity,
    )

    def entering_turn(k, before):
        reached = k < place
        new = combine(before, jax.tree.map(lambda part: part[k], everything))
        return jax.tree.map(lambda a, b: jnp.where(reached, a, b), new, before)

    return lax.fori_loop(0, size, entering_turn, start)


def carried_in(array, axis, combine, identity):
    size, place = (lax.axis_size(axis), lax.axis_index(axis))
    everything = jax.tree.map(
        lambda part, kind: lax.all_gather(part.astype(kind), axis),
        array,
        (jnp.bfloat16, jnp.bfloat16),
    )
    start = jax.tree.map(
        lambda part, zero: jnp.broadcast_to(jnp.asarray(zero, part.dtype), part.shape),
        array,
        identity,
    )

    def carried_turn(k, before):
        at = size - 1 - k
        reached = at > place
        new = combine(
            before, jax.tree.map(lambda part, own: part[at].astype(own.dtype), everything, array)
        )
        return jax.tree.map(lambda a, b: jnp.where(reached, a, b), new, before)

    return lax.fori_loop(0, size, carried_turn, start)


def for_sending(array):

    def short(part):
        return part.astype(jnp.bfloat16) if part.dtype == jnp.float32 else part

    return jax.tree.map(short, array)


def project(left, right):
    return jnp.einsum("btd,de->bte", left, right, preferred_element_type=jnp.float32)


def project_back(left, right):
    return jnp.einsum("bte,de->btd", left, right, preferred_element_type=jnp.float32)


def outer_sum(left, right):
    return jnp.einsum("btd,bte->de", left, right, preferred_element_type=jnp.float32)


def link(earlier, later):
    return (earlier[0] * later[0], later[0] * earlier[1] + later[1])


def norm_back(value, scale, gain, grad):
    weighted = grad * gain
    gain_grad = jnp.sum(grad * value * scale, axis=(0, 1))
    spread = jnp.mean(weighted * value, axis=-1, keepdims=True)
    return (scale * weighted - value * scale**3 * spread, gain_grad)


def fetch(shards):
    (
        gate_proj,
        input_proj,
        rate_proj,
        entry_proj,
        out_proj,
        ffn_gate,
        ffn_up,
        ffn_down,
        norm_gain,
        ffn_gain,
        conv_taps,
        conv_bias,
        rate_bias,
        entry_bias,
        decay_logit,
    ) = shards
    return (
        lax.all_gather(gate_proj, ("seq", "batch"), axis=0, tiled=True),
        lax.all_gather(input_proj, ("seq", "batch"), axis=0, tiled=True),
        lax.all_gather(rate_proj, ("seq", "batch"), axis=0, tiled=True),
        lax.all_gather(entry_proj, ("seq", "batch"), axis=0, tiled=True),
        lax.all_gather(out_proj, ("seq", "batch"), axis=0, tiled=True),
        lax.all_gather(ffn_gate, ("seq", "batch"), axis=0, tiled=True),
        lax.all_gather(ffn_up, ("seq", "batch"), axis=0, tiled=True),
        lax.all_gather(ffn_down, ("seq", "batch"), axis=0, tiled=True),
        lax.all_gather(norm_gain, ("seq", "batch"), axis=0, tiled=True),
        lax.all_gather(ffn_gain, ("seq", "batch"), axis=0, tiled=True),
        lax.all_gather(conv_taps, ("seq", "batch"), axis=1, tiled=True),
        lax.all_gather(conv_bias, ("seq", "batch"), axis=0, tiled=True),
        lax.all_gather(rate_bias, ("seq", "batch"), axis=0, tiled=True),
        lax.all_gather(entry_bias, ("seq", "batch"), axis=0, tiled=True),
        lax.all_gather(decay_logit, ("seq", "batch"), axis=0, tiled=True),
    )


def forward_part(tokens, mask, weights):
    (
        gate_proj,
        input_proj,
        rate_proj,
        entry_proj,
        out_proj,
        ffn_gate,
        ffn_up,
        ffn_down,
        norm_gain,
        ffn_gain,
        conv_taps,
        conv_bias,
        rate_bias,
        entry_bias,
        decay_logit,
    ) = weights
    width = tokens.shape[1]
    taps_count = conv_taps.shape[0]
    values = tokens.astype(jnp.float32)
    scale_one = lax.rsqrt(jnp.mean(values * values, axis=-1, keepdims=True) + eps)
    normed = (values * scale_one * norm_gain).astype(jnp.bfloat16)
    gate_pre = project(normed, gate_proj)
    inner = project(normed, input_proj)
    rim = from_behind(inner[:, width - (taps_count - 1) :], "seq", 1)
    extended = jnp.concatenate([rim, inner], axis=1)
    conv = jnp.zeros_like(inner) + conv_bias
    for lag in range(taps_count):
        start = taps_count - 1 - lag
        conv = conv + conv_taps[lag] * extended[:, start : start + width]
    mixed = conv.astype(jnp.bfloat16)
    mixed_full = mixed.astype(jnp.float32)
    rate = jax.nn.sigmoid(project(mixed, rate_proj) + rate_bias)
    entry = jax.nn.sigmoid(project(mixed, entry_proj) + entry_bias)
    logit = decay_logit.astype(jnp.float32)
    log_decay = -lru_scale * jax.nn.softplus(-logit) * rate
    decay = jnp.exp(mask * log_decay)
    root = jnp.sqrt(-jnp.expm1(2.0 * log_decay))
    drive = mask * root * entry * mixed_full
    reach, local = lax.associative_scan(link, (decay, drive), axis=1)
    unit_state = (jnp.ones_like(reach[:, -1]), jnp.zeros_like(local[:, -1]))
    start_state = entering((reach[:, -1], local[:, -1]), "seq", link, unit_state)[1]
    states = local + reach * start_state[:, None]
    gated = (states * jax.nn.gelu(gate_pre)).astype(jnp.bfloat16)
    first = values + project(gated, out_proj)
    scale_two = lax.rsqrt(jnp.mean(first * first, axis=-1, keepdims=True) + eps)
    normed_two = (first * scale_two * ffn_gain).astype(jnp.bfloat16)
    up_pre = project(normed_two, ffn_gate)
    mix_pre = project(normed_two, ffn_up)
    hidden = (jax.nn.gelu(up_pre) * mix_pre).astype(jnp.bfloat16)
    block_out = mask * (first + project(hidden, ffn_down))
    saved = (
        values,
        scale_one,
        normed,
        gate_pre,
        extended,
        mixed,
        mixed_full,
        rate,
        entry,
        log_decay,
        decay,
        root,
        start_state,
        states,
        gated,
        first,
        scale_two,
        normed_two,
        up_pre,
        mix_pre,
        hidden,
    )
    return (block_out, saved)


def backward_part(cotangent, mask, weights, saved):
    (
        gate_proj,
        input_proj,
        rate_proj,
        entry_proj,
        out_proj,
        ffn_gate,
        ffn_up,
        ffn_down,
        norm_gain,
        ffn_gain,
        conv_taps,
        conv_bias,
        rate_bias,
        entry_bias,
        decay_logit,
    ) = weights
    (
        values,
        scale_one,
        normed,
        gate_pre,
        extended,
        mixed,
        mixed_full,
        rate,
        entry,
        log_decay,
        decay,
        root,
        start_state,
        states,
        gated,
        first,
        scale_two,
        normed_two,
        up_pre,
        mix_pre,
        hidden,
    ) = saved
    width = values.shape[1]
    taps_count = conv_taps.shape[0]
    cot_full = mask * cotangent.astype(jnp.float32)
    cot_low = cot_full.astype(jnp.bfloat16)
    grad_ffn_down = outer_sum(hidden, cot_low)
    d_hidden = project_back(cot_low, ffn_down)
    gelu_up, gelu_pull = jax.vjp(jax.nn.gelu, up_pre)
    d_up = gelu_pull(d_hidden * mix_pre)[0].astype(jnp.bfloat16)
    d_mix = (d_hidden * gelu_up).astype(jnp.bfloat16)
    grad_ffn_gate = outer_sum(normed_two, d_up)
    grad_ffn_up = outer_sum(normed_two, d_mix)
    d_normed_two = project_back(d_up, ffn_gate) + project_back(d_mix, ffn_up)
    back_two, grad_ffn_gain = norm_back(first, scale_two, ffn_gain, d_normed_two)
    d_first = cot_full + back_two
    d_first_low = d_first.astype(jnp.bfloat16)
    grad_out_proj = outer_sum(gated, d_first_low)
    d_gated = project_back(d_first_low, out_proj)
    gate, gate_pull = jax.vjp(jax.nn.gelu, gate_pre)
    d_states = d_gated * gate
    d_gate_pre = gate_pull(d_gated * states)[0].astype(jnp.bfloat16)
    following = jnp.concatenate([decay[:, 1:], jnp.ones_like(decay[:, :1])], axis=1)
    reach_back, local_back = lax.associative_scan(link, (following, d_states), reverse=True, axis=1)
    unit_grad = (jnp.ones_like(decay[:, 0]), jnp.zeros_like(decay[:, 0]))
    end_grad = carried_in(
        (decay[:, 0] * reach_back[:, 0], decay[:, 0] * local_back[:, 0]), "seq", link, unit_grad
    )[1]
    carried = local_back + reach_back * end_grad[:, None]
    previous = jnp.concatenate([start_state[:, None], states[:, :-1]], axis=1)
    masked_grad = mask * carried
    d_log = (
        masked_grad * previous * decay
        - masked_grad * entry * mixed_full * jnp.exp(2.0 * log_decay) / root
    )
    logit = decay_logit.astype(jnp.float32)
    grad_decay_logit = jnp.sum(lru_scale * d_log * rate * jax.nn.sigmoid(-logit), axis=(0, 1))
    d_rate_pre = -lru_scale * jax.nn.softplus(-logit) * d_log * rate * (1.0 - rate)
    d_entry_pre = masked_grad * root * mixed_full * entry * (1.0 - entry)
    grad_rate_bias = jnp.sum(d_rate_pre, axis=(0, 1))
    grad_entry_bias = jnp.sum(d_entry_pre, axis=(0, 1))
    rate_low = d_rate_pre.astype(jnp.bfloat16)
    entry_low = d_entry_pre.astype(jnp.bfloat16)
    grad_rate_proj = outer_sum(mixed, rate_low)
    grad_entry_proj = outer_sum(mixed, entry_low)
    d_mixed = (
        masked_grad * root * entry
        + project_back(rate_low, rate_proj)
        + project_back(entry_low, entry_proj)
    )
    grad_conv_bias = jnp.sum(d_mixed, axis=(0, 1))
    tap_grads = []
    for lag in range(taps_count):
        start = taps_count - 1 - lag
        tap_grads.append(jnp.sum(d_mixed * extended[:, start : start + width], axis=(0, 1)))
    grad_conv_taps = jnp.stack(tap_grads, axis=0)
    rim_back = from_behind(for_sending(d_mixed[:, : taps_count - 1]), "seq", -1)
    later = jnp.concatenate([d_mixed, rim_back], axis=1)
    d_inner = jnp.zeros_like(d_mixed)
    for lag in range(taps_count):
        d_inner = d_inner + conv_taps[lag] * later[:, lag : lag + width]
    d_inner = d_inner.astype(jnp.bfloat16)
    grad_input_proj = outer_sum(normed, d_inner)
    grad_gate_proj = outer_sum(normed, d_gate_pre)
    d_normed = project_back(d_gate_pre, gate_proj) + project_back(d_inner, input_proj)
    back_one, grad_norm_gain = norm_back(values, scale_one, norm_gain, d_normed)
    token_grad = d_first + back_one
    grads = (
        grad_gate_proj,
        grad_input_proj,
        grad_rate_proj,
        grad_entry_proj,
        grad_out_proj,
        grad_ffn_gate,
        grad_ffn_up,
        grad_ffn_down,
        grad_norm_gain,
        grad_ffn_gain,
        grad_conv_taps,
        grad_conv_bias,
        grad_rate_bias,
        grad_entry_bias,
        grad_decay_logit,
    )
    return (token_grad, grads)


def reduce_grads(totals):
    shaped = []
    for index, item in enumerate(totals):
        if index == 10:
            item = item.T
        if item.ndim == 1:
            item = item[:, None]
        shaped.append(item[None])
    spread = (
        lax.all_to_all(
            shaped[0].astype(jnp.bfloat16), "seq", split_axis=1, concat_axis=0, tiled=True
        ).astype(jnp.float32),
        lax.all_to_all(
            shaped[1].astype(jnp.bfloat16), "seq", split_axis=1, concat_axis=0, tiled=True
        ).astype(jnp.float32),
        lax.all_to_all(
            shaped[2].astype(jnp.bfloat16), "seq", split_axis=1, concat_axis=0, tiled=True
        ).astype(jnp.float32),
        lax.all_to_all(
            shaped[3].astype(jnp.bfloat16), "seq", split_axis=1, concat_axis=0, tiled=True
        ).astype(jnp.float32),
        lax.all_to_all(
            shaped[4].astype(jnp.bfloat16), "seq", split_axis=1, concat_axis=0, tiled=True
        ).astype(jnp.float32),
        lax.all_to_all(
            shaped[5].astype(jnp.bfloat16), "seq", split_axis=1, concat_axis=0, tiled=True
        ).astype(jnp.float32),
        lax.all_to_all(
            shaped[6].astype(jnp.bfloat16), "seq", split_axis=1, concat_axis=0, tiled=True
        ).astype(jnp.float32),
        lax.all_to_all(
            shaped[7].astype(jnp.bfloat16), "seq", split_axis=1, concat_axis=0, tiled=True
        ).astype(jnp.float32),
        lax.all_to_all(
            shaped[8].astype(jnp.bfloat16), "seq", split_axis=1, concat_axis=0, tiled=True
        ).astype(jnp.float32),
        lax.all_to_all(
            shaped[9].astype(jnp.bfloat16), "seq", split_axis=1, concat_axis=0, tiled=True
        ).astype(jnp.float32),
        lax.all_to_all(for_sending(shaped[10]), "seq", split_axis=1, concat_axis=0, tiled=True),
        lax.all_to_all(for_sending(shaped[11]), "seq", split_axis=1, concat_axis=0, tiled=True),
        lax.all_to_all(for_sending(shaped[12]), "seq", split_axis=1, concat_axis=0, tiled=True),
        lax.all_to_all(for_sending(shaped[13]), "seq", split_axis=1, concat_axis=0, tiled=True),
        lax.all_to_all(for_sending(shaped[14]), "seq", split_axis=1, concat_axis=0, tiled=True),
    )
    folded = [jnp.sum(piece, axis=0) for piece in spread]
    summed = (
        lax.psum_scatter(
            folded[0].astype(jnp.bfloat16), "batch", scatter_dimension=0, tiled=True
        ).astype(jnp.float32),
        lax.psum_scatter(
            folded[1].astype(jnp.bfloat16), "batch", scatter_dimension=0, tiled=True
        ).astype(jnp.float32),
        lax.psum_scatter(
            folded[2].astype(jnp.bfloat16), "batch", scatter_dimension=0, tiled=True
        ).astype(jnp.float32),
        lax.psum_scatter(
            folded[3].astype(jnp.bfloat16), "batch", scatter_dimension=0, tiled=True
        ).astype(jnp.float32),
        lax.psum_scatter(
            folded[4].astype(jnp.bfloat16), "batch", scatter_dimension=0, tiled=True
        ).astype(jnp.float32),
        lax.psum_scatter(
            folded[5].astype(jnp.bfloat16), "batch", scatter_dimension=0, tiled=True
        ).astype(jnp.float32),
        lax.psum_scatter(
            folded[6].astype(jnp.bfloat16), "batch", scatter_dimension=0, tiled=True
        ).astype(jnp.float32),
        lax.psum_scatter(
            folded[7].astype(jnp.bfloat16), "batch", scatter_dimension=0, tiled=True
        ).astype(jnp.float32),
        lax.psum_scatter(
            folded[8].astype(jnp.bfloat16), "batch", scatter_dimension=0, tiled=True
        ).astype(jnp.float32),
        lax.psum_scatter(
            folded[9].astype(jnp.bfloat16), "batch", scatter_dimension=0, tiled=True
        ).astype(jnp.float32),
        lax.psum_scatter(
            folded[10].astype(jnp.bfloat16), "batch", scatter_dimension=0, tiled=True
        ).astype(jnp.float32),
        lax.psum_scatter(
            folded[11].astype(jnp.bfloat16), "batch", scatter_dimension=0, tiled=True
        ).astype(jnp.float32),
        lax.psum_scatter(
            folded[12].astype(jnp.bfloat16), "batch", scatter_dimension=0, tiled=True
        ).astype(jnp.float32),
        lax.psum_scatter(
            folded[13].astype(jnp.bfloat16), "batch", scatter_dimension=0, tiled=True
        ).astype(jnp.float32),
        lax.psum_scatter(
            folded[14].astype(jnp.bfloat16), "batch", scatter_dimension=0, tiled=True
        ).astype(jnp.float32),
    )
    result = []
    for index, item in enumerate(summed):
        if index == 10:
            result.append(item.T)
        elif totals[index].ndim == 1:
            result.append(item[:, 0])
        else:
            result.append(item)
    return tuple(result)


def per_device(
    tokens,
    cotangent,
    lengths,
    gate_proj,
    input_proj,
    rate_proj,
    entry_proj,
    out_proj,
    ffn_gate,
    ffn_up,
    ffn_down,
    norm_gain,
    ffn_gain,
    conv_taps,
    conv_bias,
    rate_bias,
    entry_bias,
    decay_logit,
):
    shards = (
        gate_proj,
        input_proj,
        rate_proj,
        entry_proj,
        out_proj,
        ffn_gate,
        ffn_up,
        ffn_down,
        norm_gain,
        ffn_gain,
        conv_taps,
        conv_bias,
        rate_bias,
        entry_bias,
        decay_logit,
    )
    rows, width = (tokens.shape[0], tokens.shape[1])
    place = lax.axis_index("seq") * width + lax.iota(jnp.int32, width)
    mask_all = (place[None, :] < lengths[:, None]).astype(jnp.float32)[:, :, None]
    group = rows // MICRO
    totals = None
    block_parts = []
    grad_parts = []
    for part in range(MICRO):
        lower = part * group
        mask = mask_all[lower : lower + group]
        weights = fetch(shards)
        block_out, saved = forward_part(tokens[lower : lower + group], mask, weights)
        weights = fetch(shards)
        token_grad, grads = backward_part(cotangent[lower : lower + group], mask, weights, saved)
        totals = grads if part == 0 else jax.tree.map(jnp.add, totals, grads)
        block_parts.append(block_out)
        grad_parts.append(token_grad)
    summed = reduce_grads(totals)
    return (jnp.concatenate(block_parts, axis=0), jnp.concatenate(grad_parts, axis=0)) + summed


F32 = jnp.float32
BF16 = jnp.bfloat16
W = 512
PACK = 2 * W
SEGS = 8
CHUNK = 32
TALL = 64
LANES = 128
GELU_A = 0.7978845608028654
GELU_B = 0.044715
TAPS, CONV_BIAS, RATE_BIAS, ENTRY_BIAS, COEF, SIG = 0, 4, 5, 6, 7, 8


def dot(left, right):
    return lax.dot_general(left, right, (((1,), (0,)), ((), ())), preferred_element_type=F32)


def dot_back(left, right):
    return lax.dot_general(left, right, (((1,), (1,)), ((), ())), preferred_element_type=F32)


def dot_outer(left, right):
    return lax.dot_general(left, right, (((0,), (0,)), ((), ())), preferred_element_type=F32)


def rows_at(start, count=CHUNK):
    return pl.ds(pl.multiple_of(start, CHUNK), count)


def gelu_both(value):
    square = value * value
    inside = GELU_A * value * (1.0 + GELU_B * square)
    tanh = jnp.tanh(inside)
    half = 0.5 + 0.5 * tanh
    slope = half + 0.5 * value * (1.0 - tanh * tanh) * (GELU_A * (1.0 + 3.0 * GELU_B * square))
    return value * half, slope


def sigmoid(value):
    return 1.0 / (1.0 + jnp.exp(-value))


def one_less_exp(z, exp_z):
    series = 1.0 + z * (1 / 2 + z * (1 / 6 + z * (1 / 24 + z * (1 / 120 + z * (1 / 720)))))
    return jnp.where(z > -0.25, -z * series, 1.0 - exp_z)


def in_row(row, width, shape):
    return row + lax.broadcasted_iota(jnp.int32, shape, 0)


def each_chunk(batch, width, body, carry=0):
    per = width // CHUNK
    for b in range(batch):
        carry = lax.fori_loop(0, per, lambda i, c, b=b: body(b, i * CHUNK, b * width + i * CHUNK, c), carry)
    return carry


def each_tile(batch, width, tiles, body, carry=None):
    carries = []
    for t in range(tiles):
        kept = carry
        for b in range(batch):
            def one(i, c, t=t, b=b):
                return body(t, b, i * TALL, rows_at(b * width + i * TALL, TALL), slice(t * LANES, (t + 1) * LANES), c)
            kept = lax.fori_loop(0, width // TALL, one, 0 if kept is None else kept)
        carries.append(kept)
    return carries


def strided(b, width, step):
    return pl.ds(b * width + step, SEGS, stride=width // SEGS)


def lanes(t):
    return slice(t * LANES, (t + 1) * LANES)


def spread(ref, value):
    for t in range(ref.shape[0]):
        ref[t] = value[:, lanes(t)]


def tiled(tokens, block, index):
    return pl.BlockSpec((block // LANES, tokens, LANES), lambda j: (index(j), 0, 0))


def pair_cols(tile, second):
    block = lax.div(tile, W // LANES)
    return pl.ds(pl.multiple_of(tile * LANES + (block + second) * W, LANES), LANES)


def inverse_norm(value, depth):
    return lax.rsqrt(jnp.sum(value * value, axis=-1, keepdims=True) * (1.0 / depth) + eps)


def fold8(value):
    total = value[:8]
    for i in range(8, value.shape[0], 8):
        total = total + value[i : i + 8]
    return total


def ffn_kernel(batch, width, info_ref, first_ref, normed_ref, cot_ref, gain_ref, wu_ref, wd_ref,
               out_ref, dfirst_ref, dlow_ref, ggain_ref, grad_ref,
               low, tall, hid, acc, dn, pair, du, stage, dstage, sem):
    step = pl.program_id(0)
    tokens, depth = first_ref.shape
    n = grad_ref.shape[0]
    group, drows = wd_ref.shape[:2]
    wide = group * drows
    rows = depth // n
    nd, nw = n // group, hid.shape[1] // W
    tiles = W // LANES

    def block_out(j):
        return pltpu.make_async_copy(stage, grad_ref.at[:, pl.ds(pl.multiple_of(UPS_AT + j * rows, rows), rows)], sem.at[0])

    def down_out(k):
        return pltpu.make_async_copy(dstage, grad_ref.at[pl.ds(k * group, group), pl.ds(DOWN_AT, drows)], sem.at[1])

    @pl.when(step == 0)
    def _():
        def masked(b, spot, row, _):
            at = rows_at(row)
            value = cot_ref[at]
            valid = in_row(spot, width, value.shape) < info_ref[b]
            low[at] = jnp.where(valid, value.astype(F32), 0.0).astype(BF16)
            return 0
        each_chunk(batch, width, masked)

    @pl.when(step < nd)
    def _():
        total = dot_back(low[...], wd_ref[...].reshape(wide, depth))
        for t in range(wide // LANES):
            tall[jnp.minimum(step, nd - 1) * (wide // LANES) + t] = total[:, lanes(t)]

    @pl.when(jnp.logical_and(step >= nd, step < nd + nw))
    def _():
        j = jnp.clip(step - nd, 0, nw - 1)
        weights = wu_ref[...].reshape(depth, PACK)
        spread(pair, dot(normed_ref[...], weights))

        def gating(t, b, spot, at, cols, _):
            gate, slope = gelu_both(pair[t, at])
            mix, d = pair[tiles + t, at], tall[j * tiles + t, at]
            hid[at, pl.ds(pl.multiple_of(j * W + t * LANES, LANES), LANES)] = (gate * mix).astype(BF16)
            du[at, cols] = (d * mix * slope).astype(BF16)
            du[at, lanes(tiles + t)] = (d * gate).astype(BF16)
            return 0
        each_tile(batch, width, tiles, gating)
        more = dot_back(du[...], weights)

        @pl.when(j == 0)
        def _():
            dn[...] = more

        @pl.when(j > 0)
        def _():
            dn[...] += more
        value = dot_outer(normed_ref[...], du[...]).astype(BF16).reshape(n, rows, PACK)
        pl.when(j > 0)(lambda: block_out(0).wait())
        stage[...] = value
        block_out(j).start()

    @pl.when(step >= nd + nw)
    def _():
        k = jnp.clip(step - nd - nw, 0, nd - 1)
        block = hid[:, pl.ds(pl.multiple_of(k * wide, wide), wide)]
        more = dot(block, wd_ref[...].reshape(wide, depth))

        @pl.when(k == 0)
        def _():
            acc[...] = more

        @pl.when(k > 0)
        def _():
            acc[...] += more
        value = dot_outer(block, low[...]).astype(BF16).reshape(group, drows, depth)
        pl.when(k > 0)(lambda: down_out(0).wait())
        dstage[...] = value
        down_out(k).start()

    @pl.when(step == pl.num_programs(0) - 1)
    def _():
        def finish(b, spot, row, total):
            at = rows_at(row)
            first, cot = first_ref[at], low[at].astype(F32)
            valid = in_row(spot, width, first.shape) < info_ref[b]
            out_ref[at] = jnp.where(valid, first + acc[at], 0.0)
            grad = dn[at]
            scale = inverse_norm(first, depth)
            weighted = grad * gain_ref[:1]
            mean = jnp.sum(weighted * first, axis=-1, keepdims=True) * (1.0 / depth)
            back = cot + scale * weighted - first * (scale * scale * scale * mean)
            for t in range(depth // LANES):
                dfirst_ref[t, at] = back[:, lanes(t)]
            dlow_ref[at] = back.astype(BF16)
            return total + fold8(grad * first * scale)
        ggain_ref[...] = each_chunk(batch, width, finish, jnp.zeros((8, depth), F32))
        block_out(0).wait()
        down_out(0).wait()


def feed_forward(info, first, normed_two, cot, gain, packed, f, batch):
    tokens, depth = first.shape
    width = tokens // batch
    n = packed.shape[0]
    rows, drows = depth // n, f // n
    group = 8
    wide = group * drows
    nd, nw = f // wide, f // W
    full = lambda shape: pl.BlockSpec(shape, lambda j: (0,) * len(shape))
    clamp = lambda j, low, count: jnp.clip(j - low, 0, count - 1)

    def down_block(j):
        return (jnp.where(j < nd, jnp.minimum(j, nd - 1), clamp(j, nd + nw, nd)), DOWN_AT // drows, 0)
    vm = pltpu.VMEM
    S = jax.ShapeDtypeStruct
    return pl.pallas_call(
        functools.partial(ffn_kernel, batch, width),
        grid=(nd + nw + nd,),
        in_specs=[pl.BlockSpec(memory_space=pltpu.SMEM), full(first.shape), full(normed_two.shape), full(cot.shape),
                  full(gain.shape), pl.BlockSpec((n, rows, PACK), lambda j: (0, UPS_AT // rows + clamp(j, nd, nw), 0)),
                  pl.BlockSpec((group, drows, depth), down_block)],
        out_specs=[full((tokens, depth)), full((depth // LANES, tokens, LANES)), full((tokens, depth)), full((8, depth)),
                   pl.BlockSpec(memory_space=pl.ANY)],
        out_shape=[S((tokens, depth), F32), S((depth // LANES, tokens, LANES), F32), S((tokens, depth), BF16),
                   S((8, depth), F32), S((n, FFN_ROWS, PACK), BF16)],
        scratch_shapes=[vm((tokens, depth), BF16), vm((f // LANES, tokens, LANES), F32), vm((tokens, f), BF16),
                        vm((tokens, depth), F32), vm((tokens, depth), F32), vm((PACK // LANES, tokens, LANES), F32),
                        vm((tokens, PACK), BF16), vm((n, rows, PACK), BF16), vm((group, drows, depth), BF16),
                        pltpu.SemaphoreType.DMA((2,))],
        compiler_params=pltpu.CompilerParams(vmem_limit_bytes=60 << 20),
    )(info, first, normed_two, cot, gain, packed, packed)


MESH = pl.DeviceIdType.MESH
ROUTES = (("z", "x", "y"), ("z", "y", "x"), ("x", "z", "y"), ("y", "z", "x"))
ZN = 4
STG = 4
SEM = pltpu.SemaphoreType.DMA


def place():
    s = lax.axis_index("seq")
    return lax.rem(s, 2), lax.rem(lax.div(s, 2), 2), lax.div(s, 4), lax.axis_index("batch")


def flip(value, by):
    return 1 - value if by else value


def seq_of(y, x, c):
    return (y * 2 + x) * 2 + c


def far(z, j):
    if j == ZN - 1:
        return z
    found = None
    for here in range(ZN):
        others = sorted((q for q in range(ZN) if q != here), key=lambda q: (-abs(q - here), q))
        found = jnp.int32(others[j]) if found is None else jnp.where(z == here, others[j], found)
    return found


class Links:
    def __init__(self):
        self.c, self.x, self.y, self.z = c, x, y, z = place()
        self.beside = {
            "x": (seq_of(y, 1 - x, c), z),
            "y": (seq_of(1 - y, x, c), z),
            "up": (seq_of(y, x, c), z + 1),
            "dn": (seq_of(y, x, c), z - 1),
            "core": (seq_of(y, x, 1 - c), z),
        }
        self.spots = [far(z, j) for j in range(ZN)]
        self.above, self.below = z < ZN - 1, z > 0

    def slot(self, dx, dy, z, core):
        return seq_of(flip(self.y, dy), flip(self.x, dx), core) * ZN + z

    def copy(self, src, dst, send, recv, d):
        return pltpu.make_async_remote_copy(src, dst, send, recv, device_id=self.beside[d], device_id_type=MESH)


def greet(links, swap):
    bar = pltpu.get_barrier_semaphore()
    count = 0
    if swap is not None:
        count = swap.n - 1
        for k in range(1, swap.n):
            pl.semaphore_signal(bar, inc=1, device_id=swap.peer(k), device_id_type=MESH)
    if links is not None:
        def signal(d):
            pl.semaphore_signal(bar, inc=1, device_id=links.beside[d], device_id_type=MESH)
        if swap is None:
            count = 3
            for d in ("x", "y", "core"):
                signal(d)
        pl.when(links.above)(lambda: signal("up"))
        pl.when(links.below)(lambda: signal("dn"))
        count = count + links.above.astype(jnp.int32) + links.below.astype(jnp.int32)
    pl.semaphore_wait(bar, count)


class Exchange:
    def __init__(self, n, rows, land, send, recv, own):
        self.n, self.rows, self.land, self.send, self.recv, self.own = n, rows, land, send, recv, own
        self.me, self.z = lax.axis_index("seq"), lax.axis_index("batch")

    @staticmethod
    def scratch(n, shape):
        return [pltpu.VMEM(shape, F32), pltpu.VMEM((n,) + shape, F32), SEM((n,)), SEM((n,)), SEM]

    def peer(self, k):
        return (lax.rem(self.me + k, self.n), self.z)

    def copies(self):
        return [
            pltpu.make_async_remote_copy(self.rows, self.land.at[self.me], self.send.at[k], self.recv.at[k],
                                         device_id=self.peer(k), device_id_type=MESH)
            for k in range(1, self.n)
        ]

    def mine(self):
        return pltpu.make_async_copy(self.rows, self.land.at[self.me], self.own)

    def begin(self):
        self.mine().start()
        for copy in self.copies():
            copy.start()

    def finish(self):
        self.mine().wait()
        for copy in self.copies():
            copy.wait()


def onward(order, dx, dy, same):
    off = {"x": dx, "y": dy, "z": 0 if same else 1}
    return [
        d for i, d in enumerate(order)
        if not any(off[e] for e in order[i + 1 :]) and not (d != "z" and off[d])
    ]


def arrival(order, dx, dy, same):
    off = {"x": dx, "y": dy, "z": 0 if same else 1}
    return [d for d in order if off[d]][-1]


def blocks(parts):
    found = [
        (dx + dy + ZN - 1 - j, r, dx, dy, j)
        for dx in range(2) for dy in range(2) for j in range(ZN) for r in range(len(parts))
    ]
    return found


class Gather:
    def __init__(self, parts, ins, outs, send, recv, csend, crecv, lsem):
        self.parts, self.ins, self.outs = parts, ins, outs
        self.send, self.recv, self.csend, self.crecv, self.lsem = send, recv, csend, crecv, lsem
        self.links = Links()
        self.events = blocks(parts)

    @staticmethod
    def scratch(parts):
        n = len(parts)
        return [SEM((n, 4, 4, ZN)), SEM((n, 4, ZN)), SEM((n, 4, ZN)), SEM((n, 4, ZN)), SEM((n,))]

    def window(self, r):
        return pl.ds(self.parts[r][2], self.parts[r][3])

    def dst(self, r, dx, dy, zs):
        return self.outs[self.parts[r][1]].at[self.links.slot(dx, dy, zs, self.links.c), self.window(r)]

    def src(self, r, dx, dy, zs, own):
        return self.ins[self.parts[r][0]].at[self.window(r)] if own else self.dst(r, dx, dy, zs)

    def hop(self, r, dx, dy, zs, d, own):
        to = (1 if d == "x" else dx) * 2 + (1 if d == "y" else dy)
        which = ("x", "y", "up", "dn").index(d)
        return self.links.copy(self.src(r, dx, dy, zs, own), self.dst(r, dx, dy, zs),
                               self.send.at[r, which, dx * 2 + dy, zs], self.recv.at[r, to, zs], d)

    def across(self, r, dx, dy, zs, own):
        return self.links.copy(self.src(r, dx, dy, zs, own), self.dst(r, dx, dy, zs),
                               self.csend.at[r, dx * 2 + dy, zs], self.crecv.at[r, dx * 2 + dy, zs], "core")

    def hops(self, r, dx, dy, j, act):
        links, zs = self.links, self.links.spots[j]
        z, same = links.z, j == ZN - 1
        own = same and not dx and not dy
        for d in onward(ROUTES[self.parts[r][4]], dx, dy, same):
            if d != "z":
                act(self.hop(r, dx, dy, zs, d, own))
                continue
            up = links.above if same else jnp.logical_and(z > zs, links.above)
            down = links.below if same else jnp.logical_and(z < zs, links.below)
            pl.when(up)(lambda: act(self.hop(r, dx, dy, zs, "up", own)))
            pl.when(down)(lambda: act(self.hop(r, dx, dy, zs, "dn", own)))

    def forward(self, event):
        _, r, dx, dy, j = event
        zs, own = self.links.spots[j], j == ZN - 1 and not dx and not dy
        if not own:
            self.links.copy(self.dst(r, dx, dy, zs), self.dst(r, dx, dy, zs), self.send.at[r, 0, 0, 0],
                            self.recv.at[r, dx * 2 + dy, zs], "core").wait_recv()
        self.hops(r, dx, dy, j, lambda copy: copy.start())
        self.across(r, dx, dy, zs, own).start()
        if own:
            self.local(r).start()

    def local(self, r):
        return pltpu.make_async_copy(self.ins[self.parts[r][0]].at[self.window(r)],
                                     self.dst(r, 0, 0, self.links.z), self.lsem.at[r])

    def arrived(self, parts):
        for _, r, dx, dy, j in self.events:
            if r in parts:
                own = j == ZN - 1 and not dx and not dy
                self.across(r, dx, dy, self.links.spots[j], own).wait_recv()
                if own:
                    self.local(r).wait()

    def sent(self):
        for _, r, dx, dy, j in self.events:
            own = j == ZN - 1 and not dx and not dy
            self.hops(r, dx, dy, j, lambda copy: copy.wait_send())
            self.across(r, dx, dy, self.links.spots[j], own).wait_send()


def layout(order):
    base, count = {}, 0
    for i, d in enumerate(order):
        base[d] = count
        free = 1
        for e in order[:i]:
            free *= ZN if e == "z" else 2
        count += free * ((ZN + 1) if d == "z" else 1)
    return base, count


class Scatter:
    def __init__(self, parts, order, ins, out, sib, stage, ring, fin, csend, crecv, lsem, send, fsem, *rest):
        self.parts, self.ins, self.out, self.sib = parts, ins, out, sib
        self.stage, self.ring, self.fin = stage, ring, fin
        self.ahead, self.slots = stage.shape[0], ring.shape[0]
        self.csend, self.crecv, self.lsem, self.send, self.fsem = csend, crecv, lsem, send, fsem
        self.bufs, self.recv = rest[: len(parts)], rest[len(parts) :]
        self.links = Links()
        self.lay = [layout(ROUTES[part[3]]) for part in parts]
        rows = [part[2] for part in parts]
        self.starts = [sum(rows[:r]) for r in range(len(parts))]
        every = blocks(parts)
        self.events = [every[number] for number in order]
        self.leaves = [bool(j != ZN - 1 or dx or dy) for _, _, dx, dy, j in self.events]

    def sent_before(self, i):
        return {k % self.slots: k for k in range(i) if self.leaves[k]}

    def finals_before(self, i):
        return [k for k in range(i) if not self.leaves[k]]

    @staticmethod
    def buffers(parts):
        total = sum(part[2] for part in parts)
        S = jax.ShapeDtypeStruct
        return [S((total, PACK), jnp.float32), S((4 * ZN * total, PACK), jnp.bfloat16)]

    @staticmethod
    def scratch(parts, ahead, slots):
        n, most = len(parts), max(part[2] for part in parts)
        counts = [layout(ROUTES[part[3]])[1] for part in parts]
        return [pltpu.VMEM((ahead, 2, most, PACK), jnp.bfloat16), pltpu.VMEM((slots, most, PACK), jnp.bfloat16),
                pltpu.VMEM((2, most, PACK), jnp.float32), SEM((n,)), SEM((n, 4, ZN)), SEM((ahead, 2)), SEM((slots,)),
                SEM((2,))] + [
            pltpu.VMEM((count, part[2], PACK), jnp.bfloat16) for count, part in zip(counts, parts)
        ] + [SEM((count,)) for count in counts]

    def source(self, r, dx, dy, zd, core):
        which, start, rows, _ = self.parts[r]
        return self.ins[which].at[self.links.slot(dx, dy, zd, core), pl.ds(start, rows)]

    def sibling(self, r, dx, dy, zd):
        count = self.parts[r][2]
        start = 4 * ZN * self.starts[r] + ((dx * 2 + dy) * ZN + zd) * count
        return self.sib.at[pl.ds(pl.multiple_of(start, 16), count)]

    def child(self, r, d, dx, dy, zd):
        order = ROUTES[self.parts[r][3]]
        dim = d if d in "xy" else "z"
        index = 0
        for e in order[: order.index(dim)]:
            index = index * ZN + zd if e == "z" else index * 2 + (dx if e == "x" else dy)
        if dim == "z":
            index = index * (ZN + 1) + (zd if d == "up" else zd + 1)
        return self.lay[r][0][dim] + index

    def across(self, i):
        _, r, dx, dy, j = self.events[i]
        zd = self.links.spots[j]
        return self.links.copy(self.source(r, dx, dy, zd, 1 - self.links.c), self.sibling(r, dx, dy, zd),
                               self.csend.at[r], self.crecv.at[r, dx * 2 + dy, zd], "core")

    def begin(self):
        for i in range(len(self.events)):
            self.across(i).start()
        for i in range(self.ahead - 1):
            self.prefetch(i)

    def loads(self, i):
        _, r, dx, dy, j = self.events[i]
        zd, s, count = self.links.spots[j], i % self.ahead, self.parts[r][2]
        return [
            pltpu.make_async_copy(ref, self.stage.at[s, k, pl.ds(0, count)], self.lsem.at[s, k])
            for k, ref in enumerate((self.source(r, dx, dy, zd, self.links.c), self.sibling(r, dx, dy, zd)))
        ]

    def prefetch(self, i):
        own, other = self.loads(i)
        own.start()
        self.across(i).wait_recv()
        other.start()

    def terms(self, i):
        _, r, dx, dy, j = self.events[i]
        same = j == ZN - 1
        kids = onward(ROUTES[self.parts[r][3]], dx, dy, same)
        z, zd = self.links.z, self.links.spots[j]
        found = [(self.child(r, d, dx, dy, zd), None) for d in kids if d != "z"]
        if "z" in kids:
            up, down = self.child(r, "up", dx, dy, zd), self.child(r, "dn", dx, dy, zd)
            if same:
                found += [(up, self.links.above), (down, self.links.below)]
            else:
                found.append((jnp.where(z > zd, up, down), jnp.logical_and(self.links.above, self.links.below)))
        return found

    def hop(self, i, d):
        _, r, dx, dy, j = self.events[i]
        zd, q = self.links.spots[j], i % self.slots
        came = {"x": "x", "y": "y", "up": "dn", "dn": "up"}[d]
        at = self.child(r, came, 0 if d == "x" else dx, 0 if d == "y" else dy, zd)
        return self.links.copy(self.ring.at[q, pl.ds(0, self.parts[r][2])], self.bufs[r].at[at],
                               self.send.at[q], self.recv[r].at[at], d)

    def result(self, i, slot):
        r = self.events[i][1]
        count = self.parts[r][2]
        return pltpu.make_async_copy(self.fin.at[slot, pl.ds(0, count)], self.out.at[pl.ds(self.starts[r], count)],
                                     self.fsem.at[slot])

    def step(self, i):
        _, r, dx, dy, j = self.events[i]
        zd, z, s, q = self.links.spots[j], self.links.z, i % self.ahead, i % self.slots
        if i + self.ahead - 1 < len(self.events):
            self.prefetch(i + self.ahead - 1)
        leaves, finals = self.leaves[i], self.finals_before(i)
        slot = len(finals) % 2
        if leaves and q in self.sent_before(i):
            self.hop(self.sent_before(i)[q], "x").wait_send()
        if not leaves and len(finals) > 1:
            self.result(finals[-2], slot).wait()
        for load in self.loads(i):
            load.wait()
        terms = self.terms(i)
        for at, cond in terms:
            slab = self.bufs[r].at[at]
            arrived = self.links.copy(slab, slab, self.send.at[0], self.recv[r].at[at], "core")
            if cond is None:
                arrived.wait_recv()
            else:
                pl.when(cond)(arrived.wait_recv)

        def body(k, _):
            rows = pl.ds(pl.multiple_of(k * 16, 16), 16)
            total = self.stage[s, 0, rows].astype(jnp.float32) + self.stage[s, 1, rows].astype(jnp.float32)
            for at, cond in terms:
                more = self.bufs[r][at, rows].astype(jnp.float32)
                total = total + (more if cond is None else jnp.where(cond, more, 0.0))
            if leaves:
                self.ring[q, rows] = total.astype(jnp.bfloat16)
            else:
                self.fin[slot, rows] = total
            return 0
        lax.fori_loop(0, self.parts[r][2] // 16, body, 0, unroll=3 if self.parts[r][2] % 48 == 0 else 1)
        if not leaves:
            self.result(i, slot).start()
            return
        d = arrival(ROUTES[self.parts[r][3]], dx, dy, j == ZN - 1)
        if d == "z":
            pl.when(zd > z)(lambda: self.hop(i, "up").start())
            pl.when(zd < z)(lambda: self.hop(i, "dn").start())
        else:
            self.hop(i, d).start()

    def finish(self):
        for i in self.sent_before(len(self.events)).values():
            self.hop(i, "x").wait_send()
        finals = self.finals_before(len(self.events))
        for k in range(max(0, len(finals) - 2), len(finals)):
            self.result(finals[k], k % 2).wait()
        for r, part in enumerate(self.parts):
            whole = self.sib.at[pl.ds(4 * ZN * self.starts[r], 4 * ZN * part[2])]
            self.links.copy(whole, whole, self.csend.at[r], self.crecv.at[r, 0, 0], "core").wait_send()


def scatter(parts, order, ins):
    n = len(ins)

    def kernel(*refs):
        job = Scatter(parts, order, refs[:n], *refs[n:])
        greet(job.links, None)
        job.begin()
        for i in range(len(job.events)):
            job.step(i)
        job.finish()
    anywhere = pl.BlockSpec(memory_space=pl.ANY)
    outs = Scatter.buffers(parts)
    return pl.pallas_call(
        kernel,
        out_shape=outs,
        in_specs=[anywhere] * n,
        out_specs=[anywhere] * len(outs),
        scratch_shapes=Scatter.scratch(parts, 4, 24),
        compiler_params=pltpu.CompilerParams(collective_id=2, has_side_effects=True, vmem_limit_bytes=60 << 20),
    )(*ins)[0]


class Sends:
    def __init__(self, sems):
        self.sems, self.used = sems, []

    def add(self, src, dst):
        copy = pltpu.make_async_copy(src, dst, self.sems.at[len(self.used)])
        self.used.append(copy)
        return copy

    def finish(self):
        for copy in self.used:
            copy.wait()


def undeal(lines, n, count):
    length = n * count
    spot = lax.broadcasted_iota(jnp.int32, (LANES, length), 1)
    row = lax.broadcasted_iota(jnp.int32, (LANES, length), 0)
    pick = jnp.where(lax.rem(spot, count) == row, 1.0, 0.0).astype(BF16)
    lane = lax.broadcasted_iota(jnp.int32, (n, length), 1)
    owner = lax.broadcasted_iota(jnp.int32, (n, length), 0)
    own = jnp.logical_and(lane >= owner * count, lane < (owner + 1) * count)
    return jnp.sum(jnp.where(own, dot(lines, pick), 0.0), axis=0, keepdims=True)


def softplus(value):
    small = jnp.exp(-jnp.abs(value))
    series = small * (1.0 - small * (1 / 2 - small * (1 / 3 - small * (1 / 4 - small * (1 / 5 - small * (1 / 6))))))
    return jnp.maximum(value, 0.0) + jnp.where(small < 0.02, series, jnp.log(1.0 + small))


FORWARD_OUTS = 13
GATHER_PARTS = ((0, 0, 0, 64, 0), (0, 0, 64, 80, 1), (0, 0, 144, 80, 2), (0, 0, 224, 80, 3),
                (1, 1, 0, 64, 0), (1, 1, 64, 80, 1), (1, 1, 144, 64, 2), (1, 1, 208, 80, 3))
REC_PARTS = (0, 1, 2, 3)
FORWARD_PLAN = (
    (24, 25, 26, 27, 89, 17, 9, 59, 1, 18, 16, 8, 19, 90, 49, 11, 91, 48, 58, 10, 2, 57, 88, 28, 0, 82, 51, 56, 3, 65, 73, 121, 113, 75, 43, 42, 74, 41, 50, 30, 33, 115, 80, 31, 123, 66, 72, 60, 35, 29, 112, 64, 81, 106, 67, 32, 120, 34, 22, 23, 105, 94, 114, 107, 122, 14, 97, 95, 98, 15, 62, 104, 83, 63, 20, 92, 21, 40, 61, 96, 99),
    (),
    (),
    (12,),
    (13,),
    (55,),
    (87,),
    (6,),
    (84,),
    (47,),
    (86,),
    (125, 4),
    (45,),
    (38,),
    (),
    (119, 7),
    (36, 5),
    (53, 124, 79, 126, 78),
    (68,),
    (),
    (111, 116, 46, 118),
    (69, 37, 76, 85, 93, 39),
    (117,),
    (77, 54, 70),
    (108, 71, 52, 109, 102, 127, 110, 44, 101, 100, 103),
)


def forward_kernel(batch, width, n_seq, info_ref, x_ref, rim_ref, lines_ref, *refs):
    shards, refs = refs[:8], refs[8:]
    outs, refs = refs[:FORWARD_OUTS], refs[FORWARD_OUTS:]
    (gate_o, inner_o, mixed_o, normed_o, rate_o, entry_o, decay_o, states_o, pseg_o, sstart_o, all_o,
     gated_o, first_o) = outs
    normed2_o, vec_o, gain_o, gain2_o, weights, ffn_weights = refs[:6]
    (ext, gate, inner, mixed, rate, entry, decay, drive, states, pseg, hseg, sstart, gated, first, normed2,
     vec_ref, gain_ref, gain2_ref, small, wbuf, shard_ref, ffn_shard_ref, sems, wsem, psem) = refs[6:31]
    swap = Exchange(n_seq, *refs[31:36])
    job = Gather(GATHER_PARTS, [shard_ref, ffn_shard_ref], [weights, ffn_weights], *refs[36:])
    step = pl.program_id(0)
    tokens, depth = x_ref.shape
    r = mixed.shape[1]
    parts, tiles = r // W, W // LANES
    step = step - 1
    steps = 3 * parts + 1
    span = width + 8
    n = weights.shape[0]
    rows, rrows = depth // n, r // n

    def pump(half, low, high):
        for s in range(low, high):
            numbers = FORWARD_PLAN[4 + 2 * s + half]
            if numbers:
                @pl.when(step == s)
                def _():
                    for number in numbers:
                        job.forward(job.events[number])

    def pack():
        gate_w, input_w, rate_w, entry_w, out_w, ffn_gate_w, ffn_up_w, ffn_down_w = shards
        moves = ([], [])
        for which, one, two, base in ((0, rate_w, entry_w, GATES_AT), (0, gate_w, input_w, IN_AT), (1, ffn_gate_w, ffn_up_w, UPS_AT)):
            count, length = one.shape
            to = (shard_ref, ffn_shard_ref)[which]
            for j in range(length // W):
                for half, src in enumerate((one, two)):
                    moves[which].append((src.at[:, pl.ds(j * W, W)], to.at[pl.ds(base + j * count, count), pl.ds(half * W, W)]))
        moves[0].append((out_w, shard_ref.at[pl.ds(OUT_AT, rrows)]))
        moves[0].append((lines_ref, shard_ref.at[pl.ds(REC_ROWS, SMALL_ROWS)]))
        moves[1].append((ffn_down_w, ffn_shard_ref.at[pl.ds(DOWN_AT, ffn_down_w.shape[0])]))
        copies, k = ([], []), 0
        for which in range(2):
            for src, dst in moves[which]:
                copies[which].append(pltpu.make_async_copy(src, dst, psem.at[k]))
                k += 1
        return copies

    blocks_at = [(IN_AT + j * rows, rows) for j in range(parts)] + [(GATES_AT + j * rrows, rrows) for j in range(parts)]
    blocks_at += [(OUT_AT, rrows)]

    def load(k):
        start, count = blocks_at[k]
        return pltpu.make_async_copy(weights.at[:, pl.ds(start, count)], wbuf.at[k % 2, :, pl.ds(0, count)], wsem.at[k % 2])

    def next_block(k):
        if k + 1 < len(blocks_at):
            load(k + 1).start()
        load(k).wait()
    sends = Sends(sems)
    branch_sends = [sends.add(gate, gate_o), sends.add(inner, inner_o), sends.add(mixed, mixed_o),
                    sends.add(ext.at[pl.ds(0, tokens)], normed_o)]
    gate_sends = [sends.add(rate, rate_o), sends.add(entry, entry_o), sends.add(decay, decay_o), sends.add(pseg, pseg_o)]
    state_sends = [sends.add(states, states_o), sends.add(sstart, sstart_o), sends.add(swap.land, all_o),
                   sends.add(gated, gated_o)]
    last_sends = [sends.add(first, first_o), sends.add(normed2, normed2_o)]
    vector_sends = [sends.add(vec_ref, vec_o), sends.add(gain_ref, gain_o), sends.add(gain2_ref, gain2_o)]

    def start(copies):
        for copy in copies:
            copy.start()

    @pl.when(step < 0)
    def _():
        packing = pack()
        start(packing[0] + packing[1])
        greet(job.links, swap)
        for copy in packing[0]:
            copy.wait()
        numbers = FORWARD_PLAN[0]
        for number in numbers[: len(REC_PARTS)]:
            job.forward(job.events[number])
        for copy in packing[1]:
            copy.wait()

        def scaled(i, _):
            at = rows_at(i * CHUNK)
            value = x_ref[at].astype(F32)
            first[at] = value * inverse_norm(value, depth)
            return 0
        lax.fori_loop(0, tokens // CHUNK, scaled, 0)
        for number in numbers[len(REC_PARTS) :]:
            job.forward(job.events[number])
        job.arrived(REC_PARTS)
        lines_in = pltpu.make_async_copy(weights.at[:, pl.ds(REC_ROWS, SMALL_ROWS), pl.ds(0, LANES)], small, wsem.at[1])
        lines_in.start()
        load(0).start()
        for number in FORWARD_PLAN[1]:
            job.forward(job.events[number])
        lines_in.wait()
        lines = small[...].astype(F32)
        found = [undeal(lines[:, k].astype(BF16), n, rows if k < 2 else rrows) for k in range(10)]
        gain_ref[...] = jnp.broadcast_to(found[0], gain_ref.shape)
        gain2_ref[...] = jnp.broadcast_to(found[1], gain2_ref.shape)
        vec_ref[...] = jnp.zeros_like(vec_ref)
        for k in range(7):
            vec_ref[k : k + 1] = found[2 + k]
        vec_ref[COEF : COEF + 1] = -lru_scale * softplus(-found[9])
        vec_ref[SIG : SIG + 1] = sigmoid(-found[9])
        for number in FORWARD_PLAN[2]:
            job.forward(job.events[number])
        gain = gain_ref[:1]

        def norm(i, _):
            at = rows_at(i * CHUNK)
            ext[at] = (first[at] * gain).astype(BF16)
            return 0
        lax.fori_loop(0, tokens // CHUNK, norm, 0)
        rim = rim_ref[...].astype(F32)
        ext[pl.ds(tokens, rim.shape[0])] = (rim * inverse_norm(rim, depth) * gain).astype(BF16)
        start(vector_sends)
        for number in FORWARD_PLAN[3]:
            job.forward(job.events[number])

    for k, s in enumerate(list(range(2 * parts)) + [3 * parts]):
        pl.when(step == s)(lambda k=k: next_block(k))

    @pl.when(jnp.logical_and(step >= 0, step < parts))
    def _():
        j = jnp.clip(step, 0, parts - 1)
        slot = lax.rem(j, 2)
        here = pl.ds(pl.multiple_of(j * W, W), W)
        pump(0, 0, parts)
        got = dot(ext[...], wbuf[slot, :, :rows].reshape(depth, PACK))
        for t in range(tiles):
            gate[j * tiles + t] = got[:tokens, lanes(t)]
        for b in range(batch):
            inner[b * span : b * span + 8, here] = got[tokens + 8 * b : tokens + 8 * b + 8, W:]
            inner[b * span + 8 : (b + 1) * span, here] = got[b * width : (b + 1) * width, W:]
        pump(1, 0, parts)
        for b in range(batch):
            conv = vec_ref[CONV_BIAS : CONV_BIAS + 1, here]
            for lag in range(4):
                conv = conv + vec_ref[lag : lag + 1, here] * inner[b * span + 8 - lag : (b + 1) * span - lag, here]
            mixed[b * width : (b + 1) * width, here] = conv.astype(BF16)

    @pl.when(step == parts - 1)
    def _():
        start(branch_sends)

    @pl.when(jnp.logical_and(step >= parts, step < 2 * parts))
    def _():
        j = jnp.clip(step - parts, 0, parts - 1)
        slot = lax.rem(j + parts, 2)
        pump(0, parts, 2 * parts)
        got = dot(mixed[...], wbuf[slot].reshape(r, PACK))
        for t in range(tiles):
            rate[j * tiles + t] = got[:, lanes(t)]
            entry[j * tiles + t] = got[:, lanes(tiles + t)]
        pump(1, parts, 2 * parts)

        def gating(t, b, spot, at, cols, _):
            g = j * tiles + t
            tile = pl.ds(pl.multiple_of(j * W + t * LANES, LANES), LANES)
            a_rate = sigmoid(rate[g, at] + vec_ref[RATE_BIAS : RATE_BIAS + 1, tile])
            an_entry = sigmoid(entry[g, at] + vec_ref[ENTRY_BIAS : ENTRY_BIAS + 1, tile])
            log_decay = vec_ref[COEF : COEF + 1, tile] * a_rate
            z = 2.0 * log_decay
            root = jnp.sqrt(one_less_exp(z, jnp.exp(z)))
            valid = in_row(spot, width, a_rate.shape) < info_ref[b]
            rate[g, at] = a_rate
            entry[g, at] = an_entry
            decay[g, at] = jnp.where(valid, jnp.exp(log_decay), 1.0)
            drive[g, at] = jnp.where(valid, root * an_entry * mixed[at, tile].astype(F32), 0.0)
            return 0
        each_tile(batch, width, tiles, gating)
        for t in range(tiles):
            g = j * tiles + t
            tile = pl.ds(pl.multiple_of(j * W + t * LANES, LANES), LANES)
            for b in range(batch):
                prod = jnp.ones((SEGS, LANES), F32)
                state = jnp.zeros((SEGS, LANES), F32)
                for s in range(width // SEGS):
                    at = strided(b, width, s)
                    a = decay[g, at]
                    state = a * state + drive[g, at]
                    prod = prod * a
                pseg[b * SEGS : (b + 1) * SEGS, tile] = prod
                hseg[b * SEGS : (b + 1) * SEGS, tile] = state
                whole, end = prod[:1], state[:1]
                for i in range(1, SEGS):
                    whole = whole * prod[i : i + 1]
                    end = prod[i : i + 1] * end + state[i : i + 1]
                swap.rows[g, b : b + 1] = whole
                swap.rows[g, batch + b : batch + b + 1] = end

    @pl.when(step == 2 * parts - 1)
    def _():
        start(gate_sends)
        swap.begin()

    @pl.when(step == 2 * parts)
    def _():
        swap.finish()

    @pl.when(jnp.logical_and(step >= 2 * parts, step < 3 * parts))
    def _():
        j = jnp.clip(step - 2 * parts, 0, parts - 1)
        me = lax.axis_index("seq")
        pump(0, 2 * parts, 3 * parts)
        for t in range(tiles):
            g = j * tiles + t
            tile = pl.ds(pl.multiple_of(j * W + t * LANES, LANES), LANES)
            for b in range(batch):
                begin = jnp.zeros((1, LANES), F32)
                for k in range(n_seq):
                    new = swap.land[k, g, b : b + 1] * begin + swap.land[k, g, batch + b : batch + b + 1]
                    begin = jnp.where(k < me, new, begin)
                for i in range(SEGS):
                    at = b * SEGS + i
                    sstart[at : at + 1, tile] = begin
                    begin = pseg[at : at + 1, tile] * begin + hseg[at : at + 1, tile]
                state = sstart[b * SEGS : (b + 1) * SEGS, tile]
                for s in range(width // SEGS):
                    at = strided(b, width, s)
                    state = decay[g, at] * state + drive[g, at]
                    states[g, at] = state
        pump(1, 2 * parts, 3 * parts)

        def gating(t, b, spot, at, cols, _):
            g = j * tiles + t
            tile = pl.ds(pl.multiple_of(j * W + t * LANES, LANES), LANES)
            gated[at, tile] = (states[g, at] * gelu_both(gate[g, at])[0]).astype(BF16)
            return 0
        each_tile(batch, width, tiles, gating)

    @pl.when(step == 3 * parts - 1)
    def _():
        start(state_sends)

    @pl.when(step >= 3 * parts)
    def _():
        pump(0, 3 * parts, steps)
        first[...] = x_ref[...].astype(F32) + dot(gated[...], wbuf[(2 * parts) % 2].reshape(r, depth))
        pump(1, 3 * parts, steps)

    @pl.when(step == steps - 1)
    def _():
        def norm(i, _):
            at = rows_at(i * CHUNK)
            value = first[at]
            normed2[at] = (value * inverse_norm(value, depth) * gain2_ref[:1]).astype(BF16)
            return 0
        lax.fori_loop(0, tokens // CHUNK, norm, 0)
        start(last_sends)
        for number in FORWARD_PLAN[-1]:
            job.forward(job.events[number])
        job.arrived([r for r in range(len(GATHER_PARTS)) if r not in REC_PARTS])
        job.sent()
        sends.finish()


def forward(info, tokens2, rim, lines, shards, batch, n_seq, r):
    tokens, depth = tokens2.shape
    n = n_seq * ZN
    parts, tiles = r // W, r // LANES
    full = lambda a: pl.BlockSpec(a.shape, lambda j: (0,) * a.ndim)
    anywhere = pl.BlockSpec(memory_space=pl.ANY)
    S = jax.ShapeDtypeStruct
    flat, tall, segs = S((tokens, r), BF16), S((tiles, tokens, LANES), F32), S((batch * SEGS, r), F32)
    inner, ends = S((tokens + 8 * batch, r), F32), S((n_seq, tiles, 2 * batch, LANES), F32)
    first, normed, vec, gain = S((tokens, depth), F32), S((tokens, depth), BF16), S((16, r), F32), S((8, depth), F32)
    outs = [tall, inner, flat, normed, tall, tall, tall, tall, segs, segs, ends, flat, first, normed, vec, gain, gain,
            S((n, REC_ROWS + SMALL_ROWS, PACK), BF16), S((n, FFN_ROWS, PACK), BF16)]
    vm = lambda s: pltpu.VMEM(s.shape, s.dtype)
    scratch = [pltpu.VMEM((tokens + 8 * batch, depth), BF16)] + [
        vm(s) for s in (tall, inner, flat, tall, tall, tall, tall, tall, segs, segs, segs, flat, first, normed, vec, gain, gain)]
    scratch += [pltpu.VMEM((n, SMALL_ROWS, LANES), BF16), pltpu.VMEM((2, n, r // n, PACK), BF16),
                pltpu.VMEM((REC_ROWS + SMALL_ROWS, PACK), BF16), pltpu.VMEM((FFN_ROWS, PACK), BF16)]
    return pl.pallas_call(
        functools.partial(forward_kernel, batch, tokens // batch, n_seq),
        grid=(3 * parts + 2,),
        in_specs=[pl.BlockSpec(memory_space=pltpu.SMEM), full(tokens2), full(rim)] + [anywhere] * (1 + len(shards)),
        out_specs=[anywhere] * len(outs),
        out_shape=outs,
        scratch_shapes=scratch + [SEM((FORWARD_OUTS + 4,)), SEM((2,)), SEM((32,))] + Exchange.scratch(n_seq, (tiles, 2 * batch, LANES))
        + Gather.scratch(GATHER_PARTS),
        compiler_params=pltpu.CompilerParams(collective_id=3, has_side_effects=True, vmem_limit_bytes=62 << 20),
    )(info, tokens2, rim, lines, *shards)


FFN_SCATTER = ((0, 0, 144, 2), (0, 144, 144, 3))
REC_SCATTER = ((0, 0, 64, 0), (0, 64, 64, 1), (0, 128, 48, 2), (0, 176, 48, 3), (0, 224, 32, 2), (0, 256, 32, 3), (1, 0, 16, 0))
BACKWARD_PLAN = (
    (17, 8, 25, 21, 26),
    (),
    (),
    (),
    (0, 19),
    (24,),
    (27, 1, 30),
    (10,),
    (12, 9),
    (),
    (),
    (),
    (16,),
    (),
    (29,),
    (),
    (),
    (31,),
    (2,),
    (28,),
    (),
    (),
    (11,),
    (),
    (),
    (18,),
    (),
    (),
    (),
    (3, 23, 20, 13),
    (),
    (),
    (4,),
    (5,),
    (14, 22, 15),
    (),
    (6, 7),
)
REC_ORDER = (
    97, 90, 88, 89, 85, 30, 84, 61, 57, 62, 86, 60, 59, 28, 91, 104, 2, 95, 98, 56,
    33, 34, 93, 58, 29, 68, 87, 94, 5, 99, 3, 35, 44, 0, 39, 103, 102, 63, 67, 92,
    46, 96, 31, 6, 109, 78, 12, 32, 38, 1, 41, 69, 64, 75, 65, 37, 7, 66, 36, 53,
    101, 100, 108, 74, 107, 51, 40, 80, 105, 47, 71, 76, 4, 70, 11, 9, 43, 106, 48, 10,
    73, 45, 13, 8, 16, 81, 72, 110, 49, 42, 111, 15, 50, 52, 18, 17, 77, 79, 14, 54,
    19, 20, 82, 83, 22, 55, 25, 21, 24, 23, 26, 27,
)


def backward_kernel(batch, width, n_seq, *refs):
    (info_ref, gain_ref, ggain2_ref, vec_ref, pseg_ref, sstart_ref, pall_ref, wo_ref, wr_ref, wi_ref,
     states_ref, decay_ref, gate_ref, rate_ref, entry_ref, gated_ref, inner_ref,
     dlow_h, dfirst_h, mixed_h, normed_h, x_h, gf, token_h, gr, gs, total_h, sib_h,
     low, tall, hid, dn, one, two, both, ext, stage, mixed, normed,
     gseg, gstart, sums, csums, ggain, rims, rim_land, ends, sem, lsem, osem, rimsem) = refs[:51]
    swap = Exchange(n_seq, *refs[51:56])
    job = Scatter(FFN_SCATTER, sum(BACKWARD_PLAN, ()), (gf,), total_h, sib_h, *refs[56:])
    step = pl.program_id(0)
    tokens, depth = low.shape
    n = gf.shape[0]
    r = mixed.shape[1]
    rows, rrows = depth // n, r // n
    group = wo_ref.shape[0]
    thin = group * rrows
    tiles, few, rt = W // LANES, thin // LANES, r // LANES
    counts = backward_steps(n, r, group)
    at, total_steps = {}, 0
    for name, count in counts:
        at[name] = total_steps
        total_steps += count
    size = dict(counts)
    span = width + 8
    me = lax.axis_index("seq")

    def phase(name):
        return jnp.logical_and(step >= at[name], step < at[name] + size[name])

    def index(name):
        return jnp.clip(step - at[name], 0, size[name] - 1)

    def cols(start, count):
        return pl.ds(pl.multiple_of(start, LANES), count)

    def when_step(s, act):
        pl.when(step == s)(act)

    def outgoing(first, value, dst):
        devices, count = value.shape[:2]
        stage[first : first + devices, :count] = value
        pltpu.make_async_copy(stage.at[pl.ds(first, devices), pl.ds(0, count)], dst, sem).start()

    def wait_out(devices, count):
        src = stage.at[pl.ds(0, devices), pl.ds(0, count)]
        pltpu.make_async_copy(src, gr.at[pl.ds(0, devices), pl.ds(0, count)], sem).wait()

    inputs = [pltpu.make_async_copy(src, dst, lsem.at[k]) for k, (src, dst) in enumerate(
        ((dlow_h, low), (mixed_h, mixed), (normed_h, normed), (x_h, low),
         (dfirst_h, tall.at[pl.ds(0, depth // LANES)])))]
    rim_copy = pltpu.make_async_remote_copy(rims, rim_land, rimsem.at[0], rimsem.at[1],
                                            device_id=(lax.rem(me + n_seq - 1, n_seq), swap.z), device_id_type=MESH)

    numbers = [list(range(sum(map(len, BACKWARD_PLAN[:k])), sum(map(len, BACKWARD_PLAN[: k + 1])))) for k in range(2 * total_steps + 1)]

    def pump(half, name):
        for s in range(at[name], at[name] + size[name]):
            if numbers[2 * s + half]:
                @pl.when(step == s)
                def _():
                    for i in numbers[2 * s + half]:
                        job.step(i)

    @pl.when(step == 0)
    def _():
        for copy in inputs[:3]:
            copy.start()
        greet(job.links, swap)
        job.begin()

        @pl.when(me == n_seq - 1)
        def _():
            rim_land[...] = jnp.zeros_like(rim_land)
        inputs[0].wait()

    for name, _ in counts:
        pump(0, name)

    @pl.when(step == at["E"])
    def _():
        wait_out(group, rrows)
        inputs[1].wait()
        inputs[3].start()
        swap.finish()
        for b in range(batch):
            grad = jnp.zeros((rt, LANES), F32)
            for q in reversed(range(n_seq)):
                new = pall_ref[q][:, b] * grad + swap.land[q][:, b]
                grad = jnp.where(q > me, new, grad)
            ends[b] = grad

    @pl.when(step == at["R"])
    def _():
        inputs[4].start()

    @pl.when(step == at["M"])
    def _():
        wait_out(n, rrows)

    @pl.when(phase("U"))
    def _():
        k = index("U")
        total = dot_back(low[...], wo_ref[...].reshape(thin, depth))
        for t in range(few):
            tall[k * few + t] = total[:, lanes(t)]

        def gating(t, b, spot, here, tile, _):
            gate, slope = gelu_both(gate_ref[t, here])
            d = tall[k * few + t, here]
            tall[k * few + t, here] = d * gate
            both[here, pair_cols(k * few + t, 0)] = (d * states_ref[t, here] * slope).astype(BF16)
            return 0
        each_tile(batch, width, few, gating)
        value = dot_outer(gated_ref[...], low[...]).astype(BF16).reshape(group, rrows, depth)
        pl.when(k > 0)(lambda: wait_out(group, rrows))
        outgoing(0, value, gr.at[pl.ds(k * group, group), pl.ds(OUT_AT, rrows)])
        pump(1, "U")
        for t in range(few):
            tile = cols(k * thin + t * LANES, LANES)
            for b in range(batch):
                grad = jnp.zeros((SEGS, LANES), F32)
                for s in reversed(range(width // SEGS)):
                    here = strided(b, width, s)
                    grad = decay_ref[t, here] * (tall[k * few + t, here] + grad)
                gseg[b * SEGS : (b + 1) * SEGS, tile] = grad
                whole = grad[SEGS - 1 :]
                for i in reversed(range(SEGS - 1)):
                    whole = grad[i : i + 1] + pseg_ref[b * SEGS + i : b * SEGS + i + 1, tile] * whole
                swap.rows[k * few + t, b : b + 1] = whole

    @pl.when(step == at["U"] + size["U"] - 1)
    def _():
        swap.begin()

    @pl.when(phase("E"))
    def _():
        k = index("E")
        for t in range(few):
            g = k * few + t
            tile = cols(k * thin + t * LANES, LANES)
            for b in range(batch):
                grad = ends[b, pl.ds(g, 1)]
                for i in reversed(range(SEGS)):
                    line = b * SEGS + i
                    gstart[i : i + 1] = grad
                    grad = pseg_ref[line : line + 1, tile] * grad + gseg[line : line + 1, tile]
                grad = gstart[...]
                for s in reversed(range(width // SEGS)):
                    here = strided(b, width, s)
                    total = tall[g, here] + grad
                    one[t, here] = total
                    grad = decay_ref[t, here] * total
                    before = states_ref[t, strided(b, width, s - 1)] if s else sstart_ref[b * SEGS : (b + 1) * SEGS, tile]
                    two[t, here] = grad * before

        pump(1, "E")

        def gating(t, b, spot, here, _, kept):
            tile = cols(k * thin + t * LANES, LANES)
            coef = vec_ref[COEF : COEF + 1, tile]
            rate, entry = rate_ref[t, here], entry_ref[t, here]
            valid = in_row(spot, width, rate.shape) < info_ref[b]
            grad = jnp.where(valid, one[t, here], 0.0)
            z = 2.0 * coef * rate
            exp_z = jnp.exp(z)
            under = one_less_exp(z, exp_z)
            inverse = lax.rsqrt(under)
            root = under * inverse
            value = mixed[here, tile].astype(F32)
            part = grad * entry
            d_log = jnp.where(valid, two[t, here], 0.0) - part * value * exp_z * inverse
            d_rate = coef * d_log * rate * (1.0 - rate)
            straight = part * root
            d_entry = straight * value * (1.0 - entry)
            tall[rt + k * few + t, here] = straight
            hid[here, pair_cols(k * few + t, 0)] = d_rate.astype(BF16)
            hid[here, pair_cols(k * few + t, 1)] = d_entry.astype(BF16)
            return (kept[0] + fold8(d_log * rate), kept[1] + fold8(d_rate), kept[2] + fold8(d_entry))
        zero = jnp.zeros((8, LANES), F32)
        for t, kept in enumerate(each_tile(batch, width, few, gating, (zero, zero, zero))):
            tile = cols(k * thin + t * LANES, LANES)
            for line in range(3):
                factor = 8.0 * vec_ref[SIG : SIG + 1, tile] if line == 0 else 1.0
                sums[line : line + 1, tile] = factor * jnp.sum(kept[line], axis=0, keepdims=True)

    @pl.when(phase("R"))
    def _():
        j = index("R")
        grads = hid[:, cols(j * PACK, PACK)]
        pl.when(j > 0)(lambda: wait_out(n, rrows))
        for half in range(2):
            value = dot_outer(mixed[:, half * r // 2 : (half + 1) * r // 2], grads).astype(BF16)
            dst = gr.at[pl.ds(half * n // 2, n // 2), pl.ds(pl.multiple_of(GATES_AT + j * rrows, 16), rrows)]
            outgoing(half * n // 2, value.reshape(n // 2, rrows, PACK), dst)
            if half == 0:
                pump(1, "R")

    @pl.when(phase("M"))
    def _():
        k = index("M")
        total = jnp.zeros((tokens, thin), F32)
        for p in range(r // W):
            weights = wr_ref[:, p * rrows : (p + 1) * rrows].reshape(thin, PACK)
            total = total + dot_back(hid[:, p * PACK : (p + 1) * PACK], weights)
        for t in range(few):
            tall[rt + k * few + t] += total[:, lanes(t)]
        pump(1, "M")

    @pl.when(step == at["M"] + size["M"] - 1)
    def _():
        for b in range(batch):
            rims[:, b * 4 : b * 4 + 4] = tall[rt : 2 * rt, b * width : b * width + 4]
        pl.when(me > 0)(rim_copy.start)

    @pl.when(step == at["I"])
    def _():
        inputs[2].wait()
        pl.when(me < n_seq - 1)(rim_copy.wait_recv)
        pl.when(me > 0)(rim_copy.wait_send)

    @pl.when(phase("I"))
    def _():
        j = index("I")
        here = cols(j * W, W)
        for t in range(tiles):
            for b in range(batch):
                ext[b * span : b * span + width, lanes(t)] = tall[rt + j * tiles + t, b * width : (b + 1) * width]
                ext[b * span + width : b * span + width + 4, lanes(t)] = rim_land[j * tiles + t, b * 4 : b * 4 + 4]
        for b in range(batch):
            total = jnp.zeros((width, W), F32)
            for lag in range(4):
                total = total + vec_ref[lag : lag + 1, here] * ext[b * span + lag : b * span + lag + width]
            both[b * width : (b + 1) * width, cols(j * PACK + W, W)] = total.astype(BF16)
        for lag in range(5):
            total = jnp.zeros((1, W), F32)
            for b in range(batch):
                value = ext[b * span : b * span + width]
                if lag < 4:
                    value = value * inner_ref[b * span + 8 - lag : (b + 1) * span - lag]
                total = total + jnp.sum(value, axis=0, keepdims=True)
            csums[lag : lag + 1, here] = total
        pump(1, "I")
        grads = both[:, cols(j * PACK, PACK)]
        more = dot_back(grads, wi_ref[...].reshape(depth, PACK))

        @pl.when(j == 0)
        def _():
            dn[...] = more

        @pl.when(j > 0)
        def _():
            dn[...] += more
        value = dot_outer(normed[...], grads).astype(BF16).reshape(n, rows, PACK)
        pl.when(j > 0)(lambda: wait_out(n, rows))
        outgoing(0, value, gr.at[:, pl.ds(pl.multiple_of(IN_AT + j * rows, 16), rows)])

    @pl.when(step == total_steps - 1)
    def _():
        inputs[3].wait()
        inputs[4].wait()

        def finish(i, total):
            here = rows_at(i * CHUNK)
            value, grad = low[here].astype(F32), dn[here]
            scale = inverse_norm(value, depth)
            weighted = grad * gain_ref[:1]
            mean = jnp.sum(weighted * value, axis=-1, keepdims=True) * (1.0 / depth)
            first = jnp.concatenate([tall[t, here] for t in range(depth // LANES)], axis=1)
            dn[here] = first + scale * weighted - value * (scale * scale * scale * mean)
            return total + fold8(grad * value * scale)
        ggain[...] = lax.fori_loop(0, tokens // CHUNK, finish, jnp.zeros((8, depth), F32))
        pltpu.make_async_copy(dn, token_h, osem.at[0]).start()
        wait_out(n, rows)
        small = stage.at[:, pl.ds(0, SMALL_ROWS)]
        small[...] = jnp.zeros((n, SMALL_ROWS, PACK), BF16)
        lines = [(jnp.sum(ggain[...], axis=0, keepdims=True), rows), (jnp.sum(ggain2_ref[...], axis=0, keepdims=True), rows)]
        lines += [(csums[k : k + 1], rrows) for k in range(5)] + [(sums[k : k + 1], rrows) for k in (1, 2, 0)]
        for k, (line, count) in enumerate(lines):
            stage[:, k, :LANES] = deal(line, n, count)
        small_out = pltpu.make_async_copy(small, gs, osem.at[1])
        small_out.start()
        small_out.wait()
        for i in numbers[-1]:
            job.step(i)
        job.finish()
        pltpu.make_async_copy(dn, token_h, osem.at[0]).wait()


def deal(line, n, count):
    length = n * count
    lane = lax.broadcasted_iota(jnp.int32, (n, length), 1)
    row = lax.broadcasted_iota(jnp.int32, (n, length), 0)
    own = jnp.where(jnp.logical_and(lane >= row * count, lane < (row + 1) * count), line, 0.0).astype(BF16)
    spot = lax.broadcasted_iota(jnp.int32, (length, LANES), 0)
    col = lax.broadcasted_iota(jnp.int32, (length, LANES), 1)
    pick = jnp.where(jnp.logical_and(lax.rem(spot, count) == col, col < count), 1.0, 0.0).astype(BF16)
    return dot(own, pick).astype(BF16)


def backward_steps(n, r, group):
    parts = n // group
    return (("U", parts), ("E", parts), ("R", r // W), ("M", parts), ("I", r // W))


def backward(info, gain, ggain2, vec, pseg, sstart, pall, packed, states, decay, gate_pre, rate, entry, gated,
             inner, d_low, d_first, mixed, normed, x, grad_ffn, batch):
    tokens, depth = x.shape
    width = tokens // batch
    n, r = packed.shape[0], vec.shape[1]
    group = 8
    rows, rrows = depth // n, r // n
    thin = group * rrows
    few, tiles = thin // LANES, W // LANES
    n_seq = pall.shape[0]
    counts = backward_steps(n, r, group)
    at, steps = {}, 0
    for name, count in counts:
        at[name] = steps
        steps += count
    size = dict(counts)
    clamp = lambda j, name: jnp.clip(j - at[name], 0, size[name] - 1)
    full = lambda a: pl.BlockSpec(a.shape, lambda j: (0,) * a.ndim, pipeline_mode=pl.Buffered(buffer_count=1))
    anywhere = pl.BlockSpec(memory_space=pl.ANY)

    def two_phases(j, one, two):
        return jnp.where(j < at[two], clamp(j, one), clamp(j, two))
    twice = pl.BlockSpec((few, tokens, LANES), lambda j: (two_phases(j, "U", "E"), 0, 0))
    early = pl.BlockSpec((few, tokens, LANES), lambda j: (clamp(j, "U"), 0, 0))
    late = pl.BlockSpec((few, tokens, LANES), lambda j: (clamp(j, "E"), 0, 0))
    in_specs = [pl.BlockSpec(memory_space=pltpu.SMEM)] + [full(a) for a in (gain, ggain2, vec, pseg, sstart, pall)] + [
        pl.BlockSpec((group, rrows, PACK), lambda j: (clamp(j, "U"), OUT_AT // rrows, 0)),
        pl.BlockSpec((group, r // W * rrows, PACK), lambda j: (clamp(j, "M"), GATES_AT // (r // W * rrows), 0)),
        pl.BlockSpec((n, rows, PACK), lambda j: (0, IN_AT // rows + clamp(j, "I"), 0)),
        twice, twice, early, late, late,
        pl.BlockSpec((tokens, thin), lambda j: (0, clamp(j, "U"))),
        pl.BlockSpec((inner.shape[0], W), lambda j: (0, clamp(j, "I"))),
    ] + [anywhere] * 6
    S = jax.ShapeDtypeStruct
    outs = [S((tokens, depth), F32), S((n, REC_ROWS, PACK), BF16), S((n, SMALL_ROWS, PACK), BF16)]
    outs += Scatter.buffers(FFN_SCATTER)
    vm = pltpu.VMEM
    scratch = [
        vm((tokens, depth), BF16), vm((2 * r // LANES, tokens, LANES), F32), vm((tokens, 2 * r), BF16),
        vm((tokens, depth), F32), vm((few, tokens, LANES), F32), vm((few, tokens, LANES), F32),
        vm((tokens, 2 * r), BF16), vm((tokens + 8 * batch, W), F32), vm((n, rrows, PACK), BF16),
        vm((tokens, r), BF16), vm((tokens, depth), BF16), vm((batch * SEGS, r), F32), vm((SEGS, LANES), F32),
        vm((8, r), F32), vm((8, r), F32), vm((8, depth), F32), vm((r // LANES, 4 * batch, LANES), F32),
        vm((r // LANES, 4 * batch, LANES), F32), vm((batch, r // LANES, LANES), F32), SEM, SEM((5,)), SEM((2,)), SEM((2,)),
    ] + Exchange.scratch(n_seq, (r // LANES, batch, LANES)) + Scatter.scratch(FFN_SCATTER, 3, 8)
    got = pl.pallas_call(
        functools.partial(backward_kernel, batch, width, n_seq),
        grid=(steps,),
        in_specs=in_specs,
        out_specs=[anywhere] * len(outs),
        out_shape=outs,
        scratch_shapes=scratch,
        compiler_params=pltpu.CompilerParams(collective_id=4, has_side_effects=True, vmem_limit_bytes=64 << 20),
    )(info, gain, ggain2, vec, pseg, sstart, pall, packed, packed, packed,
      states, decay, gate_pre, rate, entry, gated, inner, d_low, d_first, mixed, normed, x, grad_ffn)
    return got[0], got[1], got[2], got[3]


GATES_AT, OUT_AT, IN_AT, REC_ROWS = 0, 144, 192, 288
UPS_AT, DOWN_AT, FFN_ROWS, SMALL_ROWS = 0, 192, 288, 16


def unpack_pair(item, rows, cols):
    blocks = [item[j * rows : (j + 1) * rows] for j in range(cols // W)]
    return tuple(jnp.concatenate([block[:, half * W : (half + 1) * W] for block in blocks], axis=1) for half in range(2))


def pad_rows(item, before, count):
    batch, rows, cols = item.shape
    item = jnp.pad(item, ((0, 0), (before, count - rows - before), (0, 0)))
    return item.reshape(batch * count, cols)


def per_device_packed(tokens, cotangent, lengths, *shards):
    (gate_proj, input_proj, rate_proj, entry_proj, out_proj, ffn_gate, ffn_up, ffn_down) = shards[:8]
    small = shards[8:]
    batch, width, depth = tokens.shape
    r, f = gate_proj.shape[1], ffn_gate.shape[1]
    n_seq = lax.axis_size("seq")
    me = lax.axis_index("seq")
    rim = pad_rows(from_behind(tokens[:, width - 3 :], "seq", 1), 5, 8)
    widest = max(item.shape[-1] for item in small)
    flat = []
    for item in small:
        flat.append(item.reshape(-1))
        if item.shape[-1] < widest:
            flat.append(jnp.zeros((widest - item.shape[-1],), jnp.bfloat16))
    lines = jnp.concatenate(flat).reshape(-1, widest)
    lines = jnp.pad(lines, ((0, SMALL_ROWS - lines.shape[0]), (0, PACK - widest)))
    info = jnp.concatenate([jnp.clip(lengths - me * width, 0, width), me[None]]).astype(jnp.int32)
    tokens2 = tokens.reshape(batch * width, depth)
    cot2 = cotangent.reshape(batch * width, depth)

    (gate_pre, inner, mixed, normed, rate, entry, decay, states, pseg, sstart, pall, gated, first, normed_two, vec,
     norm_gain, ffn_gain, packed, packed_ffn) = forward(info, tokens2, rim, lines, shards[:8], batch, n_seq, r)
    block_out, d_first, d_low, g_ffn_gain, grad_ffn = feed_forward(
        info, first, normed_two, cot2, ffn_gain, packed_ffn, f, batch)
    token_grad, grad_rec, grad_small, total_ffn = backward(
        info, norm_gain, g_ffn_gain, vec, pseg, sstart, pall, packed, states, decay, gate_pre, rate, entry, gated, inner,
        d_low, d_first, mixed, normed, tokens2, grad_ffn, batch)
    total = scatter(REC_SCATTER, REC_ORDER, [grad_rec, grad_small])
    g_rate, g_entry = unpack_pair(total[:OUT_AT], *rate_proj.shape)
    g_gate, g_input = unpack_pair(total[IN_AT:REC_ROWS], *gate_proj.shape)
    g_ffn_gate, g_ffn_up = unpack_pair(total_ffn[:DOWN_AT], *ffn_gate.shape)
    result = [g_gate, g_input, g_rate, g_entry, total[OUT_AT:IN_AT], g_ffn_gate, g_ffn_up, total_ffn[DOWN_AT:]]
    line = REC_ROWS
    for item in small:
        count = item.shape[0] if item.ndim == 2 else 1
        part = total[line : line + count, : item.shape[-1]]
        line += count
        result.append(part.reshape(item.shape))
    return (block_out.reshape(tokens.shape), token_grad.reshape(tokens.shape), *result)


def solution(mesh):
    packs = mesh.shape["seq"] == 8 and mesh.shape["batch"] == ZN
    placed = (
        P("batch", "seq", None),
        P("batch", "seq", None),
        P("batch"),
        P(("seq", "batch"), None),
        P(("seq", "batch"), None),
        P(("seq", "batch"), None),
        P(("seq", "batch"), None),
        P(("seq", "batch"), None),
        P(("seq", "batch"), None),
        P(("seq", "batch"), None),
        P(("seq", "batch"), None),
        P(("seq", "batch")),
        P(("seq", "batch")),
        P(None, ("seq", "batch")),
        P(("seq", "batch")),
        P(("seq", "batch")),
        P(("seq", "batch")),
        P(("seq", "batch")),
    )
    return jax.shard_map(
        per_device_packed if packs else per_device,
        mesh=mesh,
        in_specs=placed,
        out_specs=(
            P("batch", "seq", None),
            P("batch", "seq", None),
            P(("seq", "batch"), None),
            P(("seq", "batch"), None),
            P(("seq", "batch"), None),
            P(("seq", "batch"), None),
            P(("seq", "batch"), None),
            P(("seq", "batch"), None),
            P(("seq", "batch"), None),
            P(("seq", "batch"), None),
            P(("seq", "batch")),
            P(("seq", "batch")),
            P(None, ("seq", "batch")),
            P(("seq", "batch")),
            P(("seq", "batch")),
            P(("seq", "batch")),
            P(("seq", "batch")),
        ),
        check_vma=False,
    )
```
